32 devices in a mesh: member: 2 (over x), horiz: 16 (over z, y, core).
Axes of the slice: x: 2, y: 2, z: 4, core: 2. Of those that a mesh axis runs over, the one named last changes fastest.
Arguments:
- perturbation: float32 [16, 80, 4, 1920], P('member', 'horiz'), parts along dimension 0, may hold values from -36 to 36
- base_state: float32 [8, 80, 4, 1920], P(None, 'horiz'), may hold values from -6 to 6
- target_state: float32 [8, 80, 4, 1920], P(None, 'horiz'), may hold values from -6 to 6
- cost_weight: float32 [80, 1920], P('horiz'), may hold values from 0.5 to 6
- diffusivity: float32 [80, 1920], P('horiz'), may hold values from 0.04 to 0.2
- chan_mix: float32 [8, 4, 4], replicated, may hold values from -3 to 3
- coupler_mix: float32 [4, 4], replicated, may hold values from -3 to 3
- owner_mix: float32 [16, 80, 80], P('horiz'), may hold values from -0.625 to 0.625
- air_temp: float32 [2, 16, 80, 128], P(None, 'horiz'), may hold values from -6 to 6
- wind_speed: float32 [2, 16, 80, 128], P(None, 'horiz'), may hold values from 2 to 12
- wet_list: int32 [16, 75], P('horiz'), may hold values from -1 to 74, as said below
- wet_owner: int32 [16, 75], P('horiz'), may hold values from -1 to 15, as said below
- remap_src: int32 [240], P('horiz'), may hold values from 0 to 79, as said below
- remap_tgt: int32 [240], P('horiz'), may hold values from 0 to 31, as said below
- remap_weight: float32 [240], P('horiz'), may hold values from 0.2 to 0.8
Outputs:
- new_perturbation: float32 [16, 80, 4, 1920], P('member', 'horiz'), parts along dimension 0
The draws below stay inside these ranges and needn't reach their ends.
There are 2 independent parts, one for each index of `member`. The reference program is written for one: setup_inputs(seed, part) draws one part's arguments, and reference() takes and returns one part's arrays. A program takes and returns all parts, laid end to end along the dimension named above; an argument that names none is the same for every part. Nothing has to cross between parts.
Inputs may be any that keep to these rules, and one draw needn't show every extreme that they name: Each row of wet_list names distinct tiles, valid entries first and -1 after them; wet_owner is -1 exactly where wet_list is. Every device lists at least 37 wet tiles and some device lists all 75. Within one device's list no owner appears more than 5 times, and some owner appears exactly 5 times in every device's list. `wet_owner`: see wet_list. `remap_src`: the source row of each entry is one of the rows of the device that holds the entry. `remap_tgt`: each entry's latitude row differs from (2 times its source row) // 5 by at most 1.
All inputs are finite; a program needn't handle non-finite values.
Results may differ from the reference program's by a relative error of at most 0.0001.
Values sent between devices are 32-bit elements; how exact they have to be, the bound alone decides.
No kernel may reach another device: no remote copies, remote signals or barrier semaphores. Data moves between devices by JAX's collectives and lax.ppermute only.
A program may use at most 64 MiB of HBM per device.

```python
import math
import jax
import jax.numpy as jnp
from jax import lax

LEV = 8
TILE = 128
TPR = 15
STEPS = 2
ROWS_DEV = 5
NLON = 1920
TILES_DEV = 75
NY = 80
NLAT = 32
CAP = 5
E_DEV = 15
NREMAP = 240
N_HORIZ = 16


def wet_tables(key):
    base_key = jax.random.fold_in(key, 7)
    key_count, key_full, key_hot, key_tiles, key_slots = jax.random.split(base_key, 5)
    counts = jax.random.randint(key_count, (N_HORIZ,), TILES_DEV // 2, TILES_DEV + 1)
    full_device = jax.random.randint(key_full, (), 0, N_HORIZ)
    counts = jnp.where(jnp.arange(N_HORIZ) == full_device, TILES_DEV, counts)
    hot_owner = jax.random.randint(key_hot, (), 0, N_HORIZ)
    slot_total = N_HORIZ * CAP

    def one_device(device):
        tile_order = jax.random.permutation(jax.random.fold_in(key_tiles, device), TILES_DEV)
        others = jax.random.permutation(jax.random.fold_in(key_slots, device), slot_total - CAP)
        others = jnp.where(others >= hot_owner * CAP, others + CAP, others)
        slot_order = jnp.concatenate([hot_owner * CAP + jnp.arange(CAP), others])[:TILES_DEV]
        owners = slot_order // CAP
        live = jnp.arange(TILES_DEV) < counts[device]
        return (jnp.where(live, tile_order, -1), jnp.where(live, owners, -1))
    wet_rows, owner_rows = jax.vmap(one_device)(jnp.arange(N_HORIZ))
    return (wet_rows.astype(jnp.int32), owner_rows.astype(jnp.int32))


def draw_wet_list(key, part):
    return wet_tables(key)[0]


def draw_wet_owner(key, part):
    return wet_tables(key)[1]


def remap_tables(key):
    base_key = jax.random.fold_in(key, 11)
    key_row, key_near = jax.random.split(base_key, 2)
    entry_total = N_HORIZ * E_DEV
    entry_index = jnp.arange(entry_total, dtype=jnp.int32)
    holder = entry_index // E_DEV
    local_row = jax.random.randint(key_row, (entry_total,), 0, ROWS_DEV)
    source = holder * ROWS_DEV + local_row
    target = jnp.clip(source * 2 // 5 + jax.random.randint(key_near, (entry_total,), -1, 2), 0, NLAT - 1)
    return (source.astype(jnp.int32), target.astype(jnp.int32))


def draw_remap_src(key, part):
    return remap_tables(key)[0]


def draw_remap_tgt(key, part):
    return remap_tables(key)[1]


def draw_perturbation(key, part):
    key_noise, key_rows, key_cols = jax.random.split(key, 3)
    shape = (LEV, NY, 4, NLON)
    noise = jnp.clip(jax.random.normal(key_noise, shape, jnp.float32), -6.0, 6.0)
    rise = 3.0 ** (jnp.arange(NY).astype(jnp.float32) / (NY - 1))
    row_scale = rise * 10.0 ** jax.random.uniform(key_rows, (NY,), jnp.float32)
    col_scale = 10.0 ** jax.random.uniform(key_cols, (NLON,), jnp.float32)
    return 0.02 * noise * row_scale[None, :, None, None] * col_scale[None, None, None, :]


def draw_cost_weight(key, part):
    rise = 3.0 ** (jnp.arange(NY).astype(jnp.float32) / (NY - 1))
    factor = 2.0 ** jax.random.uniform(key, (NY, NLON), jnp.float32, -1.0, 1.0)
    return rise[:, None] * factor


def block_scale(rng, dims, shards, smallest, largest):
    level = 1.0
    for axis_at, shards_of in shards:
        draws = jax.random.uniform(jax.random.fold_in(jax.random.fold_in(rng, 6), axis_at), (shards_of,), jnp.float32, smallest / len(shards), largest / len(shards))
        level = level * jnp.repeat(jnp.exp(draws), dims[axis_at] // shards_of).reshape((-1,) + (1,) * (len(dims) - 1 - axis_at))
    return level


def bell_draw(own_key, shape, deviation, reach, shards=(), kind=jnp.bfloat16):
    result = jax.random.normal(own_key, shape, jnp.float32) * deviation
    if len(shards) > 0:
        result = block_scale(own_key, shape, shards, -0.22, 0.18) * result
    return jnp.clip(result, min=-reach, max=reach).astype(kind)


def setup_inputs(seed: int = 0, part: int = 0) -> dict:
    seeds = jax.random.split(jax.random.key(seed), 16)
    part_keys = jax.random.split(jax.random.fold_in(seeds[15], part), 16)
    return {
        "perturbation": draw_perturbation(jax.random.fold_in(jax.random.fold_in(seeds[15], part), 71), part),
        "base_state": bell_draw(seeds[1], (LEV, NY, 4, NLON), 1.0, 6.0, ((1, 16),), jnp.float32),
        "target_state": bell_draw(seeds[2], (LEV, NY, 4, NLON), 1.0, 6.0, ((1, 16),), jnp.float32),
        "cost_weight": draw_cost_weight(jax.random.fold_in(seeds[15], 71), part),
        "diffusivity": jnp.clip(jnp.exp(math.log(0.2) - 1.609438 * jax.random.uniform(seeds[4], (NY, NLON), jnp.float32) ** block_scale(seeds[4], (NY, NLON), ((0, 16),), -0.2, 0.2)), 0.04, 0.2),
        "chan_mix": bell_draw(seeds[5], (LEV, 4, 4), 4 ** -0.5, 3.0, (), jnp.float32),
        "coupler_mix": bell_draw(seeds[6], (4, 4), 4 ** -0.5, 3.0, (), jnp.float32),
        "owner_mix": bell_draw(seeds[7], (N_HORIZ, N_HORIZ * CAP, N_HORIZ * CAP), (N_HORIZ * CAP) ** -0.5, 0.625, ((0, 16),), jnp.float32),
        "air_temp": bell_draw(seeds[8], (STEPS, N_HORIZ, N_HORIZ * CAP, TILE), 1.0, 6.0, ((1, 16),), jnp.float32),
        "wind_speed": jnp.clip(jnp.exp(math.log(12.0) - 1.7917595 * jax.random.uniform(seeds[9], (STEPS, N_HORIZ, N_HORIZ * CAP, TILE), jnp.float32) ** block_scale(seeds[9], (STEPS, N_HORIZ, N_HORIZ * CAP, TILE), ((1, 16),), -0.2, 0.2)), 2.0, 12.0),
        "wet_list": draw_wet_list(jax.random.fold_in(seeds[15], 71), part),
        "wet_owner": draw_wet_owner(jax.random.fold_in(seeds[15], 71), part),
        "remap_src": draw_remap_src(jax.random.fold_in(seeds[15], 71), part),
        "remap_tgt": draw_remap_tgt(jax.random.fold_in(seeds[15], 71), part),
        "remap_weight": jnp.clip(0.2 + 0.6 * jax.random.uniform(seeds[14], (NREMAP,), jnp.float32) ** block_scale(seeds[14], (NREMAP,), ((0, 16),), -0.2, 0.2), 0.2, 0.8),
    }


KAPPA_V = 0.1
TIME_STEP = 0.3
FLUX_RATE = 0.05
FEEDBACK = 0.5
ASCENT = 0.5
EPSILON = 1e-06

def channel_drive(ocean_field, chan_mix):
    return jnp.tanh(jnp.einsum('lck,ljkx->ljcx', chan_mix, ocean_field, precision=lax.Precision.HIGHEST))

def level_diff(ocean_field):
    padded = jnp.pad(ocean_field, ((1, 1), (0, 0), (0, 0), (0, 0)))
    return padded[2:] + padded[:-2] - 2.0 * ocean_field

def ocean_step(ocean_field, diffusivity, chan_mix):
    padded = jnp.pad(ocean_field, ((0, 0), (1, 1), (0, 0), (0, 0)))
    laplacian = padded[:, 2:] + padded[:, :-2] + jnp.roll(ocean_field, -1, axis=3) + jnp.roll(ocean_field, 1, axis=3) - 4.0 * ocean_field
    return ocean_field + diffusivity[None, :, None, :] * laplacian + KAPPA_V * level_diff(ocean_field) + TIME_STEP * channel_drive(ocean_field, chan_mix)

def bulk_flux(ocean_tiles, mixed, air_field, wind_field, coupler_mix):
    contrast = jnp.concatenate([(air_field - ocean_tiles[..., 0, :])[..., None, :], ocean_tiles[..., 1:, :]], axis=-2)
    contrast = contrast + mixed
    forcing = jnp.einsum('ck,...kx->...cx', coupler_mix, contrast, precision=lax.Precision.HIGHEST)
    return FLUX_RATE * wind_field[..., None, :] * jnp.tanh(forcing)

def reference(perturbation, base_state, target_state, cost_weight, diffusivity, chan_mix, coupler_mix, owner_mix, air_temp, wind_speed, wet_list, wet_owner, remap_src, remap_tgt, remap_weight):
    live_mask = wet_owner >= 0
    onehot = (wet_owner[:, :, None] == jnp.arange(N_HORIZ, dtype=jnp.int32)[None, None, :]).astype(jnp.int32)
    earlier = jnp.cumsum(onehot, axis=1) - onehot
    slot_rank = lax.optimization_barrier(jnp.sum(earlier * onehot, axis=2)).astype(jnp.int32)
    tile_safe = jnp.where(live_mask, wet_list, 0).astype(jnp.int32)
    owner_safe = jnp.where(live_mask, wet_owner, 0).astype(jnp.int32)
    slot_index = (jnp.arange(N_HORIZ, dtype=jnp.int32)[:, None] * CAP + jnp.where(live_mask, slot_rank, 0)).astype(jnp.int32)
    device_index = jnp.broadcast_to(jnp.arange(N_HORIZ, dtype=jnp.int32)[:, None], wet_list.shape)
    live_float = live_mask.astype(jnp.float32)

    def couple(ocean_field, hour_index):
        surface = ocean_field[0]
        tile_view = surface.reshape(N_HORIZ, ROWS_DEV, 4, TPR, TILE).transpose(0, 1, 3, 2, 4)
        tile_view = tile_view.reshape(N_HORIZ, TILES_DEV, 4, TILE)
        picked = tile_view[device_index, tile_safe] * live_float[:, :, None, None]
        received = jnp.zeros((N_HORIZ, N_HORIZ * CAP, 4, TILE), jnp.float32).at[owner_safe, slot_index].add(picked)
        mixed_all = jnp.tanh(jnp.einsum('opq,oqcx->opcx', owner_mix, received, precision=lax.Precision.HIGHEST))
        mixed_here = mixed_all[owner_safe, slot_index]
        air_here = air_temp[hour_index][owner_safe, slot_index]
        wind_here = wind_speed[hour_index][owner_safe, slot_index]
        flux_tiles = bulk_flux(picked, mixed_here, air_here, wind_here, coupler_mix) * live_float[:, :, None, None]
        added = jnp.zeros_like(tile_view).at[device_index, tile_safe].add(flux_tiles)
        surface_add = added.reshape(N_HORIZ, ROWS_DEV, TPR, 4, TILE).transpose(0, 1, 3, 2, 4).reshape(NY, 4, NLON)
        return ocean_field.at[0].add(surface_add)

    def remap(ocean_field):
        surface = ocean_field[0, :, 0, :]
        weighted = surface[remap_src] * remap_weight[:, None]
        summed = jnp.zeros((NLAT, NLON), jnp.float32).at[remap_tgt].add(weighted)
        atmos = jnp.tanh(summed)
        returned = jnp.zeros((NY, NLON), jnp.float32).at[remap_src].add(atmos[remap_tgt] * remap_weight[:, None])
        return ocean_field.at[0, :, 0, :].add(FEEDBACK * returned)

    def forward(start_pert):
        ocean_field = base_state + start_pert
        for hour_index in range(STEPS):
            ocean_field = ocean_step(ocean_field, diffusivity, chan_mix)
            ocean_field = couple(ocean_field, hour_index)
            ocean_field = remap(ocean_field)
        return ocean_field
    final_field, pullback = jax.vjp(forward, perturbation)
    weight_sq = (cost_weight * cost_weight)[None, :, None, :]
    gradient = pullback(weight_sq * (final_field - target_state))[0]
    cell_total = perturbation.size
    mean_pp = jnp.sum(perturbation * perturbation) / cell_total
    mean_pg = jnp.sum(perturbation * gradient) / cell_total
    mean_gg = jnp.sum(gradient * gradient) / cell_total
    grad_scale = lax.rsqrt(mean_gg + EPSILON)
    mean_sq = mean_pp + 2.0 * ASCENT * grad_scale * mean_pg + ASCENT * ASCENT * grad_scale * grad_scale * mean_gg
    stepped = perturbation + ASCENT * grad_scale * gradient
    return stepped * lax.rsqrt(mean_sq + EPSILON)
```

```python
import jax
import jax.numpy as jnp
from jax import lax
from jax.sharding import PartitionSpec as P

LAT_DEV = 2


KAPPA_V = 0.1
TIME_STEP = 0.3
FLUX_RATE = 0.05
FEEDBACK = 0.5
ASCENT = 0.5
EPSILON = 1e-06
HIGHEST = lax.Precision.HIGHEST


def with_halo(block, sides, width):
    for axis, dim in sides:
        count = lax.axis_size(axis)
        forward = [(i, i + 1) for i in range(count - 1)]
        backward = [(target, source) for source, target in forward]
        low = lax.ppermute(
            lax.slice_in_dim(block, block.shape[dim] - width, None, axis=dim), axis, forward
        )
        high = lax.ppermute(lax.slice_in_dim(block, 0, width, axis=dim), axis, backward)
        block = jnp.concatenate([low, block, high], axis=dim)
    return block


def channel_drive(ocean_field, chan_mix):
    return jnp.tanh(jnp.einsum("lck,ljkx->ljcx", chan_mix, ocean_field, precision=HIGHEST))


def level_diff(ocean_field):
    padded = jnp.pad(ocean_field, ((1, 1), (0, 0), (0, 0), (0, 0)))
    return padded[2:] + padded[:-2] - 2.0 * ocean_field


def horiz_lap(ocean_field):
    padded = with_halo(ocean_field, (("horiz", 1),), 1)
    return (
        padded[:, 2:]
        + padded[:, :-2]
        + jnp.roll(ocean_field, -1, axis=3)
        + jnp.roll(ocean_field, 1, axis=3)
        - 4.0 * ocean_field
    )


def owner_flux(arrived, air_field, wind_field, mixing, coupler_mix):
    cell_shape = arrived.shape
    flat = arrived.reshape((cell_shape[0] * cell_shape[1],) + cell_shape[2:])
    mixed = jnp.tanh(jnp.einsum("pq,qcx->pcx", mixing, flat, precision=HIGHEST))
    air_flat = air_field.reshape(flat.shape[0], flat.shape[2])
    wind_flat = wind_field.reshape(flat.shape[0], flat.shape[2])
    contrast = (
        jnp.concatenate([(air_flat - flat[:, 0, :])[:, None, :], flat[:, 1:, :]], axis=1) + mixed
    )
    forcing = jnp.einsum("ck,pkx->pcx", coupler_mix, contrast, precision=HIGHEST)
    return (FLUX_RATE * wind_flat[:, None, :] * jnp.tanh(forcing)).reshape(cell_shape)


def flux_cotangent(arrived, cotangent, air_field, wind_field, mixing, coupler_mix):

    def forward_flux(values):
        return owner_flux(values, air_field, wind_field, mixing, coupler_mix)

    _, pullback = jax.vjp(forward_flux, arrived)
    return pullback(cotangent)[0]


def to_tiles(surface, tile_width):
    row_count, channels, cells = surface.shape
    pieces = surface.reshape(row_count, channels, cells // tile_width, tile_width).transpose(
        0, 2, 1, 3
    )
    return pieces.reshape(row_count * (cells // tile_width), channels, tile_width)


def from_tiles(tile_view, row_count):
    tile_total, channels, tile_width = tile_view.shape
    per_row = tile_total // row_count
    pieces = tile_view.reshape(row_count, per_row, channels, tile_width).transpose(0, 2, 1, 3)
    return pieces.reshape(row_count, channels, per_row * tile_width)


def route_tables(wet_row, owner_row, device_count, capacity):
    live_mask = owner_row >= 0
    onehot = (owner_row[:, None] == jnp.arange(device_count, dtype=jnp.int32)[None, :]).astype(
        jnp.int32
    )
    earlier = jnp.cumsum(onehot, axis=0) - onehot
    slot_rank = jnp.sum(earlier * onehot, axis=1)
    slot_index = jnp.where(live_mask, owner_row * capacity + slot_rank, -1)
    tile_safe = jnp.where(live_mask, wet_row, 0)
    return (live_mask, slot_index, tile_safe)


def owner_round(picked, slot_index, live_mask, device_count, capacity, owner_work):
    entry_count = picked.shape[0]
    slot_total = device_count * capacity
    select = (slot_index[None, :] == jnp.arange(slot_total, dtype=jnp.int32)[:, None]).astype(
        jnp.float32
    )
    packed = jnp.dot(
        select,
        picked.reshape(entry_count, -1),
        precision=HIGHEST,
        preferred_element_type=jnp.float32,
    )
    result = owner_work(packed)
    taken = jnp.dot(select.T, result, precision=HIGHEST, preferred_element_type=jnp.float32)
    return taken.reshape((entry_count,) + picked.shape[1:])


def gather_mix(values, rows, device_count, capacity):
    everywhere = lax.all_gather(values, "horiz", axis=0, tiled=False)
    by_owner = everywhere.reshape(device_count, device_count, capacity, -1)
    return jnp.einsum("ordk,dokx->orx", rows.reshape(device_count, capacity, device_count, capacity),
        by_owner, precision=HIGHEST).reshape(values.shape)


def unpack_tiles(values, tile_safe, live_mask, tile_total):
    select = (
        (tile_safe[None, :] == jnp.arange(tile_total, dtype=jnp.int32)[:, None])
        & live_mask[None, :]
    ).astype(jnp.float32)
    placed = jnp.dot(
        select,
        values.reshape(values.shape[0], -1),
        precision=HIGHEST,
        preferred_element_type=jnp.float32,
    )
    return placed.reshape((tile_total,) + values.shape[1:])


def remap_cycle(surface, source_local, remap_tgt, remap_weight, lat_rows, middle):
    row_count = surface.shape[0]
    weighted = surface[source_local] * remap_weight[:, None]
    source_select = (
        source_local[None, :] == jnp.arange(row_count, dtype=jnp.int32)[:, None]
    ).astype(jnp.float32)
    first_lat = lax.axis_index("horiz") * lat_rows - 1
    select_rows = (
        remap_tgt[None, :] - first_lat == jnp.arange(lat_rows + 2, dtype=jnp.int32)[:, None]
    ).astype(jnp.float32)
    local_sums = jnp.dot(
        select_rows, weighted, precision=HIGHEST, preferred_element_type=jnp.float32
    )
    count = lax.axis_size("horiz")
    forward = [(i, i + 1) for i in range(count - 1)]
    backward = [(target, source) for source, target in forward]
    from_low = lax.ppermute(local_sums[lat_rows:], "horiz", forward)
    from_high = lax.ppermute(local_sums[:2], "horiz", backward)
    full_sums = local_sums + jnp.concatenate([from_low, from_high], axis=0)
    extended, stored = middle(full_sums)
    at_targets = jnp.dot(
        select_rows.T, extended, precision=HIGHEST, preferred_element_type=jnp.float32
    )
    at_targets = at_targets * remap_weight[:, None]
    returned = jnp.dot(
        source_select, at_targets, precision=HIGHEST, preferred_element_type=jnp.float32
    )
    return (returned, stored)


def forward_middle(summed):
    atmos = jnp.tanh(summed)
    return (atmos, atmos)


def body(
    perturbation,
    base_state,
    target_state,
    cost_weight,
    diffusivity,
    chan_mix,
    coupler_mix,
    owner_mix,
    air_temp,
    wind_speed,
    wet_list,
    wet_owner,
    remap_src,
    remap_tgt,
    remap_weight,
):
    device_count = lax.axis_size("horiz")
    row_count = base_state.shape[1]
    capacity = air_temp.shape[2] // device_count
    tile_total = wet_list.shape[1]
    hour_count = air_temp.shape[0]
    tile_width = air_temp.shape[3]
    mixing = owner_mix[0]
    slot_total = device_count * capacity

    def spread(array, lead):
        return array.reshape(device_count, capacity, lead, -1)

    static_parts = [
        mixing.reshape(device_count, capacity * slot_total),
        mixing.T.reshape(device_count, capacity * slot_total),
        air_temp[:, 0].reshape(hour_count, device_count, -1).transpose(1, 0, 2).reshape(device_count, -1),
        wind_speed[:, 0].reshape(hour_count, device_count, -1).transpose(1, 0, 2).reshape(device_count, -1),
    ]
    static_out = jnp.concatenate(static_parts, axis=1)
    static_in = lax.all_to_all(static_out, "horiz", split_axis=0, concat_axis=0, tiled=True)
    wide = capacity * slot_total
    mix_rows = static_in[:, :wide].reshape(device_count, capacity, slot_total)
    mix_cols = static_in[:, wide : 2 * wide].reshape(device_count, capacity, slot_total)
    cells = hour_count * capacity * tile_width
    air_here = static_in[:, 2 * wide : 2 * wide + cells].reshape(device_count, hour_count, capacity, tile_width)
    wind_here = static_in[:, 2 * wide + cells :].reshape(device_count, hour_count, capacity, tile_width)
    air_here = air_here.transpose(1, 0, 2, 3).reshape(hour_count, slot_total, tile_width)
    wind_here = wind_here.transpose(1, 0, 2, 3).reshape(hour_count, slot_total, tile_width)
    live_mask, slot_index, tile_safe = route_tables(
        wet_list[0], wet_owner[0], device_count, capacity
    )
    source_local = remap_src - lax.axis_index("horiz") * row_count
    coeff_field = diffusivity[None, :, None, :]
    ocean_field = base_state + perturbation
    saved = []
    for hour_index in range(hour_count):
        start_field = ocean_field
        drive = channel_drive(ocean_field, chan_mix)
        ocean_field = (
            ocean_field
            + coeff_field * horiz_lap(ocean_field)
            + KAPPA_V * level_diff(ocean_field)
            + TIME_STEP * drive
        )
        picked = (
            to_tiles(ocean_field[0], tile_width)[tile_safe]
            * live_mask.astype(jnp.float32)[:, None, None]
        )
        keep = {}

        def flux_work(packed, hour_index=hour_index, keep=keep):
            mixed = jnp.tanh(gather_mix(packed, mix_rows, device_count, capacity))
            shape = (slot_total, 4, tile_width)
            own = packed.reshape(shape)
            contrast = jnp.concatenate(
                [(air_here[hour_index] - own[:, 0, :])[:, None, :], own[:, 1:, :]], axis=1
            ) + mixed.reshape(shape)
            bent = jnp.tanh(jnp.einsum("ck,pkx->pcx", coupler_mix, contrast, precision=HIGHEST))
            keep["mixed"] = mixed
            keep["bent"] = bent
            return (FLUX_RATE * wind_here[hour_index][:, None, :] * bent).reshape(slot_total, -1)

        flux_entries = owner_round(
            picked, slot_index, live_mask, device_count, capacity, flux_work
        )
        flux_tiles = unpack_tiles(flux_entries, tile_safe, live_mask, tile_total)
        ocean_field = ocean_field.at[0].add(from_tiles(flux_tiles, row_count))
        returned, atmos = remap_cycle(
            ocean_field[0, :, 0, :], source_local, remap_tgt, remap_weight, LAT_DEV, forward_middle
        )
        ocean_field = ocean_field.at[0, :, 0, :].add(FEEDBACK * returned)
        saved.append((drive, keep, atmos))
    adjoint = (cost_weight * cost_weight)[None, :, None, :] * (ocean_field - target_state)
    for hour_index in reversed(range(hour_count)):
        drive, keep, atmos = saved[hour_index]

        def adjoint_middle(summed, atmos=atmos):
            return (summed * (1.0 - atmos * atmos), atmos)

        surface_cot, _ = remap_cycle(
            FEEDBACK * adjoint[0, :, 0, :],
            source_local,
            remap_tgt,
            remap_weight,
            LAT_DEV,
            adjoint_middle,
        )
        adjoint = adjoint.at[0, :, 0, :].add(surface_cot)
        cot_entries = to_tiles(adjoint[0], tile_width)[tile_safe]

        def cot_work(packed, hour_index=hour_index, keep=keep):
            got = packed.reshape(slot_total, 4, tile_width)
            forced = FLUX_RATE * wind_here[hour_index][:, None, :] * (1.0 - keep["bent"] * keep["bent"]) * got
            back = jnp.einsum("ck,pcx->pkx", coupler_mix, forced, precision=HIGHEST)
            flat = back.reshape(slot_total, -1) * (1.0 - keep["mixed"] * keep["mixed"])
            through = gather_mix(flat, mix_cols, device_count, capacity)
            direct = jnp.concatenate([-back[:, :1], back[:, 1:]], axis=1)
            return through + direct.reshape(slot_total, -1)

        back_entries = owner_round(
            cot_entries, slot_index, live_mask, device_count, capacity, cot_work
        )
        back_tiles = unpack_tiles(back_entries, tile_safe, live_mask, tile_total)
        adjoint = adjoint.at[0].add(from_tiles(back_tiles, row_count))
        adjoint = (
            adjoint
            + horiz_lap(coeff_field * adjoint)
            + KAPPA_V * level_diff(adjoint)
            + TIME_STEP
            * jnp.einsum(
                "lck,ljcx->ljkx", chan_mix, (1.0 - drive * drive) * adjoint, precision=HIGHEST
            )
        )
    cell_total = adjoint.size * device_count
    local = jnp.stack(
        [
            jnp.sum(perturbation * perturbation),
            jnp.sum(perturbation * adjoint),
            jnp.sum(adjoint * adjoint),
        ]
    )
    local = jnp.broadcast_to(jnp.pad(local, (0, tile_width - 3)), (device_count, tile_width))
    everyones = lax.all_to_all(local, "horiz", split_axis=0, concat_axis=0, tiled=True)
    statistics = jnp.sum(everyones, axis=0)
    mean_pp = statistics[0] / cell_total
    mean_pg = statistics[1] / cell_total
    mean_gg = statistics[2] / cell_total
    grad_scale = lax.rsqrt(mean_gg + EPSILON)
    mean_sq = (
        mean_pp
        + 2.0 * ASCENT * grad_scale * mean_pg
        + ASCENT * ASCENT * grad_scale * grad_scale * mean_gg
    )
    stepped = perturbation + ASCENT * grad_scale * adjoint
    return stepped * lax.rsqrt(mean_sq + EPSILON)


def solution(mesh):
    placed = (
        P("member", "horiz", None, None),
        P(None, "horiz", None, None),
        P(None, "horiz", None, None),
        P("horiz", None),
        P("horiz", None),
        P(),
        P(),
        P("horiz", None, None),
        P(None, "horiz", None, None),
        P(None, "horiz", None, None),
        P("horiz", None),
        P("horiz", None),
        P("horiz"),
        P("horiz"),
        P("horiz"),
    )
    return jax.shard_map(
        body,
        mesh=mesh,
        in_specs=placed,
        out_specs=P("member", "horiz", None, None),
        check_vma=False,
    )
```

```python
import functools

import jax
import jax.numpy as jnp
from jax import lax
from jax.experimental import pallas as pl
from jax.experimental.pallas import tpu as pltpu
from jax.sharding import PartitionSpec as P

LAT_DEV = 2
NEAR_LAT = LAT_DEV + 2
CHANNELS = 4
LEVELS = 8
WIDTH = 128
SUBLANES = 8

KAPPA_V = 0.1
TIME_STEP = 0.3
FLUX_RATE = 0.05
FEEDBACK = 0.5
ASCENT = 0.5
EPSILON = 1e-06
HIGHEST = lax.Precision.HIGHEST
VMEM_BYTES = 32 * 1024 * 1024


class Sizes:
    def __init__(self, devices, capacity, rows, cells):
        self.devices = devices
        self.capacity = capacity
        self.slots = devices * capacity
        self.rows = rows
        self.cells = cells
        self.row_tiles = cells // WIDTH
        self.tiles = rows * self.row_tiles
        self.pitch = -(-self.row_tiles // SUBLANES) * SUBLANES
        self.flat_rows = rows * self.pitch
        self.own_rows = CHANNELS * capacity
        self.chunk = -(-(self.own_rows + 2 * capacity) // SUBLANES) * SUBLANES
        self.edge_rows = CHANNELS * self.row_tiles * LEVELS
        self.surface_rows = CHANNELS * (self.tiles + 1)


def cols(tile):
    return slice(tile * WIDTH, (tile + 1) * WIDTH)


def lanes_sum(left_here, left_before, right_here, right_after, lane):
    return jnp.where(lane == 0, left_before, left_here) + jnp.where(
        lane == WIDTH - 1, right_after, right_here
    )


def levels_sum(field, sub):
    return jnp.where(sub == 0, 0.0, pltpu.roll(field, 1, 0)) + jnp.where(
        sub == LEVELS - 1, 0.0, pltpu.roll(field, LEVELS - 1, 0)
    )


def row_tiles_of(sz, ref, row):
    return ref[pl.ds(row * CHANNELS * sz.row_tiles, sz.row_tiles, stride=CHANNELS), :]


def put_row_tiles(sz, ref, row, value):
    ref[pl.ds(row * CHANNELS * sz.row_tiles, sz.row_tiles, stride=CHANNELS), :] = value


def load_edges(sz, padded, low, high):
    for side, edge in ((0, low), (sz.rows + 1, high)):
        for channel in range(CHANNELS):
            for tile in range(sz.row_tiles):
                at = (channel * sz.row_tiles + tile) * LEVELS
                padded[side, channel, :, cols(tile)] = edge[at : at + LEVELS, :]


def load_surface_row(sz, target, row, source, base):
    for tile in range(sz.row_tiles):
        for channel in range(CHANNELS):
            at = base + tile * CHANNELS + channel
            target[row, channel, 0:1, cols(tile)] = source[pl.ds(at, 1), :]


def forward_kernel(sz, first, last, *refs):
    refs = list(refs)
    field, low, high, diffusivity, mix, table = refs[:6]
    refs = refs[6:]
    if not first:
        surface, low_surface, high_surface = refs[:3]
        refs = refs[3:]
    if last:
        target, weight_sq = refs[:2]
        refs = refs[2:]
    out, drive, new_surface, packed, send_low, send_high, padded = refs

    load_edges(sz, padded, low, high)
    padded[1 : sz.rows + 1] = field[...]
    if not first:
        load_surface_row(sz, padded, 0, low_surface, 0)
        load_surface_row(sz, padded, sz.rows + 1, high_surface, 0)

        def fill(row, carry):
            load_surface_row(sz, padded, row + 1, surface, row * sz.row_tiles * CHANNELS)
            return carry

        lax.fori_loop(0, sz.rows, fill, 0)

    lane = lax.broadcasted_iota(jnp.int32, (LEVELS, WIDTH), 1)
    sub = lax.broadcasted_iota(jnp.int32, (LEVELS, WIDTH), 0)
    count = sz.row_tiles

    def one_row(row, carry):
        here = [[padded[row + 1, c, :, cols(t)] for t in range(count)] for c in range(CHANNELS)]
        for t in range(count):
            coeff = jnp.broadcast_to(diffusivity[row, 0:1, cols(t)], (LEVELS, WIDTH))
            for c in range(CHANNELS):
                mixed = mix[c * CHANNELS] * here[0][t]
                for k in range(1, CHANNELS):
                    mixed = mixed + mix[c * CHANNELS + k] * here[k][t]
                bent = jnp.tanh(mixed)
                drive[row, c, :, cols(t)] = bent
                field_here = here[c][t]
                around = lanes_sum(
                    pltpu.roll(field_here, 1, 1),
                    pltpu.roll(here[c][(t - 1) % count], 1, 1),
                    pltpu.roll(field_here, WIDTH - 1, 1),
                    pltpu.roll(here[c][(t + 1) % count], WIDTH - 1, 1),
                    lane,
                )
                around = around + (padded[row, c, :, cols(t)] + padded[row + 2, c, :, cols(t)])
                stepped = (
                    field_here
                    + coeff * (around - 4.0 * field_here)
                    + KAPPA_V * (levels_sum(field_here, sub) - 2.0 * field_here)
                    + TIME_STEP * bent
                )
                new_surface[pl.ds((row * count + t) * CHANNELS + c, 1), :] = stepped[0:1, :]
                flat_row = sz.edge_rows + row * sz.pitch + t
                if c == 0:
                    send_low[pl.ds(flat_row, 1), :] = stepped[0:1, :]
                    send_high[pl.ds(flat_row, 1), :] = stepped[0:1, :]
                if last:
                    scale = jnp.broadcast_to(weight_sq[row, 0:1, cols(t)], (LEVELS, WIDTH))
                    stepped = scale * (stepped - target[row, c, :, cols(t)])
                out[row, c, :, cols(t)] = stepped
        return carry

    lax.fori_loop(0, sz.rows, one_row, 0)
    new_surface[CHANNELS * sz.tiles :, :] = jnp.zeros((CHANNELS, WIDTH), jnp.float32)
    store_edges(sz, out, diffusivity if last else None, send_low, send_high)
    for slot in range(sz.slots):
        at = pl.multiple_of(table[slot] * CHANNELS, CHANNELS)
        packed[slot * CHANNELS : (slot + 1) * CHANNELS, :] = new_surface[pl.ds(at, CHANNELS), :]


def store_edges(sz, field, diffusivity, send_low, send_high):
    for row, send in ((0, send_low), (sz.rows - 1, send_high)):
        for channel in range(CHANNELS):
            for tile in range(sz.row_tiles):
                value = field[row, channel, :, cols(tile)]
                if diffusivity is not None:
                    value = value * jnp.broadcast_to(
                        diffusivity[row, 0:1, cols(tile)], (LEVELS, WIDTH)
                    )
                at = (channel * sz.row_tiles + tile) * LEVELS
                send[at : at + LEVELS, :] = value


def owner_kernel(sz, arrived, mixing, air, wind, bulk, flux, mixed_slope, flux_slope, flat, first):
    slots = sz.slots
    values = [arrived[pl.ds(c, slots, stride=CHANNELS), :] for c in range(CHANNELS)]
    mixed = jnp.tanh(
        jnp.dot(
            mixing[...],
            jnp.concatenate(values, axis=1),
            precision=HIGHEST,
            preferred_element_type=jnp.float32,
        )
    )
    contrast = []
    for c in range(CHANNELS):
        mixed_here = mixed[:, cols(c)]
        mixed_slope[c] = 1.0 - mixed_here * mixed_here
        contrast.append((air[...] - values[0] if c == 0 else values[c]) + mixed_here)
    rate = FLUX_RATE * wind[...]
    for c in range(CHANNELS):
        forcing = bulk[c, 0] * contrast[0]
        for k in range(1, CHANNELS):
            forcing = forcing + bulk[c, k] * contrast[k]
        bent = jnp.tanh(forcing)
        flux_slope[c] = rate * (1.0 - bent * bent)
        one = rate * bent
        flat[pl.ds(c, slots, stride=CHANNELS), :] = one
        if c == 0:
            first[...] = one
    flux[...] = jnp.zeros(flux.shape, jnp.float32)
    cap = sz.capacity
    for d in range(sz.devices):
        at = d * sz.chunk
        flux[at : at + sz.own_rows, :] = flat[d * sz.own_rows : (d + 1) * sz.own_rows, :]
        at = at + sz.own_rows
        if d > 0:
            flux[at : at + cap, :] = first[(d - 1) * cap : d * cap, :]
        if d < sz.devices - 1:
            flux[at + cap : at + 2 * cap, :] = first[(d + 1) * cap : (d + 2) * cap, :]


def owner_back_kernel(sz, arrived, mixing, mixed_slope, flux_slope, bulk, back, flat, extra):
    slots, cap = sz.slots, sz.capacity
    for d in range(sz.devices):
        at = d * sz.chunk
        flat[d * sz.own_rows : (d + 1) * sz.own_rows, :] = arrived[at : at + sz.own_rows, :]
        more = jnp.zeros((cap, WIDTH), jnp.float32)
        if d < sz.devices - 1:
            at = (d + 1) * sz.chunk + sz.own_rows
            more = more + arrived[at : at + cap, :]
        if d > 0:
            at = (d - 1) * sz.chunk + sz.own_rows + cap
            more = more + arrived[at : at + cap, :]
        extra[d * cap : (d + 1) * cap, :] = more
    forced = []
    for c in range(CHANNELS):
        got = flat[pl.ds(c, slots, stride=CHANNELS), :]
        if c == 0:
            got = got + extra[...]
        forced.append(flux_slope[c] * got)
    direct = []
    for k in range(CHANNELS):
        total = bulk[0, k] * forced[0]
        for c in range(1, CHANNELS):
            total = total + bulk[c, k] * forced[c]
        direct.append(total)
    through = lax.dot_general(
        mixing[...],
        jnp.concatenate([direct[k] * mixed_slope[k] for k in range(CHANNELS)], axis=1),
        (((0,), (0,)), ((), ())),
        precision=HIGHEST,
        preferred_element_type=jnp.float32,
    )
    for k in range(CHANNELS):
        sign = -1.0 if k == 0 else 1.0
        back[pl.ds(k, slots, stride=CHANNELS), :] = through[:, cols(k)] + sign * direct[k]


def weigh(remap, lat, rows_at, values):
    total = remap[lat, rows_at] * values[0]
    for index in range(1, len(values)):
        total = total + remap[lat, rows_at + index] * values[index]
    return total


def scatter_lats(remap, row_at, lats):
    total = remap[0, row_at] * lats[0]
    for lat in range(1, NEAR_LAT):
        total = total + remap[lat, row_at] * lats[lat]
    return total


def spread_back(sz, surface, slope, remap, tables, packed, near_low, near_high, send_low, send_high, base):
    rows, pitch, count = sz.rows, sz.pitch, sz.row_tiles
    own = [row_tiles_of(sz, surface, row) for row in range(rows)]
    lats = []
    for lat in range(NEAR_LAT):
        partial = FEEDBACK * weigh(remap, lat, rows, own)
        send = send_low if lat < LAT_DEV else send_high
        at = base + (lat % LAT_DEV) * pitch
        send[at : at + count, :] = partial
        lats.append(slope[lat * pitch : lat * pitch + count, :] * partial)
    for row in range(rows):
        put_row_tiles(sz, surface, row, own[row] + scatter_lats(remap, rows + row, lats))
        near_low[row * pitch : row * pitch + count, :] = scatter_lats(remap, row, lats)
        near_high[row * pitch : row * pitch + count, :] = scatter_lats(remap, 2 * rows + row, lats)
    blank = jnp.zeros((SUBLANES, WIDTH), jnp.float32)
    near_low[sz.flat_rows :, :] = blank
    near_high[sz.flat_rows :, :] = blank
    packed[...] = jnp.zeros(packed.shape, jnp.float32)
    cap = sz.capacity
    for slot in range(sz.slots):
        owner, rank = slot // cap, slot % cap
        at = owner * sz.chunk + rank * CHANNELS
        tile = pl.multiple_of(tables[0, slot] * CHANNELS, CHANNELS)
        packed[at : at + CHANNELS, :] = surface[pl.ds(tile, CHANNELS), :]
        at = owner * sz.chunk + sz.own_rows + rank
        packed[at : at + 1, :] = near_low[pl.ds(tables[1, slot], 1), :]
        packed[at + cap : at + cap + 1, :] = near_high[pl.ds(tables[2, slot], 1), :]


def surface_kernel(sz, last, *refs):
    refs = list(refs)
    flux, before, from_low, from_high, tables, remap = refs[:6]
    refs = refs[6:]
    if last:
        target, weight_sq = refs[:2]
        surface, slope, packed, send_low, send_high, near_low, near_high = refs[2:]
    else:
        surface, slope, send_low, send_high, near_low, near_high = refs
    rows, pitch, count, cap = sz.rows, sz.pitch, sz.row_tiles, sz.capacity
    surface[...] = before[...]
    for near, source in ((near_low, from_low), (near_high, from_high)):
        near[...] = source[sz.edge_rows :, :]
    for slot in range(sz.slots):
        owner, rank = slot // cap, slot % cap
        at = owner * sz.chunk + rank * CHANNELS
        tile = pl.multiple_of(tables[0, slot] * CHANNELS, CHANNELS)
        surface[pl.ds(tile, CHANNELS), :] = (
            before[pl.ds(tile, CHANNELS), :] + flux[at : at + CHANNELS, :]
        )
        at = owner * sz.chunk + sz.own_rows + rank
        for near, source, which in ((near_low, from_low, 1), (near_high, from_high, 2)):
            row = tables[which, slot]
            near[pl.ds(row, 1), :] = source[pl.ds(sz.edge_rows + row, 1), :] + flux[at : at + 1, :]
            at = at + cap
    surface[CHANNELS * sz.tiles :, :] = jnp.zeros((CHANNELS, WIDTH), jnp.float32)
    low = [near_low[row * pitch : row * pitch + count, :] for row in range(rows)]
    own = [row_tiles_of(sz, surface, row) for row in range(rows)]
    high = [near_high[row * pitch : row * pitch + count, :] for row in range(rows)]
    air = []
    for lat in range(NEAR_LAT):
        one = jnp.tanh(weigh(remap, lat, 0, low + own + high))
        slope[lat * pitch : lat * pitch + count, :] = 1.0 - one * one
        air.append(one)
    for row in range(rows):
        fed = own[row] + FEEDBACK * scatter_lats(remap, rows + row, air)
        put_row_tiles(sz, surface, row, fed)
    if last:
        end = CHANNELS * sz.tiles
        surface[0:end, :] = weight_sq[...] * (surface[0:end, :] - target[...])
        spread_back(
            sz, surface, slope, remap, tables, packed, near_low, near_high, send_low, send_high, 0
        )
    else:
        width = CHANNELS * count
        send_low[...] = surface[0:width, :]
        send_high[...] = surface[(rows - 1) * width : rows * width, :]


def merge_kernel(
    sz, recv_at, back, before, slope, from_low, from_high, tables, remap, diffusivity, surface, send_low, send_high
):
    rows, pitch, count = sz.rows, sz.pitch, sz.row_tiles
    surface[...] = before[...]
    for slot in range(sz.slots):
        tile = pl.multiple_of(tables[0, slot] * CHANNELS, CHANNELS)
        surface[pl.ds(tile, CHANNELS), :] = (
            before[pl.ds(tile, CHANNELS), :] + back[slot * CHANNELS : (slot + 1) * CHANNELS, :]
        )
    surface[CHANNELS * sz.tiles :, :] = jnp.zeros((CHANNELS, WIDTH), jnp.float32)
    lats = []
    for lat in range(NEAR_LAT):
        source = from_low if lat < LAT_DEV else from_high
        at = recv_at + (lat % LAT_DEV) * pitch
        lats.append(slope[lat * pitch : lat * pitch + count, :] * source[at : at + count, :])
    for row in range(rows):
        own = row_tiles_of(sz, surface, row)
        put_row_tiles(sz, surface, row, own + scatter_lats(remap, rows + row, lats))
    width = CHANNELS * count
    send_low[...] = diffusivity[0:width, :] * surface[0:width, :]
    send_high[...] = (
        diffusivity[(rows - 1) * width : rows * width, :]
        * surface[(rows - 1) * width : rows * width, :]
    )


def backward_kernel(sz, last, *refs):
    refs = list(refs)
    field, surface, low, high, low_surface, high_surface, drive, diffusivity, mix = refs[:9]
    refs = refs[9:]
    if last:
        perturbation, out, sums, local, padded = refs
    else:
        tables, remap, slope, out, new_surface, packed, send_low, send_high = refs[:8]
        local, padded, near_low, near_high = refs[8:]
    count = sz.row_tiles
    load_edges(sz, padded, low, high)
    load_surface_row(sz, padded, 0, low_surface, 0)
    load_surface_row(sz, padded, sz.rows + 1, high_surface, 0)
    local[...] = field[...]

    def fill(row, carry):
        load_surface_row(sz, local, row, surface, row * count * CHANNELS)
        for t in range(count):
            coeff = jnp.broadcast_to(diffusivity[row, 0:1, cols(t)], (LEVELS, WIDTH))
            for c in range(CHANNELS):
                padded[row + 1, c, :, cols(t)] = coeff * local[row, c, :, cols(t)]
        return carry

    lax.fori_loop(0, sz.rows, fill, 0)
    lane = lax.broadcasted_iota(jnp.int32, (LEVELS, WIDTH), 1)
    sub = lax.broadcasted_iota(jnp.int32, (LEVELS, WIDTH), 0)

    def one_row(row, carry):
        scaled = [[padded[row + 1, c, :, cols(t)] for t in range(count)] for c in range(CHANNELS)]
        for t in range(count):
            here, bent = [], []
            for c in range(CHANNELS):
                value = local[row, c, :, cols(t)]
                one = drive[row, c, :, cols(t)]
                here.append(value)
                bent.append((1.0 - one * one) * value)
            for c in range(CHANNELS):
                mixed = mix[c] * bent[0]
                for k in range(1, CHANNELS):
                    mixed = mixed + mix[k * CHANNELS + c] * bent[k]
                around = lanes_sum(
                    pltpu.roll(scaled[c][t], 1, 1),
                    pltpu.roll(scaled[c][(t - 1) % count], 1, 1),
                    pltpu.roll(scaled[c][t], WIDTH - 1, 1),
                    pltpu.roll(scaled[c][(t + 1) % count], WIDTH - 1, 1),
                    lane,
                )
                around = around + (padded[row, c, :, cols(t)] + padded[row + 2, c, :, cols(t)])
                stepped = (
                    here[c]
                    + (around - 4.0 * scaled[c][t])
                    + KAPPA_V * (levels_sum(here[c], sub) - 2.0 * here[c])
                    + TIME_STEP * mixed
                )
                out[row, c, :, cols(t)] = stepped
                if last:
                    start = perturbation[row, c, :, cols(t)]
                    carry = (
                        carry[0] + start * start,
                        carry[1] + start * stepped,
                        carry[2] + stepped * stepped,
                    )
                else:
                    new_surface[pl.ds((row * count + t) * CHANNELS + c, 1), :] = stepped[0:1, :]
        return carry

    blank = jnp.zeros((LEVELS, WIDTH), jnp.float32)
    totals = lax.fori_loop(0, sz.rows, one_row, (blank, blank, blank) if last else 0)
    if last:
        row = lax.broadcasted_iota(jnp.int32, (LEVELS, WIDTH), 0)
        held = blank
        for index in range(3):
            held = jnp.where(row == index, jnp.sum(totals[index], axis=0, keepdims=True), held)
        sums[...] = held
    else:
        new_surface[CHANNELS * sz.tiles :, :] = jnp.zeros((CHANNELS, WIDTH), jnp.float32)
        store_edges(sz, out, diffusivity, send_low, send_high)
        spread_back(
            sz,
            new_surface,
            slope,
            remap,
            tables,
            packed,
            near_low,
            near_high,
            send_low,
            send_high,
            sz.edge_rows,
        )


def call(kernel, name, inputs, outputs, scratch=()):
    def spec(where):
        return pl.BlockSpec(memory_space=where)

    return pl.pallas_call(
        kernel,
        name=name,
        in_specs=[spec(pltpu.SMEM if small else pltpu.VMEM) for _, small in inputs],
        out_specs=[spec(pltpu.VMEM) for _ in outputs],
        out_shape=[jax.ShapeDtypeStruct(shape, jnp.float32) for shape in outputs],
        scratch_shapes=[pltpu.VMEM(shape, jnp.float32) for shape in scratch],
        compiler_params=pltpu.CompilerParams(vmem_limit_bytes=VMEM_BYTES),
    )(*[array for array, _ in inputs])


def big(*arrays):
    return [(array, False) for array in arrays]


def small(*arrays):
    return [(array, True) for array in arrays]


def slot_tiles(wet_row, owner_row, capacity, slots, tiles):
    entries = owner_row.shape[0]
    order = jnp.arange(entries, dtype=jnp.int32)
    same = (owner_row[:, None] == owner_row[None, :]) & (order[None, :] < order[:, None])
    rank = jnp.sum(same.astype(jnp.int32), axis=1)
    slot = jnp.where(owner_row >= 0, owner_row * capacity + rank, -1)
    match = slot[None, :] == jnp.arange(slots, dtype=jnp.int32)[:, None]
    found = jnp.max(jnp.where(match, wet_row[None, :] + 1, 0), axis=1)
    return jnp.where(found > 0, found - 1, tiles)


def to_bulk(field):
    return field.transpose(1, 2, 0, 3)


def to_edge(sz, row):
    split = row.reshape(LEVELS, CHANNELS, sz.row_tiles, WIDTH).transpose(1, 2, 0, 3)
    return split.reshape(sz.edge_rows, WIDTH)


def to_surface(sz, rows):
    split = rows.reshape(sz.rows, CHANNELS, sz.row_tiles, WIDTH).transpose(0, 2, 1, 3)
    return split.reshape(CHANNELS * sz.tiles, WIDTH)


def swap(low, high):
    count = lax.axis_size("horiz")
    upward = [(i, i + 1) for i in range(count - 1)]
    downward = [(target, source) for source, target in upward]
    return lax.ppermute(high, "horiz", upward), lax.ppermute(low, "horiz", downward)


def exchange(array, devices):
    rows = array.shape[0] // devices
    split = array.reshape(devices, rows // CHANNELS, CHANNELS, WIDTH)
    moved = lax.all_to_all(split, "horiz", split_axis=0, concat_axis=0, tiled=True)
    return moved.reshape(array.shape)


def body(
    perturbation,
    base_state,
    target_state,
    cost_weight,
    diffusivity,
    chan_mix,
    coupler_mix,
    owner_mix,
    air_temp,
    wind_speed,
    wet_list,
    wet_owner,
    remap_src,
    remap_tgt,
    remap_weight,
):
    devices = lax.axis_size("horiz")
    hours = air_temp.shape[0]
    sz = Sizes(devices, air_temp.shape[2] // devices, base_state.shape[1], base_state.shape[3])
    me = lax.axis_index("horiz")
    mixing = owner_mix[0]
    rows = sz.rows

    tile_of = slot_tiles(wet_list[0], wet_owner[0], sz.capacity, sz.slots, sz.tiles)
    row_of = jnp.where(
        tile_of < sz.tiles,
        (tile_of // sz.row_tiles) * sz.pitch + tile_of % sz.row_tiles,
        sz.flat_rows,
    )
    lat_hit = (
        remap_tgt[None, :] - (me * LAT_DEV - 1) == jnp.arange(NEAR_LAT, dtype=jnp.int32)[:, None]
    )
    row_hit = remap_src[None, :] - me * rows == jnp.arange(rows, dtype=jnp.int32)[:, None]
    own_remap = jnp.sum(
        jnp.where(lat_hit[:, None, :] & row_hit[None, :, :], remap_weight[None, None, :], 0.0),
        axis=2,
    )
    facts = jnp.concatenate(
        [(sz.flat_rows - row_of).astype(jnp.float32), own_remap.reshape(-1)]
    )
    fact_rows = -(-facts.shape[0] // (WIDTH * SUBLANES)) * SUBLANES
    facts = jnp.pad(facts, (0, fact_rows * WIDTH - facts.shape[0])).reshape(fact_rows, WIDTH)

    start = [perturbation[:, row] + base_state[:, row] for row in (0, rows - 1)]
    sends = [jnp.concatenate([to_edge(sz, one), facts]) for one in start]
    from_low, from_high = swap(*sends)

    def facts_of(got):
        line = got[sz.edge_rows :].reshape(-1)
        table = sz.flat_rows - line[: sz.slots].astype(jnp.int32)
        return table, line[sz.slots : sz.slots + NEAR_LAT * rows].reshape(NEAR_LAT, rows)

    low_table, low_remap = facts_of(from_low)
    high_table, high_remap = facts_of(from_high)
    tables = jnp.stack([tile_of, low_table, high_table])
    blank = jnp.zeros((LAT_DEV, rows), jnp.float32)
    remap = jnp.concatenate(
        [
            jnp.concatenate([low_remap[LAT_DEV:], blank]),
            own_remap,
            jnp.concatenate([blank, high_remap[:LAT_DEV]]),
        ],
        axis=1,
    )
    mix = jnp.broadcast_to(
        chan_mix.transpose(1, 2, 0).reshape(CHANNELS * CHANNELS, LEVELS, 1),
        (CHANNELS * CHANNELS, LEVELS, WIDTH),
    )
    weight_sq = cost_weight * cost_weight
    start_pert = to_bulk(perturbation)
    field = start_pert + to_bulk(base_state)
    target = to_bulk(target_state)
    target_surface = to_surface(sz, target_state[0])

    def all_channels(array):
        return to_surface(sz, jnp.broadcast_to(array[:, None, :], (rows, CHANNELS, sz.cells)))

    weight_surface = all_channels(weight_sq)
    diffusivity_surface = all_channels(diffusivity)
    diffusivity = diffusivity.reshape(rows, 1, sz.cells)
    weight_sq = weight_sq.reshape(rows, 1, sz.cells)

    whole = (rows, CHANNELS, LEVELS, sz.cells)
    wider = (rows + 2, CHANNELS, LEVELS, sz.cells)
    surface_shape = (sz.surface_rows, WIDTH)
    narrow = (CHANNELS * sz.slots, WIDTH)
    wide = (devices * sz.chunk, WIDTH)
    slope_shape = (NEAR_LAT * sz.pitch, WIDTH)
    near = (sz.flat_rows + SUBLANES, WIDTH)
    lats = (LAT_DEV * sz.pitch, WIDTH)
    row_surface = (CHANNELS * sz.row_tiles, WIDTH)
    by_slot = (CHANNELS, sz.slots, WIDTH)

    saved = []
    edges = (from_low, from_high)
    surface = None
    for hour in range(hours):
        first, last = hour == 0, hour == hours - 1
        inputs = big(field, *edges, diffusivity, mix) + small(tile_of)
        if not first:
            inputs += big(surface, *surface_edges)
        if last:
            inputs += big(target, weight_sq)
        edge_send = (sz.edge_rows + sz.flat_rows + SUBLANES, WIDTH)
        field, drive, surface, packed, *sends = call(
            functools.partial(forward_kernel, sz, first, last),
            "step",
            inputs,
            [whole, whole, surface_shape, narrow, edge_send, edge_send],
            [wider],
        )
        arrived = exchange(packed, devices)
        edges = swap(*sends)
        flux, mixed_slope, flux_slope = call(
            functools.partial(owner_kernel, sz),
            "owners",
            big(arrived, mixing, air_temp[hour, 0], wind_speed[hour, 0]) + small(coupler_mix),
            [wide, by_slot, by_slot],
            [narrow, (sz.slots, WIDTH)],
        )
        flux = exchange(flux, devices)
        inputs = big(flux, surface, *edges) + small(tables, remap)
        if last:
            surface, slope, packed, *sends = call(
                functools.partial(surface_kernel, sz, True),
                "surface",
                inputs + big(target_surface, weight_surface),
                [surface_shape, slope_shape, wide, lats, lats],
                [near, near],
            )
        else:
            surface, slope, *sends = call(
                functools.partial(surface_kernel, sz, False),
                "surface",
                inputs,
                [surface_shape, slope_shape, row_surface, row_surface],
                [near, near],
            )
            surface_edges = swap(*sends)
        saved.append((drive, slope, mixed_slope, flux_slope))

    lat_at = 0
    for hour in reversed(range(hours)):
        drive, slope, mixed_slope, flux_slope = saved[hour]
        arrived = exchange(packed, devices)
        got = swap(*sends)
        back = call(
            functools.partial(owner_back_kernel, sz),
            "owners_back",
            big(arrived, mixing, mixed_slope, flux_slope) + small(coupler_mix),
            [narrow],
            [narrow, (sz.slots, WIDTH)],
        )[0]
        back = exchange(back, devices)
        if hour < hours - 1:
            edges = got
        surface, *row_sends = call(
            functools.partial(merge_kernel, sz, lat_at),
            "merge",
            big(back, surface, slope, *got) + small(tables, remap) + big(diffusivity_surface),
            [surface_shape, row_surface, row_surface],
        )
        surface_edges = swap(*row_sends)
        inputs = big(field, surface, *edges, *surface_edges, drive, diffusivity, mix)
        if hour > 0:
            lat_at = sz.edge_rows
            edge_send = (sz.edge_rows + lats[0], WIDTH)
            field, surface, packed, *sends = call(
                functools.partial(backward_kernel, sz, False),
                "step_back",
                inputs + small(tables, remap) + big(saved[hour - 1][1]),
                [whole, surface_shape, wide, edge_send, edge_send],
                [whole, wider, near, near],
            )
        else:
            gradient, sums = call(
                functools.partial(backward_kernel, sz, True),
                "step_back_sums",
                inputs + big(start_pert),
                [whole, (LEVELS, WIDTH)],
                [whole, wider],
            )

    local = jnp.pad(jnp.sum(sums, axis=1), (0, WIDTH - LEVELS))
    everyones = lax.all_to_all(
        jnp.broadcast_to(local, (devices, WIDTH)), "horiz", split_axis=0, concat_axis=0, tiled=True
    )
    cell_total = perturbation.size * devices
    statistics = jnp.sum(everyones, axis=0) / cell_total
    mean_pp, mean_pg, mean_gg = statistics[0], statistics[1], statistics[2]
    grad_scale = lax.rsqrt(mean_gg + EPSILON)
    mean_sq = (
        mean_pp
        + 2.0 * ASCENT * grad_scale * mean_pg
        + ASCENT * ASCENT * grad_scale * grad_scale * mean_gg
    )
    stepped = perturbation + ASCENT * grad_scale * gradient.transpose(2, 0, 1, 3)
    return stepped * lax.rsqrt(mean_sq + EPSILON)


def solution(mesh):
    placed = (
        P("member", "horiz", None, None),
        P(None, "horiz", None, None),
        P(None, "horiz", None, None),
        P("horiz", None),
        P("horiz", None),
        P(),
        P(),
        P("horiz", None, None),
        P(None, "horiz", None, None),
        P(None, "horiz", None, None),
        P("horiz", None),
        P("horiz", None),
        P("horiz"),
        P("horiz"),
        P("horiz"),
    )
    return jax.shard_map(
        body,
        mesh=mesh,
        in_specs=placed,
        out_specs=P("member", "horiz", None, None),
        check_vma=False,
    )
```

```python
import functools

import jax
import jax.numpy as jnp
from jax import lax
from jax.experimental import pallas as pl
from jax.experimental.pallas import tpu as pltpu
from jax.sharding import PartitionSpec as P

LAT_DEV = 2
NEAR_LAT = LAT_DEV + 2
CHANNELS = 4
LEVELS = 8
WIDTH = 128
SUBLANES = 8

KAPPA_V = 0.1
TIME_STEP = 0.3
FLUX_RATE = 0.05
FEEDBACK = 0.5
ASCENT = 0.5
EPSILON = 1e-06
HIGHEST = lax.Precision.HIGHEST
VMEM_BYTES = 32 * 1024 * 1024


class Sizes:
    def __init__(self, devices, capacity, rows, cells):
        self.devices = devices
        self.capacity = capacity
        self.slots = devices * capacity
        self.rows = rows
        self.cells = cells
        self.row_tiles = cells // WIDTH
        self.tiles = rows * self.row_tiles
        self.row_width = CHANNELS * self.row_tiles
        self.pitch = -(-self.row_tiles // SUBLANES) * SUBLANES
        self.own_rows = CHANNELS * capacity
        self.chunk = -(-(self.own_rows + 2 * capacity) // SUBLANES) * SUBLANES
        self.slot_lines = -(-self.slots // WIDTH)
        self.facts = -(-(self.slot_lines + 1) // SUBLANES) * SUBLANES
        self.lat_lines = LAT_DEV * self.pitch
        self.whole = (rows, CHANNELS, LEVELS, cells)
        self.edge = (CHANNELS, LEVELS, cells)
        self.surface = (CHANNELS * (self.tiles + 1), WIDTH)
        self.narrow = (CHANNELS * self.slots, WIDTH)
        self.wide = (devices * self.chunk, WIDTH)
        self.slope = (NEAR_LAT * self.pitch, WIDTH)
        self.lats = (self.lat_lines, WIDTH)
        self.told = (self.lat_lines + self.facts, WIDTH)
        self.near = (-(-(self.tiles + 1) // SUBLANES) * SUBLANES, WIDTH)
        self.by_slot = (CHANNELS, self.slots, WIDTH)


class Shipped:
    def __init__(self, block, home, sems):
        self.block, self.home, self.sems = block, home, sems
        self.by_row = False
        self.started = False

    def __getitem__(self, at):
        return self.block[at]

    def __setitem__(self, at, value):
        self.block[at] = value

    def row(self, index):
        self.by_row = True
        self.started = True
        return pltpu.make_async_copy(
            self.block.at[index], self.home.at[index], self.sems.at[index]
        )

    def all(self):
        return pltpu.make_async_copy(self.block, self.home, self.sems.at[0])

    def start(self):
        self.started = True
        self.all().start()

    def finish(self, rows):
        if self.by_row:
            for index in range(rows):
                self.row(index).wait()
        else:
            self.all().wait()


def cols(tile):
    return slice(tile * WIDTH, (tile + 1) * WIDTH)


def lanes_sum(left_here, left_before, right_here, right_after, lane):
    return jnp.where(lane == 0, left_before, left_here) + jnp.where(
        lane == WIDTH - 1, right_after, right_here
    )


def levels_sum(field, sub):
    return jnp.where(sub == 0, 0.0, pltpu.roll(field, 1, 0)) + jnp.where(
        sub == LEVELS - 1, 0.0, pltpu.roll(field, LEVELS - 1, 0)
    )


def row_tiles_of(sz, ref, row):
    return ref[pl.ds(row * sz.row_width, sz.row_tiles, stride=CHANNELS), :]


def put_row_tiles(sz, ref, row, value):
    ref[pl.ds(row * sz.row_width, sz.row_tiles, stride=CHANNELS), :] = value


def near_row(sz, ref, row):
    return ref[row * sz.row_tiles : (row + 1) * sz.row_tiles, :]


def load_surface_row(sz, target, row, source, base):
    for tile in range(sz.row_tiles):
        for channel in range(CHANNELS):
            at = base + tile * CHANNELS + channel
            target[row, channel, 0:1, cols(tile)] = source[pl.ds(at, 1), :]


def tables_kernel(sz, wet_list, wet_owner, remap_src, remap_tgt, remap_weight, me, tile_of, facts, used):
    def clear(index, carry):
        tile_of[index] = sz.tiles
        return carry

    lax.fori_loop(0, tile_of.shape[0], clear, 0)

    def clear_used(index, carry):
        used[index] = 0
        return carry

    lax.fori_loop(0, sz.devices, clear_used, 0)

    def place(entry, carry):
        owner = wet_owner[0, entry]
        live = owner >= 0
        owner = jnp.maximum(owner, 0)
        rank = used[owner]
        used[owner] = rank + live.astype(jnp.int32)
        slot = jnp.where(live, owner * sz.capacity + rank, sz.slots)
        tile_of[slot] = jnp.where(live, wet_list[0, entry], sz.tiles)
        return carry

    lax.fori_loop(0, wet_list.shape[1], place, 0)
    for line in range(sz.slot_lines):

        def tell(index, carry, line=line):
            facts[line, index] = (sz.tiles - tile_of[line * WIDTH + index]).astype(jnp.float32)
            return carry

        lax.fori_loop(0, min(WIDTH, sz.slots - line * WIDTH), tell, 0)
    for index in range(NEAR_LAT * sz.rows):
        facts[sz.slot_lines, index] = 0.0

    def weigh_entry(entry, carry):
        lat = remap_tgt[entry] - (me[0] * LAT_DEV - 1)
        row = remap_src[entry] - me[0] * sz.rows
        at = lat * sz.rows + row
        facts[sz.slot_lines, at] = facts[sz.slot_lines, at] + remap_weight[entry]
        return carry

    lax.fori_loop(0, remap_src.shape[0], weigh_entry, 0)


class Remap:
    def __init__(self, sz, facts, low, high):
        self.sz, self.facts, self.low, self.high = sz, facts, low, high

    def own(self, lat, row):
        return self.facts[self.sz.slot_lines, lat * self.sz.rows + row]

    def beside(self, told, lat, row):
        return told[self.sz.lat_lines + self.sz.slot_lines, lat * self.sz.rows + row]

    def of_low(self, lat, row):
        return self.beside(self.low, lat + LAT_DEV, row)

    def of_high(self, lat, row):
        return self.beside(self.high, lat - LAT_DEV, row)

    def tile(self, told, slot):
        line = self.sz.lat_lines + slot // WIDTH
        return self.sz.tiles - told[line, slot % WIDTH].astype(jnp.int32)


def sum_of(weights, values):
    total = weights[0] * values[0]
    for weight, value in zip(weights[1:], values[1:]):
        total = total + weight * value
    return total


def own_sums(sz, remap, own, factor):
    return [
        factor * sum_of([remap.own(lat, row) for row in range(sz.rows)], own)
        for lat in range(NEAR_LAT)
    ]


def send_sums(sz, sums, send_low, send_high):
    for lat in range(NEAR_LAT):
        send = send_low if lat < LAT_DEV else send_high
        at = (lat % LAT_DEV) * sz.pitch
        send[at : at + sz.row_tiles, :] = sums[lat]


def lat_rows(sz, ref, lat):
    return ref[lat * sz.pitch : lat * sz.pitch + sz.row_tiles, :]


def told_sums(sz, from_low, from_high):
    return [
        lat_rows(sz, from_low if lat < LAT_DEV else from_high, lat % LAT_DEV)
        for lat in range(NEAR_LAT)
    ]


def forward_kernel(sz, first, last, *refs):
    refs = list(refs)
    field, low, high, diffusivity, mix, table, own_facts = refs[:7]
    refs = refs[7:]
    if first:
        facts = refs[0]
        refs = refs[1:]
    else:
        surface, low_surface, high_surface = refs[:3]
        refs = refs[3:]
    if last:
        target, weight = refs[:2]
        refs = refs[2:]
    out, drive, new_surface, packed, tell_low, tell_high, edge_low, edge_high = refs[:8]
    padded, in_sems, edge_sems = refs[8:]
    remap = Remap(sz, own_facts, None, None)

    edges = [
        pltpu.make_async_copy(low, padded.at[0], edge_sems.at[0]),
        pltpu.make_async_copy(high, padded.at[sz.rows + 1], edge_sems.at[1]),
    ]

    def arrival(row):
        return pltpu.make_async_copy(field.at[row], padded.at[row + 1], in_sems.at[row])

    edges[0].start()
    for row in range(sz.rows):
        arrival(row).start()
    edges[1].start()

    def ready(row):
        arrival(row).wait()
        if not first:
            load_surface_row(sz, padded, row + 1, surface, row * sz.row_width)

    for side in (0, 1):
        edges[side].wait()
        if not first:
            source = high_surface if side else low_surface
            load_surface_row(sz, padded, (sz.rows + 1) * side, source, 0)
    ready(0)

    lane = lax.broadcasted_iota(jnp.int32, (LEVELS, WIDTH), 1)
    sub = lax.broadcasted_iota(jnp.int32, (LEVELS, WIDTH), 0)
    count = sz.row_tiles

    def one_row(row, carry):
        @pl.when(row < sz.rows - 1)
        def _():
            ready(row + 1)

        here = [[padded[row + 1, c, :, cols(t)] for t in range(count)] for c in range(CHANNELS)]
        for t in range(count):
            coeff = jnp.broadcast_to(diffusivity[row, 0:1, cols(t)], (LEVELS, WIDTH))
            if last:
                scale = weight[row, 0:1, cols(t)]
                scale = jnp.broadcast_to(scale * scale, (LEVELS, WIDTH))
            for c in range(CHANNELS):
                mixed = mix[c * CHANNELS] * here[0][t]
                for k in range(1, CHANNELS):
                    mixed = mixed + mix[c * CHANNELS + k] * here[k][t]
                bent = jnp.tanh(mixed)
                drive[row, c, :, cols(t)] = bent
                field_here = here[c][t]
                around = lanes_sum(
                    pltpu.roll(field_here, 1, 1),
                    pltpu.roll(here[c][(t - 1) % count], 1, 1),
                    pltpu.roll(field_here, WIDTH - 1, 1),
                    pltpu.roll(here[c][(t + 1) % count], WIDTH - 1, 1),
                    lane,
                )
                around = around + (padded[row, c, :, cols(t)] + padded[row + 2, c, :, cols(t)])
                stepped = (
                    field_here
                    + coeff * (around - 4.0 * field_here)
                    + KAPPA_V * (levels_sum(field_here, sub) - 2.0 * field_here)
                    + TIME_STEP * bent
                )
                new_surface[pl.ds((row * count + t) * CHANNELS + c, 1), :] = stepped[0:1, :]
                if last:
                    stepped = scale * (stepped - target[row, c, :, cols(t)])
                out[row, c, :, cols(t)] = stepped
        drive.row(row).start()
        out.row(row).start()
        return carry

    lax.fori_loop(0, sz.rows, one_row, 0)
    new_surface[CHANNELS * sz.tiles :, :] = jnp.zeros((CHANNELS, WIDTH), jnp.float32)
    new_surface.start()
    pack_slots(sz, table, new_surface, packed)
    packed.start()
    own = [row_tiles_of(sz, new_surface.block, row) for row in range(sz.rows)]
    send_sums(sz, own_sums(sz, remap, own, 1.0), tell_low, tell_high)
    blank = facts[...] if first else jnp.zeros((sz.facts, WIDTH), jnp.float32)
    for tell in (tell_low, tell_high):
        tell[sz.lat_lines :, :] = blank
        tell.start()
    store_edges(sz, out, diffusivity if last else None, edge_low, edge_high)


def pack_slots(sz, table, surface, packed):
    for slot in range(sz.slots):
        at = pl.multiple_of(table[slot] * CHANNELS, CHANNELS)
        packed[slot * CHANNELS : (slot + 1) * CHANNELS, :] = surface[pl.ds(at, CHANNELS), :]


def store_edges(sz, field, diffusivity, send_low, send_high):
    for row, send in ((0, send_low), (sz.rows - 1, send_high)):
        for channel in range(CHANNELS):
            for tile in range(sz.row_tiles):
                value = field[row, channel, :, cols(tile)]
                if diffusivity is not None:
                    value = value * jnp.broadcast_to(
                        diffusivity[row, 0:1, cols(tile)], (LEVELS, WIDTH)
                    )
                send[channel, :, cols(tile)] = value
        send.start()


def owner_kernel(sz, arrived, mixing, air, wind, bulk, flux, mixed_slope, flux_slope, flat, first):
    slots = sz.slots
    values = [arrived[pl.ds(c, slots, stride=CHANNELS), :] for c in range(CHANNELS)]
    mixed = jnp.tanh(
        jnp.dot(
            mixing[...],
            jnp.concatenate(values, axis=1),
            precision=HIGHEST,
            preferred_element_type=jnp.float32,
        )
    )
    contrast = []
    for c in range(CHANNELS):
        mixed_here = mixed[:, cols(c)]
        mixed_slope[c] = 1.0 - mixed_here * mixed_here
        contrast.append((air[...] - values[0] if c == 0 else values[c]) + mixed_here)
    mixed_slope.start()
    rate = FLUX_RATE * wind[...]
    for c in range(CHANNELS):
        forcing = bulk[c, 0] * contrast[0]
        for k in range(1, CHANNELS):
            forcing = forcing + bulk[c, k] * contrast[k]
        bent = jnp.tanh(forcing)
        flux_slope[c] = rate * (1.0 - bent * bent)
        one = rate * bent
        flat[pl.ds(c, slots, stride=CHANNELS), :] = one
        if c == 0:
            first[...] = one
    flux_slope.start()
    cap = sz.capacity
    gap = jnp.zeros((sz.chunk - sz.own_rows, WIDTH), jnp.float32)
    for d in range(sz.devices):
        at = d * sz.chunk
        flux[at : at + sz.own_rows, :] = flat[d * sz.own_rows : (d + 1) * sz.own_rows, :]
        at = at + sz.own_rows
        flux[at : (d + 1) * sz.chunk, :] = gap
        if d > 0:
            flux[at : at + cap, :] = first[(d - 1) * cap : d * cap, :]
        if d < sz.devices - 1:
            flux[at + cap : at + 2 * cap, :] = first[(d + 1) * cap : (d + 2) * cap, :]


def owner_back_kernel(sz, arrived, mixing, mixed_slope, flux_slope, bulk, back, flat, extra):
    slots, cap = sz.slots, sz.capacity
    for d in range(sz.devices):
        at = d * sz.chunk
        flat[d * sz.own_rows : (d + 1) * sz.own_rows, :] = arrived[at : at + sz.own_rows, :]
        more = jnp.zeros((cap, WIDTH), jnp.float32)
        if d < sz.devices - 1:
            at = (d + 1) * sz.chunk + sz.own_rows
            more = more + arrived[at : at + cap, :]
        if d > 0:
            at = (d - 1) * sz.chunk + sz.own_rows + cap
            more = more + arrived[at : at + cap, :]
        extra[d * cap : (d + 1) * cap, :] = more
    forced = []
    for c in range(CHANNELS):
        got = flat[pl.ds(c, slots, stride=CHANNELS), :]
        if c == 0:
            got = got + extra[...]
        forced.append(flux_slope[c] * got)
    direct = []
    for k in range(CHANNELS):
        total = bulk[0, k] * forced[0]
        for c in range(1, CHANNELS):
            total = total + bulk[c, k] * forced[c]
        direct.append(total)
    through = lax.dot_general(
        mixing[...],
        jnp.concatenate([direct[k] * mixed_slope[k] for k in range(CHANNELS)], axis=1),
        (((0,), (0,)), ((), ())),
        precision=HIGHEST,
        preferred_element_type=jnp.float32,
    )
    for k in range(CHANNELS):
        sign = -1.0 if k == 0 else 1.0
        back.block[pl.ds(k, slots, stride=CHANNELS), :] = through[:, cols(k)] + sign * direct[k]


def spread_back(sz, surface, slope, remap, table, packed, near_low, near_high, tell_low, tell_high):
    rows, count, cap = sz.rows, sz.row_tiles, sz.capacity
    block = surface.block
    own = [row_tiles_of(sz, block, row) for row in range(rows)]
    sums = own_sums(sz, remap, own, FEEDBACK)
    send_sums(sz, sums, tell_low, tell_high)
    tell_low.start()
    tell_high.start()
    lats = [lat_rows(sz, slope, lat) * sums[lat] for lat in range(NEAR_LAT)]
    every = range(NEAR_LAT)
    for row in range(rows):
        added = sum_of([remap.own(lat, row) for lat in every], lats)
        put_row_tiles(sz, block, row, own[row] + added)
        at = row * count
        near_low[at : at + count, :] = sum_of(
            [remap.of_low(lat, row) for lat in range(LAT_DEV)], lats[:LAT_DEV]
        )
        near_high[at : at + count, :] = sum_of(
            [remap.of_high(lat, row) for lat in range(LAT_DEV, NEAR_LAT)], lats[LAT_DEV:]
        )
    rest = sz.near[0] - sz.tiles
    near_low[sz.tiles :, :] = jnp.zeros((rest, WIDTH), jnp.float32)
    near_high[sz.tiles :, :] = jnp.zeros((rest, WIDTH), jnp.float32)
    surface.start()
    gap = jnp.zeros((sz.chunk - sz.own_rows, WIDTH), jnp.float32)
    for owner in range(sz.devices):
        packed[owner * sz.chunk + sz.own_rows : (owner + 1) * sz.chunk, :] = gap
    for slot in range(sz.slots):
        owner, rank = slot // cap, slot % cap
        at = owner * sz.chunk + rank * CHANNELS
        tile = pl.multiple_of(table[slot] * CHANNELS, CHANNELS)
        packed[at : at + CHANNELS, :] = surface[pl.ds(tile, CHANNELS), :]
        at = owner * sz.chunk + sz.own_rows + rank
        packed[at : at + 1, :] = near_low[pl.ds(remap.tile(remap.low, slot), 1), :]
        at = at + cap
        packed[at : at + 1, :] = near_high[pl.ds(remap.tile(remap.high, slot), 1), :]


def surface_kernel(sz, last, *refs):
    refs = list(refs)
    flux, before, from_low, from_high, table, facts, told_low, told_high = refs[:8]
    refs = refs[8:]
    if last:
        target, weight = refs[:2]
        surface, slope, packed, tell_low, tell_high, near_low, near_high = refs[2:]
        block = surface.block
    else:
        surface, send_low, send_high, slope, near_low, near_high = refs
        block = surface
    remap = Remap(sz, facts, told_low, told_high)
    rows, cap = sz.rows, sz.capacity
    block[...] = before[...]
    near_low[...] = jnp.zeros(sz.near, jnp.float32)
    near_high[...] = jnp.zeros(sz.near, jnp.float32)
    for slot in range(sz.slots):
        owner, rank = slot // cap, slot % cap
        at = owner * sz.chunk + rank * CHANNELS
        tile = pl.multiple_of(table[slot] * CHANNELS, CHANNELS)
        block[pl.ds(tile, CHANNELS), :] = (
            before[pl.ds(tile, CHANNELS), :] + flux[at : at + CHANNELS, :]
        )
        at = owner * sz.chunk + sz.own_rows + rank
        near_low[pl.ds(remap.tile(told_low, slot), 1), :] = flux[at : at + 1, :]
        at = at + cap
        near_high[pl.ds(remap.tile(told_high, slot), 1), :] = flux[at : at + 1, :]
    block[CHANNELS * sz.tiles :, :] = jnp.zeros((CHANNELS, WIDTH), jnp.float32)
    own = [row_tiles_of(sz, block, row) for row in range(rows)]
    sums = own_sums(sz, remap, own, 1.0)
    told = told_sums(sz, from_low, from_high)
    air = []
    for lat in range(NEAR_LAT):
        if lat < LAT_DEV:
            near, weights = near_low, [remap.of_low(lat, row) for row in range(rows)]
        else:
            near, weights = near_high, [remap.of_high(lat, row) for row in range(rows)]
        more = sum_of(weights, [near_row(sz, near, row) for row in range(rows)])
        one = jnp.tanh(sums[lat] + told[lat] + more)
        slope[lat * sz.pitch : lat * sz.pitch + sz.row_tiles, :] = 1.0 - one * one
        air.append(one)
    slope.start()
    for row in range(rows):
        weights = [remap.own(lat, row) for lat in range(NEAR_LAT)]
        put_row_tiles(sz, block, row, own[row] + FEEDBACK * sum_of(weights, air))
    if last:
        end = CHANNELS * sz.tiles
        scale = weight[...]
        block[0:end, :] = scale * scale * (block[0:end, :] - target[...])
        spread_back(
            sz, surface, slope, remap, table, packed, near_low, near_high, tell_low, tell_high
        )
    else:
        send_low[...] = surface[0 : sz.row_width, :]
        send_high[...] = surface[(rows - 1) * sz.row_width : rows * sz.row_width, :]


def merge_kernel(
    sz, back, before, slope, from_low, from_high, table, facts, diffusivity, surface, send_low, send_high
):
    rows, width = sz.rows, sz.row_width
    remap = Remap(sz, facts, None, None)
    surface[...] = before[...]
    for slot in range(sz.slots):
        tile = pl.multiple_of(table[slot] * CHANNELS, CHANNELS)
        surface[pl.ds(tile, CHANNELS), :] = (
            before[pl.ds(tile, CHANNELS), :] + back[slot * CHANNELS : (slot + 1) * CHANNELS, :]
        )
    surface[CHANNELS * sz.tiles :, :] = jnp.zeros((CHANNELS, WIDTH), jnp.float32)
    told = told_sums(sz, from_low, from_high)
    lats = [lat_rows(sz, slope, lat) * told[lat] for lat in range(NEAR_LAT)]
    for row in range(rows):
        own = row_tiles_of(sz, surface, row)
        weights = [remap.own(lat, row) for lat in range(NEAR_LAT)]
        put_row_tiles(sz, surface, row, own + sum_of(weights, lats))
    send_low[...] = diffusivity[0:width, :] * surface[0:width, :]
    end = rows * width
    send_high[...] = diffusivity[end - width : end, :] * surface[end - width : end, :]


def backward_kernel(sz, last, *refs):
    refs = list(refs)
    field, surface, low, high, low_surface, high_surface, drive, diffusivity, mix = refs[:9]
    refs = refs[9:]
    if last:
        perturbation, out, sums = refs[:3]
        local, bent_all, padded, in_sems, edge_sems = refs[3:]
    else:
        table, facts, told_low, told_high, slope = refs[:5]
        out, new_surface, packed, tell_low, tell_high, edge_low, edge_high = refs[5:12]
        local, bent_all, padded, near_low, near_high, in_sems, edge_sems = refs[12:]
        remap = Remap(sz, facts, told_low, told_high)
    count = sz.row_tiles

    edges = [
        pltpu.make_async_copy(low, padded.at[0], edge_sems.at[0]),
        pltpu.make_async_copy(high, padded.at[sz.rows + 1], edge_sems.at[1]),
    ]

    def arrivals(row):
        return [
            pltpu.make_async_copy(field.at[row], local.at[row], in_sems.at[0, row]),
            pltpu.make_async_copy(drive.at[row], bent_all.at[row], in_sems.at[1, row]),
        ]

    edges[0].start()
    for row in range(sz.rows):
        for arrival in arrivals(row):
            arrival.start()
    edges[1].start()

    def ready(row):
        for arrival in arrivals(row):
            arrival.wait()
        load_surface_row(sz, local, row, surface, row * sz.row_width)
        for t in range(count):
            coeff = jnp.broadcast_to(diffusivity[row, 0:1, cols(t)], (LEVELS, WIDTH))
            for c in range(CHANNELS):
                padded[row + 1, c, :, cols(t)] = coeff * local[row, c, :, cols(t)]

    for side in (0, 1):
        edges[side].wait()
        source = high_surface if side else low_surface
        load_surface_row(sz, padded, (sz.rows + 1) * side, source, 0)
    ready(0)
    lane = lax.broadcasted_iota(jnp.int32, (LEVELS, WIDTH), 1)
    sub = lax.broadcasted_iota(jnp.int32, (LEVELS, WIDTH), 0)

    def one_row(row, carry):
        @pl.when(row < sz.rows - 1)
        def _():
            ready(row + 1)

        scaled = [[padded[row + 1, c, :, cols(t)] for t in range(count)] for c in range(CHANNELS)]
        for t in range(count):
            here, bent = [], []
            for c in range(CHANNELS):
                value = local[row, c, :, cols(t)]
                one = bent_all[row, c, :, cols(t)]
                here.append(value)
                bent.append((1.0 - one * one) * value)
            for c in range(CHANNELS):
                mixed = mix[c] * bent[0]
                for k in range(1, CHANNELS):
                    mixed = mixed + mix[k * CHANNELS + c] * bent[k]
                around = lanes_sum(
                    pltpu.roll(scaled[c][t], 1, 1),
                    pltpu.roll(scaled[c][(t - 1) % count], 1, 1),
                    pltpu.roll(scaled[c][t], WIDTH - 1, 1),
                    pltpu.roll(scaled[c][(t + 1) % count], WIDTH - 1, 1),
                    lane,
                )
                around = around + (padded[row, c, :, cols(t)] + padded[row + 2, c, :, cols(t)])
                stepped = (
                    here[c]
                    + (around - 4.0 * scaled[c][t])
                    + KAPPA_V * (levels_sum(here[c], sub) - 2.0 * here[c])
                    + TIME_STEP * mixed
                )
                out[row, c, :, cols(t)] = stepped
                if last:
                    start = perturbation[row, c, :, cols(t)]
                    carry = (
                        carry[0] + start * start,
                        carry[1] + start * stepped,
                        carry[2] + stepped * stepped,
                    )
                else:
                    new_surface[pl.ds((row * count + t) * CHANNELS + c, 1), :] = stepped[0:1, :]
        out.row(row).start()
        return carry

    blank = jnp.zeros((LEVELS, WIDTH), jnp.float32)
    totals = lax.fori_loop(0, sz.rows, one_row, (blank, blank, blank) if last else 0)
    if last:
        place = lax.broadcasted_iota(jnp.int32, sums.block.shape, 1)
        held = jnp.zeros(sums.block.shape, jnp.float32)
        for index in range(3):
            total = jnp.sum(jnp.sum(totals[index], axis=0, keepdims=True), axis=1, keepdims=True)
            held = jnp.where(place == index, total, held)
        sums[...] = held
    else:
        new_surface[CHANNELS * sz.tiles :, :] = jnp.zeros((CHANNELS, WIDTH), jnp.float32)
        spread_back(
            sz, new_surface, slope, remap, table, packed, near_low, near_high, tell_low, tell_high
        )
        packed.start()
        store_edges(sz, out, diffusivity, edge_low, edge_high)


def final_kernel(cell_total, everyones, perturbation, gradient, out, start, slope, in_sems):
    levels = start.shape[0]

    def arrivals(level):
        return [
            pltpu.make_async_copy(perturbation.at[level], start.at[level], in_sems.at[0, level]),
            pltpu.make_async_copy(gradient.at[level], slope.at[level], in_sems.at[1, level]),
        ]

    for level in range(levels):
        for arrival in arrivals(level):
            arrival.start()
    sums = jnp.sum(everyones[...], axis=0, keepdims=True) / cell_total
    place = lax.broadcasted_iota(jnp.int32, sums.shape, 1)
    means = [
        jnp.broadcast_to(
            jnp.sum(jnp.where(place == index, sums, 0.0), axis=1, keepdims=True), (1, WIDTH)
        )
        for index in range(3)
    ]
    scale = lax.rsqrt(means[2] + EPSILON)
    mean_sq = means[0] + 2.0 * ASCENT * scale * means[1] + ASCENT * ASCENT * scale * scale * means[2]
    shrink = lax.rsqrt(mean_sq + EPSILON)
    step = jnp.broadcast_to(ASCENT * scale, (CHANNELS, WIDTH))
    shrink = jnp.broadcast_to(shrink, (CHANNELS, WIDTH))
    for level in range(levels):
        for arrival in arrivals(level):
            arrival.wait()
        for row in range(start.shape[1]):
            for tile in range(start.shape[3] // WIDTH):
                value = start[level, row, :, cols(tile)] + step * slope[level, row, :, cols(tile)]
                out[level, row, :, cols(tile)] = value * shrink
        out.row(level).start()


def near_by(*arrays):
    return [(array, pltpu.VMEM) for array in arrays]


def scalars(*arrays):
    return [(array, pltpu.SMEM) for array in arrays]


def anywhere(*arrays):
    return [(array, pl.ANY) for array in arrays]


def call(kernel, name, inputs, kept=(), shipped=(), scratch=()):
    n_in, n_kept, n_out = len(inputs), len(kept), len(shipped)

    def run(*refs):
        ins = refs[: n_in + n_kept]
        homes = refs[n_in + n_kept : n_in + n_kept + n_out]
        rest = refs[n_in + n_kept + n_out :]
        outs = [
            Shipped(block, home, sems)
            for block, home, sems in zip(rest[:n_out], homes, rest[n_out : 2 * n_out])
        ]
        kernel(*ins, *outs, *rest[2 * n_out :])
        for out in outs:
            if not out.started:
                out.start()
        for out in outs:
            out.finish(out.block.shape[0])

    shapes = list(kept) + list(shipped)
    spaces = [pltpu.VMEM] * n_kept + [pltpu.HBM] * n_out
    blocks = [pltpu.VMEM(shape, jnp.float32) for shape in shipped]
    sems = [
        pltpu.SemaphoreType.DMA((shape[0] if len(shape) > 3 else 1,)) for shape in shipped
    ]
    more = [
        item if not isinstance(item, tuple) else pltpu.VMEM(item, jnp.float32) for item in scratch
    ]
    return pl.pallas_call(
        run,
        name=name,
        in_specs=[pl.BlockSpec(memory_space=space) for _, space in inputs],
        out_specs=[pl.BlockSpec(memory_space=space) for space in spaces],
        out_shape=[jax.ShapeDtypeStruct(shape, jnp.float32) for shape in shapes],
        scratch_shapes=blocks + sems + more,
        compiler_params=pltpu.CompilerParams(vmem_limit_bytes=VMEM_BYTES),
    )(*[array for array, _ in inputs])


def to_bulk(field):
    return field.transpose(1, 2, 0, 3)


def to_surface(sz, rows):
    split = rows.reshape(sz.rows, CHANNELS, sz.row_tiles, WIDTH).transpose(0, 2, 1, 3)
    return split.reshape(CHANNELS * sz.tiles, WIDTH)


def swap(low, high):
    count = lax.axis_size("horiz")
    upward = [(i, i + 1) for i in range(count - 1)]
    downward = [(target, source) for source, target in upward]
    return lax.ppermute(high, "horiz", upward), lax.ppermute(low, "horiz", downward)


def exchange(array, devices):
    rows = array.shape[0] // devices
    split = array.reshape(devices, rows // CHANNELS, CHANNELS, WIDTH)
    moved = lax.all_to_all(split, "horiz", split_axis=0, concat_axis=0, tiled=True)
    return moved.reshape(array.shape)


def body(
    perturbation,
    base_state,
    target_state,
    cost_weight,
    diffusivity,
    chan_mix,
    coupler_mix,
    owner_mix,
    air_temp,
    wind_speed,
    wet_list,
    wet_owner,
    remap_src,
    remap_tgt,
    remap_weight,
):
    devices = lax.axis_size("horiz")
    hours = air_temp.shape[0]
    sz = Sizes(devices, air_temp.shape[2] // devices, base_state.shape[1], base_state.shape[3])
    mixing = owner_mix[0]
    rows = sz.rows

    start = [
        (perturbation[:, row] + base_state[:, row]).transpose(1, 0, 2) for row in (0, rows - 1)
    ]
    edges = swap(*start)
    me = lax.axis_index("horiz").astype(jnp.int32).reshape(1)
    table, facts = pl.pallas_call(
        functools.partial(tables_kernel, sz),
        name="tables",
        in_specs=[pl.BlockSpec(memory_space=pltpu.SMEM)] * 6,
        out_specs=[pl.BlockSpec(memory_space=pltpu.SMEM)] * 2,
        out_shape=[
            jax.ShapeDtypeStruct((sz.slot_lines * WIDTH + WIDTH,), jnp.int32),
            jax.ShapeDtypeStruct((sz.facts, WIDTH), jnp.float32),
        ],
        scratch_shapes=[pltpu.SMEM((devices,), jnp.int32)],
    )(wet_list, wet_owner, remap_src, remap_tgt, remap_weight, me)

    mix = jnp.broadcast_to(
        chan_mix.transpose(1, 2, 0).reshape(CHANNELS * CHANNELS, LEVELS, 1),
        (CHANNELS * CHANNELS, LEVELS, WIDTH),
    )
    start_pert = to_bulk(perturbation)
    field = start_pert + to_bulk(base_state)
    target = to_bulk(target_state)
    target_surface = to_surface(sz, target_state[0])

    def all_channels(array):
        return to_surface(sz, jnp.broadcast_to(array[:, None, :], (rows, CHANNELS, sz.cells)))

    weight_surface = all_channels(cost_weight)
    diffusivity_surface = all_channels(diffusivity)
    diffusivity = diffusivity.reshape(rows, 1, sz.cells)
    weight = cost_weight.reshape(rows, 1, sz.cells)

    wider = (rows + 2, CHANNELS, LEVELS, sz.cells)
    row_surface = (sz.row_width, WIDTH)
    row_sems = pltpu.SemaphoreType.DMA((rows,))
    two_row_sems = pltpu.SemaphoreType.DMA((2, rows))
    edge_sems = pltpu.SemaphoreType.DMA((2,))

    saved = []
    surface = None
    told = None
    for hour in range(hours):
        first, last = hour == 0, hour == hours - 1
        inputs = anywhere(field, *edges) + near_by(diffusivity, mix) + scalars(table, facts)
        if first:
            inputs += near_by(facts)
        else:
            inputs += near_by(surface, *surface_edges)
        if last:
            inputs += near_by(target, weight)
        field, drive, surface, packed, *sends = call(
            functools.partial(forward_kernel, sz, first, last),
            "step",
            inputs,
            shipped=[
                sz.whole, sz.whole, sz.surface, sz.narrow, sz.told, sz.told, sz.edge, sz.edge
            ],
            scratch=[wider, row_sems, edge_sems],
        )
        arrived = exchange(packed, devices)
        got = swap(*sends[:2])
        if first:
            told = got
        flux, mixed_slope, flux_slope = call(
            functools.partial(owner_kernel, sz),
            "owners",
            near_by(arrived, mixing, air_temp[hour, 0], wind_speed[hour, 0])
            + scalars(coupler_mix),
            shipped=[sz.wide, sz.by_slot, sz.by_slot],
            scratch=[sz.narrow, (sz.slots, WIDTH)],
        )
        flux, *sends = lax.optimization_barrier((flux, *sends[2:]))
        flux = exchange(flux, devices)
        edges = swap(*sends)
        inputs = near_by(flux, surface, *got) + scalars(table, facts, *told)
        near = [sz.near, sz.near]
        if last:
            surface, slope, packed, *sends = call(
                functools.partial(surface_kernel, sz, True),
                "surface",
                inputs + near_by(target_surface, weight_surface),
                shipped=[sz.surface, sz.slope, sz.wide, sz.lats, sz.lats],
                scratch=near,
            )
        else:
            surface, *sends, slope = call(
                functools.partial(surface_kernel, sz, False),
                "surface",
                inputs,
                kept=[sz.surface, row_surface, row_surface],
                shipped=[sz.slope],
                scratch=near,
            )
            surface_edges = swap(*sends)
        saved.append((drive, slope, mixed_slope, flux_slope))

    edge_sends = None
    for hour in reversed(range(hours)):
        drive, slope, mixed_slope, flux_slope = saved[hour]
        arrived = exchange(packed, devices)
        got = swap(*sends)
        back = call(
            functools.partial(owner_back_kernel, sz),
            "owners_back",
            near_by(arrived, mixing, mixed_slope, flux_slope) + scalars(coupler_mix),
            shipped=[sz.narrow],
            scratch=[sz.narrow, (sz.slots, WIDTH)],
        )[0]
        if edge_sends is not None:
            back, *edge_sends = lax.optimization_barrier((back, *edge_sends))
            edges = swap(*edge_sends)
        back = exchange(back, devices)
        surface, *row_sends = call(
            functools.partial(merge_kernel, sz),
            "merge",
            near_by(back, surface, slope, *got)
            + scalars(table, facts)
            + near_by(diffusivity_surface),
            kept=[sz.surface, row_surface, row_surface],
        )
        surface_edges = swap(*row_sends)
        inputs = (
            anywhere(field)
            + near_by(surface)
            + anywhere(*edges)
            + near_by(*surface_edges)
            + anywhere(drive)
            + near_by(diffusivity, mix)
        )
        if hour > 0:
            field, surface, packed, *sends = call(
                functools.partial(backward_kernel, sz, False),
                "step_back",
                inputs + scalars(table, facts, *told) + near_by(saved[hour - 1][1]),
                shipped=[sz.whole, sz.surface, sz.wide, sz.lats, sz.lats, sz.edge, sz.edge],
                scratch=[sz.whole, sz.whole, wider, sz.near, sz.near, two_row_sems, edge_sems],
            )
            sends, edge_sends = sends[:2], sends[2:]
        else:
            gradient, sums = call(
                functools.partial(backward_kernel, sz, True),
                "step_back_sums",
                inputs + near_by(start_pert),
                shipped=[sz.whole, (devices, WIDTH)],
                scratch=[sz.whole, sz.whole, wider, two_row_sems, edge_sems],
            )

    everyones = lax.all_to_all(sums, "horiz", split_axis=0, concat_axis=0, tiled=True)
    block = perturbation.shape
    return call(
        functools.partial(final_kernel, perturbation.size * devices),
        "finish",
        near_by(everyones) + anywhere(perturbation, gradient.transpose(2, 0, 1, 3)),
        shipped=[block],
        scratch=[block, block, pltpu.SemaphoreType.DMA((2, block[0]))],
    )[0]


def solution(mesh):
    placed = (
        P("member", "horiz", None, None),
        P(None, "horiz", None, None),
        P(None, "horiz", None, None),
        P("horiz", None),
        P("horiz", None),
        P(),
        P(),
        P("horiz", None, None),
        P(None, "horiz", None, None),
        P(None, "horiz", None, None),
        P("horiz", None),
        P("horiz", None),
        P("horiz"),
        P("horiz"),
        P("horiz"),
    )
    return jax.shard_map(
        body,
        mesh=mesh,
        in_specs=placed,
        out_specs=P("member", "horiz", None, None),
        check_vma=False,
    )
```

```python
import functools

import jax
import jax.numpy as jnp
from jax import lax
from jax.experimental import pallas as pl
from jax.experimental.pallas import tpu as pltpu
from jax.sharding import PartitionSpec as P

LAT_DEV = 2
NEAR_LAT = LAT_DEV + 2
CHANNELS = 4
LEVELS = 8
WIDTH = 128
SUBLANES = 8

KAPPA_V = 0.1
TIME_STEP = 0.3
FLUX_RATE = 0.05
FEEDBACK = 0.5
ASCENT = 0.5
EPSILON = 1e-06
HIGHEST = lax.Precision.HIGHEST
VMEM_BYTES = 60 * 1024 * 1024


class Sizes:
    def __init__(self, devices, capacity, rows, cells):
        self.devices = devices
        self.capacity = capacity
        self.slots = devices * capacity
        self.rows = rows
        self.cells = cells
        self.row_tiles = cells // WIDTH
        self.tiles = rows * self.row_tiles
        self.row_width = CHANNELS * self.row_tiles
        self.pitch = -(-self.row_tiles // SUBLANES) * SUBLANES
        self.own_rows = CHANNELS * capacity
        self.chunk = -(-(self.own_rows + 2 * capacity) // SUBLANES) * SUBLANES
        self.slot_lines = -(-self.slots // WIDTH)
        self.facts = -(-(self.slot_lines + 1) // SUBLANES) * SUBLANES
        self.lat_lines = LAT_DEV * self.pitch
        self.whole = (rows, CHANNELS, LEVELS, cells)
        self.edge = (CHANNELS, LEVELS, cells)
        self.surface = (CHANNELS * (self.tiles + 1), WIDTH)
        self.narrow = (CHANNELS * self.slots, WIDTH)
        self.wide = (devices * self.chunk, WIDTH)
        self.slope = (NEAR_LAT * self.pitch, WIDTH)
        self.lats = (self.lat_lines, WIDTH)
        self.told = (self.lat_lines + self.facts, WIDTH)
        self.near = (-(-(self.tiles + 1) // SUBLANES) * SUBLANES, WIDTH)
        self.by_slot = (CHANNELS, self.slots, WIDTH)


class Shipped:
    def __init__(self, block, home, sems):
        self.block, self.home, self.sems = block, home, sems
        self.by_row = False
        self.started = False

    def __getitem__(self, at):
        return self.block[at]

    def __setitem__(self, at, value):
        self.block[at] = value

    def row(self, index):
        self.by_row = True
        self.started = True
        return pltpu.make_async_copy(
            self.block.at[index], self.home.at[index], self.sems.at[index]
        )

    def all(self):
        return pltpu.make_async_copy(self.block, self.home, self.sems.at[0])

    def start(self):
        self.started = True
        self.all().start()

    def finish(self, rows):
        if self.by_row:
            for index in range(rows):
                self.row(index).wait()
        else:
            self.all().wait()


def cols(tile):
    return slice(tile * WIDTH, (tile + 1) * WIDTH)


def lanes_sum(left_here, left_before, right_here, right_after, lane):
    return jnp.where(lane == 0, left_before, left_here) + jnp.where(
        lane == WIDTH - 1, right_after, right_here
    )


def levels_sum(field, sub):
    return jnp.where(sub == 0, 0.0, pltpu.roll(field, 1, 0)) + jnp.where(
        sub == LEVELS - 1, 0.0, pltpu.roll(field, LEVELS - 1, 0)
    )


def row_tiles_of(sz, ref, row):
    return ref[pl.ds(row * sz.row_width, sz.row_tiles, stride=CHANNELS), :]


def put_row_tiles(sz, ref, row, value):
    ref[pl.ds(row * sz.row_width, sz.row_tiles, stride=CHANNELS), :] = value


def near_row(sz, ref, row):
    return ref[row * sz.row_tiles : (row + 1) * sz.row_tiles, :]


def load_surface_row(sz, target, row, source, base):
    for tile in range(sz.row_tiles):
        for channel in range(CHANNELS):
            at = base + tile * CHANNELS + channel
            target[row, channel, 0:1, cols(tile)] = source[pl.ds(at, 1), :]


def as_column(row, size):
    shape = (size, row.shape[1])
    diagonal = lax.broadcasted_iota(jnp.int32, shape, 0) == lax.broadcasted_iota(jnp.int32, shape, 1)
    return jnp.sum(jnp.where(diagonal, row, 0.0), axis=1, keepdims=True)


def tables_kernel(sz, entries, remap_entries, wet, remap, table, facts):
    tiles, owners = wet[0:1, :], wet[1:2, :]
    size = -(-entries // SUBLANES) * SUBLANES
    shape = (size, wet.shape[1])
    tile_here, owner_here = as_column(tiles, size), as_column(owners, size)
    earlier = lax.broadcasted_iota(jnp.int32, shape, 1) < lax.broadcasted_iota(jnp.int32, shape, 0)
    same = (owner_here == owners) & earlier
    rank = jnp.sum(jnp.where(same, 1.0, 0.0), axis=1, keepdims=True)
    slot = jnp.where(owner_here >= 0.0, owner_here * sz.capacity + rank, -1.0)
    facts[...] = jnp.zeros(facts.shape, jnp.float32)
    for line in range(sz.slot_lines):
        place = lax.broadcasted_iota(jnp.int32, (size, WIDTH), 1) + line * WIDTH
        match = slot.astype(jnp.int32) == place
        told = jnp.sum(jnp.where(match, sz.tiles - tile_here, 0.0), axis=0, keepdims=True)
        facts[line : line + 1, :] = told
        table[line : line + 1, :] = sz.tiles - told.astype(jnp.int32)
    size = -(-remap_entries // SUBLANES) * SUBLANES
    at, weight = as_column(remap[0:1, :], size), as_column(remap[1:2, :], size)
    place = lax.broadcasted_iota(jnp.int32, (size, WIDTH), 1)
    facts[sz.slot_lines : sz.slot_lines + 1, :] = jnp.sum(
        jnp.where(at.astype(jnp.int32) == place, weight, 0.0), axis=0, keepdims=True
    )


class Remap:
    def __init__(self, sz, facts, low, high):
        self.sz, self.facts, self.low, self.high = sz, facts, low, high

    def own(self, lat, row):
        return self.facts[self.sz.slot_lines, lat * self.sz.rows + row]

    def beside(self, told, lat, row):
        return told[self.sz.lat_lines + self.sz.slot_lines, lat * self.sz.rows + row]

    def of_low(self, lat, row):
        return self.beside(self.low, lat + LAT_DEV, row)

    def of_high(self, lat, row):
        return self.beside(self.high, lat - LAT_DEV, row)

    def tile(self, told, slot):
        line = self.sz.lat_lines + slot // WIDTH
        return self.sz.tiles - told[line, slot % WIDTH].astype(jnp.int32)


def sum_of(weights, values):
    total = weights[0] * values[0]
    for weight, value in zip(weights[1:], values[1:]):
        total = total + weight * value
    return total


def own_sums(sz, remap, own, factor):
    return [
        factor * sum_of([remap.own(lat, row) for row in range(sz.rows)], own)
        for lat in range(NEAR_LAT)
    ]


def send_sums(sz, sums, send_low, send_high):
    for lat in range(NEAR_LAT):
        send = send_low if lat < LAT_DEV else send_high
        at = (lat % LAT_DEV) * sz.pitch
        send[at : at + sz.row_tiles, :] = sums[lat]


def lat_rows(sz, ref, lat):
    return ref[lat * sz.pitch : lat * sz.pitch + sz.row_tiles, :]


def told_sums(sz, from_low, from_high):
    return [
        lat_rows(sz, from_low if lat < LAT_DEV else from_high, lat % LAT_DEV)
        for lat in range(NEAR_LAT)
    ]


def forward_kernel(sz, first, last, *refs):
    refs = list(refs)
    field, low, high, diffusivity, mix, table, own_facts = refs[:7]
    refs = refs[7:]
    if first:
        facts = refs[0]
        refs = refs[1:]
    else:
        surface, low_surface, high_surface = refs[:3]
        refs = refs[3:]
    if last:
        target, weight = refs[:2]
        refs = refs[2:]
    out, drive, new_surface, packed, tell_low, tell_high, edge_low, edge_high = refs[:8]
    padded, in_sems, edge_sems = refs[8:]
    remap = Remap(sz, own_facts, None, None)

    edges = [
        pltpu.make_async_copy(low, padded.at[0], edge_sems.at[0]),
        pltpu.make_async_copy(high, padded.at[sz.rows + 1], edge_sems.at[1]),
    ]

    def arrival(row):
        return pltpu.make_async_copy(field.at[row], padded.at[row + 1], in_sems.at[row])

    edges[0].start()
    for row in range(sz.rows):
        arrival(row).start()
    edges[1].start()

    def ready(row):
        arrival(row).wait()
        if not first:
            load_surface_row(sz, padded, row + 1, surface, row * sz.row_width)

    for side in (0, 1):
        edges[side].wait()
        if not first:
            source = high_surface if side else low_surface
            load_surface_row(sz, padded, (sz.rows + 1) * side, source, 0)
    ready(0)

    lane = lax.broadcasted_iota(jnp.int32, (LEVELS, WIDTH), 1)
    sub = lax.broadcasted_iota(jnp.int32, (LEVELS, WIDTH), 0)
    count = sz.row_tiles

    def one_row(row, carry):
        @pl.when(row < sz.rows - 1)
        def _():
            ready(row + 1)

        here = [[padded[row + 1, c, :, cols(t)] for t in range(count)] for c in range(CHANNELS)]
        for t in range(count):
            coeff = jnp.broadcast_to(diffusivity[row, 0:1, cols(t)], (LEVELS, WIDTH))
            if last:
                scale = weight[row, 0:1, cols(t)]
                scale = jnp.broadcast_to(scale * scale, (LEVELS, WIDTH))
            for c in range(CHANNELS):
                mixed = mix[c * CHANNELS] * here[0][t]
                for k in range(1, CHANNELS):
                    mixed = mixed + mix[c * CHANNELS + k] * here[k][t]
                bent = jnp.tanh(mixed)
                drive[row, c, :, cols(t)] = bent
                field_here = here[c][t]
                around = lanes_sum(
                    pltpu.roll(field_here, 1, 1),
                    pltpu.roll(here[c][(t - 1) % count], 1, 1),
                    pltpu.roll(field_here, WIDTH - 1, 1),
                    pltpu.roll(here[c][(t + 1) % count], WIDTH - 1, 1),
                    lane,
                )
                around = around + (padded[row, c, :, cols(t)] + padded[row + 2, c, :, cols(t)])
                stepped = (
                    field_here
                    + coeff * (around - 4.0 * field_here)
                    + KAPPA_V * (levels_sum(field_here, sub) - 2.0 * field_here)
                    + TIME_STEP * bent
                )
                new_surface[pl.ds((row * count + t) * CHANNELS + c, 1), :] = stepped[0:1, :]
                if last:
                    stepped = scale * (stepped - target[row, c, :, cols(t)])
                out[row, c, :, cols(t)] = stepped
        drive.row(row).start()
        out.row(row).start()
        return carry

    lax.fori_loop(0, sz.rows, one_row, 0)
    new_surface[CHANNELS * sz.tiles :, :] = jnp.zeros((CHANNELS, WIDTH), jnp.float32)
    new_surface.start()
    pack_slots(sz, table, new_surface, packed)
    packed.start()
    own = [row_tiles_of(sz, new_surface.block, row) for row in range(sz.rows)]
    send_sums(sz, own_sums(sz, remap, own, 1.0), tell_low, tell_high)
    blank = facts[...] if first else jnp.zeros((sz.facts, WIDTH), jnp.float32)
    for tell in (tell_low, tell_high):
        tell[sz.lat_lines :, :] = blank
        tell.start()
    store_edges(sz, out, diffusivity if last else None, edge_low, edge_high)


def pack_slots(sz, table, surface, packed):
    for slot in range(sz.slots):
        at = pl.multiple_of(table[slot // WIDTH, slot % WIDTH] * CHANNELS, CHANNELS)
        packed[slot * CHANNELS : (slot + 1) * CHANNELS, :] = surface[pl.ds(at, CHANNELS), :]


def store_edges(sz, field, diffusivity, send_low, send_high):
    for row, send in ((0, send_low), (sz.rows - 1, send_high)):
        for channel in range(CHANNELS):
            for tile in range(sz.row_tiles):
                value = field[row, channel, :, cols(tile)]
                if diffusivity is not None:
                    value = value * jnp.broadcast_to(
                        diffusivity[row, 0:1, cols(tile)], (LEVELS, WIDTH)
                    )
                send[channel, :, cols(tile)] = value
        send.start()


def owner_kernel(sz, arrived, mixing, air, wind, bulk, flux, mixed_slope, flux_slope, flat, first):
    slots = sz.slots
    values = [arrived[pl.ds(c, slots, stride=CHANNELS), :] for c in range(CHANNELS)]
    mixed = jnp.tanh(
        jnp.dot(
            mixing[...],
            jnp.concatenate(values, axis=1),
            precision=HIGHEST,
            preferred_element_type=jnp.float32,
        )
    )
    contrast = []
    for c in range(CHANNELS):
        mixed_here = mixed[:, cols(c)]
        mixed_slope[c] = 1.0 - mixed_here * mixed_here
        contrast.append((air[...] - values[0] if c == 0 else values[c]) + mixed_here)
    mixed_slope.start()
    rate = FLUX_RATE * wind[...]
    for c in range(CHANNELS):
        forcing = bulk[c, 0] * contrast[0]
        for k in range(1, CHANNELS):
            forcing = forcing + bulk[c, k] * contrast[k]
        bent = jnp.tanh(forcing)
        flux_slope[c] = rate * (1.0 - bent * bent)
        one = rate * bent
        flat[pl.ds(c, slots, stride=CHANNELS), :] = one
        if c == 0:
            first[...] = one
    flux_slope.start()
    cap = sz.capacity
    gap = jnp.zeros((sz.chunk - sz.own_rows, WIDTH), jnp.float32)
    for d in range(sz.devices):
        at = d * sz.chunk
        flux[at : at + sz.own_rows, :] = flat[d * sz.own_rows : (d + 1) * sz.own_rows, :]
        at = at + sz.own_rows
        flux[at : (d + 1) * sz.chunk, :] = gap
        if d > 0:
            flux[at : at + cap, :] = first[(d - 1) * cap : d * cap, :]
        if d < sz.devices - 1:
            flux[at + cap : at + 2 * cap, :] = first[(d + 1) * cap : (d + 2) * cap, :]


def owner_back_kernel(sz, arrived, mixing, mixed_slope, flux_slope, bulk, back, flat, extra):
    slots, cap = sz.slots, sz.capacity
    for d in range(sz.devices):
        at = d * sz.chunk
        flat[d * sz.own_rows : (d + 1) * sz.own_rows, :] = arrived[at : at + sz.own_rows, :]
        more = jnp.zeros((cap, WIDTH), jnp.float32)
        if d < sz.devices - 1:
            at = (d + 1) * sz.chunk + sz.own_rows
            more = more + arrived[at : at + cap, :]
        if d > 0:
            at = (d - 1) * sz.chunk + sz.own_rows + cap
            more = more + arrived[at : at + cap, :]
        extra[d * cap : (d + 1) * cap, :] = more
    forced = []
    for c in range(CHANNELS):
        got = flat[pl.ds(c, slots, stride=CHANNELS), :]
        if c == 0:
            got = got + extra[...]
        forced.append(flux_slope[c] * got)
    direct = []
    for k in range(CHANNELS):
        total = bulk[0, k] * forced[0]
        for c in range(1, CHANNELS):
            total = total + bulk[c, k] * forced[c]
        direct.append(total)
    through = lax.dot_general(
        mixing[...],
        jnp.concatenate([direct[k] * mixed_slope[k] for k in range(CHANNELS)], axis=1),
        (((0,), (0,)), ((), ())),
        precision=HIGHEST,
        preferred_element_type=jnp.float32,
    )
    for k in range(CHANNELS):
        sign = -1.0 if k == 0 else 1.0
        back.block[pl.ds(k, slots, stride=CHANNELS), :] = through[:, cols(k)] + sign * direct[k]


def spread_back(sz, surface, slope, remap, table, packed, near_low, near_high, tell_low, tell_high):
    rows, count, cap = sz.rows, sz.row_tiles, sz.capacity
    block = surface.block
    own = [row_tiles_of(sz, block, row) for row in range(rows)]
    sums = own_sums(sz, remap, own, FEEDBACK)
    send_sums(sz, sums, tell_low, tell_high)
    tell_low.start()
    tell_high.start()
    lats = [lat_rows(sz, slope, lat) * sums[lat] for lat in range(NEAR_LAT)]
    every = range(NEAR_LAT)
    for row in range(rows):
        added = sum_of([remap.own(lat, row) for lat in every], lats)
        put_row_tiles(sz, block, row, own[row] + added)
        at = row * count
        near_low[at : at + count, :] = sum_of(
            [remap.of_low(lat, row) for lat in range(LAT_DEV)], lats[:LAT_DEV]
        )
        near_high[at : at + count, :] = sum_of(
            [remap.of_high(lat, row) for lat in range(LAT_DEV, NEAR_LAT)], lats[LAT_DEV:]
        )
    rest = sz.near[0] - sz.tiles
    near_low[sz.tiles :, :] = jnp.zeros((rest, WIDTH), jnp.float32)
    near_high[sz.tiles :, :] = jnp.zeros((rest, WIDTH), jnp.float32)
    surface.start()
    gap = jnp.zeros((sz.chunk - sz.own_rows, WIDTH), jnp.float32)
    for owner in range(sz.devices):
        packed[owner * sz.chunk + sz.own_rows : (owner + 1) * sz.chunk, :] = gap
    for slot in range(sz.slots):
        owner, rank = slot // cap, slot % cap
        at = owner * sz.chunk + rank * CHANNELS
        tile = pl.multiple_of(table[slot // WIDTH, slot % WIDTH] * CHANNELS, CHANNELS)
        packed[at : at + CHANNELS, :] = surface[pl.ds(tile, CHANNELS), :]
        at = owner * sz.chunk + sz.own_rows + rank
        packed[at : at + 1, :] = near_low[pl.ds(remap.tile(remap.low, slot), 1), :]
        at = at + cap
        packed[at : at + 1, :] = near_high[pl.ds(remap.tile(remap.high, slot), 1), :]


def surface_kernel(sz, last, *refs):
    refs = list(refs)
    flux, before, from_low, from_high, table, facts, told_low, told_high = refs[:8]
    refs = refs[8:]
    if last:
        target, weight = refs[:2]
        surface, slope, packed, tell_low, tell_high, near_low, near_high = refs[2:]
        block = surface.block
    else:
        surface, send_low, send_high, slope, near_low, near_high = refs
        block = surface
    remap = Remap(sz, facts, told_low, told_high)
    rows, cap = sz.rows, sz.capacity
    block[...] = before[...]
    near_low[...] = jnp.zeros(sz.near, jnp.float32)
    near_high[...] = jnp.zeros(sz.near, jnp.float32)
    for slot in range(sz.slots):
        owner, rank = slot // cap, slot % cap
        at = owner * sz.chunk + rank * CHANNELS
        tile = pl.multiple_of(table[slot // WIDTH, slot % WIDTH] * CHANNELS, CHANNELS)
        block[pl.ds(tile, CHANNELS), :] = (
            before[pl.ds(tile, CHANNELS), :] + flux[at : at + CHANNELS, :]
        )
        at = owner * sz.chunk + sz.own_rows + rank
        near_low[pl.ds(remap.tile(told_low, slot), 1), :] = flux[at : at + 1, :]
        at = at + cap
        near_high[pl.ds(remap.tile(told_high, slot), 1), :] = flux[at : at + 1, :]
    block[CHANNELS * sz.tiles :, :] = jnp.zeros((CHANNELS, WIDTH), jnp.float32)
    own = [row_tiles_of(sz, block, row) for row in range(rows)]
    sums = own_sums(sz, remap, own, 1.0)
    told = told_sums(sz, from_low, from_high)
    air = []
    for lat in range(NEAR_LAT):
        if lat < LAT_DEV:
            near, weights = near_low, [remap.of_low(lat, row) for row in range(rows)]
        else:
            near, weights = near_high, [remap.of_high(lat, row) for row in range(rows)]
        more = sum_of(weights, [near_row(sz, near, row) for row in range(rows)])
        one = jnp.tanh(sums[lat] + told[lat] + more)
        slope[lat * sz.pitch : lat * sz.pitch + sz.row_tiles, :] = 1.0 - one * one
        air.append(one)
    slope.start()
    for row in range(rows):
        weights = [remap.own(lat, row) for lat in range(NEAR_LAT)]
        put_row_tiles(sz, block, row, own[row] + FEEDBACK * sum_of(weights, air))
    if last:
        end = CHANNELS * sz.tiles
        scale = weight[...]
        block[0:end, :] = scale * scale * (block[0:end, :] - target[...])
        spread_back(
            sz, surface, slope, remap, table, packed, near_low, near_high, tell_low, tell_high
        )
    else:
        send_low[...] = surface[0 : sz.row_width, :]
        send_high[...] = surface[(rows - 1) * sz.row_width : rows * sz.row_width, :]


def merge_kernel(
    sz, back, before, slope, from_low, from_high, table, facts, diffusivity, surface, send_low, send_high
):
    rows, width = sz.rows, sz.row_width
    remap = Remap(sz, facts, None, None)
    surface[...] = before[...]
    for slot in range(sz.slots):
        tile = pl.multiple_of(table[slot // WIDTH, slot % WIDTH] * CHANNELS, CHANNELS)
        surface[pl.ds(tile, CHANNELS), :] = (
            before[pl.ds(tile, CHANNELS), :] + back[slot * CHANNELS : (slot + 1) * CHANNELS, :]
        )
    surface[CHANNELS * sz.tiles :, :] = jnp.zeros((CHANNELS, WIDTH), jnp.float32)
    told = told_sums(sz, from_low, from_high)
    lats = [lat_rows(sz, slope, lat) * told[lat] for lat in range(NEAR_LAT)]
    for row in range(rows):
        own = row_tiles_of(sz, surface, row)
        weights = [remap.own(lat, row) for lat in range(NEAR_LAT)]
        put_row_tiles(sz, surface, row, own + sum_of(weights, lats))
    send_low[...] = diffusivity[0:width, :] * surface[0:width, :]
    end = rows * width
    send_high[...] = diffusivity[end - width : end, :] * surface[end - width : end, :]


def backward_kernel(sz, last, *refs):
    refs = list(refs)
    field, surface, low, high, low_surface, high_surface, drive, diffusivity, mix = refs[:9]
    refs = refs[9:]
    if last:
        perturbation, out, sums = refs[:3]
        local, bent_all, padded, in_sems, edge_sems = refs[3:]
    else:
        table, facts, told_low, told_high, slope = refs[:5]
        out, new_surface, packed, tell_low, tell_high, edge_low, edge_high = refs[5:12]
        local, bent_all, padded, near_low, near_high, in_sems, edge_sems = refs[12:]
        remap = Remap(sz, facts, told_low, told_high)
    count = sz.row_tiles

    edges = [
        pltpu.make_async_copy(low, padded.at[0], edge_sems.at[0]),
        pltpu.make_async_copy(high, padded.at[sz.rows + 1], edge_sems.at[1]),
    ]

    def arrivals(row):
        return [
            pltpu.make_async_copy(field.at[row], local.at[row], in_sems.at[0, row]),
            pltpu.make_async_copy(drive.at[row], bent_all.at[row], in_sems.at[1, row]),
        ]

    edges[0].start()
    for row in range(sz.rows):
        for arrival in arrivals(row):
            arrival.start()
    edges[1].start()

    def ready(row):
        for arrival in arrivals(row):
            arrival.wait()
        load_surface_row(sz, local, row, surface, row * sz.row_width)
        for t in range(count):
            coeff = jnp.broadcast_to(diffusivity[row, 0:1, cols(t)], (LEVELS, WIDTH))
            for c in range(CHANNELS):
                padded[row + 1, c, :, cols(t)] = coeff * local[row, c, :, cols(t)]

    for side in (0, 1):
        edges[side].wait()
        source = high_surface if side else low_surface
        load_surface_row(sz, padded, (sz.rows + 1) * side, source, 0)
    ready(0)
    lane = lax.broadcasted_iota(jnp.int32, (LEVELS, WIDTH), 1)
    sub = lax.broadcasted_iota(jnp.int32, (LEVELS, WIDTH), 0)

    def one_row(row, carry):
        @pl.when(row < sz.rows - 1)
        def _():
            ready(row + 1)

        scaled = [[padded[row + 1, c, :, cols(t)] for t in range(count)] for c in range(CHANNELS)]
        for t in range(count):
            here, bent = [], []
            for c in range(CHANNELS):
                value = local[row, c, :, cols(t)]
                one = bent_all[row, c, :, cols(t)]
                here.append(value)
                bent.append((1.0 - one * one) * value)
            for c in range(CHANNELS):
                mixed = mix[c] * bent[0]
                for k in range(1, CHANNELS):
                    mixed = mixed + mix[k * CHANNELS + c] * bent[k]
                around = lanes_sum(
                    pltpu.roll(scaled[c][t], 1, 1),
                    pltpu.roll(scaled[c][(t - 1) % count], 1, 1),
                    pltpu.roll(scaled[c][t], WIDTH - 1, 1),
                    pltpu.roll(scaled[c][(t + 1) % count], WIDTH - 1, 1),
                    lane,
                )
                around = around + (padded[row, c, :, cols(t)] + padded[row + 2, c, :, cols(t)])
                stepped = (
                    here[c]
                    + (around - 4.0 * scaled[c][t])
                    + KAPPA_V * (levels_sum(here[c], sub) - 2.0 * here[c])
                    + TIME_STEP * mixed
                )
                out[row, c, :, cols(t)] = stepped
                if last:
                    start = perturbation[row, c, :, cols(t)]
                    carry = (
                        carry[0] + start * start,
                        carry[1] + start * stepped,
                        carry[2] + stepped * stepped,
                    )
                else:
                    new_surface[pl.ds((row * count + t) * CHANNELS + c, 1), :] = stepped[0:1, :]
        out.row(row).start()
        return carry

    blank = jnp.zeros((LEVELS, WIDTH), jnp.float32)
    totals = lax.fori_loop(0, sz.rows, one_row, (blank, blank, blank) if last else 0)
    if last:
        place = lax.broadcasted_iota(jnp.int32, sums.block.shape, 1)
        held = jnp.zeros(sums.block.shape, jnp.float32)
        for index in range(3):
            total = jnp.sum(jnp.sum(totals[index], axis=0, keepdims=True), axis=1, keepdims=True)
            held = jnp.where(place == index, total, held)
        sums[...] = held
    else:
        new_surface[CHANNELS * sz.tiles :, :] = jnp.zeros((CHANNELS, WIDTH), jnp.float32)
        spread_back(
            sz, new_surface, slope, remap, table, packed, near_low, near_high, tell_low, tell_high
        )
        packed.start()
        store_edges(sz, out, diffusivity, edge_low, edge_high)


def final_kernel(cell_total, everyones, perturbation, gradient, out, start, slope, in_sems):
    levels = start.shape[0]

    def arrivals(level):
        return [
            pltpu.make_async_copy(perturbation.at[level], start.at[level], in_sems.at[0, level]),
            pltpu.make_async_copy(gradient.at[level], slope.at[level], in_sems.at[1, level]),
        ]

    for level in range(levels):
        for arrival in arrivals(level):
            arrival.start()
    sums = jnp.sum(everyones[...], axis=0, keepdims=True) / cell_total
    place = lax.broadcasted_iota(jnp.int32, sums.shape, 1)
    means = [
        jnp.broadcast_to(
            jnp.sum(jnp.where(place == index, sums, 0.0), axis=1, keepdims=True), (1, WIDTH)
        )
        for index in range(3)
    ]
    scale = lax.rsqrt(means[2] + EPSILON)
    mean_sq = means[0] + 2.0 * ASCENT * scale * means[1] + ASCENT * ASCENT * scale * scale * means[2]
    shrink = lax.rsqrt(mean_sq + EPSILON)
    step = jnp.broadcast_to(ASCENT * scale, (CHANNELS, WIDTH))
    shrink = jnp.broadcast_to(shrink, (CHANNELS, WIDTH))
    for level in range(levels):
        for arrival in arrivals(level):
            arrival.wait()
        for row in range(start.shape[1]):
            for tile in range(start.shape[3] // WIDTH):
                value = start[level, row, :, cols(tile)] + step * slope[level, row, :, cols(tile)]
                out[level, row, :, cols(tile)] = value * shrink
        out.row(level).start()


def near_by(*arrays):
    return [(array, pltpu.VMEM) for array in arrays]


def scalars(*arrays):
    return [(array, pltpu.SMEM) for array in arrays]


def anywhere(*arrays):
    return [(array, pl.ANY) for array in arrays]


def call(kernel, name, inputs, kept=(), shipped=(), scratch=()):
    n_in, n_kept, n_out = len(inputs), len(kept), len(shipped)

    def run(*refs):
        ins = refs[: n_in + n_kept]
        homes = refs[n_in + n_kept : n_in + n_kept + n_out]
        rest = refs[n_in + n_kept + n_out :]
        outs = [
            Shipped(block, home, sems)
            for block, home, sems in zip(rest[:n_out], homes, rest[n_out : 2 * n_out])
        ]
        kernel(*ins, *outs, *rest[2 * n_out :])
        for out in outs:
            if not out.started:
                out.start()
        for out in outs:
            out.finish(out.block.shape[0])

    shapes = list(kept) + list(shipped)
    spaces = [pltpu.VMEM] * n_kept + [pltpu.HBM] * n_out
    blocks = [pltpu.VMEM(shape, jnp.float32) for shape in shipped]
    sems = [
        pltpu.SemaphoreType.DMA((shape[0] if len(shape) > 3 else 1,)) for shape in shipped
    ]
    more = [
        item if not isinstance(item, tuple) else pltpu.VMEM(item, jnp.float32) for item in scratch
    ]
    return pl.pallas_call(
        run,
        name=name,
        in_specs=[pl.BlockSpec(memory_space=space) for _, space in inputs],
        out_specs=[pl.BlockSpec(memory_space=space) for space in spaces],
        out_shape=[jax.ShapeDtypeStruct(shape, jnp.float32) for shape in shapes],
        scratch_shapes=blocks + sems + more,
        compiler_params=pltpu.CompilerParams(vmem_limit_bytes=VMEM_BYTES),
    )(*[array for array, _ in inputs])


def to_bulk(field):
    return field.transpose(1, 2, 0, 3)


def to_surface(sz, rows):
    split = rows.reshape(sz.rows, CHANNELS, sz.row_tiles, WIDTH).transpose(0, 2, 1, 3)
    return split.reshape(CHANNELS * sz.tiles, WIDTH)


def swap(low, high):
    count = lax.axis_size("horiz")
    upward = [(i, i + 1) for i in range(count - 1)]
    downward = [(target, source) for source, target in upward]
    return lax.ppermute(high, "horiz", upward), lax.ppermute(low, "horiz", downward)


def exchange(array, devices):
    rows = array.shape[0] // devices
    split = array.reshape(devices, rows // CHANNELS, CHANNELS, WIDTH)
    moved = lax.all_to_all(split, "horiz", split_axis=0, concat_axis=0, tiled=True)
    return moved.reshape(array.shape)


def body(
    perturbation,
    base_state,
    target_state,
    cost_weight,
    diffusivity,
    chan_mix,
    coupler_mix,
    owner_mix,
    air_temp,
    wind_speed,
    wet_list,
    wet_owner,
    remap_src,
    remap_tgt,
    remap_weight,
):
    devices = lax.axis_size("horiz")
    hours = air_temp.shape[0]
    sz = Sizes(devices, air_temp.shape[2] // devices, base_state.shape[1], base_state.shape[3])
    mixing = owner_mix[0]
    rows = sz.rows

    start = [
        (perturbation[:, row] + base_state[:, row]).transpose(1, 0, 2) for row in (0, rows - 1)
    ]
    edges = swap(*start)
    me = lax.axis_index("horiz").astype(jnp.int32)

    def lined(first_row, second_row):
        size = -(-first_row.shape[0] // WIDTH) * WIDTH
        pair = jnp.stack([first_row.astype(jnp.float32), second_row.astype(jnp.float32)])
        return jnp.pad(pair, ((0, 0), (0, size - pair.shape[1])), constant_values=-1.0)

    remap_at = (remap_tgt - (me * LAT_DEV - 1)) * rows + remap_src - me * rows
    table, facts = pl.pallas_call(
        functools.partial(tables_kernel, sz, wet_list.shape[1], remap_src.shape[0]),
        name="tables",
        out_shape=[
            jax.ShapeDtypeStruct((sz.slot_lines, WIDTH), jnp.int32),
            jax.ShapeDtypeStruct((sz.facts, WIDTH), jnp.float32),
        ],
    )(lined(wet_list[0], wet_owner[0]), lined(remap_at, remap_weight))

    mix = jnp.broadcast_to(
        chan_mix.transpose(1, 2, 0).reshape(CHANNELS * CHANNELS, LEVELS, 1),
        (CHANNELS * CHANNELS, LEVELS, WIDTH),
    )
    start_pert = to_bulk(perturbation)
    field = start_pert + to_bulk(base_state)
    target = to_bulk(target_state)
    target_surface = to_surface(sz, target_state[0])

    def all_channels(array):
        return to_surface(sz, jnp.broadcast_to(array[:, None, :], (rows, CHANNELS, sz.cells)))

    weight_surface = all_channels(cost_weight)
    diffusivity_surface = all_channels(diffusivity)
    diffusivity = diffusivity.reshape(rows, 1, sz.cells)
    weight = cost_weight.reshape(rows, 1, sz.cells)

    wider = (rows + 2, CHANNELS, LEVELS, sz.cells)
    row_surface = (sz.row_width, WIDTH)
    row_sems = pltpu.SemaphoreType.DMA((rows,))
    two_row_sems = pltpu.SemaphoreType.DMA((2, rows))
    edge_sems = pltpu.SemaphoreType.DMA((2,))

    saved = []
    surface = None
    told = None
    for hour in range(hours):
        first, last = hour == 0, hour == hours - 1
        inputs = anywhere(field, *edges) + near_by(diffusivity, mix) + scalars(table, facts)
        if first:
            inputs += near_by(facts)
        else:
            inputs += near_by(surface, *surface_edges)
        if last:
            inputs += near_by(target, weight)
        field, drive, surface, packed, *sends = call(
            functools.partial(forward_kernel, sz, first, last),
            "step",
            inputs,
            shipped=[
                sz.whole, sz.whole, sz.surface, sz.narrow, sz.told, sz.told, sz.edge, sz.edge
            ],
            scratch=[wider, row_sems, edge_sems],
        )
        arrived = exchange(packed, devices)
        got = swap(*sends[:2])
        arrived, *got = lax.optimization_barrier((arrived, *got))
        if first:
            told = got
        flux, mixed_slope, flux_slope = call(
            functools.partial(owner_kernel, sz),
            "owners",
            near_by(arrived, mixing, air_temp[hour, 0], wind_speed[hour, 0])
            + scalars(coupler_mix),
            shipped=[sz.wide, sz.by_slot, sz.by_slot],
            scratch=[sz.narrow, (sz.slots, WIDTH)],
        )
        flux, *sends = lax.optimization_barrier((flux, *sends[2:]))
        flux = exchange(flux, devices)
        edges = swap(*sends)
        inputs = near_by(flux, surface, *got) + scalars(table, facts, *told)
        near = [sz.near, sz.near]
        if last:
            surface, slope, packed, *sends = call(
                functools.partial(surface_kernel, sz, True),
                "surface",
                inputs + near_by(target_surface, weight_surface),
                shipped=[sz.surface, sz.slope, sz.wide, sz.lats, sz.lats],
                scratch=near,
            )
        else:
            surface, *sends, slope = call(
                functools.partial(surface_kernel, sz, False),
                "surface",
                inputs,
                kept=[sz.surface, row_surface, row_surface],
                shipped=[sz.slope],
                scratch=near,
            )
            surface_edges = swap(*sends)
        saved.append((drive, slope, mixed_slope, flux_slope))

    edge_sends = None
    for hour in reversed(range(hours)):
        drive, slope, mixed_slope, flux_slope = saved[hour]
        arrived = exchange(packed, devices)
        got = swap(*sends)
        arrived, *got = lax.optimization_barrier((arrived, *got))
        back = call(
            functools.partial(owner_back_kernel, sz),
            "owners_back",
            near_by(arrived, mixing, mixed_slope, flux_slope) + scalars(coupler_mix),
            shipped=[sz.narrow],
            scratch=[sz.narrow, (sz.slots, WIDTH)],
        )[0]
        if edge_sends is not None:
            back, *edge_sends = lax.optimization_barrier((back, *edge_sends))
            edges = swap(*edge_sends)
        back = exchange(back, devices)
        surface, *row_sends = call(
            functools.partial(merge_kernel, sz),
            "merge",
            near_by(back, surface, slope, *got)
            + scalars(table, facts)
            + near_by(diffusivity_surface),
            kept=[sz.surface, row_surface, row_surface],
        )
        surface_edges = swap(*row_sends)
        inputs = (
            anywhere(field)
            + near_by(surface)
            + anywhere(*edges)
            + near_by(*surface_edges)
            + anywhere(drive)
            + near_by(diffusivity, mix)
        )
        if hour > 0:
            field, surface, packed, *sends = call(
                functools.partial(backward_kernel, sz, False),
                "step_back",
                inputs + scalars(table, facts, *told) + near_by(saved[hour - 1][1]),
                shipped=[sz.whole, sz.surface, sz.wide, sz.lats, sz.lats, sz.edge, sz.edge],
                scratch=[sz.whole, sz.whole, wider, sz.near, sz.near, two_row_sems, edge_sems],
            )
            sends, edge_sends = sends[:2], sends[2:]
        else:
            gradient, sums = call(
                functools.partial(backward_kernel, sz, True),
                "step_back_sums",
                inputs + near_by(start_pert),
                shipped=[sz.whole, (devices, WIDTH)],
                scratch=[sz.whole, sz.whole, wider, two_row_sems, edge_sems],
            )

    everyones = lax.all_to_all(sums, "horiz", split_axis=0, concat_axis=0, tiled=True)
    block = perturbation.shape
    return call(
        functools.partial(final_kernel, perturbation.size * devices),
        "finish",
        near_by(everyones) + anywhere(perturbation, gradient.transpose(2, 0, 1, 3)),
        shipped=[block],
        scratch=[block, block, pltpu.SemaphoreType.DMA((2, block[0]))],
    )[0]


def solution(mesh):
    placed = (
        P("member", "horiz", None, None),
        P(None, "horiz", None, None),
        P(None, "horiz", None, None),
        P("horiz", None),
        P("horiz", None),
        P(),
        P(),
        P("horiz", None, None),
        P(None, "horiz", None, None),
        P(None, "horiz", None, None),
        P("horiz", None),
        P("horiz", None),
        P("horiz"),
        P("horiz"),
        P("horiz"),
    )
    return jax.shard_map(
        body,
        mesh=mesh,
        in_specs=placed,
        out_specs=P("member", "horiz", None, None),
        check_vma=False,
    )
```

```python
import functools

import jax
import jax.numpy as jnp
from jax import lax
from jax.experimental import pallas as pl
from jax.experimental.pallas import tpu as pltpu
from jax.sharding import PartitionSpec as P

LAT_DEV = 2
NEAR_LAT = LAT_DEV + 2
CHANNELS = 4
LEVELS = 8
WIDTH = 128
SUBLANES = 8

KAPPA_V = 0.1
TIME_STEP = 0.3
FLUX_RATE = 0.05
FEEDBACK = 0.5
ASCENT = 0.5
EPSILON = 1e-06
HIGHEST = lax.Precision.HIGHEST
VMEM_BYTES = 32 * 1024 * 1024


class Sizes:
    def __init__(self, devices, capacity, rows, cells):
        self.devices = devices
        self.capacity = capacity
        self.slots = devices * capacity
        self.rows = rows
        self.cells = cells
        self.row_tiles = cells // WIDTH
        self.tiles = rows * self.row_tiles
        self.row_width = CHANNELS * self.row_tiles
        self.pitch = -(-self.row_tiles // SUBLANES) * SUBLANES
        self.own_rows = CHANNELS * capacity
        self.chunk = -(-(self.own_rows + 2 * capacity) // SUBLANES) * SUBLANES
        self.slot_lines = -(-self.slots // WIDTH)
        self.facts = -(-(self.slot_lines + 1) // SUBLANES) * SUBLANES
        self.lat_lines = LAT_DEV * self.pitch
        self.whole = (rows, CHANNELS, LEVELS, cells)
        self.edge = (CHANNELS, LEVELS, cells)
        self.surface = (CHANNELS * (self.tiles + 1), WIDTH)
        self.narrow = (CHANNELS * self.slots, WIDTH)
        self.wide = (devices * self.chunk, WIDTH)
        self.slope = (NEAR_LAT * self.pitch, WIDTH)
        self.lats = (self.lat_lines, WIDTH)
        self.told = (self.lat_lines + self.facts, WIDTH)
        self.near = (-(-(self.tiles + 1) // SUBLANES) * SUBLANES, WIDTH)
        self.by_slot = (CHANNELS, self.slots, WIDTH)


class Shipped:
    def __init__(self, block, home, sems):
        self.block, self.home, self.sems = block, home, sems
        self.by_row = False
        self.started = False

    def __getitem__(self, at):
        return self.block[at]

    def __setitem__(self, at, value):
        self.block[at] = value

    def row(self, index):
        self.by_row = True
        self.started = True
        return pltpu.make_async_copy(
            self.block.at[index], self.home.at[index], self.sems.at[index]
        )

    def all(self):
        return pltpu.make_async_copy(self.block, self.home, self.sems.at[0])

    def start(self):
        self.started = True
        self.all().start()

    def finish(self, rows):
        if self.by_row:
            for index in range(rows):
                self.row(index).wait()
        else:
            self.all().wait()


def cols(tile):
    return slice(tile * WIDTH, (tile + 1) * WIDTH)


def lanes_sum(left_here, left_before, right_here, right_after, lane):
    return jnp.where(lane == 0, left_before, left_here) + jnp.where(
        lane == WIDTH - 1, right_after, right_here
    )


def levels_sum(field, sub):
    return jnp.where(sub == 0, 0.0, pltpu.roll(field, 1, 0)) + jnp.where(
        sub == LEVELS - 1, 0.0, pltpu.roll(field, LEVELS - 1, 0)
    )


def row_tiles_of(sz, ref, row):
    return ref[pl.ds(row * sz.row_width, sz.row_tiles, stride=CHANNELS), :]


def put_row_tiles(sz, ref, row, value):
    ref[pl.ds(row * sz.row_width, sz.row_tiles, stride=CHANNELS), :] = value


def near_row(sz, ref, row):
    return ref[row * sz.row_tiles : (row + 1) * sz.row_tiles, :]


def load_surface_row(sz, target, row, source, base):
    for tile in range(sz.row_tiles):
        for channel in range(CHANNELS):
            at = base + tile * CHANNELS + channel
            target[row, channel, 0:1, cols(tile)] = source[pl.ds(at, 1), :]


def as_column(row, size):
    shape = (size, row.shape[1])
    diagonal = lax.broadcasted_iota(jnp.int32, shape, 0) == lax.broadcasted_iota(jnp.int32, shape, 1)
    return jnp.sum(jnp.where(diagonal, row, 0.0), axis=1, keepdims=True)


def tables_kernel(sz, entries, remap_entries, wet, remap, table, facts):
    tiles, owners = wet[0:1, :], wet[1:2, :]
    size = -(-entries // SUBLANES) * SUBLANES
    shape = (size, wet.shape[1])
    tile_here, owner_here = as_column(tiles, size), as_column(owners, size)
    earlier = lax.broadcasted_iota(jnp.int32, shape, 1) < lax.broadcasted_iota(jnp.int32, shape, 0)
    same = (owner_here == owners) & earlier
    rank = jnp.sum(jnp.where(same, 1.0, 0.0), axis=1, keepdims=True)
    slot = jnp.where(owner_here >= 0.0, owner_here * sz.capacity + rank, -1.0)
    facts[...] = jnp.zeros(facts.shape, jnp.float32)
    for line in range(sz.slot_lines):
        place = lax.broadcasted_iota(jnp.int32, (size, WIDTH), 1) + line * WIDTH
        match = slot.astype(jnp.int32) == place
        told = jnp.sum(jnp.where(match, sz.tiles - tile_here, 0.0), axis=0, keepdims=True)
        facts[line : line + 1, :] = told
        table[line : line + 1, :] = sz.tiles - told.astype(jnp.int32)
    size = -(-remap_entries // SUBLANES) * SUBLANES
    at, weight = as_column(remap[0:1, :], size), as_column(remap[1:2, :], size)
    place = lax.broadcasted_iota(jnp.int32, (size, WIDTH), 1)
    facts[sz.slot_lines : sz.slot_lines + 1, :] = jnp.sum(
        jnp.where(at.astype(jnp.int32) == place, weight, 0.0), axis=0, keepdims=True
    )


class Remap:
    def __init__(self, sz, facts, low, high):
        self.sz, self.facts, self.low, self.high = sz, facts, low, high

    def own(self, lat, row):
        return self.facts[self.sz.slot_lines, lat * self.sz.rows + row]

    def beside(self, told, lat, row):
        return told[self.sz.lat_lines + self.sz.slot_lines, lat * self.sz.rows + row]

    def of_low(self, lat, row):
        return self.beside(self.low, lat + LAT_DEV, row)

    def of_high(self, lat, row):
        return self.beside(self.high, lat - LAT_DEV, row)


def tile_at(table, slot):
    return table[slot // WIDTH, slot % WIDTH]


def sum_of(weights, values):
    total = weights[0] * values[0]
    for weight, value in zip(weights[1:], values[1:]):
        total = total + weight * value
    return total


def own_sums(sz, remap, own, factor):
    return [
        factor * sum_of([remap.own(lat, row) for row in range(sz.rows)], own)
        for lat in range(NEAR_LAT)
    ]


def send_sums(sz, sums, send_low, send_high):
    for lat in range(NEAR_LAT):
        send = send_low if lat < LAT_DEV else send_high
        at = (lat % LAT_DEV) * sz.pitch
        send[at : at + sz.row_tiles, :] = sums[lat]


def lat_rows(sz, ref, lat):
    return ref[lat * sz.pitch : lat * sz.pitch + sz.row_tiles, :]


def told_sums(sz, from_low, from_high):
    return [
        lat_rows(sz, from_low if lat < LAT_DEV else from_high, lat % LAT_DEV)
        for lat in range(NEAR_LAT)
    ]


def forward_kernel(sz, first, last, *refs):
    refs = list(refs)
    field, low, high, diffusivity, mix, table, own_facts = refs[:7]
    refs = refs[7:]
    if first:
        facts = refs[0]
        refs = refs[1:]
    else:
        surface, low_surface, high_surface = refs[:3]
        refs = refs[3:]
    if last:
        target, weight = refs[:2]
        refs = refs[2:]
    if last:
        refs = refs[1:3] + refs[0:1] + refs[3:]
    out, drive, new_surface, packed, tell_low, tell_high, edge_low, edge_high, padded = refs
    remap = Remap(sz, own_facts, None, None)

    padded[0] = low[...]
    padded[sz.rows + 1] = high[...]
    if not first:
        load_surface_row(sz, padded, 0, low_surface, 0)
        load_surface_row(sz, padded, sz.rows + 1, high_surface, 0)

    def fill(row, carry):
        padded[row + 1] = field[row]
        if not first:
            load_surface_row(sz, padded, row + 1, surface, row * sz.row_width)
        return carry

    lax.fori_loop(0, sz.rows, fill, 0)
    lane = lax.broadcasted_iota(jnp.int32, (LEVELS, WIDTH), 1)
    sub = lax.broadcasted_iota(jnp.int32, (LEVELS, WIDTH), 0)
    count = sz.row_tiles

    def one_row(row, carry):
        here = [[padded[row + 1, c, :, cols(t)] for t in range(count)] for c in range(CHANNELS)]
        for t in range(count):
            coeff = jnp.broadcast_to(diffusivity[row, 0:1, cols(t)], (LEVELS, WIDTH))
            if last:
                scale = weight[row, 0:1, cols(t)]
                scale = jnp.broadcast_to(scale * scale, (LEVELS, WIDTH))
            for c in range(CHANNELS):
                mixed = mix[c * CHANNELS] * here[0][t]
                for k in range(1, CHANNELS):
                    mixed = mixed + mix[c * CHANNELS + k] * here[k][t]
                bent = jnp.tanh(mixed)
                drive[row, c, :, cols(t)] = bent
                field_here = here[c][t]
                around = lanes_sum(
                    pltpu.roll(field_here, 1, 1),
                    pltpu.roll(here[c][(t - 1) % count], 1, 1),
                    pltpu.roll(field_here, WIDTH - 1, 1),
                    pltpu.roll(here[c][(t + 1) % count], WIDTH - 1, 1),
                    lane,
                )
                around = around + (padded[row, c, :, cols(t)] + padded[row + 2, c, :, cols(t)])
                stepped = (
                    field_here
                    + coeff * (around - 4.0 * field_here)
                    + KAPPA_V * (levels_sum(field_here, sub) - 2.0 * field_here)
                    + TIME_STEP * bent
                )
                new_surface[pl.ds((row * count + t) * CHANNELS + c, 1), :] = stepped[0:1, :]
                if last:
                    stepped = scale * (stepped - target[row, c, :, cols(t)])
                out[row, c, :, cols(t)] = stepped
        if last:
            drive.row(row).start()
            out.row(row).start()
        return carry

    lax.fori_loop(0, sz.rows, one_row, 0)
    new_surface[CHANNELS * sz.tiles :, :] = jnp.zeros((CHANNELS, WIDTH), jnp.float32)
    pack_slots(sz, table, new_surface, packed)
    packed.start()
    own = [row_tiles_of(sz, new_surface, row) for row in range(sz.rows)]
    send_sums(sz, own_sums(sz, remap, own, 1.0), tell_low, tell_high)
    blank = facts[...] if first else jnp.zeros((sz.facts, WIDTH), jnp.float32)
    for tell in (tell_low, tell_high):
        tell[sz.lat_lines :, :] = blank
        tell.start()
    store_edges(sz, out, diffusivity if last else None, edge_low, edge_high)


def pack_slots(sz, table, surface, packed):
    for slot in range(sz.slots):
        at = pl.multiple_of(tile_at(table, slot) * CHANNELS, CHANNELS)
        packed[slot * CHANNELS : (slot + 1) * CHANNELS, :] = surface[pl.ds(at, CHANNELS), :]


def store_edges(sz, field, diffusivity, send_low, send_high):
    for row, send in ((0, send_low), (sz.rows - 1, send_high)):
        for channel in range(CHANNELS):
            for tile in range(sz.row_tiles):
                value = field[row, channel, :, cols(tile)]
                if diffusivity is not None:
                    value = value * jnp.broadcast_to(
                        diffusivity[row, 0:1, cols(tile)], (LEVELS, WIDTH)
                    )
                send[channel, :, cols(tile)] = value
        send.start()


def owner_kernel(sz, arrived, mixing, air, wind, bulk, *refs):
    refs = list(refs)
    slots = sz.slots
    if len(refs) > 5:
        for told, table in zip(refs[:2], refs[2:4]):
            lines = told[sz.lat_lines : sz.lat_lines + sz.slot_lines, :]
            table[...] = sz.tiles - lines.astype(jnp.int32)
        refs = refs[4:]
    flux, mixed_slope, flux_slope, flat, first = refs
    values = [arrived[pl.ds(c, slots, stride=CHANNELS), :] for c in range(CHANNELS)]
    mixed = jnp.tanh(
        jnp.dot(
            mixing[...],
            jnp.concatenate(values, axis=1),
            precision=HIGHEST,
            preferred_element_type=jnp.float32,
        )
    )
    contrast = []
    for c in range(CHANNELS):
        mixed_here = mixed[:, cols(c)]
        mixed_slope[c] = 1.0 - mixed_here * mixed_here
        contrast.append((air[...] - values[0] if c == 0 else values[c]) + mixed_here)
    mixed_slope.start()
    rate = FLUX_RATE * wind[...]
    for c in range(CHANNELS):
        forcing = bulk[c, 0] * contrast[0]
        for k in range(1, CHANNELS):
            forcing = forcing + bulk[c, k] * contrast[k]
        bent = jnp.tanh(forcing)
        flux_slope[c] = rate * (1.0 - bent * bent)
        one = rate * bent
        flat[pl.ds(c, slots, stride=CHANNELS), :] = one
        if c == 0:
            first[...] = one
    flux_slope.start()
    cap = sz.capacity
    gap = jnp.zeros((sz.chunk - sz.own_rows, WIDTH), jnp.float32)
    for d in range(sz.devices):
        at = d * sz.chunk
        flux[at : at + sz.own_rows, :] = flat[d * sz.own_rows : (d + 1) * sz.own_rows, :]
        at = at + sz.own_rows
        flux[at : (d + 1) * sz.chunk, :] = gap
        if d > 0:
            flux[at : at + cap, :] = first[(d - 1) * cap : d * cap, :]
        if d < sz.devices - 1:
            flux[at + cap : at + 2 * cap, :] = first[(d + 1) * cap : (d + 2) * cap, :]


def owner_back_kernel(sz, arrived, mixing, mixed_slope, flux_slope, bulk, back, flat, extra):
    slots, cap = sz.slots, sz.capacity
    for d in range(sz.devices):
        at = d * sz.chunk
        flat[d * sz.own_rows : (d + 1) * sz.own_rows, :] = arrived[at : at + sz.own_rows, :]
        more = jnp.zeros((cap, WIDTH), jnp.float32)
        if d < sz.devices - 1:
            at = (d + 1) * sz.chunk + sz.own_rows
            more = more + arrived[at : at + cap, :]
        if d > 0:
            at = (d - 1) * sz.chunk + sz.own_rows + cap
            more = more + arrived[at : at + cap, :]
        extra[d * cap : (d + 1) * cap, :] = more
    forced = []
    for c in range(CHANNELS):
        got = flat[pl.ds(c, slots, stride=CHANNELS), :]
        if c == 0:
            got = got + extra[...]
        forced.append(flux_slope[c] * got)
    direct = []
    for k in range(CHANNELS):
        total = bulk[0, k] * forced[0]
        for c in range(1, CHANNELS):
            total = total + bulk[c, k] * forced[c]
        direct.append(total)
    through = lax.dot_general(
        mixing[...],
        jnp.concatenate([direct[k] * mixed_slope[k] for k in range(CHANNELS)], axis=1),
        (((0,), (0,)), ((), ())),
        precision=HIGHEST,
        preferred_element_type=jnp.float32,
    )
    for k in range(CHANNELS):
        sign = -1.0 if k == 0 else 1.0
        back.block[pl.ds(k, slots, stride=CHANNELS), :] = through[:, cols(k)] + sign * direct[k]


def spread_back(sz, surface, slope, remap, tables, packed, near_low, near_high, tell_low, tell_high):
    rows, count, cap = sz.rows, sz.row_tiles, sz.capacity
    block = surface.block
    own = [row_tiles_of(sz, block, row) for row in range(rows)]
    sums = own_sums(sz, remap, own, FEEDBACK)
    send_sums(sz, sums, tell_low, tell_high)
    tell_low.start()
    tell_high.start()
    lats = [lat_rows(sz, slope, lat) * sums[lat] for lat in range(NEAR_LAT)]
    every = range(NEAR_LAT)
    for row in range(rows):
        added = sum_of([remap.own(lat, row) for lat in every], lats)
        put_row_tiles(sz, block, row, own[row] + added)
        at = row * count
        near_low[at : at + count, :] = sum_of(
            [remap.of_low(lat, row) for lat in range(LAT_DEV)], lats[:LAT_DEV]
        )
        near_high[at : at + count, :] = sum_of(
            [remap.of_high(lat, row) for lat in range(LAT_DEV, NEAR_LAT)], lats[LAT_DEV:]
        )
    rest = sz.near[0] - sz.tiles
    near_low[sz.tiles :, :] = jnp.zeros((rest, WIDTH), jnp.float32)
    near_high[sz.tiles :, :] = jnp.zeros((rest, WIDTH), jnp.float32)
    surface.start()
    gap = jnp.zeros((sz.chunk - sz.own_rows, WIDTH), jnp.float32)
    for owner in range(sz.devices):
        packed[owner * sz.chunk + sz.own_rows : (owner + 1) * sz.chunk, :] = gap
    for slot in range(sz.slots):
        owner, rank = slot // cap, slot % cap
        at = owner * sz.chunk + rank * CHANNELS
        tile = pl.multiple_of(tile_at(tables[0], slot) * CHANNELS, CHANNELS)
        packed[at : at + CHANNELS, :] = surface[pl.ds(tile, CHANNELS), :]
        at = owner * sz.chunk + sz.own_rows + rank
        packed[at : at + 1, :] = near_low[pl.ds(tile_at(tables[1], slot), 1), :]
        at = at + cap
        packed[at : at + 1, :] = near_high[pl.ds(tile_at(tables[2], slot), 1), :]


def surface_kernel(sz, last, *refs):
    refs = list(refs)
    flux, before, from_low, from_high, table, low_table, high_table = refs[:7]
    facts, told_low, told_high = refs[7:10]
    refs = refs[10:]
    tables = (table, low_table, high_table)
    if last:
        target, weight = refs[:2]
        surface, slope, packed, tell_low, tell_high, near_low, near_high = refs[2:]
        block = surface.block
    else:
        surface, send_low, send_high, slope, near_low, near_high = refs
        block = surface
    remap = Remap(sz, facts, told_low, told_high)
    rows, cap = sz.rows, sz.capacity
    block[...] = before[...]
    near_low[...] = jnp.zeros(sz.near, jnp.float32)
    near_high[...] = jnp.zeros(sz.near, jnp.float32)
    for slot in range(sz.slots):
        owner, rank = slot // cap, slot % cap
        at = owner * sz.chunk + rank * CHANNELS
        tile = pl.multiple_of(tile_at(table, slot) * CHANNELS, CHANNELS)
        block[pl.ds(tile, CHANNELS), :] = (
            before[pl.ds(tile, CHANNELS), :] + flux[at : at + CHANNELS, :]
        )
        at = owner * sz.chunk + sz.own_rows + rank
        near_low[pl.ds(tile_at(low_table, slot), 1), :] = flux[at : at + 1, :]
        at = at + cap
        near_high[pl.ds(tile_at(high_table, slot), 1), :] = flux[at : at + 1, :]
    block[CHANNELS * sz.tiles :, :] = jnp.zeros((CHANNELS, WIDTH), jnp.float32)
    own = [row_tiles_of(sz, block, row) for row in range(rows)]
    sums = own_sums(sz, remap, own, 1.0)
    told = told_sums(sz, from_low, from_high)
    air = []
    for lat in range(NEAR_LAT):
        if lat < LAT_DEV:
            near, weights = near_low, [remap.of_low(lat, row) for row in range(rows)]
        else:
            near, weights = near_high, [remap.of_high(lat, row) for row in range(rows)]
        more = sum_of(weights, [near_row(sz, near, row) for row in range(rows)])
        one = jnp.tanh(sums[lat] + told[lat] + more)
        slope[lat * sz.pitch : lat * sz.pitch + sz.row_tiles, :] = 1.0 - one * one
        air.append(one)
    slope.start()
    for row in range(rows):
        weights = [remap.own(lat, row) for lat in range(NEAR_LAT)]
        put_row_tiles(sz, block, row, own[row] + FEEDBACK * sum_of(weights, air))
    if last:
        end = CHANNELS * sz.tiles
        scale = weight[...]
        block[0:end, :] = scale * scale * (block[0:end, :] - target[...])
        spread_back(
            sz, surface, slope, remap, tables, packed, near_low, near_high, tell_low, tell_high
        )
    else:
        send_low[...] = surface[0 : sz.row_width, :]
        send_high[...] = surface[(rows - 1) * sz.row_width : rows * sz.row_width, :]


def merge_kernel(
    sz, back, before, slope, from_low, from_high, table, facts, diffusivity, surface, send_low, send_high
):
    rows, width = sz.rows, sz.row_width
    remap = Remap(sz, facts, None, None)
    surface[...] = before[...]
    for slot in range(sz.slots):
        tile = pl.multiple_of(tile_at(table, slot) * CHANNELS, CHANNELS)
        surface[pl.ds(tile, CHANNELS), :] = (
            before[pl.ds(tile, CHANNELS), :] + back[slot * CHANNELS : (slot + 1) * CHANNELS, :]
        )
    surface[CHANNELS * sz.tiles :, :] = jnp.zeros((CHANNELS, WIDTH), jnp.float32)
    told = told_sums(sz, from_low, from_high)
    lats = [lat_rows(sz, slope, lat) * told[lat] for lat in range(NEAR_LAT)]
    for row in range(rows):
        own = row_tiles_of(sz, surface, row)
        weights = [remap.own(lat, row) for lat in range(NEAR_LAT)]
        put_row_tiles(sz, surface, row, own + sum_of(weights, lats))
    send_low[...] = diffusivity[0:width, :] * surface[0:width, :]
    end = rows * width
    send_high[...] = diffusivity[end - width : end, :] * surface[end - width : end, :]


def backward_kernel(sz, last, *refs):
    refs = list(refs)
    field, surface, low, high, low_surface, high_surface, drive, diffusivity, mix = refs[:9]
    refs = refs[9:]
    if last:
        perturbation, out, sums = refs[:3]
        local, padded, in_sems = refs[3:]
        bent_all = drive
    else:
        tables, facts, told_low, told_high, slope = refs[:3], *refs[3:7]
        out, new_surface, packed, tell_low, tell_high, edge_low, edge_high = refs[7:14]
        local, bent_all, padded, near_low, near_high, in_sems = refs[14:]
        remap = Remap(sz, facts, told_low, told_high)
    count = sz.row_tiles

    def arrivals(row):
        copies = [pltpu.make_async_copy(field.at[row], local.at[row], in_sems.at[0, row])]
        if not last:
            copies.append(
                pltpu.make_async_copy(drive.at[row], bent_all.at[row], in_sems.at[1, row])
            )
        return copies

    for row in range(sz.rows):
        for arrival in arrivals(row):
            arrival.start()

    def ready(row):
        for arrival in arrivals(row):
            arrival.wait()
        load_surface_row(sz, local, row, surface, row * sz.row_width)
        for t in range(count):
            coeff = jnp.broadcast_to(diffusivity[row, 0:1, cols(t)], (LEVELS, WIDTH))
            for c in range(CHANNELS):
                padded[row + 1, c, :, cols(t)] = coeff * local[row, c, :, cols(t)]

    padded[0] = low[...]
    padded[sz.rows + 1] = high[...]
    load_surface_row(sz, padded, 0, low_surface, 0)
    load_surface_row(sz, padded, sz.rows + 1, high_surface, 0)
    ready(0)
    lane = lax.broadcasted_iota(jnp.int32, (LEVELS, WIDTH), 1)
    sub = lax.broadcasted_iota(jnp.int32, (LEVELS, WIDTH), 0)

    def one_row(row, carry):
        @pl.when(row < sz.rows - 1)
        def _():
            ready(row + 1)

        scaled = [[padded[row + 1, c, :, cols(t)] for t in range(count)] for c in range(CHANNELS)]
        for t in range(count):
            here, bent = [], []
            for c in range(CHANNELS):
                value = local[row, c, :, cols(t)]
                one = bent_all[row, c, :, cols(t)]
                here.append(value)
                bent.append((1.0 - one * one) * value)
            for c in range(CHANNELS):
                mixed = mix[c] * bent[0]
                for k in range(1, CHANNELS):
                    mixed = mixed + mix[k * CHANNELS + c] * bent[k]
                around = lanes_sum(
                    pltpu.roll(scaled[c][t], 1, 1),
                    pltpu.roll(scaled[c][(t - 1) % count], 1, 1),
                    pltpu.roll(scaled[c][t], WIDTH - 1, 1),
                    pltpu.roll(scaled[c][(t + 1) % count], WIDTH - 1, 1),
                    lane,
                )
                around = around + (padded[row, c, :, cols(t)] + padded[row + 2, c, :, cols(t)])
                stepped = (
                    here[c]
                    + (around - 4.0 * scaled[c][t])
                    + KAPPA_V * (levels_sum(here[c], sub) - 2.0 * here[c])
                    + TIME_STEP * mixed
                )
                out[row, c, :, cols(t)] = stepped
                if last:
                    start = perturbation[row, c, :, cols(t)]
                    carry = (
                        carry[0] + start * start,
                        carry[1] + start * stepped,
                        carry[2] + stepped * stepped,
                    )
                else:
                    new_surface[pl.ds((row * count + t) * CHANNELS + c, 1), :] = stepped[0:1, :]
        out.row(row).start()
        return carry

    blank = jnp.zeros((LEVELS, WIDTH), jnp.float32)
    totals = lax.fori_loop(0, sz.rows, one_row, (blank, blank, blank) if last else 0)
    if last:
        place = lax.broadcasted_iota(jnp.int32, sums.block.shape, 1)
        held = jnp.zeros(sums.block.shape, jnp.float32)
        for index in range(3):
            total = jnp.sum(jnp.sum(totals[index], axis=0, keepdims=True), axis=1, keepdims=True)
            held = jnp.where(place == index, total, held)
        sums[...] = held
    else:
        new_surface[CHANNELS * sz.tiles :, :] = jnp.zeros((CHANNELS, WIDTH), jnp.float32)
        spread_back(
            sz, new_surface, slope, remap, tables, packed, near_low, near_high, tell_low, tell_high
        )
        packed.start()
        store_edges(sz, out, diffusivity, edge_low, edge_high)


def final_kernel(cell_total, everyones, perturbation, gradient, out):
    sums = jnp.sum(everyones[...], axis=0, keepdims=True) / cell_total
    place = lax.broadcasted_iota(jnp.int32, sums.shape, 1)
    means = [
        jnp.broadcast_to(
            jnp.sum(jnp.where(place == index, sums, 0.0), axis=1, keepdims=True), (1, WIDTH)
        )
        for index in range(3)
    ]
    scale = lax.rsqrt(means[2] + EPSILON)
    mean_sq = means[0] + 2.0 * ASCENT * scale * means[1] + ASCENT * ASCENT * scale * scale * means[2]
    shrink = lax.rsqrt(mean_sq + EPSILON)
    step = jnp.broadcast_to(ASCENT * scale * shrink, (CHANNELS, WIDTH))
    shrink = jnp.broadcast_to(shrink, (CHANNELS, WIDTH))
    levels, rows, _, cells = perturbation.shape

    def one_level(level, carry):
        for row in range(rows):
            for tile in range(cells // WIDTH):
                start = perturbation[level, row, :, cols(tile)]
                slope = gradient[level, row, :, cols(tile)]
                out[level, row, :, cols(tile)] = shrink * start + step * slope
        out.row(level).start()
        return carry

    lax.fori_loop(0, levels, one_level, 0)


def near_by(*arrays):
    return [(array, pltpu.VMEM) for array in arrays]


def scalars(*arrays):
    return [(array, pltpu.SMEM) for array in arrays]


def far_off(*arrays):
    return [
        (pltpu.with_memory_space_constraint(array, pltpu.HBM), pltpu.HBM) for array in arrays
    ]


def call(kernel, name, inputs, kept=(), shipped=(), scratch=()):
    n_in, n_kept, n_out = len(inputs), len(kept), len(shipped)

    def run(*refs):
        ins = refs[: n_in + n_kept]
        homes = refs[n_in + n_kept : n_in + n_kept + n_out]
        rest = refs[n_in + n_kept + n_out :]
        outs = [
            Shipped(block, home, sems)
            for block, home, sems in zip(rest[:n_out], homes, rest[n_out : 2 * n_out])
        ]
        kernel(*ins, *outs, *rest[2 * n_out :])
        for out in outs:
            if not out.started:
                out.start()
        for out in outs:
            out.finish(out.block.shape[0])

    kept_shapes = [
        item if isinstance(item, jax.ShapeDtypeStruct) else jax.ShapeDtypeStruct(item, jnp.float32)
        for item in kept
    ]
    spaces = [pltpu.VMEM] * n_kept + [pltpu.HBM] * n_out
    blocks = [pltpu.VMEM(shape, jnp.float32) for shape in shipped]
    sems = [
        pltpu.SemaphoreType.DMA((shape[0] if len(shape) > 3 else 1,)) for shape in shipped
    ]
    more = [
        item if not isinstance(item, tuple) else pltpu.VMEM(item, jnp.float32) for item in scratch
    ]
    return pl.pallas_call(
        run,
        name=name,
        in_specs=[pl.BlockSpec(memory_space=space) for _, space in inputs],
        out_specs=[pl.BlockSpec(memory_space=space) for space in spaces],
        out_shape=kept_shapes + [pltpu.HBM(shape, jnp.float32) for shape in shipped],
        scratch_shapes=blocks + sems + more,
        compiler_params=pltpu.CompilerParams(vmem_limit_bytes=VMEM_BYTES),
    )(*[array for array, _ in inputs])


def to_bulk(field):
    return field.transpose(1, 2, 0, 3)


def to_surface(sz, rows):
    split = rows.reshape(sz.rows, CHANNELS, sz.row_tiles, WIDTH).transpose(0, 2, 1, 3)
    return split.reshape(CHANNELS * sz.tiles, WIDTH)


def swap(low, high):
    count = lax.axis_size("horiz")
    upward = [(i, i + 1) for i in range(count - 1)]
    downward = [(target, source) for source, target in upward]
    return lax.ppermute(high, "horiz", upward), lax.ppermute(low, "horiz", downward)


def exchange(array, devices):
    rows = array.shape[0] // devices
    split = array.reshape(devices, rows // CHANNELS, CHANNELS, WIDTH)
    moved = lax.all_to_all(split, "horiz", split_axis=0, concat_axis=0, tiled=True)
    return moved.reshape(array.shape)


def body(
    perturbation,
    base_state,
    target_state,
    cost_weight,
    diffusivity,
    chan_mix,
    coupler_mix,
    owner_mix,
    air_temp,
    wind_speed,
    wet_list,
    wet_owner,
    remap_src,
    remap_tgt,
    remap_weight,
):
    devices = lax.axis_size("horiz")
    hours = air_temp.shape[0]
    sz = Sizes(devices, air_temp.shape[2] // devices, base_state.shape[1], base_state.shape[3])
    mixing = owner_mix[0]
    rows = sz.rows

    start = [
        (perturbation[:, row] + base_state[:, row]).transpose(1, 0, 2) for row in (0, rows - 1)
    ]
    edges = swap(*start)
    me = lax.axis_index("horiz").astype(jnp.int32)

    def lined(first_row, second_row):
        size = -(-first_row.shape[0] // WIDTH) * WIDTH
        pair = jnp.stack([first_row.astype(jnp.float32), second_row.astype(jnp.float32)])
        return jnp.pad(pair, ((0, 0), (0, size - pair.shape[1])), constant_values=-1.0)

    remap_at = (remap_tgt - (me * LAT_DEV - 1)) * rows + remap_src - me * rows
    table, facts = pl.pallas_call(
        functools.partial(tables_kernel, sz, wet_list.shape[1], remap_src.shape[0]),
        name="tables",
        out_shape=[
            jax.ShapeDtypeStruct((sz.slot_lines, WIDTH), jnp.int32),
            jax.ShapeDtypeStruct((sz.facts, WIDTH), jnp.float32),
        ],
    )(lined(wet_list[0], wet_owner[0]), lined(remap_at, remap_weight))

    mix = jnp.broadcast_to(
        chan_mix.transpose(1, 2, 0).reshape(CHANNELS * CHANNELS, LEVELS, 1),
        (CHANNELS * CHANNELS, LEVELS, WIDTH),
    )
    start_pert = to_bulk(perturbation)
    field = start_pert + to_bulk(base_state)
    target = to_bulk(target_state)
    target_surface = to_surface(sz, target_state[0])

    def all_channels(array):
        return to_surface(sz, jnp.broadcast_to(array[:, None, :], (rows, CHANNELS, sz.cells)))

    weight_surface = all_channels(cost_weight)
    diffusivity_surface = all_channels(diffusivity)
    diffusivity = diffusivity.reshape(rows, 1, sz.cells)
    weight = cost_weight.reshape(rows, 1, sz.cells)

    wider = (rows + 2, CHANNELS, LEVELS, sz.cells)
    row_surface = (sz.row_width, WIDTH)
    two_row_sems = pltpu.SemaphoreType.DMA((2, rows))

    saved = []
    surface = None
    told = None
    for hour in range(hours):
        first, last = hour == 0, hour == hours - 1
        inputs = near_by(field, *edges, diffusivity, mix) + scalars(table, facts)
        if first:
            inputs += near_by(facts)
        else:
            inputs += near_by(surface, *surface_edges)
        if last:
            inputs += near_by(target, weight)
        both = [sz.whole, sz.whole]
        rest = [sz.narrow, sz.told, sz.told, sz.edge, sz.edge]
        done = call(
            functools.partial(forward_kernel, sz, first, last),
            "step",
            inputs,
            kept=[sz.surface] if last else both + [sz.surface],
            shipped=both + rest if last else rest,
            scratch=[wider],
        )
        if last:
            surface, field, drive, packed, *sends = done
        else:
            field, drive, surface, packed, *sends = done
        arrived = exchange(packed, devices)
        got = swap(*sends[:2])
        arrived, *got = lax.optimization_barrier((arrived, *got))
        if first:
            told = got
        inputs = near_by(arrived, mixing, air_temp[hour, 0], wind_speed[hour, 0])
        inputs += scalars(coupler_mix)
        lines = [jax.ShapeDtypeStruct((sz.slot_lines, WIDTH), jnp.int32)] * 2
        *decoded, flux, mixed_slope, flux_slope = call(
            functools.partial(owner_kernel, sz),
            "owners",
            inputs + (near_by(*told) if first else []),
            kept=lines if first else [],
            shipped=[sz.wide, sz.by_slot, sz.by_slot],
            scratch=[sz.narrow, (sz.slots, WIDTH)],
        )
        if first:
            tables = [table, *decoded]
        flux, *sends = lax.optimization_barrier((flux, *sends[2:]))
        flux = exchange(flux, devices)
        edges = swap(*sends)
        inputs = near_by(flux, surface, *got) + scalars(*tables, facts, *told)
        near = [sz.near, sz.near]
        if last:
            surface, slope, packed, *sends = call(
                functools.partial(surface_kernel, sz, True),
                "surface",
                inputs + near_by(target_surface, weight_surface),
                shipped=[sz.surface, sz.slope, sz.wide, sz.lats, sz.lats],
                scratch=near,
            )
        else:
            surface, *sends, slope = call(
                functools.partial(surface_kernel, sz, False),
                "surface",
                inputs,
                kept=[sz.surface, row_surface, row_surface],
                shipped=[sz.slope],
                scratch=near,
            )
            surface_edges = swap(*sends)
        saved.append((drive, slope, mixed_slope, flux_slope))

    edge_sends = None
    for hour in reversed(range(hours)):
        drive, slope, mixed_slope, flux_slope = saved[hour]
        arrived = exchange(packed, devices)
        got = swap(*sends)
        arrived, *got = lax.optimization_barrier((arrived, *got))
        back = call(
            functools.partial(owner_back_kernel, sz),
            "owners_back",
            near_by(arrived, mixing, mixed_slope, flux_slope) + scalars(coupler_mix),
            shipped=[sz.narrow],
            scratch=[sz.narrow, (sz.slots, WIDTH)],
        )[0]
        if edge_sends is not None:
            back, *edge_sends = lax.optimization_barrier((back, *edge_sends))
            edges = swap(*edge_sends)
        back = exchange(back, devices)
        surface, *row_sends = call(
            functools.partial(merge_kernel, sz),
            "merge",
            near_by(back, surface, slope, *got)
            + scalars(table, facts)
            + near_by(diffusivity_surface),
            kept=[sz.surface, row_surface, row_surface],
        )
        surface_edges = swap(*row_sends)
        inputs = (
            far_off(field)
            + near_by(surface, *edges, *surface_edges)
            + (far_off(drive) if hour > 0 else near_by(drive))
            + near_by(diffusivity, mix)
        )
        if hour > 0:
            field, surface, packed, *sends = call(
                functools.partial(backward_kernel, sz, False),
                "step_back",
                inputs + scalars(*tables, facts, *told) + near_by(saved[hour - 1][1]),
                shipped=[sz.whole, sz.surface, sz.wide, sz.lats, sz.lats, sz.edge, sz.edge],
                scratch=[sz.whole, sz.whole, wider, sz.near, sz.near, two_row_sems],
            )
            sends, edge_sends = sends[:2], sends[2:]
        else:
            gradient, sums = call(
                functools.partial(backward_kernel, sz, True),
                "step_back_sums",
                inputs + near_by(start_pert),
                shipped=[sz.whole, (devices, WIDTH)],
                scratch=[sz.whole, wider, two_row_sems],
            )

    everyones = lax.all_to_all(sums, "horiz", split_axis=0, concat_axis=0, tiled=True)
    block = perturbation.shape
    return call(
        functools.partial(final_kernel, perturbation.size * devices),
        "finish",
        near_by(everyones, perturbation, gradient.transpose(2, 0, 1, 3)),
        shipped=[block],
    )[0]


def solution(mesh):
    placed = (
        P("member", "horiz", None, None),
        P(None, "horiz", None, None),
        P(None, "horiz", None, None),
        P("horiz", None),
        P("horiz", None),
        P(),
        P(),
        P("horiz", None, None),
        P(None, "horiz", None, None),
        P(None, "horiz", None, None),
        P("horiz", None),
        P("horiz", None),
        P("horiz"),
        P("horiz"),
        P("horiz"),
    )
    return jax.shard_map(
        body,
        mesh=mesh,
        in_specs=placed,
        out_specs=P("member", "horiz", None, None),
        check_vma=False,
    )
```

```python
import functools

import jax
import jax.numpy as jnp
from jax import lax
from jax.experimental import pallas as pl
from jax.experimental.pallas import tpu as pltpu
from jax.sharding import PartitionSpec as P

LAT_DEV = 2
NEAR_LAT = LAT_DEV + 2
CHANNELS = 4
LEVELS = 8
WIDTH = 128
SUBLANES = 8

KAPPA_V = 0.1
TIME_STEP = 0.3
FLUX_RATE = 0.05
FEEDBACK = 0.5
ASCENT = 0.5
EPSILON = 1e-06
HIGHEST = lax.Precision.HIGHEST
VMEM_BYTES = 32 * 1024 * 1024


class Sizes:
    def __init__(self, devices, capacity, rows, cells):
        self.devices = devices
        self.capacity = capacity
        self.slots = devices * capacity
        self.rows = rows
        self.cells = cells
        self.row_tiles = cells // WIDTH
        self.tiles = rows * self.row_tiles
        self.row_width = CHANNELS * self.row_tiles
        self.pitch = -(-self.row_tiles // SUBLANES) * SUBLANES
        self.own_rows = CHANNELS * capacity
        self.chunk = -(-(self.own_rows + 2 * capacity) // SUBLANES) * SUBLANES
        self.slot_lines = -(-self.slots // WIDTH)
        self.facts = -(-(self.slot_lines + 1) // SUBLANES) * SUBLANES
        self.lat_lines = LAT_DEV * self.pitch
        self.whole = (rows, CHANNELS, LEVELS, cells)
        self.edge = (CHANNELS, LEVELS, cells)
        self.surface = (CHANNELS * (self.tiles + 1), WIDTH)
        self.narrow = (CHANNELS * self.slots, WIDTH)
        self.wide = (devices * self.chunk, WIDTH)
        self.slope = (NEAR_LAT * self.pitch, WIDTH)
        self.lats = (self.lat_lines, WIDTH)
        self.told = (self.lat_lines + self.facts, WIDTH)
        self.bulk_at = NEAR_LAT * rows
        self.tables = (3 * self.slot_lines, WIDTH)
        self.weights = (3 * self.facts, WIDTH)
        self.near = (-(-(self.tiles + 1) // SUBLANES) * SUBLANES, WIDTH)
        self.by_slot = (CHANNELS, self.slots, WIDTH)


class Shipped:
    def __init__(self, block, home, sems):
        self.block, self.home, self.sems = block, home, sems
        self.by_row = False
        self.started = False

    def __getitem__(self, at):
        return self.block[at]

    def __setitem__(self, at, value):
        self.block[at] = value

    def row(self, index):
        self.by_row = True
        self.started = True
        return pltpu.make_async_copy(
            self.block.at[index], self.home.at[index], self.sems.at[index]
        )

    def all(self):
        return pltpu.make_async_copy(self.block, self.home, self.sems.at[0])

    def start(self):
        self.started = True
        self.all().start()

    def finish(self, rows):
        if self.by_row:
            for index in range(rows):
                self.row(index).wait()
        else:
            self.all().wait()


def cols(tile):
    return slice(tile * WIDTH, (tile + 1) * WIDTH)


def lanes_sum(left_here, left_before, right_here, right_after, lane):
    return jnp.where(lane == 0, left_before, left_here) + jnp.where(
        lane == WIDTH - 1, right_after, right_here
    )


def levels_sum(field, sub):
    return jnp.where(sub == 0, 0.0, pltpu.roll(field, 1, 0)) + jnp.where(
        sub == LEVELS - 1, 0.0, pltpu.roll(field, LEVELS - 1, 0)
    )


def row_tiles_of(sz, ref, row):
    return ref[pl.ds(row * sz.row_width, sz.row_tiles, stride=CHANNELS), :]


def put_row_tiles(sz, ref, row, value):
    ref[pl.ds(row * sz.row_width, sz.row_tiles, stride=CHANNELS), :] = value


def near_row(sz, ref, row):
    return ref[row * sz.row_tiles : (row + 1) * sz.row_tiles, :]


def load_surface_row(sz, target, row, source, base):
    for tile in range(sz.row_tiles):
        for channel in range(CHANNELS):
            at = base + tile * CHANNELS + channel
            target[row, channel, 0:1, cols(tile)] = source[pl.ds(at, 1), :]


def as_column(row, size):
    shape = (size, row.shape[1])
    diagonal = lax.broadcasted_iota(jnp.int32, shape, 0) == lax.broadcasted_iota(jnp.int32, shape, 1)
    return jnp.sum(jnp.where(diagonal, row, 0.0), axis=1, keepdims=True)


def setup_kernel(sz, entries, remap_entries, arrive, wet, remap, mix_rows, diffusivity, weight, *outs):
    table, facts, mix, diffusivity_rows, weight_rows, diffusivity_tiles, weight_tiles = outs
    arrive_all(arrive)
    for source, by_row, by_tile in (
        (diffusivity, diffusivity_rows, diffusivity_tiles),
        (weight, weight_rows, weight_tiles),
    ):
        for row in range(sz.rows):
            for tile in range(sz.row_tiles):
                line = source[row : row + 1, cols(tile)]
                by_row[row, 0:1, cols(tile)] = line
                at = (row * sz.row_tiles + tile) * CHANNELS
                by_tile[at : at + CHANNELS, :] = jnp.broadcast_to(line, (CHANNELS, WIDTH))
        by_row.start()
        by_tile.start()
    for index in range(CHANNELS * CHANNELS):
        column = as_column(mix_rows[index : index + 1, :], LEVELS)
        mix[index] = jnp.broadcast_to(column, (LEVELS, WIDTH))
    mix.start()
    tiles, owners = wet[0:1, :], wet[1:2, :]
    size = -(-entries // SUBLANES) * SUBLANES
    shape = (size, wet.shape[1])
    tile_here, owner_here = as_column(tiles, size), as_column(owners, size)
    earlier = lax.broadcasted_iota(jnp.int32, shape, 1) < lax.broadcasted_iota(jnp.int32, shape, 0)
    same = (owner_here == owners) & earlier
    rank = jnp.sum(jnp.where(same, 1.0, 0.0), axis=1, keepdims=True)
    slot = jnp.where(owner_here >= 0.0, owner_here * sz.capacity + rank, -1.0)
    facts[...] = jnp.zeros((sz.facts, WIDTH), jnp.float32)
    for line in range(sz.slot_lines):
        place = lax.broadcasted_iota(jnp.int32, (size, WIDTH), 1) + line * WIDTH
        match = slot.astype(jnp.int32) == place
        told = jnp.sum(jnp.where(match, sz.tiles - tile_here, 0.0), axis=0, keepdims=True)
        facts[line : line + 1, :] = told
        table[line : line + 1, :] = sz.tiles - told.astype(jnp.int32)
    size = -(-remap_entries // SUBLANES) * SUBLANES
    at, amount = as_column(remap[0:1, :], size), as_column(remap[1:2, :], size)
    place = lax.broadcasted_iota(jnp.int32, (size, WIDTH), 1)
    facts[sz.slot_lines : sz.slot_lines + 1, :] = jnp.sum(
        jnp.where(at.astype(jnp.int32) == place, amount, 0.0), axis=0, keepdims=True
    )


def gather_levels(block, rows_at, channel, tile):
    sub = lax.broadcasted_iota(jnp.int32, (LEVELS, WIDTH), 0)
    total = None
    for level in range(LEVELS):
        line = block[(level, *rows_at, slice(channel, channel + 1), cols(tile))]
        line = jnp.broadcast_to(line, (LEVELS, WIDTH))
        total = line if total is None else jnp.where(sub == level, line, total)
    return total


def edges_kernel(sz, arrive, low_start, high_start, low_base, high_base, low, high):
    arrive_all(arrive)
    for start, base, edge in ((low_start, low_base, low), (high_start, high_base, high)):
        for channel in range(CHANNELS):
            for tile in range(sz.row_tiles):
                edge[channel, :, cols(tile)] = gather_levels(
                    start, (), channel, tile
                ) + gather_levels(base, (), channel, tile)


def load_kernel(sz, arrive, perturbation, base, field, start, start_block, base_block, in_sems):
    def arrivals(row):
        return [
            pltpu.make_async_copy(source.at[:, row], block.at[row], in_sems.at[index, row])
            for index, (source, block) in enumerate(
                ((perturbation, start_block), (base, base_block))
            )
        ]

    for row in range(sz.rows):
        for arrival in arrivals(row):
            arrival.start()

    def one_row(row, carry):
        for arrival in arrivals(row):
            arrival.wait()
        for channel in range(CHANNELS):
            for tile in range(sz.row_tiles):
                here = gather_levels(start_block.at[row], (), channel, tile)
                start[row, channel, :, cols(tile)] = here
                field[row, channel, :, cols(tile)] = here + gather_levels(
                    base_block.at[row], (), channel, tile
                )
        start.row(row).start()
        return carry

    lax.fori_loop(0, sz.rows, one_row, 0)


class Remap:
    def __init__(self, sz, weights):
        self.sz, self.weights = sz, weights

    def weight(self, which, lat, row):
        line = which * self.sz.facts + self.sz.slot_lines
        return self.weights[line, lat * self.sz.rows + row]

    def own(self, lat, row):
        return self.weight(0, lat, row)

    def of_low(self, lat, row):
        return self.weight(1, lat + LAT_DEV, row)

    def of_high(self, lat, row):
        return self.weight(2, lat - LAT_DEV, row)


def tile_at(sz, tables, which, slot):
    return tables[which * sz.slot_lines + slot // WIDTH, slot % WIDTH]


def sum_of(weights, values):
    total = weights[0] * values[0]
    for weight, value in zip(weights[1:], values[1:]):
        total = total + weight * value
    return total


def own_sums(sz, remap, own, factor):
    return [
        factor * sum_of([remap.own(lat, row) for row in range(sz.rows)], own)
        for lat in range(NEAR_LAT)
    ]


def send_sums(sz, sums, send_low, send_high):
    for lat in range(NEAR_LAT):
        send = send_low if lat < LAT_DEV else send_high
        at = (lat % LAT_DEV) * sz.pitch
        send[at : at + sz.row_tiles, :] = sums[lat]


def lat_rows(sz, ref, lat):
    return ref[lat * sz.pitch : lat * sz.pitch + sz.row_tiles, :]


def told_sums(sz, from_low, from_high):
    return [
        lat_rows(sz, from_low if lat < LAT_DEV else from_high, lat % LAT_DEV)
        for lat in range(NEAR_LAT)
    ]


def forward_kernel(sz, first, last, arrive, *refs):
    refs = list(refs)
    low, high, diffusivity, mix, tables, facts, field = refs[:7]
    refs = refs[7:]
    if first:
        told_facts = refs[0]
        refs = refs[1:]
    else:
        surface, low_surface, high_surface = refs[:3]
        refs = refs[3:]
    if last:
        weight, target = refs[:2]
        refs = refs[2:]
    out, drive, new_surface, packed, tell_low, tell_high, edge_low, edge_high, padded = refs[:9]
    remap = Remap(sz, facts)
    if not first:
        in_sems = refs[9]

    def arrivals(row):
        copies = [pltpu.make_async_copy(field.at[row], padded.at[row + 1], in_sems.at[0, row])]
        if last:
            copies.append(
                pltpu.make_async_copy(target.at[:, row], refs[10].at[row], in_sems.at[1, row])
            )
        return copies

    if not first:
        for row in range(sz.rows):
            for arrival in arrivals(row):
                arrival.start()
    arrive_all(arrive)
    padded[0] = low[...]
    padded[sz.rows + 1] = high[...]
    if not first:
        load_surface_row(sz, padded, 0, low_surface, 0)
        load_surface_row(sz, padded, sz.rows + 1, high_surface, 0)

    def ready(row):
        if first:
            padded[row + 1] = field[row]
        else:
            for arrival in arrivals(row):
                arrival.wait()
            load_surface_row(sz, padded, row + 1, surface, row * sz.row_width)

    ready(0)
    lane = lax.broadcasted_iota(jnp.int32, (LEVELS, WIDTH), 1)
    sub = lax.broadcasted_iota(jnp.int32, (LEVELS, WIDTH), 0)
    count = sz.row_tiles

    def one_row(row, carry):
        @pl.when(row < sz.rows - 1)
        def _():
            ready(row + 1)

        here = [[padded[row + 1, c, :, cols(t)] for t in range(count)] for c in range(CHANNELS)]
        for t in range(count):
            coeff = jnp.broadcast_to(diffusivity[row, 0:1, cols(t)], (LEVELS, WIDTH))
            if last:
                scale = weight[row, 0:1, cols(t)]
                scale = jnp.broadcast_to(scale * scale, (LEVELS, WIDTH))
            for c in range(CHANNELS):
                mixed = mix[c * CHANNELS] * here[0][t]
                for k in range(1, CHANNELS):
                    mixed = mixed + mix[c * CHANNELS + k] * here[k][t]
                bent = jnp.tanh(mixed)
                drive[row, c, :, cols(t)] = bent
                field_here = here[c][t]
                around = lanes_sum(
                    pltpu.roll(field_here, 1, 1),
                    pltpu.roll(here[c][(t - 1) % count], 1, 1),
                    pltpu.roll(field_here, WIDTH - 1, 1),
                    pltpu.roll(here[c][(t + 1) % count], WIDTH - 1, 1),
                    lane,
                )
                around = around + (padded[row, c, :, cols(t)] + padded[row + 2, c, :, cols(t)])
                stepped = (
                    field_here
                    + coeff * (around - 4.0 * field_here)
                    + KAPPA_V * (levels_sum(field_here, sub) - 2.0 * field_here)
                    + TIME_STEP * bent
                )
                new_surface[pl.ds((row * count + t) * CHANNELS + c, 1), :] = stepped[0:1, :]
                if last:
                    stepped = scale * (stepped - gather_levels(refs[10].at[row], (), c, t))
                out[row, c, :, cols(t)] = stepped
        drive.row(row).start()
        out.row(row).start()
        return carry

    lax.fori_loop(0, sz.rows, one_row, 0)
    new_surface[CHANNELS * sz.tiles :, :] = jnp.zeros((CHANNELS, WIDTH), jnp.float32)
    new_surface.start()
    pack_slots(sz, tables, new_surface, packed)
    packed.start()
    own = [row_tiles_of(sz, new_surface.block, row) for row in range(sz.rows)]
    send_sums(sz, own_sums(sz, remap, own, 1.0), tell_low, tell_high)
    blank = told_facts[...] if first else jnp.zeros((sz.facts, WIDTH), jnp.float32)
    for tell in (tell_low, tell_high):
        tell[sz.lat_lines :, :] = blank
        tell.start()
    store_edges(sz, out, diffusivity if last else None, edge_low, edge_high)


def pack_slots(sz, tables, surface, packed):
    for slot in range(sz.slots):
        at = pl.multiple_of(tile_at(sz, tables, 0, slot) * CHANNELS, CHANNELS)
        packed[slot * CHANNELS : (slot + 1) * CHANNELS, :] = surface[pl.ds(at, CHANNELS), :]


def store_edges(sz, field, diffusivity, send_low, send_high):
    for row, send in ((0, send_low), (sz.rows - 1, send_high)):
        for channel in range(CHANNELS):
            for tile in range(sz.row_tiles):
                value = field[row, channel, :, cols(tile)]
                if diffusivity is not None:
                    value = value * jnp.broadcast_to(
                        diffusivity[row, 0:1, cols(tile)], (LEVELS, WIDTH)
                    )
                send[channel, :, cols(tile)] = value
        send.start()


def owner_kernel(sz, decode, arrive, arrived, mixing, air, wind, facts, *refs):
    slots = sz.slots
    if decode:
        told_low, told_high, own_table, own_facts, tables, weights = refs[:6]
        refs = refs[6:]
    flux, mixed_slope, flux_slope, flat, first = refs
    arrive_all(arrive)
    if decode:
        lines = sz.slot_lines
        tables[0:lines, :] = own_table[...]
        weights[0 : sz.facts, :] = own_facts[...]
        for which, told in ((1, told_low), (2, told_high)):
            got = told[sz.lat_lines : sz.lat_lines + lines, :]
            tables[which * lines : (which + 1) * lines, :] = sz.tiles - got.astype(jnp.int32)
            at = which * sz.facts
            weights[at : at + sz.facts, :] = told[sz.lat_lines :, :]
        tables.start()
        weights.start()

    def bulk(row, column):
        return facts[sz.slot_lines, sz.bulk_at + row * CHANNELS + column]

    values = [arrived[pl.ds(c, slots, stride=CHANNELS), :] for c in range(CHANNELS)]
    mixed = jnp.tanh(
        jnp.dot(
            mixing[...],
            jnp.concatenate(values, axis=1),
            precision=HIGHEST,
            preferred_element_type=jnp.float32,
        )
    )
    contrast = []
    for c in range(CHANNELS):
        mixed_here = mixed[:, cols(c)]
        mixed_slope[c] = 1.0 - mixed_here * mixed_here
        contrast.append((air[...] - values[0] if c == 0 else values[c]) + mixed_here)
    mixed_slope.start()
    rate = FLUX_RATE * wind[...]
    for c in range(CHANNELS):
        forcing = bulk(c, 0) * contrast[0]
        for k in range(1, CHANNELS):
            forcing = forcing + bulk(c, k) * contrast[k]
        bent = jnp.tanh(forcing)
        flux_slope[c] = rate * (1.0 - bent * bent)
        one = rate * bent
        flat[pl.ds(c, slots, stride=CHANNELS), :] = one
        if c == 0:
            first[...] = one
    flux_slope.start()
    cap = sz.capacity
    gap = jnp.zeros((sz.chunk - sz.own_rows, WIDTH), jnp.float32)
    for d in range(sz.devices):
        at = d * sz.chunk
        flux[at : at + sz.own_rows, :] = flat[d * sz.own_rows : (d + 1) * sz.own_rows, :]
        at = at + sz.own_rows
        flux[at : (d + 1) * sz.chunk, :] = gap
        if d > 0:
            flux[at : at + cap, :] = first[(d - 1) * cap : d * cap, :]
        if d < sz.devices - 1:
            flux[at + cap : at + 2 * cap, :] = first[(d + 1) * cap : (d + 2) * cap, :]


def owner_back_kernel(sz, arrive, arrived, mixing, mixed_slope, flux_slope, facts, back, flat, extra):
    slots, cap = sz.slots, sz.capacity

    def bulk(row, column):
        return facts[sz.slot_lines, sz.bulk_at + row * CHANNELS + column]

    for d in range(sz.devices):
        at = d * sz.chunk
        flat[d * sz.own_rows : (d + 1) * sz.own_rows, :] = arrived[at : at + sz.own_rows, :]
        more = jnp.zeros((cap, WIDTH), jnp.float32)
        if d < sz.devices - 1:
            at = (d + 1) * sz.chunk + sz.own_rows
            more = more + arrived[at : at + cap, :]
        if d > 0:
            at = (d - 1) * sz.chunk + sz.own_rows + cap
            more = more + arrived[at : at + cap, :]
        extra[d * cap : (d + 1) * cap, :] = more
    arrive_all(arrive)
    forced = []
    for c in range(CHANNELS):
        got = flat[pl.ds(c, slots, stride=CHANNELS), :]
        if c == 0:
            got = got + extra[...]
        forced.append(flux_slope[c] * got)
    direct = []
    for k in range(CHANNELS):
        total = bulk(0, k) * forced[0]
        for c in range(1, CHANNELS):
            total = total + bulk(c, k) * forced[c]
        direct.append(total)
    through = lax.dot_general(
        mixing[...],
        jnp.concatenate([direct[k] * mixed_slope[k] for k in range(CHANNELS)], axis=1),
        (((0,), (0,)), ((), ())),
        precision=HIGHEST,
        preferred_element_type=jnp.float32,
    )
    for k in range(CHANNELS):
        sign = -1.0 if k == 0 else 1.0
        back.block[pl.ds(k, slots, stride=CHANNELS), :] = through[:, cols(k)] + sign * direct[k]


def spread_back(sz, surface, slope, remap, tables, packed, near_low, near_high, tell_low, tell_high):
    rows, count, cap = sz.rows, sz.row_tiles, sz.capacity
    block = surface.block
    own = [row_tiles_of(sz, block, row) for row in range(rows)]
    sums = own_sums(sz, remap, own, FEEDBACK)
    send_sums(sz, sums, tell_low, tell_high)
    tell_low.start()
    tell_high.start()
    lats = [lat_rows(sz, slope, lat) * sums[lat] for lat in range(NEAR_LAT)]
    every = range(NEAR_LAT)
    for row in range(rows):
        added = sum_of([remap.own(lat, row) for lat in every], lats)
        put_row_tiles(sz, block, row, own[row] + added)
        at = row * count
        near_low[at : at + count, :] = sum_of(
            [remap.of_low(lat, row) for lat in range(LAT_DEV)], lats[:LAT_DEV]
        )
        near_high[at : at + count, :] = sum_of(
            [remap.of_high(lat, row) for lat in range(LAT_DEV, NEAR_LAT)], lats[LAT_DEV:]
        )
    rest = sz.near[0] - sz.tiles
    near_low[sz.tiles :, :] = jnp.zeros((rest, WIDTH), jnp.float32)
    near_high[sz.tiles :, :] = jnp.zeros((rest, WIDTH), jnp.float32)
    surface.start()
    gap = jnp.zeros((sz.chunk - sz.own_rows, WIDTH), jnp.float32)
    for owner in range(sz.devices):
        packed[owner * sz.chunk + sz.own_rows : (owner + 1) * sz.chunk, :] = gap
    for slot in range(sz.slots):
        owner, rank = slot // cap, slot % cap
        at = owner * sz.chunk + rank * CHANNELS
        tile = pl.multiple_of(tile_at(sz, tables, 0, slot) * CHANNELS, CHANNELS)
        packed[at : at + CHANNELS, :] = surface[pl.ds(tile, CHANNELS), :]
        at = owner * sz.chunk + sz.own_rows + rank
        packed[at : at + 1, :] = near_low[pl.ds(tile_at(sz, tables, 1, slot), 1), :]
        at = at + cap
        packed[at : at + 1, :] = near_high[pl.ds(tile_at(sz, tables, 2, slot), 1), :]


def surface_kernel(sz, last, arrive, *refs):
    refs = list(refs)
    flux, from_low, from_high, before, tables, weights = refs[:6]
    refs = refs[6:]
    if last:
        target, weight = refs[:2]
        surface, slope, packed, tell_low, tell_high, near_low, near_high = refs[2:]
        block = surface.block
    else:
        surface, send_low, send_high, slope, near_low, near_high = refs
        block = surface
    remap = Remap(sz, weights)
    arrive_all(arrive)
    rows, cap = sz.rows, sz.capacity
    block[...] = before[...]
    near_low[...] = jnp.zeros(sz.near, jnp.float32)
    near_high[...] = jnp.zeros(sz.near, jnp.float32)
    for slot in range(sz.slots):
        owner, rank = slot // cap, slot % cap
        at = owner * sz.chunk + rank * CHANNELS
        tile = pl.multiple_of(tile_at(sz, tables, 0, slot) * CHANNELS, CHANNELS)
        block[pl.ds(tile, CHANNELS), :] = (
            before[pl.ds(tile, CHANNELS), :] + flux[at : at + CHANNELS, :]
        )
        at = owner * sz.chunk + sz.own_rows + rank
        near_low[pl.ds(tile_at(sz, tables, 1, slot), 1), :] = flux[at : at + 1, :]
        at = at + cap
        near_high[pl.ds(tile_at(sz, tables, 2, slot), 1), :] = flux[at : at + 1, :]
    block[CHANNELS * sz.tiles :, :] = jnp.zeros((CHANNELS, WIDTH), jnp.float32)
    own = [row_tiles_of(sz, block, row) for row in range(rows)]
    sums = own_sums(sz, remap, own, 1.0)
    told = told_sums(sz, from_low, from_high)
    air = []
    for lat in range(NEAR_LAT):
        if lat < LAT_DEV:
            near, weights = near_low, [remap.of_low(lat, row) for row in range(rows)]
        else:
            near, weights = near_high, [remap.of_high(lat, row) for row in range(rows)]
        more = sum_of(weights, [near_row(sz, near, row) for row in range(rows)])
        one = jnp.tanh(sums[lat] + told[lat] + more)
        slope[lat * sz.pitch : lat * sz.pitch + sz.row_tiles, :] = 1.0 - one * one
        air.append(one)
    slope.start()
    for row in range(rows):
        weights = [remap.own(lat, row) for lat in range(NEAR_LAT)]
        put_row_tiles(sz, block, row, own[row] + FEEDBACK * sum_of(weights, air))
    if last:
        for row in range(rows):
            for tile in range(sz.row_tiles):
                at = row * sz.row_width + tile * CHANNELS
                scale = weight[at : at + CHANNELS, :]
                off = block[at : at + CHANNELS, :] - target[row, :, cols(tile)]
                block[at : at + CHANNELS, :] = scale * scale * off
        spread_back(
            sz, surface, slope, remap, tables, packed, near_low, near_high, tell_low, tell_high
        )
    else:
        send_low[...] = surface[0 : sz.row_width, :]
        send_high[...] = surface[(rows - 1) * sz.row_width : rows * sz.row_width, :]


def merge_kernel(
    sz, arrive, back, from_low, from_high, before, slope, tables, facts, diffusivity, surface, send_low, send_high
):
    rows, width = sz.rows, sz.row_width
    remap = Remap(sz, facts)
    arrive_all(arrive)
    surface[...] = before[...]
    for slot in range(sz.slots):
        tile = pl.multiple_of(tile_at(sz, tables, 0, slot) * CHANNELS, CHANNELS)
        surface[pl.ds(tile, CHANNELS), :] = (
            before[pl.ds(tile, CHANNELS), :] + back[slot * CHANNELS : (slot + 1) * CHANNELS, :]
        )
    surface[CHANNELS * sz.tiles :, :] = jnp.zeros((CHANNELS, WIDTH), jnp.float32)
    told = told_sums(sz, from_low, from_high)
    lats = [lat_rows(sz, slope, lat) * told[lat] for lat in range(NEAR_LAT)]
    for row in range(rows):
        own = row_tiles_of(sz, surface, row)
        weights = [remap.own(lat, row) for lat in range(NEAR_LAT)]
        put_row_tiles(sz, surface, row, own + sum_of(weights, lats))
    send_low[...] = diffusivity[0:width, :] * surface[0:width, :]
    end = rows * width
    send_high[...] = diffusivity[end - width : end, :] * surface[end - width : end, :]


def backward_kernel(sz, last, arrive, *refs):
    refs = list(refs)
    surface, low, high, low_surface, high_surface, diffusivity, mix = refs[:7]
    field, drive = refs[7:9]
    refs = refs[9:]
    if last:
        perturbation, out, sums = refs[:3]
        local, bent_all, padded, in_sems, start_all = refs[3:]
    else:
        tables, weights, slope = refs[:3]
        out, new_surface, packed, tell_low, tell_high, edge_low, edge_high = refs[3:10]
        local, bent_all, padded, in_sems, near_low, near_high = refs[10:]
        remap = Remap(sz, weights)
    count = sz.row_tiles

    def arrivals(row):
        copies = [
            pltpu.make_async_copy(field.at[row], local.at[row], in_sems.at[0, row]),
            pltpu.make_async_copy(drive.at[row], bent_all.at[row], in_sems.at[1, row]),
        ]
        if last:
            copies.append(
                pltpu.make_async_copy(perturbation.at[row], start_all.at[row], in_sems.at[2, row])
            )
        return copies

    for row in range(sz.rows):
        for arrival in arrivals(row):
            arrival.start()
    arrive_all(arrive)

    def ready(row):
        for arrival in arrivals(row):
            arrival.wait()
        load_surface_row(sz, local, row, surface, row * sz.row_width)
        for t in range(count):
            coeff = jnp.broadcast_to(diffusivity[row, 0:1, cols(t)], (LEVELS, WIDTH))
            for c in range(CHANNELS):
                padded[row + 1, c, :, cols(t)] = coeff * local[row, c, :, cols(t)]

    padded[0] = low[...]
    padded[sz.rows + 1] = high[...]
    load_surface_row(sz, padded, 0, low_surface, 0)
    load_surface_row(sz, padded, sz.rows + 1, high_surface, 0)
    ready(0)
    lane = lax.broadcasted_iota(jnp.int32, (LEVELS, WIDTH), 1)
    sub = lax.broadcasted_iota(jnp.int32, (LEVELS, WIDTH), 0)

    def one_row(row, carry):
        @pl.when(row < sz.rows - 1)
        def _():
            ready(row + 1)

        scaled = [[padded[row + 1, c, :, cols(t)] for t in range(count)] for c in range(CHANNELS)]
        for t in range(count):
            here, bent = [], []
            for c in range(CHANNELS):
                value = local[row, c, :, cols(t)]
                one = bent_all[row, c, :, cols(t)]
                here.append(value)
                bent.append((1.0 - one * one) * value)
            for c in range(CHANNELS):
                mixed = mix[c] * bent[0]
                for k in range(1, CHANNELS):
                    mixed = mixed + mix[k * CHANNELS + c] * bent[k]
                around = lanes_sum(
                    pltpu.roll(scaled[c][t], 1, 1),
                    pltpu.roll(scaled[c][(t - 1) % count], 1, 1),
                    pltpu.roll(scaled[c][t], WIDTH - 1, 1),
                    pltpu.roll(scaled[c][(t + 1) % count], WIDTH - 1, 1),
                    lane,
                )
                around = around + (padded[row, c, :, cols(t)] + padded[row + 2, c, :, cols(t)])
                stepped = (
                    here[c]
                    + (around - 4.0 * scaled[c][t])
                    + KAPPA_V * (levels_sum(here[c], sub) - 2.0 * here[c])
                    + TIME_STEP * mixed
                )
                out[row, c, :, cols(t)] = stepped
                if last:
                    start = start_all[row, c, :, cols(t)]
                    carry = (
                        carry[0] + start * start,
                        carry[1] + start * stepped,
                        carry[2] + stepped * stepped,
                    )
                else:
                    new_surface[pl.ds((row * count + t) * CHANNELS + c, 1), :] = stepped[0:1, :]
        out.row(row).start()
        return carry

    blank = jnp.zeros((LEVELS, WIDTH), jnp.float32)
    totals = lax.fori_loop(0, sz.rows, one_row, (blank, blank, blank) if last else 0)
    if last:
        place = lax.broadcasted_iota(jnp.int32, sums.block.shape, 1)
        held = jnp.zeros(sums.block.shape, jnp.float32)
        for index in range(3):
            total = jnp.sum(jnp.sum(totals[index], axis=0, keepdims=True), axis=1, keepdims=True)
            held = jnp.where(place == index, total, held)
        sums[...] = held
    else:
        new_surface[CHANNELS * sz.tiles :, :] = jnp.zeros((CHANNELS, WIDTH), jnp.float32)
        spread_back(
            sz, new_surface, slope, remap, tables, packed, near_low, near_high, tell_low, tell_high
        )
        packed.start()
        store_edges(sz, out, diffusivity, edge_low, edge_high)


def final_kernel(cell_total, arrive, everyones, perturbation, gradient, out):
    sums = jnp.sum(everyones[...], axis=0, keepdims=True) / cell_total
    place = lax.broadcasted_iota(jnp.int32, sums.shape, 1)
    means = [
        jnp.broadcast_to(
            jnp.sum(jnp.where(place == index, sums, 0.0), axis=1, keepdims=True), (1, WIDTH)
        )
        for index in range(3)
    ]
    scale = lax.rsqrt(means[2] + EPSILON)
    mean_sq = means[0] + 2.0 * ASCENT * scale * means[1] + ASCENT * ASCENT * scale * scale * means[2]
    shrink = lax.rsqrt(mean_sq + EPSILON)
    step = jnp.broadcast_to(ASCENT * scale * shrink, (CHANNELS, WIDTH))
    shrink = jnp.broadcast_to(shrink, (CHANNELS, WIDTH))
    levels, rows, _, cells = perturbation.shape

    def one_level(level, carry):
        for row in range(rows):
            for tile in range(cells // WIDTH):
                start = perturbation[level, row, :, cols(tile)]
                slope = gradient[level, row, :, cols(tile)]
                out[level, row, :, cols(tile)] = shrink * start + step * slope
        out.row(level).start()
        return carry

    lax.fori_loop(0, levels, one_level, 0)


class Operand:
    def __init__(self, array, space, fetch=None, at=()):
        self.array, self.space, self.fetch, self.at = array, space, fetch, at

    def block(self):
        whole = self.array.shape
        taken = [size for size, index in zip(whole, self.at) if isinstance(index, slice)]
        return self.fetch((*taken, *whole[len(self.at) :]), self.array.dtype)


def near_by(*arrays):
    return [Operand(array, pltpu.VMEM) for array in arrays]


def far_off(*arrays):
    return [
        Operand(pltpu.with_memory_space_constraint(array, pltpu.HBM), pltpu.HBM)
        for array in arrays
    ]


def fetched(*arrays, at=(), into=pltpu.VMEM):
    return [
        Operand(pltpu.with_memory_space_constraint(array, pltpu.HBM), pltpu.HBM, into, at)
        for array in arrays
    ]


def scalars(*arrays):
    return fetched(*arrays, into=pltpu.SMEM)


def call(kernel, name, inputs, kept=(), shipped=(), scratch=()):
    n_in, n_kept, n_out = len(inputs), len(kept), len(shipped)
    brought = [index for index, item in enumerate(inputs) if item.fetch is not None]

    def as_shape(item):
        return item if isinstance(item, jax.ShapeDtypeStruct) else jax.ShapeDtypeStruct(item, jnp.float32)

    kept = [as_shape(item) for item in kept]
    shipped = [as_shape(item) for item in shipped]

    def run(*refs):
        ins = list(refs[:n_in])
        kept_refs = refs[n_in : n_in + n_kept]
        homes = refs[n_in + n_kept : n_in + n_kept + n_out]
        rest = refs[n_in + n_kept + n_out :]
        outs = [
            Shipped(block, home, sems)
            for block, home, sems in zip(rest[:n_out], homes, rest[n_out : 2 * n_out])
        ]
        rest = rest[2 * n_out :]
        if brought:
            blocks, arrive_sems = rest[: len(brought)], rest[len(brought)]
            rest = rest[len(brought) + 1 :]
            copies = []
            for place, (index, block) in enumerate(zip(brought, blocks)):
                source = ins[index]
                if inputs[index].at:
                    source = source.at[inputs[index].at]
                copies.append(pltpu.make_async_copy(source, block, arrive_sems.at[place]))
                ins[index] = block
            for copy in copies:
                copy.start()
            arrive = [copy.wait for copy in copies]
        else:
            arrive = []
        kernel(arrive, *ins, *kept_refs, *outs, *rest)
        for out in outs:
            if not out.started:
                out.start()
        for out in outs:
            out.finish(out.block.shape[0])

    spaces = [pltpu.VMEM] * n_kept + [pltpu.HBM] * n_out
    blocks = [pltpu.VMEM(item.shape, item.dtype) for item in shipped]
    sems = [
        pltpu.SemaphoreType.DMA((item.shape[0] if len(item.shape) > 3 else 1,)) for item in shipped
    ]
    arriving = [inputs[index].block() for index in brought]
    if brought:
        arriving.append(pltpu.SemaphoreType.DMA((len(brought),)))
    more = [
        item if not isinstance(item, tuple) else pltpu.VMEM(item, jnp.float32) for item in scratch
    ]
    return pl.pallas_call(
        run,
        name=name,
        in_specs=[pl.BlockSpec(memory_space=item.space) for item in inputs],
        out_specs=[pl.BlockSpec(memory_space=space) for space in spaces],
        out_shape=kept + [pltpu.HBM(item.shape, item.dtype) for item in shipped],
        scratch_shapes=blocks + sems + arriving + more,
        compiler_params=pltpu.CompilerParams(vmem_limit_bytes=VMEM_BYTES),
    )(*[item.array for item in inputs])


def arrive_all(arrive):
    for wait in arrive:
        wait()


def swap(low, high):
    count = lax.axis_size("horiz")
    upward = [(i, i + 1) for i in range(count - 1)]
    downward = [(target, source) for source, target in upward]
    return lax.ppermute(high, "horiz", upward), lax.ppermute(low, "horiz", downward)


def exchange(array, devices):
    rows = array.shape[0] // devices
    split = array.reshape(devices, rows // CHANNELS, CHANNELS, WIDTH)
    moved = lax.all_to_all(split, "horiz", split_axis=0, concat_axis=0, tiled=True)
    return moved.reshape(array.shape)


def body(
    perturbation,
    base_state,
    target_state,
    cost_weight,
    diffusivity,
    chan_mix,
    coupler_mix,
    owner_mix,
    air_temp,
    wind_speed,
    wet_list,
    wet_owner,
    remap_src,
    remap_tgt,
    remap_weight,
):
    devices = lax.axis_size("horiz")
    hours = air_temp.shape[0]
    sz = Sizes(devices, air_temp.shape[2] // devices, base_state.shape[1], base_state.shape[3])
    rows = sz.rows
    native_row = (LEVELS, CHANNELS, sz.cells)

    edge_inputs = []
    for array in (perturbation, base_state):
        for row in (0, rows - 1):
            edge_inputs += fetched(array, at=(slice(None), row))
    edges = swap(
        *call(functools.partial(edges_kernel, sz), "edges", edge_inputs, kept=[sz.edge, sz.edge])
    )
    me = lax.axis_index("horiz").astype(jnp.int32)

    def lined(first_row, second_row):
        size = -(-first_row.shape[0] // WIDTH) * WIDTH
        pair = jnp.stack([first_row.astype(jnp.float32), second_row.astype(jnp.float32)])
        return jnp.pad(pair, ((0, 0), (0, size - pair.shape[1])), constant_values=-1.0)

    places = jnp.arange(CHANNELS * CHANNELS, dtype=jnp.int32) + sz.bulk_at
    remap_at = (remap_tgt - (me * LAT_DEV - 1)) * rows + remap_src - me * rows
    remap_lines = lined(
        jnp.concatenate([remap_at, places]),
        jnp.concatenate([remap_weight, coupler_mix.reshape(-1)]),
    )
    mix_rows = chan_mix.transpose(1, 2, 0).reshape(CHANNELS * CHANNELS, LEVELS)
    row_lines = (rows, 1, sz.cells)
    tiles_lines = (CHANNELS * sz.tiles, WIDTH)
    table, facts, mix, diffusivity_rows, weight_rows, diffusivity_tiles, weight_tiles = call(
        functools.partial(setup_kernel, sz, wet_list.shape[1], remap_at.shape[0] + places.shape[0]),
        "setup",
        near_by(lined(wet_list[0], wet_owner[0]), remap_lines, mix_rows)
        + fetched(diffusivity, cost_weight),
        shipped=[
            jax.ShapeDtypeStruct((sz.slot_lines, WIDTH), jnp.int32),
            (sz.facts, WIDTH),
            (CHANNELS * CHANNELS, LEVELS, WIDTH),
            row_lines,
            row_lines,
            tiles_lines,
            tiles_lines,
        ],
    )
    wider = (rows + 2, CHANNELS, LEVELS, sz.cells)
    row_surface = (sz.row_width, WIDTH)
    by_row = (rows, *native_row)

    def row_sems(kinds):
        return pltpu.SemaphoreType.DMA((kinds, rows))

    field, start_field = call(
        functools.partial(load_kernel, sz),
        "load",
        far_off(perturbation, base_state),
        kept=[sz.whole],
        shipped=[sz.whole],
        scratch=[by_row, by_row, row_sems(2)],
    )

    saved = []
    surface = None
    told = None
    for hour in range(hours):
        first, last = hour == 0, hour == hours - 1
        inputs = near_by(*edges) + fetched(diffusivity_rows, mix) + scalars(table, facts)
        scratch = [wider]
        if first:
            inputs += near_by(field) + fetched(facts)
        else:
            inputs += far_off(field) + near_by(surface, *surface_edges)
            scratch += [row_sems(2)]
        if last:
            inputs += fetched(weight_rows) + far_off(target_state)
            scratch += [by_row]
        field, drive, surface, packed, *sends = call(
            functools.partial(forward_kernel, sz, first, last),
            "step",
            inputs,
            shipped=[
                sz.whole, sz.whole, sz.surface, sz.narrow, sz.told, sz.told, sz.edge, sz.edge
            ],
            scratch=scratch,
        )
        arrived = exchange(packed, devices)
        got = swap(*sends[:2])
        arrived, *got = lax.optimization_barrier((arrived, *got))
        if first:
            told = got
        inputs = (
            near_by(arrived)
            + fetched(owner_mix, at=(0,))
            + fetched(air_temp, wind_speed, at=(hour, 0))
            + scalars(facts)
        )
        decoded = []
        if first:
            inputs += near_by(*told) + fetched(table, facts)
            decoded = [jax.ShapeDtypeStruct(sz.tables, jnp.int32), sz.weights]
        *decoded, flux, mixed_slope, flux_slope = call(
            functools.partial(owner_kernel, sz, first),
            "owners",
            inputs,
            shipped=[*decoded, sz.wide, sz.by_slot, sz.by_slot],
            scratch=[sz.narrow, (sz.slots, WIDTH)],
        )
        if first:
            tables, weights = decoded
        flux, *sends = lax.optimization_barrier((flux, *sends[2:]))
        flux = exchange(flux, devices)
        edges = swap(*sends)
        inputs = near_by(flux, *got) + fetched(surface) + scalars(tables, weights)
        near = [sz.near, sz.near]
        if last:
            surface, slope, packed, *sends = call(
                functools.partial(surface_kernel, sz, True),
                "surface",
                inputs + fetched(target_state, at=(0,)) + fetched(weight_tiles),
                shipped=[sz.surface, sz.slope, sz.wide, sz.lats, sz.lats],
                scratch=near,
            )
        else:
            surface, *sends, slope = call(
                functools.partial(surface_kernel, sz, False),
                "surface",
                inputs,
                kept=[sz.surface, row_surface, row_surface],
                shipped=[sz.slope],
                scratch=near,
            )
            surface_edges = swap(*sends)
        saved.append((drive, slope, mixed_slope, flux_slope))

    edge_sends = None
    for hour in reversed(range(hours)):
        drive, slope, mixed_slope, flux_slope = saved[hour]
        arrived = exchange(packed, devices)
        got = swap(*sends)
        arrived, *got = lax.optimization_barrier((arrived, *got))
        back = call(
            functools.partial(owner_back_kernel, sz),
            "owners_back",
            near_by(arrived)
            + fetched(owner_mix, at=(0,))
            + fetched(mixed_slope, flux_slope)
            + scalars(facts),
            shipped=[sz.narrow],
            scratch=[sz.narrow, (sz.slots, WIDTH)],
        )[0]
        if edge_sends is not None:
            back, *edge_sends = lax.optimization_barrier((back, *edge_sends))
            edges = swap(*edge_sends)
        back = exchange(back, devices)
        surface, *row_sends = call(
            functools.partial(merge_kernel, sz),
            "merge",
            near_by(back, *got)
            + fetched(surface, slope)
            + scalars(table, facts)
            + fetched(diffusivity_tiles),
            kept=[sz.surface, row_surface, row_surface],
        )
        surface_edges = swap(*row_sends)
        inputs = (
            near_by(surface, *edges, *surface_edges)
            + fetched(diffusivity_rows, mix)
            + far_off(field, drive)
        )
        if hour > 0:
            field, surface, packed, *sends = call(
                functools.partial(backward_kernel, sz, False),
                "step_back",
                inputs + scalars(tables, weights) + fetched(saved[hour - 1][1]),
                shipped=[sz.whole, sz.surface, sz.wide, sz.lats, sz.lats, sz.edge, sz.edge],
                scratch=[sz.whole, sz.whole, wider, row_sems(2), sz.near, sz.near],
            )
            sends, edge_sends = sends[:2], sends[2:]
        else:
            gradient, sums = call(
                functools.partial(backward_kernel, sz, True),
                "step_back_sums",
                inputs + far_off(start_field),
                shipped=[sz.whole, (devices, WIDTH)],
                scratch=[sz.whole, sz.whole, wider, row_sems(3), sz.whole],
            )

    everyones = lax.all_to_all(sums, "horiz", split_axis=0, concat_axis=0, tiled=True)
    block = perturbation.shape
    return call(
        functools.partial(final_kernel, perturbation.size * devices),
        "finish",
        near_by(everyones, perturbation, gradient.transpose(2, 0, 1, 3)),
        shipped=[block],
    )[0]


def solution(mesh):
    placed = (
        P("member", "horiz", None, None),
        P(None, "horiz", None, None),
        P(None, "horiz", None, None),
        P("horiz", None),
        P("horiz", None),
        P(),
        P(),
        P("horiz", None, None),
        P(None, "horiz", None, None),
        P(None, "horiz", None, None),
        P("horiz", None),
        P("horiz", None),
        P("horiz"),
        P("horiz"),
        P("horiz"),
    )
    return jax.shard_map(
        body,
        mesh=mesh,
        in_specs=placed,
        out_specs=P("member", "horiz", None, None),
        check_vma=False,
    )
```

```python
import functools

import jax
import jax.numpy as jnp
from jax import lax
from jax.experimental import pallas as pl
from jax.experimental.pallas import tpu as pltpu
from jax.sharding import PartitionSpec as P

LAT_DEV = 2
NEAR_LAT = LAT_DEV + 2
CHANNELS = 4
LEVELS = 8
WIDTH = 128
SUBLANES = 8

KAPPA_V = 0.1
TIME_STEP = 0.3
FLUX_RATE = 0.05
FEEDBACK = 0.5
ASCENT = 0.5
EPSILON = 1e-06
HIGHEST = lax.Precision.HIGHEST
VMEM_BYTES = 32 * 1024 * 1024


class Sizes:
    def __init__(self, devices, capacity, rows, cells):
        self.devices = devices
        self.capacity = capacity
        self.slots = devices * capacity
        self.rows = rows
        self.cells = cells
        self.row_tiles = cells // WIDTH
        self.tiles = rows * self.row_tiles
        self.row_width = CHANNELS * self.row_tiles
        self.pitch = -(-self.row_tiles // SUBLANES) * SUBLANES
        self.own_rows = CHANNELS * capacity
        self.chunk = -(-(self.own_rows + 2 * capacity) // SUBLANES) * SUBLANES
        self.slot_lines = -(-self.slots // WIDTH)
        self.facts = -(-(self.slot_lines + 1) // SUBLANES) * SUBLANES
        self.lat_lines = LAT_DEV * self.pitch
        self.whole = (rows, CHANNELS, LEVELS, cells)
        self.edge = (CHANNELS, LEVELS, cells)
        self.surface = (CHANNELS * (self.tiles + 1), WIDTH)
        self.narrow = (CHANNELS * self.slots, WIDTH)
        self.wide = (devices * self.chunk, WIDTH)
        self.slope = (NEAR_LAT * self.pitch, WIDTH)
        self.lats = (self.lat_lines, WIDTH)
        self.told = (self.lat_lines + self.facts, WIDTH)
        self.bulk_at = NEAR_LAT * rows
        self.tables = (3 * self.slot_lines, WIDTH)
        self.weights = (3 * self.facts, WIDTH)
        self.near = (-(-(self.tiles + 1) // SUBLANES) * SUBLANES, WIDTH)
        self.by_slot = (CHANNELS, self.slots, WIDTH)


class Shipped:
    def __init__(self, block, home, sems):
        self.block, self.home, self.sems = block, home, sems
        self.by_row = False
        self.started = False

    def __getitem__(self, at):
        return self.block[at]

    def __setitem__(self, at, value):
        self.block[at] = value

    def row(self, index):
        self.by_row = True
        self.started = True
        return pltpu.make_async_copy(
            self.block.at[index], self.home.at[index], self.sems.at[index]
        )

    def all(self):
        return pltpu.make_async_copy(self.block, self.home, self.sems.at[0])

    def start(self):
        self.started = True
        self.all().start()

    def finish(self, rows):
        if self.by_row:
            for index in range(rows):
                self.row(index).wait()
        else:
            self.all().wait()


def cols(tile):
    return slice(tile * WIDTH, (tile + 1) * WIDTH)


def lanes_sum(left_here, left_before, right_here, right_after, lane):
    return jnp.where(lane == 0, left_before, left_here) + jnp.where(
        lane == WIDTH - 1, right_after, right_here
    )


def levels_sum(field, sub):
    return jnp.where(sub == 0, 0.0, pltpu.roll(field, 1, 0)) + jnp.where(
        sub == LEVELS - 1, 0.0, pltpu.roll(field, LEVELS - 1, 0)
    )


def row_tiles_of(sz, ref, row):
    return ref[pl.ds(row * sz.row_width, sz.row_tiles, stride=CHANNELS), :]


def put_row_tiles(sz, ref, row, value):
    ref[pl.ds(row * sz.row_width, sz.row_tiles, stride=CHANNELS), :] = value


def near_row(sz, ref, row):
    return ref[row * sz.row_tiles : (row + 1) * sz.row_tiles, :]


def high_first():
    return 1 - lax.rem(lax.axis_index("horiz").astype(jnp.int32), 2)


def pick(flag, one, other):
    return jnp.where(jnp.full(one.shape, flag, jnp.int32) == 1, one, other)


def sided(first, second):
    flag = high_first()
    return pick(flag, second, first), pick(flag, first, second)


def load_surface_row(sz, target, row, source, base):
    for tile in range(sz.row_tiles):
        for channel in range(CHANNELS):
            at = base + tile * CHANNELS + channel
            target[row, channel, 0:1, cols(tile)] = source[pl.ds(at, 1), :]


def as_column(row, size):
    shape = (size, row.shape[1])
    diagonal = lax.broadcasted_iota(jnp.int32, shape, 0) == lax.broadcasted_iota(jnp.int32, shape, 1)
    return jnp.sum(jnp.where(diagonal, row, 0.0), axis=1, keepdims=True)


def setup_kernel(sz, entries, remap_entries, arrive, wet, remap, mix_rows, diffusivity, weight, *outs):
    table, facts, mix, diffusivity_rows, weight_rows, diffusivity_tiles, weight_tiles = outs
    arrive_all(arrive)
    for source, by_row, by_tile in (
        (diffusivity, diffusivity_rows, diffusivity_tiles),
        (weight, weight_rows, weight_tiles),
    ):
        for row in range(sz.rows):
            for tile in range(sz.row_tiles):
                line = source[row : row + 1, cols(tile)]
                by_row[row, 0:1, cols(tile)] = line
                at = (row * sz.row_tiles + tile) * CHANNELS
                by_tile[at : at + CHANNELS, :] = jnp.broadcast_to(line, (CHANNELS, WIDTH))
        by_row.start()
        by_tile.start()
    for index in range(CHANNELS * CHANNELS):
        column = as_column(mix_rows[index : index + 1, :], LEVELS)
        mix[index] = jnp.broadcast_to(column, (LEVELS, WIDTH))
    mix.start()
    tiles, owners = wet[0:1, :], wet[1:2, :]
    size = -(-entries // SUBLANES) * SUBLANES
    shape = (size, wet.shape[1])
    tile_here, owner_here = as_column(tiles, size), as_column(owners, size)
    earlier = lax.broadcasted_iota(jnp.int32, shape, 1) < lax.broadcasted_iota(jnp.int32, shape, 0)
    same = (owner_here == owners) & earlier
    rank = jnp.sum(jnp.where(same, 1.0, 0.0), axis=1, keepdims=True)
    slot = jnp.where(owner_here >= 0.0, owner_here * sz.capacity + rank, -1.0)
    facts[...] = jnp.zeros((sz.facts, WIDTH), jnp.float32)
    for line in range(sz.slot_lines):
        place = lax.broadcasted_iota(jnp.int32, (size, WIDTH), 1) + line * WIDTH
        match = slot.astype(jnp.int32) == place
        told = jnp.sum(jnp.where(match, sz.tiles - tile_here, 0.0), axis=0, keepdims=True)
        facts[line : line + 1, :] = told
        table[line : line + 1, :] = sz.tiles - told.astype(jnp.int32)
    size = -(-remap_entries // SUBLANES) * SUBLANES
    at, amount = as_column(remap[0:1, :], size), as_column(remap[1:2, :], size)
    place = lax.broadcasted_iota(jnp.int32, (size, WIDTH), 1)
    facts[sz.slot_lines : sz.slot_lines + 1, :] = jnp.sum(
        jnp.where(at.astype(jnp.int32) == place, amount, 0.0), axis=0, keepdims=True
    )


def gather_levels(block, rows_at, channel, tile):
    sub = lax.broadcasted_iota(jnp.int32, (LEVELS, WIDTH), 0)
    total = None
    for level in range(LEVELS):
        line = block[(level, *rows_at, slice(channel, channel + 1), cols(tile))]
        line = jnp.broadcast_to(line, (LEVELS, WIDTH))
        total = line if total is None else jnp.where(sub == level, line, total)
    return total


def edges_kernel(sz, arrive, low_start, high_start, low_base, high_base, send_first, send_second):
    arrive_all(arrive)
    flag = high_first()
    for channel in range(CHANNELS):
        for tile in range(sz.row_tiles):
            low = gather_levels(low_start, (), channel, tile)
            low = low + gather_levels(low_base, (), channel, tile)
            high = gather_levels(high_start, (), channel, tile)
            high = high + gather_levels(high_base, (), channel, tile)
            send_first[channel, :, cols(tile)] = pick(flag, high, low)
            send_second[channel, :, cols(tile)] = pick(flag, low, high)


def load_kernel(sz, arrive, perturbation, base, field, start, start_block, base_block, in_sems):
    def arrivals(row):
        return [
            pltpu.make_async_copy(source.at[:, row], block.at[row], in_sems.at[index, row])
            for index, (source, block) in enumerate(
                ((perturbation, start_block), (base, base_block))
            )
        ]

    for row in range(sz.rows):
        for arrival in arrivals(row):
            arrival.start()

    def one_row(row, carry):
        for arrival in arrivals(row):
            arrival.wait()
        for channel in range(CHANNELS):
            for tile in range(sz.row_tiles):
                here = gather_levels(start_block.at[row], (), channel, tile)
                start[row, channel, :, cols(tile)] = here
                field[row, channel, :, cols(tile)] = here + gather_levels(
                    base_block.at[row], (), channel, tile
                )
        start.row(row).start()
        return carry

    lax.fori_loop(0, sz.rows, one_row, 0)


class Remap:
    def __init__(self, sz, weights):
        self.sz, self.weights = sz, weights

    def weight(self, which, lat, row):
        line = which * self.sz.facts + self.sz.slot_lines
        return self.weights[line, lat * self.sz.rows + row]

    def own(self, lat, row):
        return self.weight(0, lat, row)

    def of_low(self, lat, row):
        return self.weight(1, lat + LAT_DEV, row)

    def of_high(self, lat, row):
        return self.weight(2, lat - LAT_DEV, row)


def tile_at(sz, tables, which, slot):
    return tables[which * sz.slot_lines + slot // WIDTH, slot % WIDTH]


def sum_of(weights, values):
    total = weights[0] * values[0]
    for weight, value in zip(weights[1:], values[1:]):
        total = total + weight * value
    return total


def own_sums(sz, remap, own, factor):
    return [
        factor * sum_of([remap.own(lat, row) for row in range(sz.rows)], own)
        for lat in range(NEAR_LAT)
    ]


def send_sums(sz, sums, tell_first, tell_second):
    flag = high_first()
    for index in range(LAT_DEV):
        low, high = sums[index], sums[LAT_DEV + index]
        at = index * sz.pitch
        tell_first[at : at + sz.row_tiles, :] = pick(flag, high, low)
        tell_second[at : at + sz.row_tiles, :] = pick(flag, low, high)


def lat_rows(sz, ref, lat):
    return ref[lat * sz.pitch : lat * sz.pitch + sz.row_tiles, :]


def told_sums(sz, from_first, from_second):
    lows, highs = [], []
    for index in range(LAT_DEV):
        low, high = sided(lat_rows(sz, from_first, index), lat_rows(sz, from_second, index))
        lows.append(low)
        highs.append(high)
    return lows + highs


def place_edges(sz, padded, first, second, first_surface=None, second_surface=None):
    side = high_first() * (sz.rows + 1)
    for at, edge, surface in ((side, first, first_surface), (sz.rows + 1 - side, second, second_surface)):
        padded[at] = edge[...]
        if surface is not None:
            load_surface_row(sz, padded, at, surface, 0)


def store_rows(sz, surface, send_first, send_second, factor=None):
    row = high_first() * (sz.rows - 1)
    for at, send in ((row, send_first), (sz.rows - 1 - row, send_second)):
        for tile in range(sz.row_tiles):
            start = pl.multiple_of((at * sz.row_tiles + tile) * CHANNELS, CHANNELS)
            value = surface[pl.ds(start, CHANNELS), :]
            if factor is not None:
                value = factor[pl.ds(start, CHANNELS), :] * value
            send[tile * CHANNELS : (tile + 1) * CHANNELS, :] = value


def forward_kernel(sz, first, last, arrive, *refs):
    refs = list(refs)
    low, high, diffusivity, mix, tables, facts, field = refs[:7]
    refs = refs[7:]
    if first:
        told_facts = refs[0]
        refs = refs[1:]
    else:
        surface, first_surface, second_surface = refs[:3]
        refs = refs[3:]
    if last:
        weight, target = refs[:2]
        refs = refs[2:]
    out, drive, new_surface, packed, tell_first, tell_second, edge_first, edge_second, padded = refs[:9]
    remap = Remap(sz, facts)
    if not first:
        in_sems = refs[9]

    def arrivals(row):
        copies = [pltpu.make_async_copy(field.at[row], padded.at[row + 1], in_sems.at[0, row])]
        if last:
            copies.append(
                pltpu.make_async_copy(target.at[:, row], refs[10].at[row], in_sems.at[1, row])
            )
        return copies

    if not first:
        for row in range(sz.rows):
            for arrival in arrivals(row):
                arrival.start()
    arrive_all(arrive)
    if first:
        place_edges(sz, padded, low, high)
    else:
        place_edges(sz, padded, low, high, first_surface, second_surface)

    def ready(row):
        if first:
            padded[row + 1] = field[row]
        else:
            for arrival in arrivals(row):
                arrival.wait()
            load_surface_row(sz, padded, row + 1, surface, row * sz.row_width)

    ready(0)
    lane = lax.broadcasted_iota(jnp.int32, (LEVELS, WIDTH), 1)
    sub = lax.broadcasted_iota(jnp.int32, (LEVELS, WIDTH), 0)
    count = sz.row_tiles

    def one_row(row, carry):
        @pl.when(row < sz.rows - 1)
        def _():
            ready(row + 1)

        here = [[padded[row + 1, c, :, cols(t)] for t in range(count)] for c in range(CHANNELS)]
        for t in range(count):
            coeff = jnp.broadcast_to(diffusivity[row, 0:1, cols(t)], (LEVELS, WIDTH))
            if last:
                scale = weight[row, 0:1, cols(t)]
                scale = jnp.broadcast_to(scale * scale, (LEVELS, WIDTH))
            for c in range(CHANNELS):
                mixed = mix[c * CHANNELS] * here[0][t]
                for k in range(1, CHANNELS):
                    mixed = mixed + mix[c * CHANNELS + k] * here[k][t]
                bent = jnp.tanh(mixed)
                drive[row, c, :, cols(t)] = bent
                field_here = here[c][t]
                around = lanes_sum(
                    pltpu.roll(field_here, 1, 1),
                    pltpu.roll(here[c][(t - 1) % count], 1, 1),
                    pltpu.roll(field_here, WIDTH - 1, 1),
                    pltpu.roll(here[c][(t + 1) % count], WIDTH - 1, 1),
                    lane,
                )
                around = around + (padded[row, c, :, cols(t)] + padded[row + 2, c, :, cols(t)])
                stepped = (
                    field_here
                    + coeff * (around - 4.0 * field_here)
                    + KAPPA_V * (levels_sum(field_here, sub) - 2.0 * field_here)
                    + TIME_STEP * bent
                )
                new_surface[pl.ds((row * count + t) * CHANNELS + c, 1), :] = stepped[0:1, :]
                if last:
                    stepped = scale * (stepped - gather_levels(refs[10].at[row], (), c, t))
                out[row, c, :, cols(t)] = stepped
        drive.row(row).start()
        out.row(row).start()
        return carry

    lax.fori_loop(0, sz.rows, one_row, 0)
    new_surface[CHANNELS * sz.tiles :, :] = jnp.zeros((CHANNELS, WIDTH), jnp.float32)
    new_surface.start()
    pack_slots(sz, tables, new_surface, packed)
    packed.start()
    own = [row_tiles_of(sz, new_surface.block, row) for row in range(sz.rows)]
    send_sums(sz, own_sums(sz, remap, own, 1.0), tell_first, tell_second)
    blank = told_facts[...] if first else jnp.zeros((sz.facts, WIDTH), jnp.float32)
    for tell in (tell_first, tell_second):
        tell[sz.lat_lines :, :] = blank
        tell.start()
    store_edges(sz, out, diffusivity if last else None, edge_first, edge_second)


def pack_slots(sz, tables, surface, packed):
    for slot in range(sz.slots):
        at = pl.multiple_of(tile_at(sz, tables, 0, slot) * CHANNELS, CHANNELS)
        packed[slot * CHANNELS : (slot + 1) * CHANNELS, :] = surface[pl.ds(at, CHANNELS), :]


def store_edges(sz, field, diffusivity, send_first, send_second):
    outer = high_first() * (sz.rows - 1)
    for row, send in ((outer, send_first), (sz.rows - 1 - outer, send_second)):
        for channel in range(CHANNELS):
            for tile in range(sz.row_tiles):
                value = field[row, channel, :, cols(tile)]
                if diffusivity is not None:
                    value = value * jnp.broadcast_to(
                        diffusivity[row, 0:1, cols(tile)], (LEVELS, WIDTH)
                    )
                send[channel, :, cols(tile)] = value
        send.start()


def owner_kernel(sz, decode, arrive, arrived, mixing, air, wind, facts, *refs):
    slots = sz.slots
    if decode:
        told_first, told_second, own_table, own_facts, tables, weights = refs[:6]
        refs = refs[6:]
    flux, mixed_slope, flux_slope, flat, first = refs
    arrive_all(arrive)
    if decode:
        lines = sz.slot_lines
        tables[0:lines, :] = own_table[...]
        weights[0 : sz.facts, :] = own_facts[...]
        both = sided(told_first[sz.lat_lines :, :], told_second[sz.lat_lines :, :])
        for which, told in ((1, both[0]), (2, both[1])):
            got = told[0:lines, :].astype(jnp.int32)
            tables[which * lines : (which + 1) * lines, :] = sz.tiles - got
            at = which * sz.facts
            weights[at : at + sz.facts, :] = told
        tables.start()
        weights.start()

    def bulk(row, column):
        return facts[sz.slot_lines, sz.bulk_at + row * CHANNELS + column]

    values = [arrived[pl.ds(c, slots, stride=CHANNELS), :] for c in range(CHANNELS)]
    mixed = jnp.tanh(
        jnp.dot(
            mixing[...],
            jnp.concatenate(values, axis=1),
            precision=HIGHEST,
            preferred_element_type=jnp.float32,
        )
    )
    contrast = []
    for c in range(CHANNELS):
        mixed_here = mixed[:, cols(c)]
        mixed_slope[c] = 1.0 - mixed_here * mixed_here
        contrast.append((air[...] - values[0] if c == 0 else values[c]) + mixed_here)
    mixed_slope.start()
    rate = FLUX_RATE * wind[...]
    for c in range(CHANNELS):
        forcing = bulk(c, 0) * contrast[0]
        for k in range(1, CHANNELS):
            forcing = forcing + bulk(c, k) * contrast[k]
        bent = jnp.tanh(forcing)
        flux_slope[c] = rate * (1.0 - bent * bent)
        one = rate * bent
        flat[pl.ds(c, slots, stride=CHANNELS), :] = one
        if c == 0:
            first[...] = one
    flux_slope.start()
    cap = sz.capacity
    gap = jnp.zeros((sz.chunk - sz.own_rows, WIDTH), jnp.float32)
    for d in range(sz.devices):
        at = d * sz.chunk
        flux[at : at + sz.own_rows, :] = flat[d * sz.own_rows : (d + 1) * sz.own_rows, :]
        at = at + sz.own_rows
        flux[at : (d + 1) * sz.chunk, :] = gap
        if d > 0:
            flux[at : at + cap, :] = first[(d - 1) * cap : d * cap, :]
        if d < sz.devices - 1:
            flux[at + cap : at + 2 * cap, :] = first[(d + 1) * cap : (d + 2) * cap, :]


def owner_back_kernel(sz, arrive, arrived, mixing, mixed_slope, flux_slope, facts, back, flat, extra):
    slots, cap = sz.slots, sz.capacity

    def bulk(row, column):
        return facts[sz.slot_lines, sz.bulk_at + row * CHANNELS + column]

    for d in range(sz.devices):
        at = d * sz.chunk
        flat[d * sz.own_rows : (d + 1) * sz.own_rows, :] = arrived[at : at + sz.own_rows, :]
        more = jnp.zeros((cap, WIDTH), jnp.float32)
        if d < sz.devices - 1:
            at = (d + 1) * sz.chunk + sz.own_rows
            more = more + arrived[at : at + cap, :]
        if d > 0:
            at = (d - 1) * sz.chunk + sz.own_rows + cap
            more = more + arrived[at : at + cap, :]
        extra[d * cap : (d + 1) * cap, :] = more
    arrive_all(arrive)
    forced = []
    for c in range(CHANNELS):
        got = flat[pl.ds(c, slots, stride=CHANNELS), :]
        if c == 0:
            got = got + extra[...]
        forced.append(flux_slope[c] * got)
    direct = []
    for k in range(CHANNELS):
        total = bulk(0, k) * forced[0]
        for c in range(1, CHANNELS):
            total = total + bulk(c, k) * forced[c]
        direct.append(total)
    through = lax.dot_general(
        mixing[...],
        jnp.concatenate([direct[k] * mixed_slope[k] for k in range(CHANNELS)], axis=1),
        (((0,), (0,)), ((), ())),
        precision=HIGHEST,
        preferred_element_type=jnp.float32,
    )
    for k in range(CHANNELS):
        sign = -1.0 if k == 0 else 1.0
        back.block[pl.ds(k, slots, stride=CHANNELS), :] = through[:, cols(k)] + sign * direct[k]


def spread_back(sz, surface, slope, remap, tables, packed, near_low, near_high, tell_first, tell_second):
    rows, count, cap = sz.rows, sz.row_tiles, sz.capacity
    block = surface.block
    own = [row_tiles_of(sz, block, row) for row in range(rows)]
    sums = own_sums(sz, remap, own, FEEDBACK)
    send_sums(sz, sums, tell_first, tell_second)
    tell_first.start()
    tell_second.start()
    lats = [lat_rows(sz, slope, lat) * sums[lat] for lat in range(NEAR_LAT)]
    every = range(NEAR_LAT)
    for row in range(rows):
        added = sum_of([remap.own(lat, row) for lat in every], lats)
        put_row_tiles(sz, block, row, own[row] + added)
        at = row * count
        near_low[at : at + count, :] = sum_of(
            [remap.of_low(lat, row) for lat in range(LAT_DEV)], lats[:LAT_DEV]
        )
        near_high[at : at + count, :] = sum_of(
            [remap.of_high(lat, row) for lat in range(LAT_DEV, NEAR_LAT)], lats[LAT_DEV:]
        )
    rest = sz.near[0] - sz.tiles
    near_low[sz.tiles :, :] = jnp.zeros((rest, WIDTH), jnp.float32)
    near_high[sz.tiles :, :] = jnp.zeros((rest, WIDTH), jnp.float32)
    surface.start()
    gap = jnp.zeros((sz.chunk - sz.own_rows, WIDTH), jnp.float32)
    for owner in range(sz.devices):
        packed[owner * sz.chunk + sz.own_rows : (owner + 1) * sz.chunk, :] = gap
    for slot in range(sz.slots):
        owner, rank = slot // cap, slot % cap
        at = owner * sz.chunk + rank * CHANNELS
        tile = pl.multiple_of(tile_at(sz, tables, 0, slot) * CHANNELS, CHANNELS)
        packed[at : at + CHANNELS, :] = surface[pl.ds(tile, CHANNELS), :]
        at = owner * sz.chunk + sz.own_rows + rank
        packed[at : at + 1, :] = near_low[pl.ds(tile_at(sz, tables, 1, slot), 1), :]
        at = at + cap
        packed[at : at + 1, :] = near_high[pl.ds(tile_at(sz, tables, 2, slot), 1), :]


def surface_kernel(sz, last, arrive, *refs):
    refs = list(refs)
    flux, from_first, from_second, before, tables, weights = refs[:6]
    refs = refs[6:]
    if last:
        target, weight = refs[:2]
        surface, slope, packed, tell_first, tell_second, near_low, near_high = refs[2:]
        block = surface.block
    else:
        surface, send_first, send_second, slope, near_low, near_high = refs
        block = surface
    remap = Remap(sz, weights)
    arrive_all(arrive)
    rows, cap = sz.rows, sz.capacity
    block[...] = before[...]
    near_low[...] = jnp.zeros(sz.near, jnp.float32)
    near_high[...] = jnp.zeros(sz.near, jnp.float32)
    for slot in range(sz.slots):
        owner, rank = slot // cap, slot % cap
        at = owner * sz.chunk + rank * CHANNELS
        tile = pl.multiple_of(tile_at(sz, tables, 0, slot) * CHANNELS, CHANNELS)
        block[pl.ds(tile, CHANNELS), :] = (
            before[pl.ds(tile, CHANNELS), :] + flux[at : at + CHANNELS, :]
        )
        at = owner * sz.chunk + sz.own_rows + rank
        near_low[pl.ds(tile_at(sz, tables, 1, slot), 1), :] = flux[at : at + 1, :]
        at = at + cap
        near_high[pl.ds(tile_at(sz, tables, 2, slot), 1), :] = flux[at : at + 1, :]
    block[CHANNELS * sz.tiles :, :] = jnp.zeros((CHANNELS, WIDTH), jnp.float32)
    own = [row_tiles_of(sz, block, row) for row in range(rows)]
    sums = own_sums(sz, remap, own, 1.0)
    told = told_sums(sz, from_first, from_second)
    air = []
    for lat in range(NEAR_LAT):
        if lat < LAT_DEV:
            near, weights = near_low, [remap.of_low(lat, row) for row in range(rows)]
        else:
            near, weights = near_high, [remap.of_high(lat, row) for row in range(rows)]
        more = sum_of(weights, [near_row(sz, near, row) for row in range(rows)])
        one = jnp.tanh(sums[lat] + told[lat] + more)
        slope[lat * sz.pitch : lat * sz.pitch + sz.row_tiles, :] = 1.0 - one * one
        air.append(one)
    slope.start()
    for row in range(rows):
        weights = [remap.own(lat, row) for lat in range(NEAR_LAT)]
        put_row_tiles(sz, block, row, own[row] + FEEDBACK * sum_of(weights, air))
    if last:
        for row in range(rows):
            for tile in range(sz.row_tiles):
                at = row * sz.row_width + tile * CHANNELS
                scale = weight[at : at + CHANNELS, :]
                off = block[at : at + CHANNELS, :] - target[row, :, cols(tile)]
                block[at : at + CHANNELS, :] = scale * scale * off
        spread_back(
            sz, surface, slope, remap, tables, packed, near_low, near_high, tell_first, tell_second
        )
    else:
        store_rows(sz, surface, send_first, send_second)


def merge_kernel(
    sz, arrive, back, from_first, from_second, before, slope, tables, facts, diffusivity, surface, send_first, send_second
):
    rows = sz.rows
    remap = Remap(sz, facts)
    arrive_all(arrive)
    surface[...] = before[...]
    for slot in range(sz.slots):
        tile = pl.multiple_of(tile_at(sz, tables, 0, slot) * CHANNELS, CHANNELS)
        surface[pl.ds(tile, CHANNELS), :] = (
            before[pl.ds(tile, CHANNELS), :] + back[slot * CHANNELS : (slot + 1) * CHANNELS, :]
        )
    surface[CHANNELS * sz.tiles :, :] = jnp.zeros((CHANNELS, WIDTH), jnp.float32)
    told = told_sums(sz, from_first, from_second)
    lats = [lat_rows(sz, slope, lat) * told[lat] for lat in range(NEAR_LAT)]
    for row in range(rows):
        own = row_tiles_of(sz, surface, row)
        weights = [remap.own(lat, row) for lat in range(NEAR_LAT)]
        put_row_tiles(sz, surface, row, own + sum_of(weights, lats))
    store_rows(sz, surface, send_first, send_second, diffusivity)


def backward_kernel(sz, last, arrive, *refs):
    refs = list(refs)
    surface, low, high, first_surface, second_surface, diffusivity, mix = refs[:7]
    field, drive = refs[7:9]
    refs = refs[9:]
    if last:
        perturbation, out, sums = refs[:3]
        local, bent_all, padded, in_sems, start_all = refs[3:]
    else:
        tables, weights, slope = refs[:3]
        out, new_surface, packed, tell_first, tell_second, edge_first, edge_second = refs[3:10]
        local, bent_all, padded, in_sems, near_low, near_high = refs[10:]
        remap = Remap(sz, weights)
    count = sz.row_tiles

    def arrivals(row):
        copies = [
            pltpu.make_async_copy(field.at[row], local.at[row], in_sems.at[0, row]),
            pltpu.make_async_copy(drive.at[row], bent_all.at[row], in_sems.at[1, row]),
        ]
        if last:
            copies.append(
                pltpu.make_async_copy(perturbation.at[row], start_all.at[row], in_sems.at[2, row])
            )
        return copies

    for row in range(sz.rows):
        for arrival in arrivals(row):
            arrival.start()
    arrive_all(arrive)

    def ready(row):
        for arrival in arrivals(row):
            arrival.wait()
        load_surface_row(sz, local, row, surface, row * sz.row_width)
        for t in range(count):
            coeff = jnp.broadcast_to(diffusivity[row, 0:1, cols(t)], (LEVELS, WIDTH))
            for c in range(CHANNELS):
                padded[row + 1, c, :, cols(t)] = coeff * local[row, c, :, cols(t)]

    place_edges(sz, padded, low, high, first_surface, second_surface)
    ready(0)
    lane = lax.broadcasted_iota(jnp.int32, (LEVELS, WIDTH), 1)
    sub = lax.broadcasted_iota(jnp.int32, (LEVELS, WIDTH), 0)

    def one_row(row, carry):
        @pl.when(row < sz.rows - 1)
        def _():
            ready(row + 1)

        scaled = [[padded[row + 1, c, :, cols(t)] for t in range(count)] for c in range(CHANNELS)]
        for t in range(count):
            here, bent = [], []
            for c in range(CHANNELS):
                value = local[row, c, :, cols(t)]
                one = bent_all[row, c, :, cols(t)]
                here.append(value)
                bent.append((1.0 - one * one) * value)
            for c in range(CHANNELS):
                mixed = mix[c] * bent[0]
                for k in range(1, CHANNELS):
                    mixed = mixed + mix[k * CHANNELS + c] * bent[k]
                around = lanes_sum(
                    pltpu.roll(scaled[c][t], 1, 1),
                    pltpu.roll(scaled[c][(t - 1) % count], 1, 1),
                    pltpu.roll(scaled[c][t], WIDTH - 1, 1),
                    pltpu.roll(scaled[c][(t + 1) % count], WIDTH - 1, 1),
                    lane,
                )
                around = around + (padded[row, c, :, cols(t)] + padded[row + 2, c, :, cols(t)])
                stepped = (
                    here[c]
                    + (around - 4.0 * scaled[c][t])
                    + KAPPA_V * (levels_sum(here[c], sub) - 2.0 * here[c])
                    + TIME_STEP * mixed
                )
                out[row, c, :, cols(t)] = stepped
                if last:
                    start = start_all[row, c, :, cols(t)]
                    carry = (
                        carry[0] + start * start,
                        carry[1] + start * stepped,
                        carry[2] + stepped * stepped,
                    )
                else:
                    new_surface[pl.ds((row * count + t) * CHANNELS + c, 1), :] = stepped[0:1, :]
        out.row(row).start()
        return carry

    blank = jnp.zeros((LEVELS, WIDTH), jnp.float32)
    totals = lax.fori_loop(0, sz.rows, one_row, (blank, blank, blank) if last else 0)
    if last:
        place = lax.broadcasted_iota(jnp.int32, sums.block.shape, 1)
        held = jnp.zeros(sums.block.shape, jnp.float32)
        for index in range(3):
            total = jnp.sum(jnp.sum(totals[index], axis=0, keepdims=True), axis=1, keepdims=True)
            held = jnp.where(place == index, total, held)
        sums[...] = held
    else:
        new_surface[CHANNELS * sz.tiles :, :] = jnp.zeros((CHANNELS, WIDTH), jnp.float32)
        spread_back(
            sz, new_surface, slope, remap, tables, packed, near_low, near_high, tell_first, tell_second
        )
        packed.start()
        store_edges(sz, out, diffusivity, edge_first, edge_second)


def final_kernel(cell_total, arrive, everyones, perturbation, gradient, out):
    sums = jnp.sum(everyones[...], axis=0, keepdims=True) / cell_total
    place = lax.broadcasted_iota(jnp.int32, sums.shape, 1)
    means = [
        jnp.broadcast_to(
            jnp.sum(jnp.where(place == index, sums, 0.0), axis=1, keepdims=True), (1, WIDTH)
        )
        for index in range(3)
    ]
    scale = lax.rsqrt(means[2] + EPSILON)
    mean_sq = means[0] + 2.0 * ASCENT * scale * means[1] + ASCENT * ASCENT * scale * scale * means[2]
    shrink = lax.rsqrt(mean_sq + EPSILON)
    step = jnp.broadcast_to(ASCENT * scale * shrink, (CHANNELS, WIDTH))
    shrink = jnp.broadcast_to(shrink, (CHANNELS, WIDTH))
    levels, rows, _, cells = perturbation.shape

    def one_level(level, carry):
        for row in range(rows):
            for tile in range(cells // WIDTH):
                start = perturbation[level, row, :, cols(tile)]
                slope = gradient[level, row, :, cols(tile)]
                out[level, row, :, cols(tile)] = shrink * start + step * slope
        out.row(level).start()
        return carry

    lax.fori_loop(0, levels, one_level, 0)


class Operand:
    def __init__(self, array, space, fetch=None, at=()):
        self.array, self.space, self.fetch, self.at = array, space, fetch, at

    def block(self):
        whole = self.array.shape
        taken = [size for size, index in zip(whole, self.at) if isinstance(index, slice)]
        return self.fetch((*taken, *whole[len(self.at) :]), self.array.dtype)


def near_by(*arrays):
    return [Operand(array, pltpu.VMEM) for array in arrays]


def far_off(*arrays):
    return [
        Operand(pltpu.with_memory_space_constraint(array, pltpu.HBM), pltpu.HBM)
        for array in arrays
    ]


def fetched(*arrays, at=(), into=pltpu.VMEM):
    return [
        Operand(pltpu.with_memory_space_constraint(array, pltpu.HBM), pltpu.HBM, into, at)
        for array in arrays
    ]


def scalars(*arrays):
    return fetched(*arrays, into=pltpu.SMEM)


def call(kernel, name, inputs, kept=(), shipped=(), scratch=()):
    n_in, n_kept, n_out = len(inputs), len(kept), len(shipped)
    brought = [index for index, item in enumerate(inputs) if item.fetch is not None]

    def as_shape(item):
        return item if isinstance(item, jax.ShapeDtypeStruct) else jax.ShapeDtypeStruct(item, jnp.float32)

    kept = [as_shape(item) for item in kept]
    shipped = [as_shape(item) for item in shipped]

    def run(*refs):
        ins = list(refs[:n_in])
        kept_refs = refs[n_in : n_in + n_kept]
        homes = refs[n_in + n_kept : n_in + n_kept + n_out]
        rest = refs[n_in + n_kept + n_out :]
        outs = [
            Shipped(block, home, sems)
            for block, home, sems in zip(rest[:n_out], homes, rest[n_out : 2 * n_out])
        ]
        rest = rest[2 * n_out :]
        if brought:
            blocks, arrive_sems = rest[: len(brought)], rest[len(brought)]
            rest = rest[len(brought) + 1 :]
            copies = []
            for place, (index, block) in enumerate(zip(brought, blocks)):
                source = ins[index]
                if inputs[index].at:
                    source = source.at[inputs[index].at]
                copies.append(pltpu.make_async_copy(source, block, arrive_sems.at[place]))
                ins[index] = block
            for copy in copies:
                copy.start()
            arrive = [copy.wait for copy in copies]
        else:
            arrive = []
        kernel(arrive, *ins, *kept_refs, *outs, *rest)
        for out in outs:
            if not out.started:
                out.start()
        for out in outs:
            out.finish(out.block.shape[0])

    spaces = [pltpu.VMEM] * n_kept + [pltpu.HBM] * n_out
    blocks = [pltpu.VMEM(item.shape, item.dtype) for item in shipped]
    sems = [
        pltpu.SemaphoreType.DMA((item.shape[0] if len(item.shape) > 3 else 1,)) for item in shipped
    ]
    arriving = [inputs[index].block() for index in brought]
    if brought:
        arriving.append(pltpu.SemaphoreType.DMA((len(brought),)))
    more = [
        item if not isinstance(item, tuple) else pltpu.VMEM(item, jnp.float32) for item in scratch
    ]
    return pl.pallas_call(
        run,
        name=name,
        in_specs=[pl.BlockSpec(memory_space=item.space) for item in inputs],
        out_specs=[pl.BlockSpec(memory_space=space) for space in spaces],
        out_shape=kept + [pltpu.HBM(item.shape, item.dtype) for item in shipped],
        scratch_shapes=blocks + sems + arriving + more,
        compiler_params=pltpu.CompilerParams(vmem_limit_bytes=VMEM_BYTES),
    )(*[item.array for item in inputs])


def arrive_all(arrive):
    for wait in arrive:
        wait()


def swap(first, second):
    count = lax.axis_size("horiz")
    inner = [(i, i ^ 1) for i in range(count)]
    outer = [(i, i + 1) for i in range(1, count - 1, 2)]
    outer = outer + [(target, source) for source, target in outer]
    return lax.ppermute(first, "horiz", inner), lax.ppermute(second, "horiz", outer)


def exchange(array, devices):
    rows = array.shape[0] // devices
    split = array.reshape(devices, rows // CHANNELS, CHANNELS, WIDTH)
    moved = lax.all_to_all(split, "horiz", split_axis=0, concat_axis=0, tiled=True)
    return moved.reshape(array.shape)


def body(
    perturbation,
    base_state,
    target_state,
    cost_weight,
    diffusivity,
    chan_mix,
    coupler_mix,
    owner_mix,
    air_temp,
    wind_speed,
    wet_list,
    wet_owner,
    remap_src,
    remap_tgt,
    remap_weight,
):
    devices = lax.axis_size("horiz")
    hours = air_temp.shape[0]
    sz = Sizes(devices, air_temp.shape[2] // devices, base_state.shape[1], base_state.shape[3])
    rows = sz.rows
    native_row = (LEVELS, CHANNELS, sz.cells)

    edge_inputs = []
    for array in (perturbation, base_state):
        for row in (0, rows - 1):
            edge_inputs += fetched(array, at=(slice(None), row))
    edges = swap(
        *call(functools.partial(edges_kernel, sz), "edges", edge_inputs, kept=[sz.edge, sz.edge])
    )
    me = lax.axis_index("horiz").astype(jnp.int32)

    def lined(first_row, second_row):
        size = -(-first_row.shape[0] // WIDTH) * WIDTH
        pair = jnp.stack([first_row.astype(jnp.float32), second_row.astype(jnp.float32)])
        return jnp.pad(pair, ((0, 0), (0, size - pair.shape[1])), constant_values=-1.0)

    places = jnp.arange(CHANNELS * CHANNELS, dtype=jnp.int32) + sz.bulk_at
    remap_at = (remap_tgt - (me * LAT_DEV - 1)) * rows + remap_src - me * rows
    remap_lines = lined(
        jnp.concatenate([remap_at, places]),
        jnp.concatenate([remap_weight, coupler_mix.reshape(-1)]),
    )
    mix_rows = chan_mix.transpose(1, 2, 0).reshape(CHANNELS * CHANNELS, LEVELS)
    row_lines = (rows, 1, sz.cells)
    tiles_lines = (CHANNELS * sz.tiles, WIDTH)
    table, facts, mix, diffusivity_rows, weight_rows, diffusivity_tiles, weight_tiles = call(
        functools.partial(setup_kernel, sz, wet_list.shape[1], remap_at.shape[0] + places.shape[0]),
        "setup",
        near_by(lined(wet_list[0], wet_owner[0]), remap_lines, mix_rows)
        + fetched(diffusivity, cost_weight),
        shipped=[
            jax.ShapeDtypeStruct((sz.slot_lines, WIDTH), jnp.int32),
            (sz.facts, WIDTH),
            (CHANNELS * CHANNELS, LEVELS, WIDTH),
            row_lines,
            row_lines,
            tiles_lines,
            tiles_lines,
        ],
    )
    wider = (rows + 2, CHANNELS, LEVELS, sz.cells)
    row_surface = (sz.row_width, WIDTH)
    by_row = (rows, *native_row)

    def row_sems(kinds):
        return pltpu.SemaphoreType.DMA((kinds, rows))

    field, start_field = call(
        functools.partial(load_kernel, sz),
        "load",
        far_off(perturbation, base_state),
        kept=[sz.whole],
        shipped=[sz.whole],
        scratch=[by_row, by_row, row_sems(2)],
    )

    saved = []
    surface = None
    told = None
    for hour in range(hours):
        first, last = hour == 0, hour == hours - 1
        inputs = near_by(*edges) + fetched(diffusivity_rows, mix) + scalars(table, facts)
        scratch = [wider]
        if first:
            inputs += near_by(field) + fetched(facts)
        else:
            inputs += far_off(field) + near_by(surface, *surface_edges)
            scratch += [row_sems(2)]
        if last:
            inputs += fetched(weight_rows) + far_off(target_state)
            scratch += [by_row]
        field, drive, surface, packed, *sends = call(
            functools.partial(forward_kernel, sz, first, last),
            "step",
            inputs,
            shipped=[
                sz.whole, sz.whole, sz.surface, sz.narrow, sz.told, sz.told, sz.edge, sz.edge
            ],
            scratch=scratch,
        )
        arrived = exchange(packed, devices)
        got = swap(*sends[:2])
        arrived, *got = lax.optimization_barrier((arrived, *got))
        if first:
            told = got
        inputs = (
            near_by(arrived)
            + fetched(owner_mix, at=(0,))
            + fetched(air_temp, wind_speed, at=(hour, 0))
            + scalars(facts)
        )
        decoded = []
        if first:
            inputs += near_by(*told) + fetched(table, facts)
            decoded = [jax.ShapeDtypeStruct(sz.tables, jnp.int32), sz.weights]
        *decoded, flux, mixed_slope, flux_slope = call(
            functools.partial(owner_kernel, sz, first),
            "owners",
            inputs,
            shipped=[*decoded, sz.wide, sz.by_slot, sz.by_slot],
            scratch=[sz.narrow, (sz.slots, WIDTH)],
        )
        if first:
            tables, weights = decoded
        flux, *sends = lax.optimization_barrier((flux, *sends[2:]))
        flux = exchange(flux, devices)
        edges = swap(*sends)
        inputs = near_by(flux, *got) + fetched(surface) + scalars(tables, weights)
        near = [sz.near, sz.near]
        if last:
            surface, slope, packed, *sends = call(
                functools.partial(surface_kernel, sz, True),
                "surface",
                inputs + fetched(target_state, at=(0,)) + fetched(weight_tiles),
                shipped=[sz.surface, sz.slope, sz.wide, sz.lats, sz.lats],
                scratch=near,
            )
        else:
            surface, *sends, slope = call(
                functools.partial(surface_kernel, sz, False),
                "surface",
                inputs,
                kept=[sz.surface, row_surface, row_surface],
                shipped=[sz.slope],
                scratch=near,
            )
            surface_edges = swap(*sends)
        saved.append((drive, slope, mixed_slope, flux_slope))

    edge_sends = None
    for hour in reversed(range(hours)):
        drive, slope, mixed_slope, flux_slope = saved[hour]
        arrived = exchange(packed, devices)
        got = swap(*sends)
        arrived, *got = lax.optimization_barrier((arrived, *got))
        back = call(
            functools.partial(owner_back_kernel, sz),
            "owners_back",
            near_by(arrived)
            + fetched(owner_mix, at=(0,))
            + fetched(mixed_slope, flux_slope)
            + scalars(facts),
            shipped=[sz.narrow],
            scratch=[sz.narrow, (sz.slots, WIDTH)],
        )[0]
        if edge_sends is not None:
            back, *edge_sends = lax.optimization_barrier((back, *edge_sends))
            edges = swap(*edge_sends)
        back = exchange(back, devices)
        surface, *row_sends = call(
            functools.partial(merge_kernel, sz),
            "merge",
            near_by(back, *got)
            + fetched(surface, slope)
            + scalars(table, facts)
            + fetched(diffusivity_tiles),
            kept=[sz.surface, row_surface, row_surface],
        )
        surface_edges = swap(*row_sends)
        inputs = (
            near_by(surface, *edges, *surface_edges)
            + fetched(diffusivity_rows, mix)
            + far_off(field, drive)
        )
        if hour > 0:
            field, surface, packed, *sends = call(
                functools.partial(backward_kernel, sz, False),
                "step_back",
                inputs + scalars(tables, weights) + fetched(saved[hour - 1][1]),
                shipped=[sz.whole, sz.surface, sz.wide, sz.lats, sz.lats, sz.edge, sz.edge],
                scratch=[sz.whole, sz.whole, wider, row_sems(2), sz.near, sz.near],
            )
            sends, edge_sends = sends[:2], sends[2:]
        else:
            gradient, sums = call(
                functools.partial(backward_kernel, sz, True),
                "step_back_sums",
                inputs + far_off(start_field),
                shipped=[sz.whole, (devices, WIDTH)],
                scratch=[sz.whole, sz.whole, wider, row_sems(3), sz.whole],
            )

    everyones = lax.all_to_all(sums, "horiz", split_axis=0, concat_axis=0, tiled=True)
    block = perturbation.shape
    return call(
        functools.partial(final_kernel, perturbation.size * devices),
        "finish",
        near_by(everyones, perturbation, gradient.transpose(2, 0, 1, 3)),
        shipped=[block],
    )[0]


def solution(mesh):
    placed = (
        P("member", "horiz", None, None),
        P(None, "horiz", None, None),
        P(None, "horiz", None, None),
        P("horiz", None),
        P("horiz", None),
        P(),
        P(),
        P("horiz", None, None),
        P(None, "horiz", None, None),
        P(None, "horiz", None, None),
        P("horiz", None),
        P("horiz", None),
        P("horiz"),
        P("horiz"),
        P("horiz"),
    )
    return jax.shard_map(
        body,
        mesh=mesh,
        in_specs=placed,
        out_specs=P("member", "horiz", None, None),
        check_vma=False,
    )
```

```python
import functools

import jax
import jax.numpy as jnp
from jax import lax
from jax.experimental import pallas as pl
from jax.experimental.pallas import tpu as pltpu
from jax.sharding import PartitionSpec as P

LAT_DEV = 2
NEAR_LAT = LAT_DEV + 2
CHANNELS = 4
LEVELS = 8
WIDTH = 128
SUBLANES = 8

KAPPA_V = 0.1
TIME_STEP = 0.3
FLUX_RATE = 0.05
FEEDBACK = 0.5
ASCENT = 0.5
EPSILON = 1e-06
HIGHEST = lax.Precision.HIGHEST
VMEM_BYTES = 32 * 1024 * 1024


class Sizes:
    def __init__(self, devices, capacity, rows, cells):
        self.devices = devices
        self.capacity = capacity
        self.slots = devices * capacity
        self.rows = rows
        self.cells = cells
        self.row_tiles = cells // WIDTH
        self.tiles = rows * self.row_tiles
        self.row_width = CHANNELS * self.row_tiles
        self.pitch = -(-self.row_tiles // SUBLANES) * SUBLANES
        self.own_rows = CHANNELS * capacity
        self.chunk = -(-(self.own_rows + 2 * capacity) // SUBLANES) * SUBLANES
        self.slot_lines = -(-self.slots // WIDTH)
        self.facts = -(-(self.slot_lines + 1) // SUBLANES) * SUBLANES
        self.lat_lines = LAT_DEV * self.pitch
        self.edge_lines = CHANNELS * self.row_tiles * LEVELS
        self.whole = (rows, CHANNELS, LEVELS, cells)
        self.edge = (self.edge_lines, WIDTH)
        self.edge_and_lats = (self.edge_lines + self.lat_lines, WIDTH)
        self.surface = (CHANNELS * (self.tiles + 1), WIDTH)
        self.narrow = (CHANNELS * self.slots, WIDTH)
        self.wide = (devices * self.chunk, WIDTH)
        self.slope = (NEAR_LAT * self.pitch, WIDTH)
        self.lats = (self.lat_lines, WIDTH)
        self.bulk_at = NEAR_LAT * rows
        self.tables = (3 * self.slot_lines, WIDTH)
        self.weights = (3 * self.facts, WIDTH)
        self.near = (-(-(self.tiles + 1) // SUBLANES) * SUBLANES, WIDTH)
        self.by_slot = (CHANNELS, self.slots, WIDTH)


class Shipped:
    def __init__(self, block, home, sems):
        self.block, self.home, self.sems = block, home, sems
        self.by_row = False
        self.started = False

    def __getitem__(self, at):
        return self.block[at]

    def __setitem__(self, at, value):
        self.block[at] = value

    def row(self, index):
        self.by_row = True
        self.started = True
        return pltpu.make_async_copy(
            self.block.at[index], self.home.at[index], self.sems.at[index]
        )

    def all(self):
        return pltpu.make_async_copy(self.block, self.home, self.sems.at[0])

    def start(self):
        self.started = True
        self.all().start()

    def finish(self, rows):
        if self.by_row:
            for index in range(rows):
                self.row(index).wait()
        else:
            self.all().wait()


def cols(tile):
    return slice(tile * WIDTH, (tile + 1) * WIDTH)


def lanes_sum(left_here, left_before, right_here, right_after, lane):
    return jnp.where(lane == 0, left_before, left_here) + jnp.where(
        lane == WIDTH - 1, right_after, right_here
    )


def levels_sum(field, sub):
    return jnp.where(sub == 0, 0.0, pltpu.roll(field, 1, 0)) + jnp.where(
        sub == LEVELS - 1, 0.0, pltpu.roll(field, LEVELS - 1, 0)
    )


def row_tiles_of(sz, ref, row):
    return ref[pl.ds(row * sz.row_width, sz.row_tiles, stride=CHANNELS), :]


def put_row_tiles(sz, ref, row, value):
    ref[pl.ds(row * sz.row_width, sz.row_tiles, stride=CHANNELS), :] = value


def near_row(sz, ref, row):
    return ref[row * sz.row_tiles : (row + 1) * sz.row_tiles, :]


def high_first():
    return 1 - lax.rem(lax.axis_index("horiz").astype(jnp.int32), 2)


def pick(flag, one, other):
    return jnp.where(jnp.full(one.shape, flag, jnp.int32) == 1, one, other)


def sided(first, second):
    flag = high_first()
    return pick(flag, second, first), pick(flag, first, second)


def load_surface_row(sz, target, row, source, base):
    for tile in range(sz.row_tiles):
        for channel in range(CHANNELS):
            at = base + tile * CHANNELS + channel
            target[row, channel, 0:1, cols(tile)] = source[pl.ds(at, 1), :]


def as_column(row, size):
    shape = (size, row.shape[1])
    diagonal = lax.broadcasted_iota(jnp.int32, shape, 0) == lax.broadcasted_iota(jnp.int32, shape, 1)
    return jnp.sum(jnp.where(diagonal, row, 0.0), axis=1, keepdims=True)


def setup_kernel(sz, entries, remap_entries, arrive, wet, remap, mix_rows, diffusivity, weight, *outs):
    first_mix, first_rows, table, facts, mix = outs[:5]
    diffusivity_rows, weight_rows, diffusivity_tiles, weight_tiles = outs[5:]
    arrive_all(arrive)
    for source, by_row, by_tile in (
        (diffusivity, diffusivity_rows, diffusivity_tiles),
        (weight, weight_rows, weight_tiles),
    ):
        for row in range(sz.rows):
            for tile in range(sz.row_tiles):
                line = source[row : row + 1, cols(tile)]
                by_row[row, 0:1, cols(tile)] = line
                at = (row * sz.row_tiles + tile) * CHANNELS
                by_tile[at : at + CHANNELS, :] = jnp.broadcast_to(line, (CHANNELS, WIDTH))
        by_row.start()
        by_tile.start()
    first_rows[...] = diffusivity_rows[...]
    for index in range(CHANNELS * CHANNELS):
        column = as_column(mix_rows[index : index + 1, :], LEVELS)
        mix[index] = jnp.broadcast_to(column, (LEVELS, WIDTH))
    mix.start()
    first_mix[...] = mix[...]
    tiles, owners = wet[0:1, :], wet[1:2, :]
    size = -(-entries // SUBLANES) * SUBLANES
    shape = (size, wet.shape[1])
    tile_here, owner_here = as_column(tiles, size), as_column(owners, size)
    earlier = lax.broadcasted_iota(jnp.int32, shape, 1) < lax.broadcasted_iota(jnp.int32, shape, 0)
    same = (owner_here == owners) & earlier
    rank = jnp.sum(jnp.where(same, 1.0, 0.0), axis=1, keepdims=True)
    slot = jnp.where(owner_here >= 0.0, owner_here * sz.capacity + rank, -1.0)
    facts[...] = jnp.zeros((sz.facts, WIDTH), jnp.float32)
    for line in range(sz.slot_lines):
        place = lax.broadcasted_iota(jnp.int32, (size, WIDTH), 1) + line * WIDTH
        match = slot.astype(jnp.int32) == place
        told = jnp.sum(jnp.where(match, sz.tiles - tile_here, 0.0), axis=0, keepdims=True)
        facts[line : line + 1, :] = told
        table[line : line + 1, :] = sz.tiles - told.astype(jnp.int32)
    size = -(-remap_entries // SUBLANES) * SUBLANES
    at, amount = as_column(remap[0:1, :], size), as_column(remap[1:2, :], size)
    place = lax.broadcasted_iota(jnp.int32, (size, WIDTH), 1)
    facts[sz.slot_lines : sz.slot_lines + 1, :] = jnp.sum(
        jnp.where(at.astype(jnp.int32) == place, amount, 0.0), axis=0, keepdims=True
    )


def gather_levels(block, rows_at, channel, tile):
    sub = lax.broadcasted_iota(jnp.int32, (LEVELS, WIDTH), 0)
    total = None
    for level in range(LEVELS):
        line = block[(level, *rows_at, slice(channel, channel + 1), cols(tile))]
        line = jnp.broadcast_to(line, (LEVELS, WIDTH))
        total = line if total is None else jnp.where(sub == level, line, total)
    return total


def edges_kernel(sz, arrive, low_start, high_start, low_base, high_base, send_first, send_second):
    arrive_all(arrive)
    flag = high_first()
    for channel in range(CHANNELS):
        for tile in range(sz.row_tiles):
            low = gather_levels(low_start, (), channel, tile)
            low = low + gather_levels(low_base, (), channel, tile)
            high = gather_levels(high_start, (), channel, tile)
            high = high + gather_levels(high_base, (), channel, tile)
            at = (channel * sz.row_tiles + tile) * LEVELS
            send_first[at : at + LEVELS, :] = pick(flag, high, low)
            send_second[at : at + LEVELS, :] = pick(flag, low, high)


def load_kernel(sz, arrive, perturbation, base, field, start, start_block, base_block, in_sems):
    def arrivals(row):
        return [
            pltpu.make_async_copy(source.at[:, row], block.at[row], in_sems.at[index, row])
            for index, (source, block) in enumerate(
                ((perturbation, start_block), (base, base_block))
            )
        ]

    for row in range(sz.rows):
        for arrival in arrivals(row):
            arrival.start()

    def one_row(row, carry):
        for arrival in arrivals(row):
            arrival.wait()
        for channel in range(CHANNELS):
            for tile in range(sz.row_tiles):
                here = gather_levels(start_block.at[row], (), channel, tile)
                start[row, channel, :, cols(tile)] = here
                field[row, channel, :, cols(tile)] = here + gather_levels(
                    base_block.at[row], (), channel, tile
                )
        start.row(row).start()
        return carry

    lax.fori_loop(0, sz.rows, one_row, 0)


class Remap:
    def __init__(self, sz, weights):
        self.sz, self.weights = sz, weights

    def weight(self, which, lat, row):
        line = which * self.sz.facts + self.sz.slot_lines
        return self.weights[line, lat * self.sz.rows + row]

    def own(self, lat, row):
        return self.weight(0, lat, row)

    def of_low(self, lat, row):
        return self.weight(1, lat + LAT_DEV, row)

    def of_high(self, lat, row):
        return self.weight(2, lat - LAT_DEV, row)


def tile_at(sz, tables, which, slot):
    return tables[which * sz.slot_lines + slot // WIDTH, slot % WIDTH]


def sum_of(weights, values):
    total = weights[0] * values[0]
    for weight, value in zip(weights[1:], values[1:]):
        total = total + weight * value
    return total


def own_sums(sz, remap, own, factor):
    return [
        factor * sum_of([remap.own(lat, row) for row in range(sz.rows)], own)
        for lat in range(NEAR_LAT)
    ]


def send_sums(sz, sums, tell_first, tell_second, base):
    flag = high_first()
    for index in range(LAT_DEV):
        low, high = sums[index], sums[LAT_DEV + index]
        at = base + index * sz.pitch
        tell_first[at : at + sz.row_tiles, :] = pick(flag, high, low)
        tell_second[at : at + sz.row_tiles, :] = pick(flag, low, high)


def lat_rows(sz, ref, lat, base=0):
    at = base + lat * sz.pitch
    return ref[at : at + sz.row_tiles, :]


def told_sums(sz, from_first, from_second, base):
    lows, highs = [], []
    for index in range(LAT_DEV):
        low, high = sided(
            lat_rows(sz, from_first, index, base), lat_rows(sz, from_second, index, base)
        )
        lows.append(low)
        highs.append(high)
    return lows + highs


def place_edges(sz, padded, first, second, first_surface=None, second_surface=None):
    side = high_first() * (sz.rows + 1)
    for at, edge, surface in ((side, first, first_surface), (sz.rows + 1 - side, second, second_surface)):
        for channel in range(CHANNELS):
            for tile in range(sz.row_tiles):
                line = (channel * sz.row_tiles + tile) * LEVELS
                padded[at, channel, :, cols(tile)] = edge[line : line + LEVELS, :]
        if surface is not None:
            load_surface_row(sz, padded, at, surface, 0)


def store_rows(sz, surface, send_first, send_second, factor=None):
    row = high_first() * (sz.rows - 1)
    for at, send in ((row, send_first), (sz.rows - 1 - row, send_second)):
        for tile in range(sz.row_tiles):
            start = pl.multiple_of((at * sz.row_tiles + tile) * CHANNELS, CHANNELS)
            value = surface[pl.ds(start, CHANNELS), :]
            if factor is not None:
                value = factor[pl.ds(start, CHANNELS), :] * value
            send[tile * CHANNELS : (tile + 1) * CHANNELS, :] = value


def forward_load_kernel(sz, last, arrive, mix, diffusivity, *refs):
    refs = list(refs)
    if last:
        weight = refs.pop(0)
    field, surface = refs[:2]
    refs = refs[2:]
    if last:
        target = refs.pop(0)
    mix_out, rows_out, field_out = refs[:3]
    refs = refs[3:]
    if last:
        weight_out, target_out = refs[:2]
        refs = refs[2:]
    in_sems = refs[0]

    def arrivals(row):
        copies = [pltpu.make_async_copy(field.at[row], field_out.at[row], in_sems.at[0, row])]
        if last:
            copies.append(
                pltpu.make_async_copy(target.at[:, row], refs[1].at[row], in_sems.at[1, row])
            )
        return copies

    for row in range(sz.rows):
        for arrival in arrivals(row):
            arrival.start()
    arrive_all(arrive)
    mix_out[...] = mix[...]
    rows_out[...] = diffusivity[...]
    if last:
        weight_out[...] = weight[...]

    def one_row(row, carry):
        for arrival in arrivals(row):
            arrival.wait()
        load_surface_row(sz, field_out, row, surface, row * sz.row_width)
        if last:
            for c in range(CHANNELS):
                for t in range(sz.row_tiles):
                    target_out[row, c, :, cols(t)] = gather_levels(refs[1].at[row], (), c, t)
        return carry

    lax.fori_loop(0, sz.rows, one_row, 0)


def forward_kernel(sz, first, last, arrive, *refs):
    refs = list(refs)
    tables, facts, low, high, diffusivity, mix, field = refs[:7]
    refs = refs[7:]
    surfaces = ()
    if not first:
        surfaces = refs[:2]
        refs = refs[2:]
    if last:
        weight, target = refs[:2]
        refs = refs[2:]
    out, drive, new_surface, packed, tell_first, tell_second, padded = refs
    remap = Remap(sz, facts)
    place_edges(sz, padded, low, high, *surfaces)

    def ready(row):
        padded[row + 1] = field[row]

    ready(0)
    lane = lax.broadcasted_iota(jnp.int32, (LEVELS, WIDTH), 1)
    sub = lax.broadcasted_iota(jnp.int32, (LEVELS, WIDTH), 0)
    count = sz.row_tiles

    def one_row(row, carry):
        @pl.when(row < sz.rows - 1)
        def _():
            ready(row + 1)

        here = [[padded[row + 1, c, :, cols(t)] for t in range(count)] for c in range(CHANNELS)]
        for t in range(count):
            coeff = jnp.broadcast_to(diffusivity[row, 0:1, cols(t)], (LEVELS, WIDTH))
            if last:
                scale = weight[row, 0:1, cols(t)]
                scale = jnp.broadcast_to(scale * scale, (LEVELS, WIDTH))
            for c in range(CHANNELS):
                mixed = mix[c * CHANNELS] * here[0][t]
                for k in range(1, CHANNELS):
                    mixed = mixed + mix[c * CHANNELS + k] * here[k][t]
                bent = jnp.tanh(mixed)
                drive[row, c, :, cols(t)] = bent
                field_here = here[c][t]
                around = lanes_sum(
                    pltpu.roll(field_here, 1, 1),
                    pltpu.roll(here[c][(t - 1) % count], 1, 1),
                    pltpu.roll(field_here, WIDTH - 1, 1),
                    pltpu.roll(here[c][(t + 1) % count], WIDTH - 1, 1),
                    lane,
                )
                around = around + (padded[row, c, :, cols(t)] + padded[row + 2, c, :, cols(t)])
                stepped = (
                    field_here
                    + coeff * (around - 4.0 * field_here)
                    + KAPPA_V * (levels_sum(field_here, sub) - 2.0 * field_here)
                    + TIME_STEP * bent
                )
                new_surface[pl.ds((row * count + t) * CHANNELS + c, 1), :] = stepped[0:1, :]
                if last:
                    stepped = scale * (stepped - target[row, c, :, cols(t)])
                out[row, c, :, cols(t)] = stepped
        drive.row(row).start()
        out.row(row).start()
        return carry

    lax.fori_loop(0, sz.rows, one_row, 0)
    new_surface[CHANNELS * sz.tiles :, :] = jnp.zeros((CHANNELS, WIDTH), jnp.float32)
    new_surface.start()
    arrive_all(arrive)
    pack_slots(sz, tables, new_surface, packed)
    packed.start()
    own = [row_tiles_of(sz, new_surface.block, row) for row in range(sz.rows)]
    send_sums(sz, own_sums(sz, remap, own, 1.0), tell_first, tell_second, sz.edge_lines)
    store_edges(sz, out, diffusivity if last else None, tell_first, tell_second)


def pack_slots(sz, tables, surface, packed):
    for slot in range(sz.slots):
        at = pl.multiple_of(tile_at(sz, tables, 0, slot) * CHANNELS, CHANNELS)
        packed[slot * CHANNELS : (slot + 1) * CHANNELS, :] = surface[pl.ds(at, CHANNELS), :]


def store_edges(sz, field, diffusivity, send_first, send_second):
    outer = high_first() * (sz.rows - 1)
    for row, send in ((outer, send_first), (sz.rows - 1 - outer, send_second)):
        for channel in range(CHANNELS):
            for tile in range(sz.row_tiles):
                value = field[row, channel, :, cols(tile)]
                if diffusivity is not None:
                    value = value * jnp.broadcast_to(
                        diffusivity[row, 0:1, cols(tile)], (LEVELS, WIDTH)
                    )
                at = (channel * sz.row_tiles + tile) * LEVELS
                send[at : at + LEVELS, :] = value
        send.start()


def owner_kernel(sz, decode, arrive, arrived, mixing, air, wind, facts, *refs):
    slots = sz.slots
    if decode:
        told_first, told_second, own_table, own_facts, tables, weights = refs[:6]
        refs = refs[6:]
    flux, mixed_slope, flux_slope, flat, first = refs
    arrive_all(arrive)
    if decode:
        lines = sz.slot_lines
        tables[0:lines, :] = own_table[...]
        weights[0 : sz.facts, :] = own_facts[...]
        both = sided(told_first[...], told_second[...])
        for which, told in ((1, both[0]), (2, both[1])):
            got = told[0:lines, :].astype(jnp.int32)
            tables[which * lines : (which + 1) * lines, :] = sz.tiles - got
            at = which * sz.facts
            weights[at : at + sz.facts, :] = told
        tables.start()
        weights.start()

    def bulk(row, column):
        return facts[sz.slot_lines, sz.bulk_at + row * CHANNELS + column]

    values = [arrived[pl.ds(c, slots, stride=CHANNELS), :] for c in range(CHANNELS)]
    mixed = jnp.tanh(
        jnp.dot(
            mixing[...],
            jnp.concatenate(values, axis=1),
            precision=HIGHEST,
            preferred_element_type=jnp.float32,
        )
    )
    contrast = []
    for c in range(CHANNELS):
        mixed_here = mixed[:, cols(c)]
        mixed_slope[c] = 1.0 - mixed_here * mixed_here
        contrast.append((air[...] - values[0] if c == 0 else values[c]) + mixed_here)
    mixed_slope.start()
    rate = FLUX_RATE * wind[...]
    for c in range(CHANNELS):
        forcing = bulk(c, 0) * contrast[0]
        for k in range(1, CHANNELS):
            forcing = forcing + bulk(c, k) * contrast[k]
        bent = jnp.tanh(forcing)
        flux_slope[c] = rate * (1.0 - bent * bent)
        one = rate * bent
        flat[pl.ds(c, slots, stride=CHANNELS), :] = one
        if c == 0:
            first[...] = one
    flux_slope.start()
    cap = sz.capacity
    gap = jnp.zeros((sz.chunk - sz.own_rows, WIDTH), jnp.float32)
    for d in range(sz.devices):
        at = d * sz.chunk
        flux[at : at + sz.own_rows, :] = flat[d * sz.own_rows : (d + 1) * sz.own_rows, :]
        at = at + sz.own_rows
        flux[at : (d + 1) * sz.chunk, :] = gap
        if d > 0:
            flux[at : at + cap, :] = first[(d - 1) * cap : d * cap, :]
        if d < sz.devices - 1:
            flux[at + cap : at + 2 * cap, :] = first[(d + 1) * cap : (d + 2) * cap, :]


def owner_back_kernel(sz, arrive, arrived, mixing, mixed_slope, flux_slope, facts, back, flat, extra):
    slots, cap = sz.slots, sz.capacity

    def bulk(row, column):
        return facts[sz.slot_lines, sz.bulk_at + row * CHANNELS + column]

    for d in range(sz.devices):
        at = d * sz.chunk
        flat[d * sz.own_rows : (d + 1) * sz.own_rows, :] = arrived[at : at + sz.own_rows, :]
        more = jnp.zeros((cap, WIDTH), jnp.float32)
        if d < sz.devices - 1:
            at = (d + 1) * sz.chunk + sz.own_rows
            more = more + arrived[at : at + cap, :]
        if d > 0:
            at = (d - 1) * sz.chunk + sz.own_rows + cap
            more = more + arrived[at : at + cap, :]
        extra[d * cap : (d + 1) * cap, :] = more
    arrive_all(arrive)
    forced = []
    for c in range(CHANNELS):
        got = flat[pl.ds(c, slots, stride=CHANNELS), :]
        if c == 0:
            got = got + extra[...]
        forced.append(flux_slope[c] * got)
    direct = []
    for k in range(CHANNELS):
        total = bulk(0, k) * forced[0]
        for c in range(1, CHANNELS):
            total = total + bulk(c, k) * forced[c]
        direct.append(total)
    through = lax.dot_general(
        mixing[...],
        jnp.concatenate([direct[k] * mixed_slope[k] for k in range(CHANNELS)], axis=1),
        (((0,), (0,)), ((), ())),
        precision=HIGHEST,
        preferred_element_type=jnp.float32,
    )
    for k in range(CHANNELS):
        sign = -1.0 if k == 0 else 1.0
        back.block[pl.ds(k, slots, stride=CHANNELS), :] = through[:, cols(k)] + sign * direct[k]


def spread_back(sz, surface, slope, remap, tables, packed, near_low, near_high, tell_first, tell_second, base):
    rows, count, cap = sz.rows, sz.row_tiles, sz.capacity
    block = surface.block
    own = [row_tiles_of(sz, block, row) for row in range(rows)]
    sums = own_sums(sz, remap, own, FEEDBACK)
    send_sums(sz, sums, tell_first, tell_second, base)
    lats = [lat_rows(sz, slope, lat) * sums[lat] for lat in range(NEAR_LAT)]
    every = range(NEAR_LAT)
    for row in range(rows):
        added = sum_of([remap.own(lat, row) for lat in every], lats)
        put_row_tiles(sz, block, row, own[row] + added)
        at = row * count
        near_low[at : at + count, :] = sum_of(
            [remap.of_low(lat, row) for lat in range(LAT_DEV)], lats[:LAT_DEV]
        )
        near_high[at : at + count, :] = sum_of(
            [remap.of_high(lat, row) for lat in range(LAT_DEV, NEAR_LAT)], lats[LAT_DEV:]
        )
    rest = sz.near[0] - sz.tiles
    near_low[sz.tiles :, :] = jnp.zeros((rest, WIDTH), jnp.float32)
    near_high[sz.tiles :, :] = jnp.zeros((rest, WIDTH), jnp.float32)
    surface.start()
    gap = jnp.zeros((sz.chunk - sz.own_rows, WIDTH), jnp.float32)
    for owner in range(sz.devices):
        packed[owner * sz.chunk + sz.own_rows : (owner + 1) * sz.chunk, :] = gap
    for slot in range(sz.slots):
        owner, rank = slot // cap, slot % cap
        at = owner * sz.chunk + rank * CHANNELS
        tile = pl.multiple_of(tile_at(sz, tables, 0, slot) * CHANNELS, CHANNELS)
        packed[at : at + CHANNELS, :] = surface[pl.ds(tile, CHANNELS), :]
        at = owner * sz.chunk + sz.own_rows + rank
        packed[at : at + 1, :] = near_low[pl.ds(tile_at(sz, tables, 1, slot), 1), :]
        at = at + cap
        packed[at : at + 1, :] = near_high[pl.ds(tile_at(sz, tables, 2, slot), 1), :]


def surface_kernel(sz, last, arrive, *refs):
    refs = list(refs)
    flux, from_first, from_second, before, tables, weights = refs[:6]
    refs = refs[6:]
    if last:
        target, weight = refs[:2]
        surface, slope, packed, tell_first, tell_second, near_low, near_high = refs[2:]
        block = surface.block
    else:
        surface, send_first, send_second, slope, near_low, near_high = refs
        block = surface
    remap = Remap(sz, weights)
    arrive_all(arrive)
    rows, cap = sz.rows, sz.capacity
    block[...] = before[...]
    near_low[...] = jnp.zeros(sz.near, jnp.float32)
    near_high[...] = jnp.zeros(sz.near, jnp.float32)
    for slot in range(sz.slots):
        owner, rank = slot // cap, slot % cap
        at = owner * sz.chunk + rank * CHANNELS
        tile = pl.multiple_of(tile_at(sz, tables, 0, slot) * CHANNELS, CHANNELS)
        block[pl.ds(tile, CHANNELS), :] = (
            before[pl.ds(tile, CHANNELS), :] + flux[at : at + CHANNELS, :]
        )
        at = owner * sz.chunk + sz.own_rows + rank
        near_low[pl.ds(tile_at(sz, tables, 1, slot), 1), :] = flux[at : at + 1, :]
        at = at + cap
        near_high[pl.ds(tile_at(sz, tables, 2, slot), 1), :] = flux[at : at + 1, :]
    block[CHANNELS * sz.tiles :, :] = jnp.zeros((CHANNELS, WIDTH), jnp.float32)
    own = [row_tiles_of(sz, block, row) for row in range(rows)]
    sums = own_sums(sz, remap, own, 1.0)
    told = told_sums(sz, from_first, from_second, sz.edge_lines)
    air = []
    for lat in range(NEAR_LAT):
        if lat < LAT_DEV:
            near, weights = near_low, [remap.of_low(lat, row) for row in range(rows)]
        else:
            near, weights = near_high, [remap.of_high(lat, row) for row in range(rows)]
        more = sum_of(weights, [near_row(sz, near, row) for row in range(rows)])
        one = jnp.tanh(sums[lat] + told[lat] + more)
        slope[lat * sz.pitch : lat * sz.pitch + sz.row_tiles, :] = 1.0 - one * one
        air.append(one)
    slope.start()
    for row in range(rows):
        weights = [remap.own(lat, row) for lat in range(NEAR_LAT)]
        put_row_tiles(sz, block, row, own[row] + FEEDBACK * sum_of(weights, air))
    if last:
        for row in range(rows):
            for tile in range(sz.row_tiles):
                at = row * sz.row_width + tile * CHANNELS
                scale = weight[at : at + CHANNELS, :]
                off = block[at : at + CHANNELS, :] - target[row, :, cols(tile)]
                block[at : at + CHANNELS, :] = scale * scale * off
        spread_back(
            sz, surface, slope, remap, tables, packed, near_low, near_high, tell_first, tell_second, 0
        )
    else:
        store_rows(sz, surface, send_first, send_second)


def merge_kernel(
    sz, base, arrive, back, from_first, from_second, before, slope, tables, facts, diffusivity, surface, send_first, send_second
):
    rows = sz.rows
    remap = Remap(sz, facts)
    arrive_all(arrive)
    surface[...] = before[...]
    for slot in range(sz.slots):
        tile = pl.multiple_of(tile_at(sz, tables, 0, slot) * CHANNELS, CHANNELS)
        surface[pl.ds(tile, CHANNELS), :] = (
            before[pl.ds(tile, CHANNELS), :] + back[slot * CHANNELS : (slot + 1) * CHANNELS, :]
        )
    surface[CHANNELS * sz.tiles :, :] = jnp.zeros((CHANNELS, WIDTH), jnp.float32)
    told = told_sums(sz, from_first, from_second, base)
    lats = [lat_rows(sz, slope, lat) * told[lat] for lat in range(NEAR_LAT)]
    for row in range(rows):
        own = row_tiles_of(sz, surface, row)
        weights = [remap.own(lat, row) for lat in range(NEAR_LAT)]
        put_row_tiles(sz, surface, row, own + sum_of(weights, lats))
    store_rows(sz, surface, send_first, send_second, diffusivity)


def backward_load_kernel(sz, last, arrive, mix, diffusivity, field, drive, surface, *refs):
    refs = list(refs)
    if last:
        perturbation = refs.pop(0)
    mix_out, rows_out, local, bent_all, scaled = refs[:5]
    refs = refs[5:]
    if last:
        start_all = refs.pop(0)
    in_sems = refs[0]

    def arrivals(row):
        copies = [
            pltpu.make_async_copy(field.at[row], local.at[row], in_sems.at[0, row]),
            pltpu.make_async_copy(drive.at[row], bent_all.at[row], in_sems.at[1, row]),
        ]
        if last:
            copies.append(
                pltpu.make_async_copy(perturbation.at[row], start_all.at[row], in_sems.at[2, row])
            )
        return copies

    for row in range(sz.rows):
        for arrival in arrivals(row):
            arrival.start()
    arrive_all(arrive)
    mix_out[...] = mix[...]
    rows_out[...] = diffusivity[...]

    def one_row(row, carry):
        for arrival in arrivals(row):
            arrival.wait()
        load_surface_row(sz, local, row, surface, row * sz.row_width)
        for t in range(sz.row_tiles):
            coeff = jnp.broadcast_to(diffusivity[row, 0:1, cols(t)], (LEVELS, WIDTH))
            for c in range(CHANNELS):
                scaled[row, c, :, cols(t)] = coeff * local[row, c, :, cols(t)]
        return carry

    lax.fori_loop(0, sz.rows, one_row, 0)


def backward_kernel(sz, last, arrive, *refs):
    refs = list(refs)
    if not last:
        tables, weights, slope = refs[:3]
        refs = refs[3:]
    low, high, first_surface, second_surface, diffusivity, mix = refs[:6]
    local, bent_all, scaled_all = refs[6:9]
    refs = refs[9:]
    if last:
        start_all, out, sums, padded = refs
    else:
        out, new_surface, packed, tell_first, tell_second, padded, near_low, near_high = refs
        remap = Remap(sz, weights)
    count = sz.row_tiles
    place_edges(sz, padded, low, high, first_surface, second_surface)

    def ready(row):
        padded[row + 1] = scaled_all[row]

    ready(0)
    lane = lax.broadcasted_iota(jnp.int32, (LEVELS, WIDTH), 1)
    sub = lax.broadcasted_iota(jnp.int32, (LEVELS, WIDTH), 0)

    def one_row(row, carry):
        @pl.when(row < sz.rows - 1)
        def _():
            ready(row + 1)

        scaled = [[padded[row + 1, c, :, cols(t)] for t in range(count)] for c in range(CHANNELS)]
        for t in range(count):
            here, bent = [], []
            for c in range(CHANNELS):
                value = local[row, c, :, cols(t)]
                one = bent_all[row, c, :, cols(t)]
                here.append(value)
                bent.append((1.0 - one * one) * value)
            for c in range(CHANNELS):
                mixed = mix[c] * bent[0]
                for k in range(1, CHANNELS):
                    mixed = mixed + mix[k * CHANNELS + c] * bent[k]
                around = lanes_sum(
                    pltpu.roll(scaled[c][t], 1, 1),
                    pltpu.roll(scaled[c][(t - 1) % count], 1, 1),
                    pltpu.roll(scaled[c][t], WIDTH - 1, 1),
                    pltpu.roll(scaled[c][(t + 1) % count], WIDTH - 1, 1),
                    lane,
                )
                around = around + (padded[row, c, :, cols(t)] + padded[row + 2, c, :, cols(t)])
                stepped = (
                    here[c]
                    + (around - 4.0 * scaled[c][t])
                    + KAPPA_V * (levels_sum(here[c], sub) - 2.0 * here[c])
                    + TIME_STEP * mixed
                )
                out[row, c, :, cols(t)] = stepped
                if last:
                    start = start_all[row, c, :, cols(t)]
                    carry = (
                        carry[0] + start * start,
                        carry[1] + start * stepped,
                        carry[2] + stepped * stepped,
                    )
                else:
                    new_surface[pl.ds((row * count + t) * CHANNELS + c, 1), :] = stepped[0:1, :]
        out.row(row).start()
        return carry

    blank = jnp.zeros((LEVELS, WIDTH), jnp.float32)
    totals = lax.fori_loop(0, sz.rows, one_row, (blank, blank, blank) if last else 0)
    if last:
        place = lax.broadcasted_iota(jnp.int32, sums.block.shape, 1)
        held = jnp.zeros(sums.block.shape, jnp.float32)
        for index in range(3):
            total = jnp.sum(jnp.sum(totals[index], axis=0, keepdims=True), axis=1, keepdims=True)
            held = jnp.where(place == index, total, held)
        sums[...] = held
    else:
        new_surface[CHANNELS * sz.tiles :, :] = jnp.zeros((CHANNELS, WIDTH), jnp.float32)
        arrive_all(arrive)
        spread_back(
            sz,
            new_surface,
            slope,
            remap,
            tables,
            packed,
            near_low,
            near_high,
            tell_first,
            tell_second,
            sz.edge_lines,
        )
        packed.start()
        store_edges(sz, out, diffusivity, tell_first, tell_second)


def final_kernel(cell_total, arrive, everyones, perturbation, gradient, out):
    sums = jnp.sum(everyones[...], axis=0, keepdims=True) / cell_total
    place = lax.broadcasted_iota(jnp.int32, sums.shape, 1)
    means = [
        jnp.broadcast_to(
            jnp.sum(jnp.where(place == index, sums, 0.0), axis=1, keepdims=True), (1, WIDTH)
        )
        for index in range(3)
    ]
    scale = lax.rsqrt(means[2] + EPSILON)
    mean_sq = means[0] + 2.0 * ASCENT * scale * means[1] + ASCENT * ASCENT * scale * scale * means[2]
    shrink = lax.rsqrt(mean_sq + EPSILON)
    step = jnp.broadcast_to(ASCENT * scale * shrink, (CHANNELS, WIDTH))
    shrink = jnp.broadcast_to(shrink, (CHANNELS, WIDTH))
    levels, rows, _, cells = perturbation.shape

    def one_level(level, carry):
        for row in range(rows):
            for tile in range(cells // WIDTH):
                start = perturbation[level, row, :, cols(tile)]
                slope = gradient[level, row, :, cols(tile)]
                out[level, row, :, cols(tile)] = shrink * start + step * slope
        out.row(level).start()
        return carry

    lax.fori_loop(0, levels, one_level, 0)


class Operand:
    def __init__(self, array, space, fetch=None, at=()):
        self.array, self.space, self.fetch, self.at = array, space, fetch, at

    def block(self):
        whole = self.array.shape
        taken = [size for size, index in zip(whole, self.at) if isinstance(index, slice)]
        return self.fetch((*taken, *whole[len(self.at) :]), self.array.dtype)


def near_by(*arrays):
    return [Operand(array, pltpu.VMEM) for array in arrays]


def far_off(*arrays):
    return [
        Operand(pltpu.with_memory_space_constraint(array, pltpu.HBM), pltpu.HBM)
        for array in arrays
    ]


def fetched(*arrays, at=(), into=pltpu.VMEM):
    return [
        Operand(pltpu.with_memory_space_constraint(array, pltpu.HBM), pltpu.HBM, into, at)
        for array in arrays
    ]


def scalars(*arrays):
    return fetched(*arrays, into=pltpu.SMEM)


def call(kernel, name, inputs, kept=(), shipped=(), scratch=()):
    n_in, n_kept, n_out = len(inputs), len(kept), len(shipped)
    brought = [index for index, item in enumerate(inputs) if item.fetch is not None]

    def as_shape(item):
        return item if isinstance(item, jax.ShapeDtypeStruct) else jax.ShapeDtypeStruct(item, jnp.float32)

    kept = [as_shape(item) for item in kept]
    shipped = [as_shape(item) for item in shipped]

    def run(*refs):
        ins = list(refs[:n_in])
        kept_refs = refs[n_in : n_in + n_kept]
        homes = refs[n_in + n_kept : n_in + n_kept + n_out]
        rest = refs[n_in + n_kept + n_out :]
        outs = [
            Shipped(block, home, sems)
            for block, home, sems in zip(rest[:n_out], homes, rest[n_out : 2 * n_out])
        ]
        rest = rest[2 * n_out :]
        if brought:
            blocks, arrive_sems = rest[: len(brought)], rest[len(brought)]
            rest = rest[len(brought) + 1 :]
            copies = []
            for place, (index, block) in enumerate(zip(brought, blocks)):
                source = ins[index]
                if inputs[index].at:
                    source = source.at[inputs[index].at]
                copies.append(pltpu.make_async_copy(source, block, arrive_sems.at[place]))
                ins[index] = block
            for copy in copies:
                copy.start()
            arrive = [copy.wait for copy in copies]
        else:
            arrive = []
        kernel(arrive, *ins, *kept_refs, *outs, *rest)
        for out in outs:
            if not out.started:
                out.start()
        for out in outs:
            out.finish(out.block.shape[0])

    spaces = [pltpu.VMEM] * n_kept + [pltpu.HBM] * n_out
    blocks = [pltpu.VMEM(item.shape, item.dtype) for item in shipped]
    sems = [
        pltpu.SemaphoreType.DMA((item.shape[0] if len(item.shape) > 3 else 1,)) for item in shipped
    ]
    arriving = [inputs[index].block() for index in brought]
    if brought:
        arriving.append(pltpu.SemaphoreType.DMA((len(brought),)))
    more = [
        item if not isinstance(item, tuple) else pltpu.VMEM(item, jnp.float32) for item in scratch
    ]
    return pl.pallas_call(
        run,
        name=name,
        in_specs=[pl.BlockSpec(memory_space=item.space) for item in inputs],
        out_specs=[pl.BlockSpec(memory_space=space) for space in spaces],
        out_shape=kept + [pltpu.HBM(item.shape, item.dtype) for item in shipped],
        scratch_shapes=blocks + sems + arriving + more,
        compiler_params=pltpu.CompilerParams(vmem_limit_bytes=VMEM_BYTES),
    )(*[item.array for item in inputs])


def arrive_all(arrive):
    for wait in arrive:
        wait()


def swap(first, second):
    count = lax.axis_size("horiz")
    inner = [(i, i ^ 1) for i in range(count)]
    outer = [(i, i + 1) for i in range(1, count - 1, 2)]
    outer = outer + [(target, source) for source, target in outer]
    return lax.ppermute(first, "horiz", inner), lax.ppermute(second, "horiz", outer)


def exchange(array, devices):
    rows = array.shape[0] // devices
    split = array.reshape(devices, rows // CHANNELS, CHANNELS, WIDTH)
    moved = lax.all_to_all(split, "horiz", split_axis=0, concat_axis=0, tiled=True)
    return moved.reshape(array.shape)


def body(
    perturbation,
    base_state,
    target_state,
    cost_weight,
    diffusivity,
    chan_mix,
    coupler_mix,
    owner_mix,
    air_temp,
    wind_speed,
    wet_list,
    wet_owner,
    remap_src,
    remap_tgt,
    remap_weight,
):
    devices = lax.axis_size("horiz")
    hours = air_temp.shape[0]
    sz = Sizes(devices, air_temp.shape[2] // devices, base_state.shape[1], base_state.shape[3])
    rows = sz.rows
    native_row = (LEVELS, CHANNELS, sz.cells)

    edge_inputs = []
    for array in (perturbation, base_state):
        for row in (0, rows - 1):
            edge_inputs += fetched(array, at=(slice(None), row))
    edges = swap(
        *call(functools.partial(edges_kernel, sz), "edges", edge_inputs, kept=[sz.edge, sz.edge])
    )
    me = lax.axis_index("horiz").astype(jnp.int32)

    def lined(first_row, second_row):
        size = -(-first_row.shape[0] // WIDTH) * WIDTH
        pair = jnp.stack([first_row.astype(jnp.float32), second_row.astype(jnp.float32)])
        return jnp.pad(pair, ((0, 0), (0, size - pair.shape[1])), constant_values=-1.0)

    places = jnp.arange(CHANNELS * CHANNELS, dtype=jnp.int32) + sz.bulk_at
    remap_at = (remap_tgt - (me * LAT_DEV - 1)) * rows + remap_src - me * rows
    remap_lines = lined(
        jnp.concatenate([remap_at, places]),
        jnp.concatenate([remap_weight, coupler_mix.reshape(-1)]),
    )
    mix_rows = chan_mix.transpose(1, 2, 0).reshape(CHANNELS * CHANNELS, LEVELS)
    row_lines = (rows, 1, sz.cells)
    tiles_lines = (CHANNELS * sz.tiles, WIDTH)
    first_mix, first_rows, table, facts, mix, *lines = call(
        functools.partial(setup_kernel, sz, wet_list.shape[1], remap_at.shape[0] + places.shape[0]),
        "setup",
        near_by(lined(wet_list[0], wet_owner[0]), remap_lines, mix_rows)
        + fetched(diffusivity, cost_weight),
        kept=[(CHANNELS * CHANNELS, LEVELS, WIDTH), row_lines],
        shipped=[
            jax.ShapeDtypeStruct((sz.slot_lines, WIDTH), jnp.int32),
            (sz.facts, WIDTH),
            (CHANNELS * CHANNELS, LEVELS, WIDTH),
            row_lines,
            row_lines,
            tiles_lines,
            tiles_lines,
        ],
    )
    diffusivity_rows, weight_rows, diffusivity_tiles, weight_tiles = lines
    wider = (rows + 2, CHANNELS, LEVELS, sz.cells)
    row_surface = (sz.row_width, WIDTH)
    by_row = (rows, *native_row)

    def row_sems(kinds):
        return pltpu.SemaphoreType.DMA((kinds, rows))

    field, start_field = call(
        functools.partial(load_kernel, sz),
        "load",
        far_off(perturbation, base_state),
        kept=[sz.whole],
        shipped=[sz.whole],
        scratch=[by_row, by_row, row_sems(2)],
    )

    saved = []
    near = [sz.near, sz.near]
    mix_shape = (CHANNELS * CHANNELS, LEVELS, WIDTH)
    by_slot = (sz.slots, WIDTH)
    for hour in range(hours):
        first, last = hour == 0, hour == hours - 1
        inputs = scalars(table, facts)
        if first:
            inputs += near_by(*edges, first_rows, first_mix, field)
            assert not last
        else:
            loads = fetched(mix, diffusivity_rows, *([weight_rows] if last else []))
            loads += far_off(field) + near_by(surface) + (far_off(target_state) if last else [])
            mix_here, rows_here, field, *more = call(
                functools.partial(forward_load_kernel, sz, last),
                "step_load",
                loads,
                kept=[mix_shape, row_lines, sz.whole] + ([row_lines, sz.whole] if last else []),
                scratch=[row_sems(2)] + ([by_row] if last else []),
            )
            inputs += near_by(*edges, rows_here, mix_here, field, *surface_edges, *more)
        field, drive, surface, packed, *sends = call(
            functools.partial(forward_kernel, sz, first, last),
            "step",
            inputs,
            shipped=[
                sz.whole, sz.whole, sz.surface, sz.narrow, sz.edge_and_lats, sz.edge_and_lats
            ],
            scratch=[wider],
        )
        if first:
            packed, tell = lax.optimization_barrier((packed, facts))
        arrived = exchange(packed, devices)
        inputs = (
            near_by(arrived, owner_mix[0], air_temp[hour, 0], wind_speed[hour, 0])
            + scalars(facts)
        )
        decoded = []
        if first:
            told = swap(tell, tell)
            inputs += near_by(*told) + fetched(table, facts)
            decoded = [jax.ShapeDtypeStruct(sz.tables, jnp.int32), sz.weights]
        *decoded, flux, mixed_slope, flux_slope = call(
            functools.partial(owner_kernel, sz, first),
            "owners",
            inputs,
            shipped=[*decoded, sz.wide, sz.by_slot, sz.by_slot],
            scratch=[sz.narrow, by_slot],
        )
        if first:
            tables, weights = decoded
        flux, *sends = lax.optimization_barrier((flux, *sends))
        flux = exchange(flux, devices)
        edges = swap(*sends)
        inputs = near_by(flux, *edges) + fetched(surface) + scalars(tables, weights)
        if last:
            surface, slope, packed, *sends = call(
                functools.partial(surface_kernel, sz, True),
                "surface",
                inputs + fetched(target_state, at=(0,)) + fetched(weight_tiles),
                shipped=[sz.surface, sz.slope, sz.wide, sz.lats, sz.lats],
                scratch=near,
            )
        else:
            surface, *sends, slope = call(
                functools.partial(surface_kernel, sz, False),
                "surface",
                inputs,
                kept=[sz.surface, row_surface, row_surface],
                shipped=[sz.slope],
                scratch=near,
            )
            surface_edges = swap(*sends)
        saved.append((drive, slope, mixed_slope, flux_slope))

    for hour in reversed(range(hours)):
        drive, slope, mixed_slope, flux_slope = saved[hour]
        arrived = exchange(packed, devices)
        back = call(
            functools.partial(owner_back_kernel, sz),
            "owners_back",
            near_by(arrived, owner_mix[0]) + fetched(mixed_slope, flux_slope) + scalars(facts),
            shipped=[sz.narrow],
            scratch=[sz.narrow, by_slot],
        )[0]
        back, *sends = lax.optimization_barrier((back, *sends))
        got = swap(*sends)
        back = exchange(back, devices)
        if hour < hours - 1:
            edges = got
        surface, *row_sends = call(
            functools.partial(merge_kernel, sz, sz.edge_lines if hour < hours - 1 else 0),
            "merge",
            near_by(back, *got)
            + fetched(surface, slope)
            + scalars(table, facts)
            + fetched(diffusivity_tiles),
            kept=[sz.surface, row_surface, row_surface],
        )
        surface_edges = swap(*row_sends)
        last = hour == 0
        mix_here, rows_here, *loaded = call(
            functools.partial(backward_load_kernel, sz, last),
            "step_back_load",
            fetched(mix, diffusivity_rows)
            + far_off(field, drive)
            + near_by(surface)
            + (far_off(start_field) if last else []),
            kept=[mix_shape, row_lines] + [sz.whole] * (4 if last else 3),
            scratch=[row_sems(3)],
        )
        inputs = near_by(*edges, *surface_edges, rows_here, mix_here, *loaded)
        if last:
            gradient, sums = call(
                functools.partial(backward_kernel, sz, True),
                "step_back_sums",
                inputs,
                shipped=[sz.whole, (devices, WIDTH)],
                scratch=[wider],
            )
        else:
            field, surface, packed, *sends = call(
                functools.partial(backward_kernel, sz, False),
                "step_back",
                scalars(tables, weights) + fetched(saved[hour - 1][1]) + inputs,
                shipped=[sz.whole, sz.surface, sz.wide, sz.edge_and_lats, sz.edge_and_lats],
                scratch=[wider, *near],
            )

    everyones = lax.all_to_all(sums, "horiz", split_axis=0, concat_axis=0, tiled=True)
    block = perturbation.shape
    return call(
        functools.partial(final_kernel, perturbation.size * devices),
        "finish",
        near_by(everyones, perturbation, gradient.transpose(2, 0, 1, 3)),
        shipped=[block],
    )[0]


def solution(mesh):
    placed = (
        P("member", "horiz", None, None),
        P(None, "horiz", None, None),
        P(None, "horiz", None, None),
        P("horiz", None),
        P("horiz", None),
        P(),
        P(),
        P("horiz", None, None),
        P(None, "horiz", None, None),
        P(None, "horiz", None, None),
        P("horiz", None),
        P("horiz", None),
        P("horiz"),
        P("horiz"),
        P("horiz"),
    )
    return jax.shard_map(
        body,
        mesh=mesh,
        in_specs=placed,
        out_specs=P("member", "horiz", None, None),
        check_vma=False,
    )
```

```python
import functools

import jax
import jax.numpy as jnp
from jax import lax
from jax.experimental import pallas as pl
from jax.experimental.pallas import tpu as pltpu
from jax.sharding import PartitionSpec as P

LAT_DEV = 2
NEAR_LAT = LAT_DEV + 2
CHANNELS = 4
LEVELS = 8
WIDTH = 128
SUBLANES = 8

KAPPA_V = 0.1
TIME_STEP = 0.3
FLUX_RATE = 0.05
FEEDBACK = 0.5
ASCENT = 0.5
EPSILON = 1e-06
HIGHEST = lax.Precision.HIGHEST
VMEM_BYTES = 32 * 1024 * 1024


class Sizes:
    def __init__(self, devices, capacity, rows, cells):
        self.devices = devices
        self.capacity = capacity
        self.slots = devices * capacity
        self.rows = rows
        self.cells = cells
        self.row_tiles = cells // WIDTH
        self.tiles = rows * self.row_tiles
        self.row_width = CHANNELS * self.row_tiles
        self.pitch = -(-self.row_tiles // SUBLANES) * SUBLANES
        self.own_rows = CHANNELS * capacity
        self.chunk = -(-(self.own_rows + 2 * capacity) // SUBLANES) * SUBLANES
        self.slot_lines = -(-self.slots // WIDTH)
        self.facts = -(-(self.slot_lines + 1) // SUBLANES) * SUBLANES
        self.lat_lines = LAT_DEV * self.pitch
        self.edge_lines = CHANNELS * self.row_tiles * LEVELS
        self.whole = (rows, CHANNELS, LEVELS, cells)
        self.edge = (self.edge_lines, WIDTH)
        self.told = (self.lat_lines + self.facts, WIDTH)
        self.surface = (CHANNELS * (self.tiles + 1), WIDTH)
        self.narrow = (CHANNELS * self.slots, WIDTH)
        self.wide = (devices * self.chunk, WIDTH)
        self.slope = (NEAR_LAT * self.pitch, WIDTH)
        self.lats = (self.lat_lines, WIDTH)
        self.bulk_at = NEAR_LAT * rows
        self.tables = (3 * self.slot_lines, WIDTH)
        self.weights = (3 * self.facts, WIDTH)
        self.near = (-(-(self.tiles + 1) // SUBLANES) * SUBLANES, WIDTH)
        self.by_slot = (CHANNELS, self.slots, WIDTH)


class Shipped:
    def __init__(self, block, home, sems):
        self.block, self.home, self.sems = block, home, sems
        self.by_row = False
        self.started = False

    def __getitem__(self, at):
        return self.block[at]

    def __setitem__(self, at, value):
        self.block[at] = value

    def row(self, index):
        self.by_row = True
        self.started = True
        return pltpu.make_async_copy(
            self.block.at[index], self.home.at[index], self.sems.at[index]
        )

    def all(self):
        return pltpu.make_async_copy(self.block, self.home, self.sems.at[0])

    def start(self):
        self.started = True
        self.all().start()

    def finish(self, rows):
        if self.by_row:
            for index in range(rows):
                self.row(index).wait()
        else:
            self.all().wait()


def cols(tile):
    return slice(tile * WIDTH, (tile + 1) * WIDTH)


def lanes_sum(left_here, left_before, right_here, right_after, lane):
    return jnp.where(lane == 0, left_before, left_here) + jnp.where(
        lane == WIDTH - 1, right_after, right_here
    )


def levels_sum(field, sub):
    return jnp.where(sub == 0, 0.0, pltpu.roll(field, 1, 0)) + jnp.where(
        sub == LEVELS - 1, 0.0, pltpu.roll(field, LEVELS - 1, 0)
    )


def row_tiles_of(sz, ref, row):
    return ref[pl.ds(row * sz.row_width, sz.row_tiles, stride=CHANNELS), :]


def put_row_tiles(sz, ref, row, value):
    ref[pl.ds(row * sz.row_width, sz.row_tiles, stride=CHANNELS), :] = value


def near_row(sz, ref, row):
    return ref[row * sz.row_tiles : (row + 1) * sz.row_tiles, :]


def high_first():
    return 1 - lax.rem(lax.axis_index("horiz").astype(jnp.int32), 2)


def pick(flag, one, other):
    return jnp.where(jnp.full(one.shape, flag, jnp.int32) == 1, one, other)


def sided(first, second):
    flag = high_first()
    return pick(flag, second, first), pick(flag, first, second)


def load_surface_row(sz, target, row, source, base):
    for tile in range(sz.row_tiles):
        for channel in range(CHANNELS):
            at = base + tile * CHANNELS + channel
            target[row, channel, 0:1, cols(tile)] = source[pl.ds(at, 1), :]


def as_column(row, size):
    shape = (size, row.shape[1])
    diagonal = lax.broadcasted_iota(jnp.int32, shape, 0) == lax.broadcasted_iota(jnp.int32, shape, 1)
    return jnp.sum(jnp.where(diagonal, row, 0.0), axis=1, keepdims=True)


def setup_kernel(sz, entries, remap_entries, arrive, wet, remap, mix_rows, diffusivity, *outs):
    first_mix, first_rows, table, facts, mix = outs
    arrive_all(arrive)
    for row in range(sz.rows):
        first_rows[row] = diffusivity[row : row + 1, :]
    for index in range(CHANNELS * CHANNELS):
        column = as_column(mix_rows[index : index + 1, :], LEVELS)
        mix[index] = jnp.broadcast_to(column, (LEVELS, WIDTH))
    mix.start()
    first_mix[...] = mix[...]
    tiles, owners = wet[0:1, :], wet[1:2, :]
    size = -(-entries // SUBLANES) * SUBLANES
    shape = (size, wet.shape[1])
    tile_here, owner_here = as_column(tiles, size), as_column(owners, size)
    earlier = lax.broadcasted_iota(jnp.int32, shape, 1) < lax.broadcasted_iota(jnp.int32, shape, 0)
    same = (owner_here == owners) & earlier
    rank = jnp.sum(jnp.where(same, 1.0, 0.0), axis=1, keepdims=True)
    slot = jnp.where(owner_here >= 0.0, owner_here * sz.capacity + rank, -1.0)
    facts[...] = jnp.zeros((sz.facts, WIDTH), jnp.float32)
    for line in range(sz.slot_lines):
        place = lax.broadcasted_iota(jnp.int32, (size, WIDTH), 1) + line * WIDTH
        match = slot.astype(jnp.int32) == place
        told = jnp.sum(jnp.where(match, sz.tiles - tile_here, 0.0), axis=0, keepdims=True)
        facts[line : line + 1, :] = told
        table[line : line + 1, :] = sz.tiles - told.astype(jnp.int32)
    size = -(-remap_entries // SUBLANES) * SUBLANES
    at, amount = as_column(remap[0:1, :], size), as_column(remap[1:2, :], size)
    place = lax.broadcasted_iota(jnp.int32, (size, WIDTH), 1)
    facts[sz.slot_lines : sz.slot_lines + 1, :] = jnp.sum(
        jnp.where(at.astype(jnp.int32) == place, amount, 0.0), axis=0, keepdims=True
    )


def columns_kernel(sz, arrive, diffusivity, weight, *outs):
    diffusivity_rows, weight_rows, diffusivity_tiles, weight_tiles = outs
    arrive_all(arrive)
    for source, by_row, by_tile in (
        (diffusivity, diffusivity_rows, diffusivity_tiles),
        (weight, weight_rows, weight_tiles),
    ):
        for row in range(sz.rows):
            by_row[row] = source[row : row + 1, :]
            for tile in range(sz.row_tiles):
                line = source[row : row + 1, cols(tile)]
                at = (row * sz.row_tiles + tile) * CHANNELS
                by_tile[at : at + CHANNELS, :] = jnp.broadcast_to(line, (CHANNELS, WIDTH))


def gather_levels(block, channel, tile):
    sub = lax.broadcasted_iota(jnp.int32, (LEVELS, WIDTH), 0)
    total = None
    for level in range(LEVELS):
        line = block[level, channel : channel + 1, cols(tile)]
        line = jnp.broadcast_to(line, (LEVELS, WIDTH))
        total = line if total is None else jnp.where(sub == level, line, total)
    return total


def edges_kernel(sz, arrive, low_start, high_start, low_base, high_base, send_first, send_second):
    arrive_all(arrive)
    low_start[...] = low_start[...] + low_base[...]
    high_start[...] = high_start[...] + high_base[...]
    flag = high_first()
    for channel in range(CHANNELS):
        for tile in range(sz.row_tiles):
            low = gather_levels(low_start, channel, tile)
            high = gather_levels(high_start, channel, tile)
            at = (channel * sz.row_tiles + tile) * LEVELS
            send_first[at : at + LEVELS, :] = pick(flag, high, low)
            send_second[at : at + LEVELS, :] = pick(flag, low, high)


def load_kernel(sz, arrive, perturbation, base, field, start_block, base_block, in_sems):
    def arrivals(row):
        return [
            pltpu.make_async_copy(source.at[:, row], block.at[row], in_sems.at[index, row])
            for index, (source, block) in enumerate(
                ((perturbation, start_block), (base, base_block))
            )
        ]

    for row in range(sz.rows):
        for arrival in arrivals(row):
            arrival.start()

    def one_row(row, carry):
        for arrival in arrivals(row):
            arrival.wait()
        start_block[row] = start_block[row] + base_block[row]
        for channel in range(CHANNELS):
            for tile in range(sz.row_tiles):
                field[row, channel, :, cols(tile)] = gather_levels(
                    start_block.at[row], channel, tile
                )
        return carry

    lax.fori_loop(0, sz.rows, one_row, 0)


def relayout_kernel(sz, arrive, source, out, block, in_sems):
    def arrival(row):
        return pltpu.make_async_copy(source.at[:, row], block.at[row], in_sems.at[0, row])

    for row in range(sz.rows):
        arrival(row).start()

    def one_row(row, carry):
        arrival(row).wait()
        for channel in range(CHANNELS):
            for tile in range(sz.row_tiles):
                out[row, channel, :, cols(tile)] = gather_levels(block.at[row], channel, tile)
        out.row(row).start()
        return carry

    lax.fori_loop(0, sz.rows, one_row, 0)


class Remap:
    def __init__(self, sz, weights):
        self.sz, self.weights = sz, weights

    def weight(self, which, lat, row):
        line = which * self.sz.facts + self.sz.slot_lines
        return self.weights[line, lat * self.sz.rows + row]

    def own(self, lat, row):
        return self.weight(0, lat, row)

    def of_low(self, lat, row):
        return self.weight(1, lat + LAT_DEV, row)

    def of_high(self, lat, row):
        return self.weight(2, lat - LAT_DEV, row)


def tile_at(sz, tables, which, slot):
    return tables[which * sz.slot_lines + slot // WIDTH, slot % WIDTH]


def sum_of(weights, values):
    total = weights[0] * values[0]
    for weight, value in zip(weights[1:], values[1:]):
        total = total + weight * value
    return total


def own_sums(sz, remap, own, factor):
    return [
        factor * sum_of([remap.own(lat, row) for row in range(sz.rows)], own)
        for lat in range(NEAR_LAT)
    ]


def send_sums(sz, sums, tell_first, tell_second):
    flag = high_first()
    for index in range(LAT_DEV):
        low, high = sums[index], sums[LAT_DEV + index]
        at = index * sz.pitch
        tell_first[at : at + sz.row_tiles, :] = pick(flag, high, low)
        tell_second[at : at + sz.row_tiles, :] = pick(flag, low, high)


def lat_rows(sz, ref, lat):
    at = lat * sz.pitch
    return ref[at : at + sz.row_tiles, :]


def told_sums(sz, from_first, from_second):
    lows, highs = [], []
    for index in range(LAT_DEV):
        low, high = sided(lat_rows(sz, from_first, index), lat_rows(sz, from_second, index))
        lows.append(low)
        highs.append(high)
    return lows + highs


def place_edges(sz, padded, first, second, first_surface=None, second_surface=None):
    side = high_first() * (sz.rows + 1)
    for at, edge, surface in ((side, first, first_surface), (sz.rows + 1 - side, second, second_surface)):
        for channel in range(CHANNELS):
            for tile in range(sz.row_tiles):
                line = (channel * sz.row_tiles + tile) * LEVELS
                padded[at, channel, :, cols(tile)] = edge[line : line + LEVELS, :]
        if surface is not None:
            load_surface_row(sz, padded, at, surface, 0)


def store_rows(sz, surface, send_first, send_second, factor=None):
    row = high_first() * (sz.rows - 1)
    for at, send in ((row, send_first), (sz.rows - 1 - row, send_second)):
        for tile in range(sz.row_tiles):
            start = pl.multiple_of((at * sz.row_tiles + tile) * CHANNELS, CHANNELS)
            value = surface[pl.ds(start, CHANNELS), :]
            if factor is not None:
                value = factor[pl.ds(start, CHANNELS), :] * value
            send[tile * CHANNELS : (tile + 1) * CHANNELS, :] = value


def forward_load_kernel(sz, last, arrive, mix, diffusivity, *refs):
    refs = list(refs)
    if last:
        weight = refs.pop(0)
    field, surface = refs[:2]
    refs = refs[2:]
    if last:
        target = refs.pop(0)
    mix_out, rows_out, field_out = refs[:3]
    refs = refs[3:]
    if last:
        weight_out, target_out = refs[:2]
        refs = refs[2:]
    in_sems = refs[0]

    def arrivals(row):
        copies = [pltpu.make_async_copy(field.at[row], field_out.at[row], in_sems.at[0, row])]
        if last:
            copies.append(
                pltpu.make_async_copy(target.at[:, row], refs[1].at[row], in_sems.at[1, row])
            )
        return copies

    for row in range(sz.rows):
        for arrival in arrivals(row):
            arrival.start()
    arrive_all(arrive)
    mix_out[...] = mix[...]
    rows_out[...] = diffusivity[...]
    if last:
        weight_out[...] = weight[...]

    def one_row(row, carry):
        for arrival in arrivals(row):
            arrival.wait()
        load_surface_row(sz, field_out, row, surface, row * sz.row_width)
        if last:
            for c in range(CHANNELS):
                for t in range(sz.row_tiles):
                    target_out[row, c, :, cols(t)] = gather_levels(refs[1].at[row], c, t)
        return carry

    lax.fori_loop(0, sz.rows, one_row, 0)


def forward_kernel(sz, first, last, arrive, *refs):
    refs = list(refs)
    tables, facts, low, high, diffusivity, mix, field = refs[:7]
    refs = refs[7:]
    if first:
        facts_block = refs.pop(0)
    surfaces = ()
    if not first:
        surfaces = refs[:2]
        refs = refs[2:]
    if last:
        weight, target = refs[:2]
        refs = refs[2:]
    out, drive, new_surface, packed, tell_first, tell_second, edge_first, edge_second, padded = refs
    remap = Remap(sz, facts)
    place_edges(sz, padded, low, high, *surfaces)

    def ready(row):
        padded[row + 1] = field[row]

    ready(0)
    lane = lax.broadcasted_iota(jnp.int32, (LEVELS, WIDTH), 1)
    sub = lax.broadcasted_iota(jnp.int32, (LEVELS, WIDTH), 0)
    count = sz.row_tiles

    def one_row(row, carry):
        @pl.when(row < sz.rows - 1)
        def _():
            ready(row + 1)

        here = [[padded[row + 1, c, :, cols(t)] for t in range(count)] for c in range(CHANNELS)]
        for t in range(count):
            coeff = jnp.broadcast_to(diffusivity[row, 0:1, cols(t)], (LEVELS, WIDTH))
            center = (1.0 - 2.0 * KAPPA_V) - 4.0 * coeff
            if last:
                scale = weight[row, 0:1, cols(t)]
                scale = jnp.broadcast_to(scale * scale, (LEVELS, WIDTH))
            for c in range(CHANNELS):
                mixed = mix[c * CHANNELS] * here[0][t]
                for k in range(1, CHANNELS):
                    mixed = mixed + mix[c * CHANNELS + k] * here[k][t]
                bent = jnp.tanh(mixed)
                drive[row, c, :, cols(t)] = bent
                field_here = here[c][t]
                around = lanes_sum(
                    pltpu.roll(field_here, 1, 1),
                    pltpu.roll(here[c][(t - 1) % count], 1, 1),
                    pltpu.roll(field_here, WIDTH - 1, 1),
                    pltpu.roll(here[c][(t + 1) % count], WIDTH - 1, 1),
                    lane,
                )
                around = around + (padded[row, c, :, cols(t)] + padded[row + 2, c, :, cols(t)])
                stepped = (
                    center * field_here
                    + coeff * around
                    + KAPPA_V * levels_sum(field_here, sub)
                    + TIME_STEP * bent
                )
                new_surface[pl.ds((row * count + t) * CHANNELS + c, 1), :] = stepped[0:1, :]
                if last:
                    stepped = scale * (stepped - target[row, c, :, cols(t)])
                out[row, c, :, cols(t)] = stepped
        drive.row(row).start()
        out.row(row).start()
        return carry

    lax.fori_loop(0, sz.rows, one_row, 0)
    new_surface[CHANNELS * sz.tiles :, :] = jnp.zeros((CHANNELS, WIDTH), jnp.float32)
    new_surface.start()
    arrive_all(arrive)
    pack_slots(sz, tables, new_surface, packed)
    packed.start()
    own = [row_tiles_of(sz, new_surface.block, row) for row in range(sz.rows)]
    send_sums(sz, own_sums(sz, remap, own, 1.0), tell_first, tell_second)
    for tell in (tell_first, tell_second):
        if first:
            tell[sz.lat_lines :, :] = facts_block[...]
        tell.start()
    store_edges(sz, out, diffusivity if last else None, edge_first, edge_second)


def pack_slots(sz, tables, surface, packed):
    for slot in range(sz.slots):
        at = pl.multiple_of(tile_at(sz, tables, 0, slot) * CHANNELS, CHANNELS)
        packed[slot * CHANNELS : (slot + 1) * CHANNELS, :] = surface[pl.ds(at, CHANNELS), :]


def store_edges(sz, field, diffusivity, send_first, send_second):
    outer = high_first() * (sz.rows - 1)
    for row, send in ((outer, send_first), (sz.rows - 1 - outer, send_second)):
        for channel in range(CHANNELS):
            for tile in range(sz.row_tiles):
                value = field[row, channel, :, cols(tile)]
                if diffusivity is not None:
                    value = value * jnp.broadcast_to(
                        diffusivity[row, 0:1, cols(tile)], (LEVELS, WIDTH)
                    )
                at = (channel * sz.row_tiles + tile) * LEVELS
                send[at : at + LEVELS, :] = value
        send.start()


def owner_kernel(sz, decode, arrive, arrived, mixing, air, wind, facts, *refs):
    slots = sz.slots
    if decode:
        told_first, told_second, own_table, own_facts, tables, weights = refs[:6]
        refs = refs[6:]
    flux, mixed_slope, flux_slope, flat, first = refs
    arrive_all(arrive)
    if decode:
        lines = sz.slot_lines
        tables[0:lines, :] = own_table[...]
        weights[0 : sz.facts, :] = own_facts[...]
        both = sided(told_first[sz.lat_lines :, :], told_second[sz.lat_lines :, :])
        for which, told in ((1, both[0]), (2, both[1])):
            got = told[0:lines, :].astype(jnp.int32)
            tables[which * lines : (which + 1) * lines, :] = sz.tiles - got
            at = which * sz.facts
            weights[at : at + sz.facts, :] = told
        tables.start()
        weights.start()

    def bulk(row, column):
        return facts[sz.slot_lines, sz.bulk_at + row * CHANNELS + column]

    values = [arrived[pl.ds(c, slots, stride=CHANNELS), :] for c in range(CHANNELS)]
    mixed = jnp.tanh(
        jnp.dot(
            mixing[...],
            jnp.concatenate(values, axis=1),
            precision=HIGHEST,
            preferred_element_type=jnp.float32,
        )
    )
    contrast = []
    for c in range(CHANNELS):
        mixed_here = mixed[:, cols(c)]
        mixed_slope[c] = 1.0 - mixed_here * mixed_here
        contrast.append((air[...] - values[0] if c == 0 else values[c]) + mixed_here)
    mixed_slope.start()
    rate = FLUX_RATE * wind[...]
    for c in range(CHANNELS):
        forcing = bulk(c, 0) * contrast[0]
        for k in range(1, CHANNELS):
            forcing = forcing + bulk(c, k) * contrast[k]
        bent = jnp.tanh(forcing)
        flux_slope[c] = rate * (1.0 - bent * bent)
        one = rate * bent
        flat[pl.ds(c, slots, stride=CHANNELS), :] = one
        if c == 0:
            first[...] = one
    flux_slope.start()
    cap = sz.capacity
    gap = jnp.zeros((sz.chunk - sz.own_rows, WIDTH), jnp.float32)
    for d in range(sz.devices):
        at = d * sz.chunk
        flux[at : at + sz.own_rows, :] = flat[d * sz.own_rows : (d + 1) * sz.own_rows, :]
        at = at + sz.own_rows
        flux[at : (d + 1) * sz.chunk, :] = gap
        if d > 0:
            flux[at : at + cap, :] = first[(d - 1) * cap : d * cap, :]
        if d < sz.devices - 1:
            flux[at + cap : at + 2 * cap, :] = first[(d + 1) * cap : (d + 2) * cap, :]


def owner_back_kernel(sz, arrive, arrived, mixing, mixed_slope, flux_slope, facts, back, flat, extra):
    slots, cap = sz.slots, sz.capacity

    def bulk(row, column):
        return facts[sz.slot_lines, sz.bulk_at + row * CHANNELS + column]

    for d in range(sz.devices):
        at = d * sz.chunk
        flat[d * sz.own_rows : (d + 1) * sz.own_rows, :] = arrived[at : at + sz.own_rows, :]
        more = jnp.zeros((cap, WIDTH), jnp.float32)
        if d < sz.devices - 1:
            at = (d + 1) * sz.chunk + sz.own_rows
            more = more + arrived[at : at + cap, :]
        if d > 0:
            at = (d - 1) * sz.chunk + sz.own_rows + cap
            more = more + arrived[at : at + cap, :]
        extra[d * cap : (d + 1) * cap, :] = more
    arrive_all(arrive)
    forced = []
    for c in range(CHANNELS):
        got = flat[pl.ds(c, slots, stride=CHANNELS), :]
        if c == 0:
            got = got + extra[...]
        forced.append(flux_slope[c] * got)
    direct = []
    for k in range(CHANNELS):
        total = bulk(0, k) * forced[0]
        for c in range(1, CHANNELS):
            total = total + bulk(c, k) * forced[c]
        direct.append(total)
    through = lax.dot_general(
        mixing[...],
        jnp.concatenate([direct[k] * mixed_slope[k] for k in range(CHANNELS)], axis=1),
        (((0,), (0,)), ((), ())),
        precision=HIGHEST,
        preferred_element_type=jnp.float32,
    )
    for k in range(CHANNELS):
        sign = -1.0 if k == 0 else 1.0
        back.block[pl.ds(k, slots, stride=CHANNELS), :] = through[:, cols(k)] + sign * direct[k]


def spread_back(sz, surface, slope, remap, tables, packed, near_low, near_high, tell_first, tell_second):
    rows, count, cap = sz.rows, sz.row_tiles, sz.capacity
    block = surface.block
    own = [row_tiles_of(sz, block, row) for row in range(rows)]
    sums = own_sums(sz, remap, own, FEEDBACK)
    send_sums(sz, sums, tell_first, tell_second)
    tell_first.start()
    tell_second.start()
    lats = [lat_rows(sz, slope, lat) * sums[lat] for lat in range(NEAR_LAT)]
    every = range(NEAR_LAT)
    for row in range(rows):
        added = sum_of([remap.own(lat, row) for lat in every], lats)
        put_row_tiles(sz, block, row, own[row] + added)
        at = row * count
        near_low[at : at + count, :] = sum_of(
            [remap.of_low(lat, row) for lat in range(LAT_DEV)], lats[:LAT_DEV]
        )
        near_high[at : at + count, :] = sum_of(
            [remap.of_high(lat, row) for lat in range(LAT_DEV, NEAR_LAT)], lats[LAT_DEV:]
        )
    rest = sz.near[0] - sz.tiles
    near_low[sz.tiles :, :] = jnp.zeros((rest, WIDTH), jnp.float32)
    near_high[sz.tiles :, :] = jnp.zeros((rest, WIDTH), jnp.float32)
    surface.start()
    gap = jnp.zeros((sz.chunk - sz.own_rows, WIDTH), jnp.float32)
    for owner in range(sz.devices):
        packed[owner * sz.chunk + sz.own_rows : (owner + 1) * sz.chunk, :] = gap
    for slot in range(sz.slots):
        owner, rank = slot // cap, slot % cap
        at = owner * sz.chunk + rank * CHANNELS
        tile = pl.multiple_of(tile_at(sz, tables, 0, slot) * CHANNELS, CHANNELS)
        packed[at : at + CHANNELS, :] = surface[pl.ds(tile, CHANNELS), :]
        at = owner * sz.chunk + sz.own_rows + rank
        packed[at : at + 1, :] = near_low[pl.ds(tile_at(sz, tables, 1, slot), 1), :]
        at = at + cap
        packed[at : at + 1, :] = near_high[pl.ds(tile_at(sz, tables, 2, slot), 1), :]


def surface_kernel(sz, last, arrive, *refs):
    refs = list(refs)
    flux, from_first, from_second, before, tables, weights = refs[:6]
    refs = refs[6:]
    if last:
        target, weight = refs[:2]
        surface, slope, packed, tell_first, tell_second, near_low, near_high = refs[2:]
        block = surface.block
    else:
        surface, send_first, send_second, slope, near_low, near_high = refs
        block = surface
    remap = Remap(sz, weights)
    arrive_all(arrive)
    rows, cap = sz.rows, sz.capacity
    block[...] = before[...]
    near_low[...] = jnp.zeros(sz.near, jnp.float32)
    near_high[...] = jnp.zeros(sz.near, jnp.float32)
    for slot in range(sz.slots):
        owner, rank = slot // cap, slot % cap
        at = owner * sz.chunk + rank * CHANNELS
        tile = pl.multiple_of(tile_at(sz, tables, 0, slot) * CHANNELS, CHANNELS)
        block[pl.ds(tile, CHANNELS), :] = (
            before[pl.ds(tile, CHANNELS), :] + flux[at : at + CHANNELS, :]
        )
        at = owner * sz.chunk + sz.own_rows + rank
        near_low[pl.ds(tile_at(sz, tables, 1, slot), 1), :] = flux[at : at + 1, :]
        at = at + cap
        near_high[pl.ds(tile_at(sz, tables, 2, slot), 1), :] = flux[at : at + 1, :]
    block[CHANNELS * sz.tiles :, :] = jnp.zeros((CHANNELS, WIDTH), jnp.float32)
    own = [row_tiles_of(sz, block, row) for row in range(rows)]
    sums = own_sums(sz, remap, own, 1.0)
    told = told_sums(sz, from_first, from_second)
    air = []
    for lat in range(NEAR_LAT):
        if lat < LAT_DEV:
            near, weights = near_low, [remap.of_low(lat, row) for row in range(rows)]
        else:
            near, weights = near_high, [remap.of_high(lat, row) for row in range(rows)]
        more = sum_of(weights, [near_row(sz, near, row) for row in range(rows)])
        one = jnp.tanh(sums[lat] + told[lat] + more)
        slope[lat * sz.pitch : lat * sz.pitch + sz.row_tiles, :] = 1.0 - one * one
        air.append(one)
    slope.start()
    for row in range(rows):
        weights = [remap.own(lat, row) for lat in range(NEAR_LAT)]
        put_row_tiles(sz, block, row, own[row] + FEEDBACK * sum_of(weights, air))
    if last:
        for row in range(rows):
            for tile in range(sz.row_tiles):
                at = row * sz.row_width + tile * CHANNELS
                scale = weight[at : at + CHANNELS, :]
                off = block[at : at + CHANNELS, :] - target[row, :, cols(tile)]
                block[at : at + CHANNELS, :] = scale * scale * off
        spread_back(
            sz, surface, slope, remap, tables, packed, near_low, near_high, tell_first, tell_second
        )
    else:
        store_rows(sz, surface, send_first, send_second)


def merge_kernel(
    sz, arrive, back, from_first, from_second, before, slope, tables, facts, diffusivity, surface, send_first, send_second
):
    rows = sz.rows
    remap = Remap(sz, facts)
    arrive_all(arrive)
    surface[...] = before[...]
    for slot in range(sz.slots):
        tile = pl.multiple_of(tile_at(sz, tables, 0, slot) * CHANNELS, CHANNELS)
        surface[pl.ds(tile, CHANNELS), :] = (
            before[pl.ds(tile, CHANNELS), :] + back[slot * CHANNELS : (slot + 1) * CHANNELS, :]
        )
    surface[CHANNELS * sz.tiles :, :] = jnp.zeros((CHANNELS, WIDTH), jnp.float32)
    told = told_sums(sz, from_first, from_second)
    lats = [lat_rows(sz, slope, lat) * told[lat] for lat in range(NEAR_LAT)]
    for row in range(rows):
        own = row_tiles_of(sz, surface, row)
        weights = [remap.own(lat, row) for lat in range(NEAR_LAT)]
        put_row_tiles(sz, surface, row, own + sum_of(weights, lats))
    store_rows(sz, surface, send_first, send_second, diffusivity)


def backward_load_kernel(sz, last, arrive, mix, diffusivity, field, drive, surface, *refs):
    refs = list(refs)
    if last:
        perturbation = refs.pop(0)
    mix_out, rows_out, local, bent_all, scaled = refs[:5]
    refs = refs[5:]
    if last:
        start_all = refs.pop(0)
    in_sems = refs[0]

    def arrivals(row):
        copies = [
            pltpu.make_async_copy(field.at[row], local.at[row], in_sems.at[0, row]),
            pltpu.make_async_copy(drive.at[row], bent_all.at[row], in_sems.at[1, row]),
        ]
        if last:
            copies.append(
                pltpu.make_async_copy(perturbation.at[row], start_all.at[row], in_sems.at[2, row])
            )
        return copies

    for row in range(sz.rows):
        for arrival in arrivals(row):
            arrival.start()
    arrive_all(arrive)
    mix_out[...] = mix[...]
    rows_out[...] = diffusivity[...]

    def one_row(row, carry):
        for arrival in arrivals(row):
            arrival.wait()
        load_surface_row(sz, local, row, surface, row * sz.row_width)
        for t in range(sz.row_tiles):
            coeff = jnp.broadcast_to(diffusivity[row, 0:1, cols(t)], (LEVELS, WIDTH))
            for c in range(CHANNELS):
                scaled[row, c, :, cols(t)] = coeff * local[row, c, :, cols(t)]
        return carry

    lax.fori_loop(0, sz.rows, one_row, 0)


def backward_kernel(sz, last, arrive, *refs):
    refs = list(refs)
    if not last:
        tables, weights, slope = refs[:3]
        refs = refs[3:]
    low, high, first_surface, second_surface, diffusivity, mix = refs[:6]
    local, bent_all, scaled_all = refs[6:9]
    refs = refs[9:]
    if last:
        start_all, out, sums, padded = refs
    else:
        out, new_surface, packed, tell_first, tell_second, edge_first, edge_second = refs[:7]
        padded, near_low, near_high = refs[7:]
        remap = Remap(sz, weights)
    count = sz.row_tiles
    place_edges(sz, padded, low, high, first_surface, second_surface)

    def ready(row):
        padded[row + 1] = scaled_all[row]

    ready(0)
    lane = lax.broadcasted_iota(jnp.int32, (LEVELS, WIDTH), 1)
    sub = lax.broadcasted_iota(jnp.int32, (LEVELS, WIDTH), 0)

    def one_row(row, carry):
        @pl.when(row < sz.rows - 1)
        def _():
            ready(row + 1)

        scaled = [[padded[row + 1, c, :, cols(t)] for t in range(count)] for c in range(CHANNELS)]
        for t in range(count):
            here, bent = [], []
            for c in range(CHANNELS):
                value = local[row, c, :, cols(t)]
                one = bent_all[row, c, :, cols(t)]
                here.append(value)
                bent.append((1.0 - one * one) * value)
            for c in range(CHANNELS):
                mixed = mix[c] * bent[0]
                for k in range(1, CHANNELS):
                    mixed = mixed + mix[k * CHANNELS + c] * bent[k]
                around = lanes_sum(
                    pltpu.roll(scaled[c][t], 1, 1),
                    pltpu.roll(scaled[c][(t - 1) % count], 1, 1),
                    pltpu.roll(scaled[c][t], WIDTH - 1, 1),
                    pltpu.roll(scaled[c][(t + 1) % count], WIDTH - 1, 1),
                    lane,
                )
                around = around + (padded[row, c, :, cols(t)] + padded[row + 2, c, :, cols(t)])
                stepped = (
                    ((1.0 - 2.0 * KAPPA_V) * here[c] - 4.0 * scaled[c][t])
                    + around
                    + KAPPA_V * levels_sum(here[c], sub)
                    + TIME_STEP * mixed
                )
                out[row, c, :, cols(t)] = stepped
                if last:
                    start = start_all[row, c, :, cols(t)]
                    carry = (
                        carry[0] + start * start,
                        carry[1] + start * stepped,
                        carry[2] + stepped * stepped,
                    )
                else:
                    new_surface[pl.ds((row * count + t) * CHANNELS + c, 1), :] = stepped[0:1, :]
        out.row(row).start()
        return carry

    blank = jnp.zeros((LEVELS, WIDTH), jnp.float32)
    totals = lax.fori_loop(0, sz.rows, one_row, (blank, blank, blank) if last else 0)
    if last:
        place = lax.broadcasted_iota(jnp.int32, sums.block.shape, 1)
        held = jnp.zeros(sums.block.shape, jnp.float32)
        for index in range(3):
            total = jnp.sum(jnp.sum(totals[index], axis=0, keepdims=True), axis=1, keepdims=True)
            held = jnp.where(place == index, total, held)
        sums[...] = held
    else:
        new_surface[CHANNELS * sz.tiles :, :] = jnp.zeros((CHANNELS, WIDTH), jnp.float32)
        arrive_all(arrive)
        spread_back(
            sz,
            new_surface,
            slope,
            remap,
            tables,
            packed,
            near_low,
            near_high,
            tell_first,
            tell_second,
        )
        packed.start()
        store_edges(sz, out, diffusivity, edge_first, edge_second)


def final_kernel(cell_total, arrive, everyones, perturbation, gradient, out):
    sums = jnp.sum(everyones[...], axis=0, keepdims=True) / cell_total
    place = lax.broadcasted_iota(jnp.int32, sums.shape, 1)
    means = [
        jnp.broadcast_to(
            jnp.sum(jnp.where(place == index, sums, 0.0), axis=1, keepdims=True), (1, WIDTH)
        )
        for index in range(3)
    ]
    scale = lax.rsqrt(means[2] + EPSILON)
    mean_sq = means[0] + 2.0 * ASCENT * scale * means[1] + ASCENT * ASCENT * scale * scale * means[2]
    shrink = lax.rsqrt(mean_sq + EPSILON)
    step = jnp.broadcast_to(ASCENT * scale * shrink, (CHANNELS, WIDTH))
    shrink = jnp.broadcast_to(shrink, (CHANNELS, WIDTH))
    levels, rows, _, cells = perturbation.shape

    def one_level(level, carry):
        for row in range(rows):
            for tile in range(cells // WIDTH):
                start = perturbation[level, row, :, cols(tile)]
                slope = gradient[level, row, :, cols(tile)]
                out[level, row, :, cols(tile)] = shrink * start + step * slope
        out.row(level).start()
        return carry

    lax.fori_loop(0, levels, one_level, 0)


class Operand:
    def __init__(self, array, space, fetch=None, at=()):
        self.array, self.space, self.fetch, self.at = array, space, fetch, at

    def block(self):
        whole = self.array.shape
        taken = [size for size, index in zip(whole, self.at) if isinstance(index, slice)]
        return self.fetch((*taken, *whole[len(self.at) :]), self.array.dtype)


def near_by(*arrays):
    return [Operand(array, pltpu.VMEM) for array in arrays]


def far_off(*arrays):
    return [
        Operand(pltpu.with_memory_space_constraint(array, pltpu.HBM), pltpu.HBM)
        for array in arrays
    ]


def fetched(*arrays, at=(), into=pltpu.VMEM):
    return [
        Operand(pltpu.with_memory_space_constraint(array, pltpu.HBM), pltpu.HBM, into, at)
        for array in arrays
    ]


def scalars(*arrays):
    return fetched(*arrays, into=pltpu.SMEM)


def call(kernel, name, inputs, kept=(), shipped=(), scratch=()):
    n_in, n_kept, n_out = len(inputs), len(kept), len(shipped)
    brought = [index for index, item in enumerate(inputs) if item.fetch is not None]

    def as_shape(item):
        return item if isinstance(item, jax.ShapeDtypeStruct) else jax.ShapeDtypeStruct(item, jnp.float32)

    kept = [as_shape(item) for item in kept]
    shipped = [as_shape(item) for item in shipped]

    def run(*refs):
        ins = list(refs[:n_in])
        kept_refs = refs[n_in : n_in + n_kept]
        homes = refs[n_in + n_kept : n_in + n_kept + n_out]
        rest = refs[n_in + n_kept + n_out :]
        outs = [
            Shipped(block, home, sems)
            for block, home, sems in zip(rest[:n_out], homes, rest[n_out : 2 * n_out])
        ]
        rest = rest[2 * n_out :]
        if brought:
            blocks, arrive_sems = rest[: len(brought)], rest[len(brought)]
            rest = rest[len(brought) + 1 :]
            copies = []
            for place, (index, block) in enumerate(zip(brought, blocks)):
                source = ins[index]
                if inputs[index].at:
                    source = source.at[inputs[index].at]
                copies.append(pltpu.make_async_copy(source, block, arrive_sems.at[place]))
                ins[index] = block
            for copy in copies:
                copy.start()
            arrive = [copy.wait for copy in copies]
        else:
            arrive = []
        kernel(arrive, *ins, *kept_refs, *outs, *rest)
        for out in outs:
            if not out.started:
                out.start()
        for out in outs:
            out.finish(out.block.shape[0])

    spaces = [pltpu.VMEM] * n_kept + [pltpu.HBM] * n_out
    blocks = [pltpu.VMEM(item.shape, item.dtype) for item in shipped]
    sems = [
        pltpu.SemaphoreType.DMA((item.shape[0] if len(item.shape) > 3 else 1,)) for item in shipped
    ]
    arriving = [inputs[index].block() for index in brought]
    if brought:
        arriving.append(pltpu.SemaphoreType.DMA((len(brought),)))
    more = [
        item if not isinstance(item, tuple) else pltpu.VMEM(item, jnp.float32) for item in scratch
    ]
    return pl.pallas_call(
        run,
        name=name,
        in_specs=[pl.BlockSpec(memory_space=item.space) for item in inputs],
        out_specs=[pl.BlockSpec(memory_space=space) for space in spaces],
        out_shape=kept + [pltpu.HBM(item.shape, item.dtype) for item in shipped],
        scratch_shapes=blocks + sems + arriving + more,
        compiler_params=pltpu.CompilerParams(vmem_limit_bytes=VMEM_BYTES),
    )(*[item.array for item in inputs])


def arrive_all(arrive):
    for wait in arrive:
        wait()


def swap(first, second):
    count = lax.axis_size("horiz")
    inner = [(i, i ^ 1) for i in range(count)]
    outer = [(i, i + 1) for i in range(1, count - 1, 2)]
    outer = outer + [(target, source) for source, target in outer]
    return lax.ppermute(first, "horiz", inner), lax.ppermute(second, "horiz", outer)


def exchange(array, devices):
    rows = array.shape[0] // devices
    split = array.reshape(devices, rows // CHANNELS, CHANNELS, WIDTH)
    moved = lax.all_to_all(split, "horiz", split_axis=0, concat_axis=0, tiled=True)
    return moved.reshape(array.shape)


def body(
    perturbation,
    base_state,
    target_state,
    cost_weight,
    diffusivity,
    chan_mix,
    coupler_mix,
    owner_mix,
    air_temp,
    wind_speed,
    wet_list,
    wet_owner,
    remap_src,
    remap_tgt,
    remap_weight,
):
    devices = lax.axis_size("horiz")
    hours = air_temp.shape[0]
    sz = Sizes(devices, air_temp.shape[2] // devices, base_state.shape[1], base_state.shape[3])
    rows = sz.rows
    native_row = (LEVELS, CHANNELS, sz.cells)

    edge_inputs = []
    for array in (perturbation, base_state):
        for row in (0, rows - 1):
            edge_inputs += fetched(array, at=(slice(None), row))
    edges = swap(
        *call(functools.partial(edges_kernel, sz), "edges", edge_inputs, kept=[sz.edge, sz.edge])
    )
    me = lax.axis_index("horiz").astype(jnp.int32)

    def lined(first_row, second_row):
        size = -(-first_row.shape[0] // WIDTH) * WIDTH
        pair = jnp.stack([first_row.astype(jnp.float32), second_row.astype(jnp.float32)])
        return jnp.pad(pair, ((0, 0), (0, size - pair.shape[1])), constant_values=-1.0)

    places = jnp.arange(CHANNELS * CHANNELS, dtype=jnp.int32) + sz.bulk_at
    remap_at = (remap_tgt - (me * LAT_DEV - 1)) * rows + remap_src - me * rows
    remap_lines = lined(
        jnp.concatenate([remap_at, places]),
        jnp.concatenate([remap_weight, coupler_mix.reshape(-1)]),
    )
    mix_rows = chan_mix.transpose(1, 2, 0).reshape(CHANNELS * CHANNELS, LEVELS)
    row_lines = (rows, 1, sz.cells)
    tiles_lines = (CHANNELS * sz.tiles, WIDTH)
    first_mix, first_rows, table, facts, mix = call(
        functools.partial(setup_kernel, sz, wet_list.shape[1], remap_at.shape[0] + places.shape[0]),
        "setup",
        near_by(lined(wet_list[0], wet_owner[0]), remap_lines, mix_rows)
        + fetched(diffusivity),
        kept=[(CHANNELS * CHANNELS, LEVELS, WIDTH), row_lines],
        shipped=[
            jax.ShapeDtypeStruct((sz.slot_lines, WIDTH), jnp.int32),
            (sz.facts, WIDTH),
            (CHANNELS * CHANNELS, LEVELS, WIDTH),
        ],
    )
    wider = (rows + 2, CHANNELS, LEVELS, sz.cells)
    row_surface = (sz.row_width, WIDTH)
    by_row = (rows, *native_row)

    def row_sems(kinds):
        return pltpu.SemaphoreType.DMA((kinds, rows))

    (field,) = call(
        functools.partial(load_kernel, sz),
        "load",
        far_off(perturbation, base_state),
        kept=[sz.whole],
        scratch=[by_row, by_row, row_sems(2)],
    )

    saved = []
    near = [sz.near, sz.near]
    mix_shape = (CHANNELS * CHANNELS, LEVELS, WIDTH)
    by_slot = (sz.slots, WIDTH)
    for hour in range(hours):
        first, last = hour == 0, hour == hours - 1
        inputs = scalars(table, facts)
        if first:
            inputs += near_by(*edges, first_rows, first_mix, field) + fetched(facts)
            assert not last
        else:
            loads = fetched(mix, diffusivity_rows, *([weight_rows] if last else []))
            loads += far_off(field) + near_by(surface) + (far_off(target_state) if last else [])
            mix_here, rows_here, field, *more = call(
                functools.partial(forward_load_kernel, sz, last),
                "step_load",
                loads,
                kept=[mix_shape, row_lines, sz.whole] + ([row_lines, sz.whole] if last else []),
                scratch=[row_sems(2)] + ([by_row] if last else []),
            )
            inputs += near_by(*edges, rows_here, mix_here, field, *surface_edges, *more)
        field, drive, surface, packed, *sends = call(
            functools.partial(forward_kernel, sz, first, last),
            "step",
            inputs,
            shipped=[sz.whole, sz.whole, sz.surface, sz.narrow]
            + [sz.told if first else sz.lats] * 2
            + [sz.edge] * 2,
            scratch=[wider],
        )
        arrived = exchange(packed, devices)
        got = swap(*sends[:2])
        arrived, *got = lax.optimization_barrier((arrived, *got))
        inputs = (
            near_by(arrived, owner_mix[0], air_temp[hour, 0], wind_speed[hour, 0])
            + scalars(facts)
        )
        decoded = []
        if first:
            inputs += near_by(*got) + fetched(table, facts)
            decoded = [jax.ShapeDtypeStruct(sz.tables, jnp.int32), sz.weights]
        *decoded, flux, mixed_slope, flux_slope = call(
            functools.partial(owner_kernel, sz, first),
            "owners",
            inputs,
            shipped=[*decoded, sz.wide, sz.by_slot, sz.by_slot],
            scratch=[sz.narrow, by_slot],
        )
        if first:
            tables, weights = decoded
        flux, *sends = lax.optimization_barrier((flux, *sends[2:]))
        if first:
            flux, diffusivity = lax.optimization_barrier((flux, diffusivity))
            diffusivity_rows, weight_rows, diffusivity_tiles, weight_tiles = call(
                functools.partial(columns_kernel, sz),
                "columns",
                fetched(diffusivity, cost_weight),
                shipped=[row_lines, row_lines, tiles_lines, tiles_lines],
            )
        flux = exchange(flux, devices)
        edges = swap(*sends)
        inputs = near_by(flux, *got) + fetched(surface) + scalars(tables, weights)
        if last:
            surface, slope, packed, *sends = call(
                functools.partial(surface_kernel, sz, True),
                "surface",
                inputs + fetched(target_state, at=(0,)) + fetched(weight_tiles),
                shipped=[sz.surface, sz.slope, sz.wide, sz.lats, sz.lats],
                scratch=near,
            )
        else:
            surface, *sends, slope = call(
                functools.partial(surface_kernel, sz, False),
                "surface",
                inputs,
                kept=[sz.surface, row_surface, row_surface],
                shipped=[sz.slope],
                scratch=near,
            )
            surface_edges = swap(*sends)
        saved.append((drive, slope, mixed_slope, flux_slope))

    edge_sends = None
    for hour in reversed(range(hours)):
        drive, slope, mixed_slope, flux_slope = saved[hour]
        arrived = exchange(packed, devices)
        got = swap(*sends)
        arrived, *got = lax.optimization_barrier((arrived, *got))
        back = call(
            functools.partial(owner_back_kernel, sz),
            "owners_back",
            near_by(arrived, owner_mix[0]) + fetched(mixed_slope, flux_slope) + scalars(facts),
            shipped=[sz.narrow],
            scratch=[sz.narrow, by_slot],
        )[0]
        if edge_sends is not None:
            back, *edge_sends = lax.optimization_barrier((back, *edge_sends))
            edges = swap(*edge_sends)
        else:
            back, perturbation = lax.optimization_barrier((back, perturbation))
            start_field = call(
                functools.partial(relayout_kernel, sz),
                "relayout",
                far_off(perturbation),
                shipped=[sz.whole],
                scratch=[by_row, row_sems(1)],
            )[0]
        back = exchange(back, devices)
        surface, *row_sends = call(
            functools.partial(merge_kernel, sz),
            "merge",
            near_by(back, *got)
            + fetched(surface, slope)
            + scalars(table, facts)
            + fetched(diffusivity_tiles),
            kept=[sz.surface, row_surface, row_surface],
        )
        surface_edges = swap(*row_sends)
        last = hour == 0
        mix_here, rows_here, *loaded = call(
            functools.partial(backward_load_kernel, sz, last),
            "step_back_load",
            fetched(mix, diffusivity_rows)
            + far_off(field, drive)
            + near_by(surface)
            + (far_off(start_field) if last else []),
            kept=[mix_shape, row_lines] + [sz.whole] * (4 if last else 3),
            scratch=[row_sems(3)],
        )
        inputs = near_by(*edges, *surface_edges, rows_here, mix_here, *loaded)
        if last:
            gradient, sums = call(
                functools.partial(backward_kernel, sz, True),
                "step_back_sums",
                inputs,
                shipped=[sz.whole, (devices, WIDTH)],
                scratch=[wider],
            )
        else:
            field, surface, packed, *outs = call(
                functools.partial(backward_kernel, sz, False),
                "step_back",
                scalars(tables, weights) + fetched(saved[hour - 1][1]) + inputs,
                shipped=[sz.whole, sz.surface, sz.wide, sz.lats, sz.lats, sz.edge, sz.edge],
                scratch=[wider, *near],
            )
            sends, edge_sends = outs[:2], outs[2:]

    everyones = lax.all_to_all(sums, "horiz", split_axis=0, concat_axis=0, tiled=True)
    block = perturbation.shape
    return call(
        functools.partial(final_kernel, perturbation.size * devices),
        "finish",
        near_by(everyones, perturbation, gradient.transpose(2, 0, 1, 3)),
        shipped=[block],
    )[0]


def solution(mesh):
    placed = (
        P("member", "horiz", None, None),
        P(None, "horiz", None, None),
        P(None, "horiz", None, None),
        P("horiz", None),
        P("horiz", None),
        P(),
        P(),
        P("horiz", None, None),
        P(None, "horiz", None, None),
        P(None, "horiz", None, None),
        P("horiz", None),
        P("horiz", None),
        P("horiz"),
        P("horiz"),
        P("horiz"),
    )
    return jax.shard_map(
        body,
        mesh=mesh,
        in_specs=placed,
        out_specs=P("member", "horiz", None, None),
        check_vma=False,
    )
```

```python
import functools

import jax
import jax.numpy as jnp
from jax import lax
from jax.experimental import pallas as pl
from jax.experimental.pallas import tpu as pltpu
from jax.sharding import PartitionSpec as P

LAT_DEV = 2
NEAR_LAT = LAT_DEV + 2
CHANNELS = 4
LEVELS = 8
WIDTH = 128
SUBLANES = 8

KAPPA_V = 0.1
TIME_STEP = 0.3
FLUX_RATE = 0.05
FEEDBACK = 0.5
ASCENT = 0.5
EPSILON = 1e-06
HIGHEST = lax.Precision.HIGHEST
VMEM_BYTES = 32 * 1024 * 1024


class Sizes:
    def __init__(self, devices, capacity, rows, cells):
        self.devices = devices
        self.capacity = capacity
        self.slots = devices * capacity
        self.rows = rows
        self.cells = cells
        self.row_tiles = cells // WIDTH
        self.tiles = rows * self.row_tiles
        self.row_width = CHANNELS * self.row_tiles
        self.pitch = -(-self.row_tiles // SUBLANES) * SUBLANES
        self.own_rows = CHANNELS * capacity
        self.chunk = -(-(self.own_rows + 2 * capacity) // SUBLANES) * SUBLANES
        self.slot_lines = -(-self.slots // WIDTH)
        self.facts = -(-(self.slot_lines + 1) // SUBLANES) * SUBLANES
        self.lat_lines = LAT_DEV * self.pitch
        self.edge_lines = CHANNELS * self.row_tiles * LEVELS
        self.whole = (rows, CHANNELS, LEVELS, cells)
        self.edge = (self.edge_lines, WIDTH)
        self.told = (self.lat_lines + self.facts, WIDTH)
        self.surface = (CHANNELS * (self.tiles + 1), WIDTH)
        self.narrow = (CHANNELS * self.slots, WIDTH)
        self.wide = (devices * self.chunk, WIDTH)
        self.slope = (NEAR_LAT * self.pitch, WIDTH)
        self.lats = (self.lat_lines, WIDTH)
        self.bulk_at = NEAR_LAT * rows
        self.tables = (3 * self.slot_lines, WIDTH)
        self.weights = (3 * self.facts, WIDTH)
        self.near = (-(-(self.tiles + 1) // SUBLANES) * SUBLANES, WIDTH)
        self.by_slot = (CHANNELS, self.slots, WIDTH)


class Shipped:
    def __init__(self, block, home, sems):
        self.block, self.home, self.sems = block, home, sems
        self.by_row = False
        self.started = False

    def __getitem__(self, at):
        return self.block[at]

    def __setitem__(self, at, value):
        self.block[at] = value

    def row(self, index):
        self.by_row = True
        self.started = True
        return pltpu.make_async_copy(
            self.block.at[index], self.home.at[index], self.sems.at[index]
        )

    def all(self):
        return pltpu.make_async_copy(self.block, self.home, self.sems.at[0])

    def start(self):
        self.started = True
        self.all().start()

    def finish(self, rows):
        if self.by_row:
            for index in range(rows):
                self.row(index).wait()
        else:
            self.all().wait()


def cols(tile):
    return slice(tile * WIDTH, (tile + 1) * WIDTH)


def lanes_sum(left_here, left_before, right_here, right_after, lane):
    return jnp.where(lane == 0, left_before, left_here) + jnp.where(
        lane == WIDTH - 1, right_after, right_here
    )


def levels_sum(field, sub):
    return jnp.where(sub == 0, 0.0, pltpu.roll(field, 1, 0)) + jnp.where(
        sub == LEVELS - 1, 0.0, pltpu.roll(field, LEVELS - 1, 0)
    )


def row_tiles_of(sz, ref, row):
    return ref[pl.ds(row * sz.row_width, sz.row_tiles, stride=CHANNELS), :]


def put_row_tiles(sz, ref, row, value):
    ref[pl.ds(row * sz.row_width, sz.row_tiles, stride=CHANNELS), :] = value


def near_row(sz, ref, row):
    return ref[row * sz.row_tiles : (row + 1) * sz.row_tiles, :]


def high_first():
    return 1 - lax.rem(lax.axis_index("horiz").astype(jnp.int32), 2)


def pick(flag, one, other):
    return jnp.where(jnp.full(one.shape, flag, jnp.int32) == 1, one, other)


def sided(first, second):
    flag = high_first()
    return pick(flag, second, first), pick(flag, first, second)


def load_surface_row(sz, target, row, source, base):
    for tile in range(sz.row_tiles):
        for channel in range(CHANNELS):
            at = base + tile * CHANNELS + channel
            target[row, channel, 0:1, cols(tile)] = source[pl.ds(at, 1), :]


def as_column(row, size):
    shape = (size, row.shape[1])
    diagonal = lax.broadcasted_iota(jnp.int32, shape, 0) == lax.broadcasted_iota(jnp.int32, shape, 1)
    return jnp.sum(jnp.where(diagonal, row, 0.0), axis=1, keepdims=True)


def setup_kernel(sz, entries, remap_entries, arrive, wet, remap, mix_rows, diffusivity, *outs):
    first_mix, first_rows, table, facts, mix = outs
    arrive_all(arrive)
    for row in range(sz.rows):
        first_rows[row] = diffusivity[row : row + 1, :]
    for index in range(CHANNELS * CHANNELS):
        column = as_column(mix_rows[index : index + 1, :], LEVELS)
        mix[index] = jnp.broadcast_to(column, (LEVELS, WIDTH))
    mix.start()
    first_mix[...] = mix[...]
    tiles, owners = wet[0:1, :], wet[1:2, :]
    size = -(-entries // SUBLANES) * SUBLANES
    shape = (size, wet.shape[1])
    tile_here, owner_here = as_column(tiles, size), as_column(owners, size)
    earlier = lax.broadcasted_iota(jnp.int32, shape, 1) < lax.broadcasted_iota(jnp.int32, shape, 0)
    same = (owner_here == owners) & earlier
    rank = jnp.sum(jnp.where(same, 1.0, 0.0), axis=1, keepdims=True)
    slot = jnp.where(owner_here >= 0.0, owner_here * sz.capacity + rank, -1.0)
    facts[...] = jnp.zeros((sz.facts, WIDTH), jnp.float32)
    for line in range(sz.slot_lines):
        place = lax.broadcasted_iota(jnp.int32, (size, WIDTH), 1) + line * WIDTH
        match = slot.astype(jnp.int32) == place
        told = jnp.sum(jnp.where(match, sz.tiles - tile_here, 0.0), axis=0, keepdims=True)
        facts[line : line + 1, :] = told
        table[line : line + 1, :] = sz.tiles - told.astype(jnp.int32)
    size = -(-remap_entries // SUBLANES) * SUBLANES
    at, amount = as_column(remap[0:1, :], size), as_column(remap[1:2, :], size)
    place = lax.broadcasted_iota(jnp.int32, (size, WIDTH), 1)
    facts[sz.slot_lines : sz.slot_lines + 1, :] = jnp.sum(
        jnp.where(at.astype(jnp.int32) == place, amount, 0.0), axis=0, keepdims=True
    )


def columns_kernel(sz, arrive, diffusivity, weight, *outs):
    diffusivity_rows, weight_rows, diffusivity_tiles, weight_tiles = outs
    arrive_all(arrive)
    for source, by_row, by_tile in (
        (diffusivity, diffusivity_rows, diffusivity_tiles),
        (weight, weight_rows, weight_tiles),
    ):
        for row in range(sz.rows):
            by_row[row] = source[row : row + 1, :]
            for tile in range(sz.row_tiles):
                line = source[row : row + 1, cols(tile)]
                at = (row * sz.row_tiles + tile) * CHANNELS
                by_tile[at : at + CHANNELS, :] = jnp.broadcast_to(line, (CHANNELS, WIDTH))


def gather_levels(block, channel, tile):
    sub = lax.broadcasted_iota(jnp.int32, (LEVELS, WIDTH), 0)
    total = None
    for level in range(LEVELS):
        line = block[level, channel : channel + 1, cols(tile)]
        line = jnp.broadcast_to(line, (LEVELS, WIDTH))
        total = line if total is None else jnp.where(sub == level, line, total)
    return total


def edges_kernel(sz, arrive, low_start, high_start, low_base, high_base, send_first, send_second):
    arrive_all(arrive)
    low_start[...] = low_start[...] + low_base[...]
    high_start[...] = high_start[...] + high_base[...]
    flag = high_first()
    for channel in range(CHANNELS):
        for tile in range(sz.row_tiles):
            low = gather_levels(low_start, channel, tile)
            high = gather_levels(high_start, channel, tile)
            at = (channel * sz.row_tiles + tile) * LEVELS
            send_first[at : at + LEVELS, :] = pick(flag, high, low)
            send_second[at : at + LEVELS, :] = pick(flag, low, high)


def load_kernel(sz, arrive, perturbation, base, field, start_block, base_block, in_sems):
    def arrivals(row):
        return [
            pltpu.make_async_copy(source.at[:, row], block.at[row], in_sems.at[index, row])
            for index, (source, block) in enumerate(
                ((perturbation, start_block), (base, base_block))
            )
        ]

    for row in range(sz.rows):
        for arrival in arrivals(row):
            arrival.start()

    def one_row(row, carry):
        for arrival in arrivals(row):
            arrival.wait()
        start_block[row] = start_block[row] + base_block[row]
        for channel in range(CHANNELS):
            for tile in range(sz.row_tiles):
                field[row, channel, :, cols(tile)] = gather_levels(
                    start_block.at[row], channel, tile
                )
        return carry

    lax.fori_loop(0, sz.rows, one_row, 0)


def relayout_kernel(sz, arrive, source, out, block, in_sems):
    def arrival(row):
        return pltpu.make_async_copy(source.at[:, row], block.at[row], in_sems.at[0, row])

    for row in range(sz.rows):
        arrival(row).start()

    def one_row(row, carry):
        arrival(row).wait()
        for channel in range(CHANNELS):
            for tile in range(sz.row_tiles):
                out[row, channel, :, cols(tile)] = gather_levels(block.at[row], channel, tile)
        out.row(row).start()
        return carry

    lax.fori_loop(0, sz.rows, one_row, 0)


class Remap:
    def __init__(self, sz, weights):
        self.sz, self.weights = sz, weights

    def weight(self, which, lat, row):
        line = which * self.sz.facts + self.sz.slot_lines
        return self.weights[line, lat * self.sz.rows + row]

    def own(self, lat, row):
        return self.weight(0, lat, row)

    def of_low(self, lat, row):
        return self.weight(1, lat + LAT_DEV, row)

    def of_high(self, lat, row):
        return self.weight(2, lat - LAT_DEV, row)


def tile_at(sz, tables, which, slot):
    return tables[which * sz.slot_lines + slot // WIDTH, slot % WIDTH]


def sum_of(weights, values):
    total = weights[0] * values[0]
    for weight, value in zip(weights[1:], values[1:]):
        total = total + weight * value
    return total


def own_sums(sz, remap, own, factor):
    return [
        factor * sum_of([remap.own(lat, row) for row in range(sz.rows)], own)
        for lat in range(NEAR_LAT)
    ]


def send_sums(sz, sums, tell_first, tell_second):
    flag = high_first()
    for index in range(LAT_DEV):
        low, high = sums[index], sums[LAT_DEV + index]
        at = index * sz.pitch
        tell_first[at : at + sz.row_tiles, :] = pick(flag, high, low)
        tell_second[at : at + sz.row_tiles, :] = pick(flag, low, high)


def lat_rows(sz, ref, lat):
    at = lat * sz.pitch
    return ref[at : at + sz.row_tiles, :]


def told_sums(sz, from_first, from_second):
    lows, highs = [], []
    for index in range(LAT_DEV):
        low, high = sided(lat_rows(sz, from_first, index), lat_rows(sz, from_second, index))
        lows.append(low)
        highs.append(high)
    return lows + highs


def place_edges(sz, padded, first, second, first_surface=None, second_surface=None):
    side = high_first() * (sz.rows + 1)
    for at, edge, surface in ((side, first, first_surface), (sz.rows + 1 - side, second, second_surface)):
        for channel in range(CHANNELS):
            for tile in range(sz.row_tiles):
                line = (channel * sz.row_tiles + tile) * LEVELS
                padded[at, channel, :, cols(tile)] = edge[line : line + LEVELS, :]
        if surface is not None:
            load_surface_row(sz, padded, at, surface, 0)


def store_rows(sz, surface, send_first, send_second, factor=None):
    row = high_first() * (sz.rows - 1)
    for at, send in ((row, send_first), (sz.rows - 1 - row, send_second)):
        for tile in range(sz.row_tiles):
            start = pl.multiple_of((at * sz.row_tiles + tile) * CHANNELS, CHANNELS)
            value = surface[pl.ds(start, CHANNELS), :]
            if factor is not None:
                value = factor[pl.ds(start, CHANNELS), :] * value
            send[tile * CHANNELS : (tile + 1) * CHANNELS, :] = value


def forward_load_kernel(sz, last, arrive, mix, diffusivity, *refs):
    refs = list(refs)
    if last:
        weight = refs.pop(0)
    field, surface = refs[:2]
    refs = refs[2:]
    if last:
        target = refs.pop(0)
    mix_out, rows_out, field_out = refs[:3]
    refs = refs[3:]
    if last:
        weight_out, target_out = refs[:2]
        refs = refs[2:]
    in_sems = refs[0]

    def arrivals(row):
        copies = [pltpu.make_async_copy(field.at[row], field_out.at[row], in_sems.at[0, row])]
        if last:
            copies.append(
                pltpu.make_async_copy(target.at[row], target_out.at[row], in_sems.at[1, row])
            )
        return copies

    for row in range(sz.rows):
        for arrival in arrivals(row):
            arrival.start()
    arrive_all(arrive)
    mix_out[...] = mix[...]
    rows_out[...] = diffusivity[...]
    if last:
        weight_out[...] = weight[...]

    def one_row(row, carry):
        for arrival in arrivals(row):
            arrival.wait()
        load_surface_row(sz, field_out, row, surface, row * sz.row_width)
        return carry

    lax.fori_loop(0, sz.rows, one_row, 0)


def forward_kernel(sz, first, last, arrive, *refs):
    refs = list(refs)
    tables, facts, low, high, diffusivity, mix, field = refs[:7]
    refs = refs[7:]
    if first:
        facts_block = refs.pop(0)
    surfaces = ()
    if not first:
        surfaces = refs[:2]
        refs = refs[2:]
    if last:
        weight, target = refs[:2]
        refs = refs[2:]
    out, drive, new_surface, packed, tell_first, tell_second, edge_first, edge_second, padded = refs
    remap = Remap(sz, facts)
    place_edges(sz, padded, low, high, *surfaces)

    def ready(row):
        padded[row + 1] = field[row]

    ready(0)
    lane = lax.broadcasted_iota(jnp.int32, (LEVELS, WIDTH), 1)
    sub = lax.broadcasted_iota(jnp.int32, (LEVELS, WIDTH), 0)
    count = sz.row_tiles

    def one_row(row, carry):
        @pl.when(row < sz.rows - 1)
        def _():
            ready(row + 1)

        here = [[padded[row + 1, c, :, cols(t)] for t in range(count)] for c in range(CHANNELS)]
        for t in range(count):
            coeff = jnp.broadcast_to(diffusivity[row, 0:1, cols(t)], (LEVELS, WIDTH))
            center = (1.0 - 2.0 * KAPPA_V) - 4.0 * coeff
            if last:
                scale = weight[row, 0:1, cols(t)]
                scale = jnp.broadcast_to(scale * scale, (LEVELS, WIDTH))
            for c in range(CHANNELS):
                mixed = mix[c * CHANNELS] * here[0][t]
                for k in range(1, CHANNELS):
                    mixed = mixed + mix[c * CHANNELS + k] * here[k][t]
                bent = jnp.tanh(mixed)
                drive[row, c, :, cols(t)] = bent
                field_here = here[c][t]
                around = lanes_sum(
                    pltpu.roll(field_here, 1, 1),
                    pltpu.roll(here[c][(t - 1) % count], 1, 1),
                    pltpu.roll(field_here, WIDTH - 1, 1),
                    pltpu.roll(here[c][(t + 1) % count], WIDTH - 1, 1),
                    lane,
                )
                around = around + (padded[row, c, :, cols(t)] + padded[row + 2, c, :, cols(t)])
                stepped = (
                    center * field_here
                    + coeff * around
                    + KAPPA_V * levels_sum(field_here, sub)
                    + TIME_STEP * bent
                )
                new_surface[pl.ds((row * count + t) * CHANNELS + c, 1), :] = stepped[0:1, :]
                if last:
                    stepped = scale * (stepped - target[row, c, :, cols(t)])
                out[row, c, :, cols(t)] = stepped
        drive.row(row).start()
        out.row(row).start()
        return carry

    lax.fori_loop(0, sz.rows, one_row, 0)
    new_surface[CHANNELS * sz.tiles :, :] = jnp.zeros((CHANNELS, WIDTH), jnp.float32)
    new_surface.start()
    arrive_all(arrive)
    pack_slots(sz, tables, new_surface, packed)
    packed.start()
    own = [row_tiles_of(sz, new_surface.block, row) for row in range(sz.rows)]
    send_sums(sz, own_sums(sz, remap, own, 1.0), tell_first, tell_second)
    for tell in (tell_first, tell_second):
        if first:
            tell[sz.lat_lines :, :] = facts_block[...]
        tell.start()
    store_edges(sz, out, diffusivity if last else None, edge_first, edge_second)


def pack_slots(sz, tables, surface, packed):
    for slot in range(sz.slots):
        at = pl.multiple_of(tile_at(sz, tables, 0, slot) * CHANNELS, CHANNELS)
        packed[slot * CHANNELS : (slot + 1) * CHANNELS, :] = surface[pl.ds(at, CHANNELS), :]


def store_edges(sz, field, diffusivity, send_first, send_second):
    outer = high_first() * (sz.rows - 1)
    for row, send in ((outer, send_first), (sz.rows - 1 - outer, send_second)):
        for channel in range(CHANNELS):
            for tile in range(sz.row_tiles):
                value = field[row, channel, :, cols(tile)]
                if diffusivity is not None:
                    value = value * jnp.broadcast_to(
                        diffusivity[row, 0:1, cols(tile)], (LEVELS, WIDTH)
                    )
                at = (channel * sz.row_tiles + tile) * LEVELS
                send[at : at + LEVELS, :] = value
        send.start()


def owner_kernel(sz, decode, arrive, arrived, mixing, air, wind, facts, *refs):
    slots = sz.slots
    if decode:
        told_first, told_second, own_table, own_facts, tables, weights = refs[:6]
        refs = refs[6:]
    flux, mixed_slope, flux_slope, flat, first = refs
    if decode:
        arrive_all(arrive)
        lines = sz.slot_lines
        tables[0:lines, :] = own_table[...]
        weights[0 : sz.facts, :] = own_facts[...]
        both = sided(told_first[sz.lat_lines :, :], told_second[sz.lat_lines :, :])
        for which, told in ((1, both[0]), (2, both[1])):
            got = told[0:lines, :].astype(jnp.int32)
            tables[which * lines : (which + 1) * lines, :] = sz.tiles - got
            at = which * sz.facts
            weights[at : at + sz.facts, :] = told
        tables.start()
        weights.start()

    def bulk(row, column):
        return facts[sz.slot_lines, sz.bulk_at + row * CHANNELS + column]

    values = [arrived[pl.ds(c, slots, stride=CHANNELS), :] for c in range(CHANNELS)]
    mixed = jnp.tanh(
        jnp.dot(
            mixing[...],
            jnp.concatenate(values, axis=1),
            precision=HIGHEST,
            preferred_element_type=jnp.float32,
        )
    )
    contrast = []
    for c in range(CHANNELS):
        mixed_here = mixed[:, cols(c)]
        mixed_slope[c] = 1.0 - mixed_here * mixed_here
        contrast.append((air[...] - values[0] if c == 0 else values[c]) + mixed_here)
    mixed_slope.start()
    if not decode:
        arrive_all(arrive)
    rate = FLUX_RATE * wind[...]
    for c in range(CHANNELS):
        forcing = bulk(c, 0) * contrast[0]
        for k in range(1, CHANNELS):
            forcing = forcing + bulk(c, k) * contrast[k]
        bent = jnp.tanh(forcing)
        flux_slope[c] = rate * (1.0 - bent * bent)
        one = rate * bent
        flat[pl.ds(c, slots, stride=CHANNELS), :] = one
        if c == 0:
            first[...] = one
    flux_slope.start()
    cap = sz.capacity
    gap = jnp.zeros((sz.chunk - sz.own_rows, WIDTH), jnp.float32)
    for d in range(sz.devices):
        at = d * sz.chunk
        flux[at : at + sz.own_rows, :] = flat[d * sz.own_rows : (d + 1) * sz.own_rows, :]
        at = at + sz.own_rows
        flux[at : (d + 1) * sz.chunk, :] = gap
        if d > 0:
            flux[at : at + cap, :] = first[(d - 1) * cap : d * cap, :]
        if d < sz.devices - 1:
            flux[at + cap : at + 2 * cap, :] = first[(d + 1) * cap : (d + 2) * cap, :]


def owner_back_kernel(sz, arrive, arrived, mixing, mixed_slope, flux_slope, facts, back, flat, extra):
    slots, cap = sz.slots, sz.capacity

    def bulk(row, column):
        return facts[sz.slot_lines, sz.bulk_at + row * CHANNELS + column]

    for d in range(sz.devices):
        at = d * sz.chunk
        flat[d * sz.own_rows : (d + 1) * sz.own_rows, :] = arrived[at : at + sz.own_rows, :]
        more = jnp.zeros((cap, WIDTH), jnp.float32)
        if d < sz.devices - 1:
            at = (d + 1) * sz.chunk + sz.own_rows
            more = more + arrived[at : at + cap, :]
        if d > 0:
            at = (d - 1) * sz.chunk + sz.own_rows + cap
            more = more + arrived[at : at + cap, :]
        extra[d * cap : (d + 1) * cap, :] = more
    arrive_all(arrive)
    forced = []
    for c in range(CHANNELS):
        got = flat[pl.ds(c, slots, stride=CHANNELS), :]
        if c == 0:
            got = got + extra[...]
        forced.append(flux_slope[c] * got)
    direct = []
    for k in range(CHANNELS):
        total = bulk(0, k) * forced[0]
        for c in range(1, CHANNELS):
            total = total + bulk(c, k) * forced[c]
        direct.append(total)
    through = lax.dot_general(
        mixing[...],
        jnp.concatenate([direct[k] * mixed_slope[k] for k in range(CHANNELS)], axis=1),
        (((0,), (0,)), ((), ())),
        precision=HIGHEST,
        preferred_element_type=jnp.float32,
    )
    for k in range(CHANNELS):
        sign = -1.0 if k == 0 else 1.0
        back.block[pl.ds(k, slots, stride=CHANNELS), :] = through[:, cols(k)] + sign * direct[k]


def spread_back(sz, surface, slope, remap, tables, packed, near_low, near_high, tell_first, tell_second):
    rows, count, cap = sz.rows, sz.row_tiles, sz.capacity
    block = surface.block
    own = [row_tiles_of(sz, block, row) for row in range(rows)]
    sums = own_sums(sz, remap, own, FEEDBACK)
    send_sums(sz, sums, tell_first, tell_second)
    tell_first.start()
    tell_second.start()
    lats = [lat_rows(sz, slope, lat) * sums[lat] for lat in range(NEAR_LAT)]
    every = range(NEAR_LAT)
    for row in range(rows):
        added = sum_of([remap.own(lat, row) for lat in every], lats)
        put_row_tiles(sz, block, row, own[row] + added)
        at = row * count
        near_low[at : at + count, :] = sum_of(
            [remap.of_low(lat, row) for lat in range(LAT_DEV)], lats[:LAT_DEV]
        )
        near_high[at : at + count, :] = sum_of(
            [remap.of_high(lat, row) for lat in range(LAT_DEV, NEAR_LAT)], lats[LAT_DEV:]
        )
    rest = sz.near[0] - sz.tiles
    near_low[sz.tiles :, :] = jnp.zeros((rest, WIDTH), jnp.float32)
    near_high[sz.tiles :, :] = jnp.zeros((rest, WIDTH), jnp.float32)
    surface.start()
    gap = jnp.zeros((sz.chunk - sz.own_rows, WIDTH), jnp.float32)
    for owner in range(sz.devices):
        packed[owner * sz.chunk + sz.own_rows : (owner + 1) * sz.chunk, :] = gap
    for slot in range(sz.slots):
        owner, rank = slot // cap, slot % cap
        at = owner * sz.chunk + rank * CHANNELS
        tile = pl.multiple_of(tile_at(sz, tables, 0, slot) * CHANNELS, CHANNELS)
        packed[at : at + CHANNELS, :] = surface[pl.ds(tile, CHANNELS), :]
        at = owner * sz.chunk + sz.own_rows + rank
        packed[at : at + 1, :] = near_low[pl.ds(tile_at(sz, tables, 1, slot), 1), :]
        at = at + cap
        packed[at : at + 1, :] = near_high[pl.ds(tile_at(sz, tables, 2, slot), 1), :]


def surface_kernel(sz, last, arrive, *refs):
    refs = list(refs)
    flux, from_first, from_second, before, tables, weights = refs[:6]
    refs = refs[6:]
    if last:
        target, weight = refs[:2]
        surface, slope, packed, tell_first, tell_second, near_low, near_high = refs[2:]
        block = surface.block
    else:
        surface, send_first, send_second, slope, near_low, near_high = refs
        block = surface
    remap = Remap(sz, weights)
    arrive_all(arrive)
    rows, cap = sz.rows, sz.capacity
    block[...] = before[...]
    near_low[...] = jnp.zeros(sz.near, jnp.float32)
    near_high[...] = jnp.zeros(sz.near, jnp.float32)
    for slot in range(sz.slots):
        owner, rank = slot // cap, slot % cap
        at = owner * sz.chunk + rank * CHANNELS
        tile = pl.multiple_of(tile_at(sz, tables, 0, slot) * CHANNELS, CHANNELS)
        block[pl.ds(tile, CHANNELS), :] = (
            before[pl.ds(tile, CHANNELS), :] + flux[at : at + CHANNELS, :]
        )
        at = owner * sz.chunk + sz.own_rows + rank
        near_low[pl.ds(tile_at(sz, tables, 1, slot), 1), :] = flux[at : at + 1, :]
        at = at + cap
        near_high[pl.ds(tile_at(sz, tables, 2, slot), 1), :] = flux[at : at + 1, :]
    block[CHANNELS * sz.tiles :, :] = jnp.zeros((CHANNELS, WIDTH), jnp.float32)
    own = [row_tiles_of(sz, block, row) for row in range(rows)]
    sums = own_sums(sz, remap, own, 1.0)
    told = told_sums(sz, from_first, from_second)
    air = []
    for lat in range(NEAR_LAT):
        if lat < LAT_DEV:
            near, weights = near_low, [remap.of_low(lat, row) for row in range(rows)]
        else:
            near, weights = near_high, [remap.of_high(lat, row) for row in range(rows)]
        more = sum_of(weights, [near_row(sz, near, row) for row in range(rows)])
        one = jnp.tanh(sums[lat] + told[lat] + more)
        slope[lat * sz.pitch : lat * sz.pitch + sz.row_tiles, :] = 1.0 - one * one
        air.append(one)
    slope.start()
    for row in range(rows):
        weights = [remap.own(lat, row) for lat in range(NEAR_LAT)]
        put_row_tiles(sz, block, row, own[row] + FEEDBACK * sum_of(weights, air))
    if last:
        for row in range(rows):
            for tile in range(sz.row_tiles):
                at = row * sz.row_width + tile * CHANNELS
                scale = weight[at : at + CHANNELS, :]
                off = block[at : at + CHANNELS, :] - target[row, :, cols(tile)]
                block[at : at + CHANNELS, :] = scale * scale * off
        spread_back(
            sz, surface, slope, remap, tables, packed, near_low, near_high, tell_first, tell_second
        )
    else:
        store_rows(sz, surface, send_first, send_second)


def merge_kernel(
    sz, arrive, back, from_first, from_second, before, slope, tables, facts, diffusivity, surface, send_first, send_second
):
    rows = sz.rows
    remap = Remap(sz, facts)
    arrive_all(arrive)
    surface[...] = before[...]
    for slot in range(sz.slots):
        tile = pl.multiple_of(tile_at(sz, tables, 0, slot) * CHANNELS, CHANNELS)
        surface[pl.ds(tile, CHANNELS), :] = (
            before[pl.ds(tile, CHANNELS), :] + back[slot * CHANNELS : (slot + 1) * CHANNELS, :]
        )
    surface[CHANNELS * sz.tiles :, :] = jnp.zeros((CHANNELS, WIDTH), jnp.float32)
    told = told_sums(sz, from_first, from_second)
    lats = [lat_rows(sz, slope, lat) * told[lat] for lat in range(NEAR_LAT)]
    for row in range(rows):
        own = row_tiles_of(sz, surface, row)
        weights = [remap.own(lat, row) for lat in range(NEAR_LAT)]
        put_row_tiles(sz, surface, row, own + sum_of(weights, lats))
    store_rows(sz, surface, send_first, send_second, diffusivity)


def backward_load_kernel(sz, last, arrive, mix, diffusivity, field, drive, surface, *refs):
    refs = list(refs)
    if last:
        perturbation = refs.pop(0)
    mix_out, rows_out, local, bent_all, scaled = refs[:5]
    refs = refs[5:]
    if last:
        start_all = refs.pop(0)
    in_sems = refs[0]

    def arrivals(row):
        copies = [
            pltpu.make_async_copy(field.at[row], local.at[row], in_sems.at[0, row]),
            pltpu.make_async_copy(drive.at[row], bent_all.at[row], in_sems.at[1, row]),
        ]
        if last:
            copies.append(
                pltpu.make_async_copy(perturbation.at[row], start_all.at[row], in_sems.at[2, row])
            )
        return copies

    for row in range(sz.rows):
        for arrival in arrivals(row):
            arrival.start()
    arrive_all(arrive)
    mix_out[...] = mix[...]
    rows_out[...] = diffusivity[...]

    def one_row(row, carry):
        for arrival in arrivals(row):
            arrival.wait()
        load_surface_row(sz, local, row, surface, row * sz.row_width)
        for t in range(sz.row_tiles):
            coeff = jnp.broadcast_to(diffusivity[row, 0:1, cols(t)], (LEVELS, WIDTH))
            for c in range(CHANNELS):
                scaled[row, c, :, cols(t)] = coeff * local[row, c, :, cols(t)]
        return carry

    lax.fori_loop(0, sz.rows, one_row, 0)


def backward_kernel(sz, last, arrive, *refs):
    refs = list(refs)
    if not last:
        tables, weights, slope = refs[:3]
        refs = refs[3:]
    low, high, first_surface, second_surface, diffusivity, mix = refs[:6]
    local, bent_all, scaled_all = refs[6:9]
    refs = refs[9:]
    if last:
        start_all, out, sums, padded = refs
    else:
        out, new_surface, packed, tell_first, tell_second, edge_first, edge_second = refs[:7]
        padded, near_low, near_high = refs[7:]
        remap = Remap(sz, weights)
    count = sz.row_tiles
    place_edges(sz, padded, low, high, first_surface, second_surface)

    def ready(row):
        padded[row + 1] = scaled_all[row]

    ready(0)
    lane = lax.broadcasted_iota(jnp.int32, (LEVELS, WIDTH), 1)
    sub = lax.broadcasted_iota(jnp.int32, (LEVELS, WIDTH), 0)

    def one_row(row, carry):
        @pl.when(row < sz.rows - 1)
        def _():
            ready(row + 1)

        scaled = [[padded[row + 1, c, :, cols(t)] for t in range(count)] for c in range(CHANNELS)]
        for t in range(count):
            here, bent = [], []
            for c in range(CHANNELS):
                value = local[row, c, :, cols(t)]
                one = bent_all[row, c, :, cols(t)]
                here.append(value)
                bent.append((1.0 - one * one) * value)
            for c in range(CHANNELS):
                mixed = mix[c] * bent[0]
                for k in range(1, CHANNELS):
                    mixed = mixed + mix[k * CHANNELS + c] * bent[k]
                around = lanes_sum(
                    pltpu.roll(scaled[c][t], 1, 1),
                    pltpu.roll(scaled[c][(t - 1) % count], 1, 1),
                    pltpu.roll(scaled[c][t], WIDTH - 1, 1),
                    pltpu.roll(scaled[c][(t + 1) % count], WIDTH - 1, 1),
                    lane,
                )
                around = around + (padded[row, c, :, cols(t)] + padded[row + 2, c, :, cols(t)])
                stepped = (
                    ((1.0 - 2.0 * KAPPA_V) * here[c] - 4.0 * scaled[c][t])
                    + around
                    + KAPPA_V * levels_sum(here[c], sub)
                    + TIME_STEP * mixed
                )
                out[row, c, :, cols(t)] = stepped
                if last:
                    start = start_all[row, c, :, cols(t)]
                    carry = (
                        carry[0] + start * start,
                        carry[1] + start * stepped,
                        carry[2] + stepped * stepped,
                    )
                else:
                    new_surface[pl.ds((row * count + t) * CHANNELS + c, 1), :] = stepped[0:1, :]
        out.row(row).start()
        return carry

    blank = jnp.zeros((LEVELS, WIDTH), jnp.float32)
    totals = lax.fori_loop(0, sz.rows, one_row, (blank, blank, blank) if last else 0)
    if last:
        place = lax.broadcasted_iota(jnp.int32, sums.block.shape, 1)
        held = jnp.zeros(sums.block.shape, jnp.float32)
        for index in range(3):
            total = jnp.sum(jnp.sum(totals[index], axis=0, keepdims=True), axis=1, keepdims=True)
            held = jnp.where(place == index, total, held)
        sums[...] = held
    else:
        new_surface[CHANNELS * sz.tiles :, :] = jnp.zeros((CHANNELS, WIDTH), jnp.float32)
        arrive_all(arrive)
        spread_back(
            sz,
            new_surface,
            slope,
            remap,
            tables,
            packed,
            near_low,
            near_high,
            tell_first,
            tell_second,
        )
        packed.start()
        store_edges(sz, out, diffusivity, edge_first, edge_second)


def final_kernel(cell_total, arrive, everyones, perturbation, gradient, out):
    sums = jnp.sum(everyones[...], axis=0, keepdims=True) / cell_total
    place = lax.broadcasted_iota(jnp.int32, sums.shape, 1)
    means = [
        jnp.broadcast_to(
            jnp.sum(jnp.where(place == index, sums, 0.0), axis=1, keepdims=True), (1, WIDTH)
        )
        for index in range(3)
    ]
    scale = lax.rsqrt(means[2] + EPSILON)
    mean_sq = means[0] + 2.0 * ASCENT * scale * means[1] + ASCENT * ASCENT * scale * scale * means[2]
    shrink = lax.rsqrt(mean_sq + EPSILON)
    step = jnp.broadcast_to(ASCENT * scale * shrink, (CHANNELS, WIDTH))
    shrink = jnp.broadcast_to(shrink, (CHANNELS, WIDTH))
    levels, rows, _, cells = perturbation.shape

    def one_level(level, carry):
        for row in range(rows):
            for tile in range(cells // WIDTH):
                start = perturbation[level, row, :, cols(tile)]
                slope = gradient[level, row, :, cols(tile)]
                out[level, row, :, cols(tile)] = shrink * start + step * slope
        out.row(level).start()
        return carry

    lax.fori_loop(0, levels, one_level, 0)


class Operand:
    def __init__(self, array, space, fetch=None, at=()):
        self.array, self.space, self.fetch, self.at = array, space, fetch, at

    def block(self):
        whole = self.array.shape
        taken = [size for size, index in zip(whole, self.at) if isinstance(index, slice)]
        return self.fetch((*taken, *whole[len(self.at) :]), self.array.dtype)


def near_by(*arrays):
    return [Operand(array, pltpu.VMEM) for array in arrays]


def far_off(*arrays):
    return [
        Operand(pltpu.with_memory_space_constraint(array, pltpu.HBM), pltpu.HBM)
        for array in arrays
    ]


def fetched(*arrays, at=(), into=pltpu.VMEM):
    return [
        Operand(pltpu.with_memory_space_constraint(array, pltpu.HBM), pltpu.HBM, into, at)
        for array in arrays
    ]


def scalars(*arrays):
    return fetched(*arrays, into=pltpu.SMEM)


def call(kernel, name, inputs, kept=(), shipped=(), scratch=()):
    n_in, n_kept, n_out = len(inputs), len(kept), len(shipped)
    brought = [index for index, item in enumerate(inputs) if item.fetch is not None]

    def as_shape(item):
        return item if isinstance(item, jax.ShapeDtypeStruct) else jax.ShapeDtypeStruct(item, jnp.float32)

    kept = [as_shape(item) for item in kept]
    shipped = [as_shape(item) for item in shipped]

    def run(*refs):
        ins = list(refs[:n_in])
        kept_refs = refs[n_in : n_in + n_kept]
        homes = refs[n_in + n_kept : n_in + n_kept + n_out]
        rest = refs[n_in + n_kept + n_out :]
        outs = [
            Shipped(block, home, sems)
            for block, home, sems in zip(rest[:n_out], homes, rest[n_out : 2 * n_out])
        ]
        rest = rest[2 * n_out :]
        if brought:
            blocks, arrive_sems = rest[: len(brought)], rest[len(brought)]
            rest = rest[len(brought) + 1 :]
            copies = []
            for place, (index, block) in enumerate(zip(brought, blocks)):
                source = ins[index]
                if inputs[index].at:
                    source = source.at[inputs[index].at]
                copies.append(pltpu.make_async_copy(source, block, arrive_sems.at[place]))
                ins[index] = block
            for copy in copies:
                copy.start()
            arrive = [copy.wait for copy in copies]
        else:
            arrive = []
        kernel(arrive, *ins, *kept_refs, *outs, *rest)
        for out in outs:
            if not out.started:
                out.start()
        for out in outs:
            out.finish(out.block.shape[0])

    spaces = [pltpu.VMEM] * n_kept + [pltpu.HBM] * n_out
    blocks = [pltpu.VMEM(item.shape, item.dtype) for item in shipped]
    sems = [
        pltpu.SemaphoreType.DMA((item.shape[0] if len(item.shape) > 3 else 1,)) for item in shipped
    ]
    arriving = [inputs[index].block() for index in brought]
    if brought:
        arriving.append(pltpu.SemaphoreType.DMA((len(brought),)))
    more = [
        item if not isinstance(item, tuple) else pltpu.VMEM(item, jnp.float32) for item in scratch
    ]
    return pl.pallas_call(
        run,
        name=name,
        in_specs=[pl.BlockSpec(memory_space=item.space) for item in inputs],
        out_specs=[pl.BlockSpec(memory_space=space) for space in spaces],
        out_shape=kept + [pltpu.HBM(item.shape, item.dtype) for item in shipped],
        scratch_shapes=blocks + sems + arriving + more,
        compiler_params=pltpu.CompilerParams(vmem_limit_bytes=VMEM_BYTES),
    )(*[item.array for item in inputs])


def arrive_all(arrive):
    for wait in arrive:
        wait()


def swap(first, second):
    count = lax.axis_size("horiz")
    inner = [(i, i ^ 1) for i in range(count)]
    outer = [(i, i + 1) for i in range(1, count - 1, 2)]
    outer = outer + [(target, source) for source, target in outer]
    return lax.ppermute(first, "horiz", inner), lax.ppermute(second, "horiz", outer)


def exchange(array, devices):
    rows = array.shape[0] // devices
    split = array.reshape(devices, rows // CHANNELS, CHANNELS, WIDTH)
    moved = lax.all_to_all(split, "horiz", split_axis=0, concat_axis=0, tiled=True)
    return moved.reshape(array.shape)


def body(
    perturbation,
    base_state,
    target_state,
    cost_weight,
    diffusivity,
    chan_mix,
    coupler_mix,
    owner_mix,
    air_temp,
    wind_speed,
    wet_list,
    wet_owner,
    remap_src,
    remap_tgt,
    remap_weight,
):
    devices = lax.axis_size("horiz")
    hours = air_temp.shape[0]
    sz = Sizes(devices, air_temp.shape[2] // devices, base_state.shape[1], base_state.shape[3])
    rows = sz.rows
    native_row = (LEVELS, CHANNELS, sz.cells)

    edge_inputs = []
    for array in (perturbation, base_state):
        for row in (0, rows - 1):
            edge_inputs += fetched(array, at=(slice(None), row))
    edges = swap(
        *call(functools.partial(edges_kernel, sz), "edges", edge_inputs, kept=[sz.edge, sz.edge])
    )
    me = lax.axis_index("horiz").astype(jnp.int32)

    def lined(first_row, second_row):
        size = -(-first_row.shape[0] // WIDTH) * WIDTH
        pair = jnp.stack([first_row.astype(jnp.float32), second_row.astype(jnp.float32)])
        return jnp.pad(pair, ((0, 0), (0, size - pair.shape[1])), constant_values=-1.0)

    places = jnp.arange(CHANNELS * CHANNELS, dtype=jnp.int32) + sz.bulk_at
    remap_at = (remap_tgt - (me * LAT_DEV - 1)) * rows + remap_src - me * rows
    remap_lines = lined(
        jnp.concatenate([remap_at, places]),
        jnp.concatenate([remap_weight, coupler_mix.reshape(-1)]),
    )
    mix_rows = chan_mix.transpose(1, 2, 0).reshape(CHANNELS * CHANNELS, LEVELS)
    row_lines = (rows, 1, sz.cells)
    tiles_lines = (CHANNELS * sz.tiles, WIDTH)
    first_mix, first_rows, table, facts, mix = call(
        functools.partial(setup_kernel, sz, wet_list.shape[1], remap_at.shape[0] + places.shape[0]),
        "setup",
        near_by(lined(wet_list[0], wet_owner[0]), remap_lines, mix_rows)
        + fetched(diffusivity),
        kept=[(CHANNELS * CHANNELS, LEVELS, WIDTH), row_lines],
        shipped=[
            jax.ShapeDtypeStruct((sz.slot_lines, WIDTH), jnp.int32),
            (sz.facts, WIDTH),
            (CHANNELS * CHANNELS, LEVELS, WIDTH),
        ],
    )
    wider = (rows + 2, CHANNELS, LEVELS, sz.cells)
    row_surface = (sz.row_width, WIDTH)
    by_row = (rows, *native_row)

    def row_sems(kinds):
        return pltpu.SemaphoreType.DMA((kinds, rows))

    (field,) = call(
        functools.partial(load_kernel, sz),
        "load",
        far_off(perturbation, base_state),
        kept=[sz.whole],
        scratch=[by_row, by_row, row_sems(2)],
    )

    def relayout(array):
        return call(
            functools.partial(relayout_kernel, sz),
            "relayout",
            far_off(array),
            shipped=[sz.whole],
            scratch=[by_row, row_sems(1)],
        )

    saved = []
    near = [sz.near, sz.near]
    mix_shape = (CHANNELS * CHANNELS, LEVELS, WIDTH)
    by_slot = (sz.slots, WIDTH)
    for hour in range(hours):
        first, last = hour == 0, hour == hours - 1
        inputs = scalars(table, facts)
        if first:
            inputs += near_by(*edges, first_rows, first_mix, field) + fetched(facts)
            assert not last
        else:
            loads = fetched(mix, diffusivity_rows, *([weight_rows] if last else []))
            loads += far_off(field) + near_by(surface) + (far_off(target) if last else [])
            mix_here, rows_here, field, *more = call(
                functools.partial(forward_load_kernel, sz, last),
                "step_load",
                loads,
                kept=[mix_shape, row_lines, sz.whole] + ([row_lines, sz.whole] if last else []),
                scratch=[row_sems(2)],
            )
            inputs += near_by(*edges, rows_here, mix_here, field, *surface_edges, *more)
        field, drive, surface, packed, *sends = call(
            functools.partial(forward_kernel, sz, first, last),
            "step",
            inputs,
            shipped=[sz.whole, sz.whole, sz.surface, sz.narrow]
            + [sz.told if first else sz.lats] * 2
            + [sz.edge] * 2,
            scratch=[wider],
        )
        arrived = exchange(packed, devices)
        got = swap(*sends[:2])
        arrived, *got = lax.optimization_barrier((arrived, *got))
        inputs = (
            near_by(arrived, owner_mix[0], air_temp[hour, 0], wind_speed[hour, 0])
            + scalars(facts)
        )
        decoded = []
        if first:
            inputs += near_by(*got) + fetched(table, facts)
            decoded = [jax.ShapeDtypeStruct(sz.tables, jnp.int32), sz.weights]
        *decoded, flux, mixed_slope, flux_slope = call(
            functools.partial(owner_kernel, sz, first),
            "owners",
            inputs,
            shipped=[*decoded, sz.wide, sz.by_slot, sz.by_slot],
            scratch=[sz.narrow, by_slot],
        )
        if first:
            tables, weights = decoded
        flux, *sends = lax.optimization_barrier((flux, *sends[2:]))
        if first:
            flux, diffusivity, target_state = lax.optimization_barrier(
                (flux, diffusivity, target_state)
            )
            beside = call(
                functools.partial(columns_kernel, sz),
                "columns",
                fetched(diffusivity, cost_weight),
                shipped=[row_lines, row_lines, tiles_lines, tiles_lines],
            ) + relayout(target_state)
        else:
            flux, perturbation = lax.optimization_barrier((flux, perturbation))
            beside = relayout(perturbation)
        flux = exchange(flux, devices)
        flux, *beside = lax.optimization_barrier((flux, *beside))
        if first:
            diffusivity_rows, weight_rows, diffusivity_tiles, weight_tiles, target = beside
        else:
            start_field = beside[0]
        edges = swap(*sends)
        inputs = near_by(flux, *got) + fetched(surface) + scalars(tables, weights)
        if last:
            surface, slope, packed, *sends = call(
                functools.partial(surface_kernel, sz, True),
                "surface",
                inputs + fetched(target_state, at=(0,)) + fetched(weight_tiles),
                shipped=[sz.surface, sz.slope, sz.wide, sz.lats, sz.lats],
                scratch=near,
            )
        else:
            surface, *sends, slope = call(
                functools.partial(surface_kernel, sz, False),
                "surface",
                inputs,
                kept=[sz.surface, row_surface, row_surface],
                shipped=[sz.slope],
                scratch=near,
            )
            surface_edges = swap(*sends)
        saved.append((drive, slope, mixed_slope, flux_slope))

    edge_sends = None
    for hour in reversed(range(hours)):
        drive, slope, mixed_slope, flux_slope = saved[hour]
        arrived = exchange(packed, devices)
        got = swap(*sends)
        arrived, *got = lax.optimization_barrier((arrived, *got))
        back = call(
            functools.partial(owner_back_kernel, sz),
            "owners_back",
            near_by(arrived, owner_mix[0]) + fetched(mixed_slope, flux_slope) + scalars(facts),
            shipped=[sz.narrow],
            scratch=[sz.narrow, by_slot],
        )[0]
        if edge_sends is not None:
            back, *edge_sends = lax.optimization_barrier((back, *edge_sends))
            edges = swap(*edge_sends)
        back = exchange(back, devices)
        surface, *row_sends = call(
            functools.partial(merge_kernel, sz),
            "merge",
            near_by(back, *got)
            + fetched(surface, slope)
            + scalars(table, facts)
            + fetched(diffusivity_tiles),
            kept=[sz.surface, row_surface, row_surface],
        )
        surface_edges = swap(*row_sends)
        last = hour == 0
        mix_here, rows_here, *loaded = call(
            functools.partial(backward_load_kernel, sz, last),
            "step_back_load",
            fetched(mix, diffusivity_rows)
            + far_off(field, drive)
            + near_by(surface)
            + (far_off(start_field) if last else []),
            kept=[mix_shape, row_lines] + [sz.whole] * (4 if last else 3),
            scratch=[row_sems(3)],
        )
        inputs = near_by(*edges, *surface_edges, rows_here, mix_here, *loaded)
        if last:
            gradient, sums = call(
                functools.partial(backward_kernel, sz, True),
                "step_back_sums",
                inputs,
                shipped=[sz.whole, (devices, WIDTH)],
                scratch=[wider],
            )
        else:
            field, surface, packed, *outs = call(
                functools.partial(backward_kernel, sz, False),
                "step_back",
                scalars(tables, weights) + fetched(saved[hour - 1][1]) + inputs,
                shipped=[sz.whole, sz.surface, sz.wide, sz.lats, sz.lats, sz.edge, sz.edge],
                scratch=[wider, *near],
            )
            sends, edge_sends = outs[:2], outs[2:]

    everyones = lax.all_to_all(sums, "horiz", split_axis=0, concat_axis=0, tiled=True)
    block = perturbation.shape
    return call(
        functools.partial(final_kernel, perturbation.size * devices),
        "finish",
        near_by(everyones, perturbation, gradient.transpose(2, 0, 1, 3)),
        shipped=[block],
    )[0]


def solution(mesh):
    placed = (
        P("member", "horiz", None, None),
        P(None, "horiz", None, None),
        P(None, "horiz", None, None),
        P("horiz", None),
        P("horiz", None),
        P(),
        P(),
        P("horiz", None, None),
        P(None, "horiz", None, None),
        P(None, "horiz", None, None),
        P("horiz", None),
        P("horiz", None),
        P("horiz"),
        P("horiz"),
        P("horiz"),
    )
    return jax.shard_map(
        body,
        mesh=mesh,
        in_specs=placed,
        out_specs=P("member", "horiz", None, None),
        check_vma=False,
    )
```

```python
import functools

import jax
import jax.numpy as jnp
from jax import lax
from jax.experimental import pallas as pl
from jax.experimental.pallas import tpu as pltpu
from jax.sharding import PartitionSpec as P

LAT_DEV = 2
NEAR_LAT = LAT_DEV + 2
CHANNELS = 4
LEVELS = 8
WIDTH = 128
SUBLANES = 8

KAPPA_V = 0.1
TIME_STEP = 0.3
FLUX_RATE = 0.05
FEEDBACK = 0.5
ASCENT = 0.5
EPSILON = 1e-06
HIGHEST = lax.Precision.HIGHEST
VMEM_BYTES = 32 * 1024 * 1024


class Sizes:
    def __init__(self, devices, capacity, rows, cells):
        self.devices = devices
        self.capacity = capacity
        self.slots = devices * capacity
        self.rows = rows
        self.cells = cells
        self.row_tiles = cells // WIDTH
        self.tiles = rows * self.row_tiles
        self.row_width = CHANNELS * self.row_tiles
        self.pitch = -(-self.row_tiles // SUBLANES) * SUBLANES
        self.own_rows = CHANNELS * capacity
        self.chunk = self.own_rows + 2 * capacity
        self.slot_lines = -(-self.slots // WIDTH)
        self.facts = -(-(self.slot_lines + 1) // SUBLANES) * SUBLANES
        self.lat_lines = LAT_DEV * self.pitch
        self.edge_lines = CHANNELS * self.row_tiles * LEVELS
        self.whole = (rows, CHANNELS, LEVELS, cells)
        self.edge = (self.edge_lines, WIDTH)
        self.told = (self.lat_lines + self.facts, WIDTH)
        self.surface = (CHANNELS * (self.tiles + 1), WIDTH)
        self.narrow = (CHANNELS * self.slots, WIDTH)
        self.wide = (devices * self.chunk, WIDTH)
        self.slope = (NEAR_LAT * self.pitch, WIDTH)
        self.lats = (self.lat_lines, WIDTH)
        self.bulk_at = NEAR_LAT * rows
        self.tables = (3 * self.slot_lines, WIDTH)
        self.weights = (3 * self.facts, WIDTH)
        self.near = (-(-(self.tiles + 1) // SUBLANES) * SUBLANES, WIDTH)
        self.by_slot = (CHANNELS, self.slots, WIDTH)


class Shipped:
    def __init__(self, block, home, sems):
        self.block, self.home, self.sems = block, home, sems
        self.by_row = False
        self.started = False

    def __getitem__(self, at):
        return self.block[at]

    def __setitem__(self, at, value):
        self.block[at] = value

    def row(self, index):
        self.by_row = True
        self.started = True
        return pltpu.make_async_copy(
            self.block.at[index], self.home.at[index], self.sems.at[index]
        )

    def all(self):
        return pltpu.make_async_copy(self.block, self.home, self.sems.at[0])

    def start(self):
        self.started = True
        self.all().start()

    def finish(self, rows):
        if self.by_row:
            for index in range(rows):
                self.row(index).wait()
        else:
            self.all().wait()


def cols(tile):
    return slice(tile * WIDTH, (tile + 1) * WIDTH)


def lanes_sum(left_here, left_before, right_here, right_after, lane):
    return jnp.where(lane == 0, left_before, left_here) + jnp.where(
        lane == WIDTH - 1, right_after, right_here
    )


def levels_sum(field, sub):
    return jnp.where(sub == 0, 0.0, pltpu.roll(field, 1, 0)) + jnp.where(
        sub == LEVELS - 1, 0.0, pltpu.roll(field, LEVELS - 1, 0)
    )


def row_tiles_of(sz, ref, row):
    return ref[pl.ds(row * sz.row_width, sz.row_tiles, stride=CHANNELS), :]


def put_row_tiles(sz, ref, row, value):
    ref[pl.ds(row * sz.row_width, sz.row_tiles, stride=CHANNELS), :] = value


def near_row(sz, ref, row):
    return ref[row * sz.row_tiles : (row + 1) * sz.row_tiles, :]


def high_first():
    return 1 - lax.rem(lax.axis_index("horiz").astype(jnp.int32), 2)


def pick(flag, one, other):
    return jnp.where(jnp.full(one.shape, flag, jnp.int32) == 1, one, other)


def sided(first, second):
    flag = high_first()
    return pick(flag, second, first), pick(flag, first, second)


def load_surface_row(sz, target, row, source, base):
    for tile in range(sz.row_tiles):
        for channel in range(CHANNELS):
            at = base + tile * CHANNELS + channel
            target[row, channel, 0:1, cols(tile)] = source[pl.ds(at, 1), :]


def as_column(row, size):
    shape = (size, row.shape[1])
    diagonal = lax.broadcasted_iota(jnp.int32, shape, 0) == lax.broadcasted_iota(jnp.int32, shape, 1)
    return jnp.sum(jnp.where(diagonal, row, 0.0), axis=1, keepdims=True)


def setup_kernel(sz, entries, remap_entries, arrive, wet, remap, mix_rows, diffusivity, *outs):
    first_mix, first_rows, table, facts, mix = outs
    arrive_all(arrive)
    for row in range(sz.rows):
        first_rows[row] = diffusivity[row : row + 1, :]
    for index in range(CHANNELS * CHANNELS):
        column = as_column(mix_rows[index : index + 1, :], LEVELS)
        mix[index] = jnp.broadcast_to(column, (LEVELS, WIDTH))
    mix.start()
    first_mix[...] = mix[...]
    tiles, owners = wet[0:1, :], wet[1:2, :]
    size = -(-entries // SUBLANES) * SUBLANES
    shape = (size, wet.shape[1])
    tile_here, owner_here = as_column(tiles, size), as_column(owners, size)
    earlier = lax.broadcasted_iota(jnp.int32, shape, 1) < lax.broadcasted_iota(jnp.int32, shape, 0)
    same = (owner_here == owners) & earlier
    rank = jnp.sum(jnp.where(same, 1.0, 0.0), axis=1, keepdims=True)
    slot = jnp.where(owner_here >= 0.0, owner_here * sz.capacity + rank, -1.0)
    facts[...] = jnp.zeros((sz.facts, WIDTH), jnp.float32)
    for line in range(sz.slot_lines):
        place = lax.broadcasted_iota(jnp.int32, (size, WIDTH), 1) + line * WIDTH
        match = slot.astype(jnp.int32) == place
        told = jnp.sum(jnp.where(match, sz.tiles - tile_here, 0.0), axis=0, keepdims=True)
        facts[line : line + 1, :] = told
        table[line : line + 1, :] = sz.tiles - told.astype(jnp.int32)
    size = -(-remap_entries // SUBLANES) * SUBLANES
    at, amount = as_column(remap[0:1, :], size), as_column(remap[1:2, :], size)
    place = lax.broadcasted_iota(jnp.int32, (size, WIDTH), 1)
    facts[sz.slot_lines : sz.slot_lines + 1, :] = jnp.sum(
        jnp.where(at.astype(jnp.int32) == place, amount, 0.0), axis=0, keepdims=True
    )


def columns_kernel(sz, arrive, diffusivity, weight, *outs):
    diffusivity_rows, weight_rows, diffusivity_tiles, weight_tiles = outs
    arrive_all(arrive)
    for source, by_row, by_tile in (
        (diffusivity, diffusivity_rows, diffusivity_tiles),
        (weight, weight_rows, weight_tiles),
    ):
        for row in range(sz.rows):
            by_row[row] = source[row : row + 1, :]
            for tile in range(sz.row_tiles):
                line = source[row : row + 1, cols(tile)]
                at = (row * sz.row_tiles + tile) * CHANNELS
                by_tile[at : at + CHANNELS, :] = jnp.broadcast_to(line, (CHANNELS, WIDTH))


def gather_levels(block, channel, tile):
    sub = lax.broadcasted_iota(jnp.int32, (LEVELS, WIDTH), 0)
    total = None
    for level in range(LEVELS):
        line = block[level, channel : channel + 1, cols(tile)]
        line = jnp.broadcast_to(line, (LEVELS, WIDTH))
        total = line if total is None else jnp.where(sub == level, line, total)
    return total


def edges_kernel(sz, arrive, low_start, high_start, low_base, high_base, send_first, send_second):
    arrive_all(arrive)
    low_start[...] = low_start[...] + low_base[...]
    high_start[...] = high_start[...] + high_base[...]
    flag = high_first()
    for channel in range(CHANNELS):
        for tile in range(sz.row_tiles):
            low = gather_levels(low_start, channel, tile)
            high = gather_levels(high_start, channel, tile)
            at = (channel * sz.row_tiles + tile) * LEVELS
            send_first[at : at + LEVELS, :] = pick(flag, high, low)
            send_second[at : at + LEVELS, :] = pick(flag, low, high)


def load_kernel(sz, arrive, perturbation, base, field, start_block, base_block, in_sems):
    def arrivals(row):
        return [
            pltpu.make_async_copy(source.at[:, row], block.at[row], in_sems.at[index, row])
            for index, (source, block) in enumerate(
                ((perturbation, start_block), (base, base_block))
            )
        ]

    for row in range(sz.rows):
        for arrival in arrivals(row):
            arrival.start()

    def one_row(row, carry):
        for arrival in arrivals(row):
            arrival.wait()
        start_block[row] = start_block[row] + base_block[row]
        for channel in range(CHANNELS):
            for tile in range(sz.row_tiles):
                field[row, channel, :, cols(tile)] = gather_levels(
                    start_block.at[row], channel, tile
                )
        return carry

    lax.fori_loop(0, sz.rows, one_row, 0)


def relayout_kernel(sz, arrive, source, out, block, in_sems):
    def arrival(row):
        return pltpu.make_async_copy(source.at[:, row], block.at[row], in_sems.at[0, row])

    for row in range(sz.rows):
        arrival(row).start()

    def one_row(row, carry):
        arrival(row).wait()
        for channel in range(CHANNELS):
            for tile in range(sz.row_tiles):
                out[row, channel, :, cols(tile)] = gather_levels(block.at[row], channel, tile)
        out.row(row).start()
        return carry

    lax.fori_loop(0, sz.rows, one_row, 0)


class Remap:
    def __init__(self, sz, weights):
        self.sz, self.weights = sz, weights

    def weight(self, which, lat, row):
        line = which * self.sz.facts + self.sz.slot_lines
        return self.weights[line, lat * self.sz.rows + row]

    def own(self, lat, row):
        return self.weight(0, lat, row)

    def of_low(self, lat, row):
        return self.weight(1, lat + LAT_DEV, row)

    def of_high(self, lat, row):
        return self.weight(2, lat - LAT_DEV, row)


def tile_at(sz, tables, which, slot):
    return tables[which * sz.slot_lines + slot // WIDTH, slot % WIDTH]


def sum_of(weights, values):
    total = weights[0] * values[0]
    for weight, value in zip(weights[1:], values[1:]):
        total = total + weight * value
    return total


def own_sums(sz, remap, own, factor):
    return [
        factor * sum_of([remap.own(lat, row) for row in range(sz.rows)], own)
        for lat in range(NEAR_LAT)
    ]


def send_sums(sz, sums, tell_first, tell_second):
    flag = high_first()
    for index in range(LAT_DEV):
        low, high = sums[index], sums[LAT_DEV + index]
        at = index * sz.pitch
        tell_first[at : at + sz.row_tiles, :] = pick(flag, high, low)
        tell_second[at : at + sz.row_tiles, :] = pick(flag, low, high)


def lat_rows(sz, ref, lat):
    at = lat * sz.pitch
    return ref[at : at + sz.row_tiles, :]


def told_sums(sz, from_first, from_second):
    lows, highs = [], []
    for index in range(LAT_DEV):
        low, high = sided(lat_rows(sz, from_first, index), lat_rows(sz, from_second, index))
        lows.append(low)
        highs.append(high)
    return lows + highs


def place_edges(sz, padded, first, second, first_surface=None, second_surface=None):
    side = high_first() * (sz.rows + 1)
    for at, edge, surface in ((side, first, first_surface), (sz.rows + 1 - side, second, second_surface)):
        for channel in range(CHANNELS):
            for tile in range(sz.row_tiles):
                line = (channel * sz.row_tiles + tile) * LEVELS
                padded[at, channel, :, cols(tile)] = edge[line : line + LEVELS, :]
        if surface is not None:
            load_surface_row(sz, padded, at, surface, 0)


def store_rows(sz, surface, send_first, send_second, factor=None):
    row = high_first() * (sz.rows - 1)
    for at, send in ((row, send_first), (sz.rows - 1 - row, send_second)):
        for tile in range(sz.row_tiles):
            start = pl.multiple_of((at * sz.row_tiles + tile) * CHANNELS, CHANNELS)
            value = surface[pl.ds(start, CHANNELS), :]
            if factor is not None:
                value = factor[pl.ds(start, CHANNELS), :] * value
            send[tile * CHANNELS : (tile + 1) * CHANNELS, :] = value


def forward_load_kernel(sz, last, arrive, mix, diffusivity, *refs):
    refs = list(refs)
    if last:
        weight = refs.pop(0)
    field, surface = refs[:2]
    refs = refs[2:]
    if last:
        target = refs.pop(0)
    mix_out, rows_out, field_out = refs[:3]
    refs = refs[3:]
    if last:
        weight_out, target_out = refs[:2]
        refs = refs[2:]
    in_sems = refs[0]

    def arrivals(row):
        copies = [pltpu.make_async_copy(field.at[row], field_out.at[row], in_sems.at[0, row])]
        if last:
            copies.append(
                pltpu.make_async_copy(target.at[row], target_out.at[row], in_sems.at[1, row])
            )
        return copies

    for row in range(sz.rows):
        for arrival in arrivals(row):
            arrival.start()
    arrive_all(arrive)
    mix_out[...] = mix[...]
    rows_out[...] = diffusivity[...]
    if last:
        weight_out[...] = weight[...]

    def one_row(row, carry):
        for arrival in arrivals(row):
            arrival.wait()
        load_surface_row(sz, field_out, row, surface, row * sz.row_width)
        return carry

    lax.fori_loop(0, sz.rows, one_row, 0)


def forward_kernel(sz, first, last, arrive, *refs):
    refs = list(refs)
    tables, facts, low, high, diffusivity, mix, field = refs[:7]
    refs = refs[7:]
    if first:
        facts_block = refs.pop(0)
    surfaces = ()
    if not first:
        surfaces = refs[:2]
        refs = refs[2:]
    if last:
        weight, target = refs[:2]
        refs = refs[2:]
    out, drive, new_surface, packed, tell_first, tell_second, edge_first, edge_second, padded = refs
    remap = Remap(sz, facts)
    place_edges(sz, padded, low, high, *surfaces)

    def ready(row):
        padded[row + 1] = field[row]

    ready(0)
    lane = lax.broadcasted_iota(jnp.int32, (LEVELS, WIDTH), 1)
    sub = lax.broadcasted_iota(jnp.int32, (LEVELS, WIDTH), 0)
    count = sz.row_tiles

    def one_row(row, carry):
        @pl.when(row < sz.rows - 1)
        def _():
            ready(row + 1)

        here = [[padded[row + 1, c, :, cols(t)] for t in range(count)] for c in range(CHANNELS)]
        for t in range(count):
            coeff = jnp.broadcast_to(diffusivity[row, 0:1, cols(t)], (LEVELS, WIDTH))
            center = (1.0 - 2.0 * KAPPA_V) - 4.0 * coeff
            if last:
                scale = weight[row, 0:1, cols(t)]
                scale = jnp.broadcast_to(scale * scale, (LEVELS, WIDTH))
            for c in range(CHANNELS):
                mixed = mix[c * CHANNELS] * here[0][t]
                for k in range(1, CHANNELS):
                    mixed = mixed + mix[c * CHANNELS + k] * here[k][t]
                bent = jnp.tanh(mixed)
                drive[row, c, :, cols(t)] = bent
                field_here = here[c][t]
                around = lanes_sum(
                    pltpu.roll(field_here, 1, 1),
                    pltpu.roll(here[c][(t - 1) % count], 1, 1),
                    pltpu.roll(field_here, WIDTH - 1, 1),
                    pltpu.roll(here[c][(t + 1) % count], WIDTH - 1, 1),
                    lane,
                )
                around = around + (padded[row, c, :, cols(t)] + padded[row + 2, c, :, cols(t)])
                stepped = (
                    center * field_here
                    + coeff * around
                    + KAPPA_V * levels_sum(field_here, sub)
                    + TIME_STEP * bent
                )
                new_surface[pl.ds((row * count + t) * CHANNELS + c, 1), :] = stepped[0:1, :]
                if last:
                    stepped = scale * (stepped - target[row, c, :, cols(t)])
                out[row, c, :, cols(t)] = stepped
        drive.row(row).start()
        out.row(row).start()
        return carry

    lax.fori_loop(0, sz.rows, one_row, 0)
    new_surface[CHANNELS * sz.tiles :, :] = jnp.zeros((CHANNELS, WIDTH), jnp.float32)
    new_surface.start()
    arrive_all(arrive)
    pack_slots(sz, tables, new_surface, packed)
    packed.start()
    own = [row_tiles_of(sz, new_surface.block, row) for row in range(sz.rows)]
    send_sums(sz, own_sums(sz, remap, own, 1.0), tell_first, tell_second)
    for tell in (tell_first, tell_second):
        if first:
            tell[sz.lat_lines :, :] = facts_block[...]
        tell.start()
    store_edges(sz, out, diffusivity if last else None, edge_first, edge_second)


def pack_slots(sz, tables, surface, packed):
    for slot in range(sz.slots):
        at = pl.multiple_of(tile_at(sz, tables, 0, slot) * CHANNELS, CHANNELS)
        packed[slot * CHANNELS : (slot + 1) * CHANNELS, :] = surface[pl.ds(at, CHANNELS), :]


def store_edges(sz, field, diffusivity, send_first, send_second):
    outer = high_first() * (sz.rows - 1)
    for row, send in ((outer, send_first), (sz.rows - 1 - outer, send_second)):
        for channel in range(CHANNELS):
            for tile in range(sz.row_tiles):
                value = field[row, channel, :, cols(tile)]
                if diffusivity is not None:
                    value = value * jnp.broadcast_to(
                        diffusivity[row, 0:1, cols(tile)], (LEVELS, WIDTH)
                    )
                at = (channel * sz.row_tiles + tile) * LEVELS
                send[at : at + LEVELS, :] = value
        send.start()


def owner_kernel(sz, decode, arrive, arrived, mixing, air, wind, facts, *refs):
    slots = sz.slots
    if decode:
        told_first, told_second, own_table, own_facts, tables, weights = refs[:6]
        refs = refs[6:]
    flux, mixed_slope, flux_slope, flat, first = refs
    if decode:
        arrive_all(arrive)
        lines = sz.slot_lines
        tables[0:lines, :] = own_table[...]
        weights[0 : sz.facts, :] = own_facts[...]
        both = sided(told_first[sz.lat_lines :, :], told_second[sz.lat_lines :, :])
        for which, told in ((1, both[0]), (2, both[1])):
            got = told[0:lines, :].astype(jnp.int32)
            tables[which * lines : (which + 1) * lines, :] = sz.tiles - got
            at = which * sz.facts
            weights[at : at + sz.facts, :] = told
        tables.start()
        weights.start()

    def bulk(row, column):
        return facts[sz.slot_lines, sz.bulk_at + row * CHANNELS + column]

    values = [arrived[pl.ds(c, slots, stride=CHANNELS), :] for c in range(CHANNELS)]
    mixed = jnp.tanh(
        jnp.dot(
            mixing[...],
            jnp.concatenate(values, axis=1),
            precision=HIGHEST,
            preferred_element_type=jnp.float32,
        )
    )
    contrast = []
    for c in range(CHANNELS):
        mixed_here = mixed[:, cols(c)]
        mixed_slope[c] = 1.0 - mixed_here * mixed_here
        contrast.append((air[...] - values[0] if c == 0 else values[c]) + mixed_here)
    mixed_slope.start()
    if not decode:
        arrive_all(arrive)
    rate = FLUX_RATE * wind[...]
    for c in range(CHANNELS):
        forcing = bulk(c, 0) * contrast[0]
        for k in range(1, CHANNELS):
            forcing = forcing + bulk(c, k) * contrast[k]
        bent = jnp.tanh(forcing)
        flux_slope[c] = rate * (1.0 - bent * bent)
        one = rate * bent
        flat[pl.ds(c, slots, stride=CHANNELS), :] = one
        if c == 0:
            first[...] = one
    flux_slope.start()
    cap = sz.capacity
    gap = jnp.zeros((sz.chunk - sz.own_rows, WIDTH), jnp.float32)
    for d in range(sz.devices):
        at = d * sz.chunk
        flux[at : at + sz.own_rows, :] = flat[d * sz.own_rows : (d + 1) * sz.own_rows, :]
        at = at + sz.own_rows
        flux[at : (d + 1) * sz.chunk, :] = gap
        if d > 0:
            flux[at : at + cap, :] = first[(d - 1) * cap : d * cap, :]
        if d < sz.devices - 1:
            flux[at + cap : at + 2 * cap, :] = first[(d + 1) * cap : (d + 2) * cap, :]


def owner_back_kernel(sz, arrive, arrived, mixing, mixed_slope, flux_slope, facts, back, flat, extra):
    slots, cap = sz.slots, sz.capacity

    def bulk(row, column):
        return facts[sz.slot_lines, sz.bulk_at + row * CHANNELS + column]

    for d in range(sz.devices):
        at = d * sz.chunk
        flat[d * sz.own_rows : (d + 1) * sz.own_rows, :] = arrived[at : at + sz.own_rows, :]
        more = jnp.zeros((cap, WIDTH), jnp.float32)
        if d < sz.devices - 1:
            at = (d + 1) * sz.chunk + sz.own_rows
            more = more + arrived[at : at + cap, :]
        if d > 0:
            at = (d - 1) * sz.chunk + sz.own_rows + cap
            more = more + arrived[at : at + cap, :]
        extra[d * cap : (d + 1) * cap, :] = more
    arrive_all(arrive)
    forced = []
    for c in range(CHANNELS):
        got = flat[pl.ds(c, slots, stride=CHANNELS), :]
        if c == 0:
            got = got + extra[...]
        forced.append(flux_slope[c] * got)
    direct = []
    for k in range(CHANNELS):
        total = bulk(0, k) * forced[0]
        for c in range(1, CHANNELS):
            total = total + bulk(c, k) * forced[c]
        direct.append(total)
    through = lax.dot_general(
        mixing[...],
        jnp.concatenate([direct[k] * mixed_slope[k] for k in range(CHANNELS)], axis=1),
        (((0,), (0,)), ((), ())),
        precision=HIGHEST,
        preferred_element_type=jnp.float32,
    )
    for k in range(CHANNELS):
        sign = -1.0 if k == 0 else 1.0
        back.block[pl.ds(k, slots, stride=CHANNELS), :] = through[:, cols(k)] + sign * direct[k]


def spread_back(sz, surface, slope, remap, tables, packed, near_low, near_high, tell_first, tell_second):
    rows, count, cap = sz.rows, sz.row_tiles, sz.capacity
    block = surface.block
    own = [row_tiles_of(sz, block, row) for row in range(rows)]
    sums = own_sums(sz, remap, own, FEEDBACK)
    send_sums(sz, sums, tell_first, tell_second)
    tell_first.start()
    tell_second.start()
    lats = [lat_rows(sz, slope, lat) * sums[lat] for lat in range(NEAR_LAT)]
    every = range(NEAR_LAT)
    for row in range(rows):
        added = sum_of([remap.own(lat, row) for lat in every], lats)
        put_row_tiles(sz, block, row, own[row] + added)
        at = row * count
        near_low[at : at + count, :] = sum_of(
            [remap.of_low(lat, row) for lat in range(LAT_DEV)], lats[:LAT_DEV]
        )
        near_high[at : at + count, :] = sum_of(
            [remap.of_high(lat, row) for lat in range(LAT_DEV, NEAR_LAT)], lats[LAT_DEV:]
        )
    rest = sz.near[0] - sz.tiles
    near_low[sz.tiles :, :] = jnp.zeros((rest, WIDTH), jnp.float32)
    near_high[sz.tiles :, :] = jnp.zeros((rest, WIDTH), jnp.float32)
    surface.start()
    gap = jnp.zeros((sz.chunk - sz.own_rows, WIDTH), jnp.float32)
    for owner in range(sz.devices):
        packed[owner * sz.chunk + sz.own_rows : (owner + 1) * sz.chunk, :] = gap
    for slot in range(sz.slots):
        owner, rank = slot // cap, slot % cap
        at = owner * sz.chunk + rank * CHANNELS
        tile = pl.multiple_of(tile_at(sz, tables, 0, slot) * CHANNELS, CHANNELS)
        packed[at : at + CHANNELS, :] = surface[pl.ds(tile, CHANNELS), :]
        at = owner * sz.chunk + sz.own_rows + rank
        packed[at : at + 1, :] = near_low[pl.ds(tile_at(sz, tables, 1, slot), 1), :]
        at = at + cap
        packed[at : at + 1, :] = near_high[pl.ds(tile_at(sz, tables, 2, slot), 1), :]


def surface_kernel(sz, last, arrive, *refs):
    refs = list(refs)
    flux, from_first, from_second, before, tables, weights = refs[:6]
    refs = refs[6:]
    if last:
        target, weight = refs[:2]
        surface, slope, packed, tell_first, tell_second, near_low, near_high = refs[2:]
        block = surface.block
    else:
        surface, send_first, send_second, slope, near_low, near_high = refs
        block = surface
    remap = Remap(sz, weights)
    arrive_all(arrive)
    rows, cap = sz.rows, sz.capacity
    block[...] = before[...]
    near_low[...] = jnp.zeros(sz.near, jnp.float32)
    near_high[...] = jnp.zeros(sz.near, jnp.float32)
    for slot in range(sz.slots):
        owner, rank = slot // cap, slot % cap
        at = owner * sz.chunk + rank * CHANNELS
        tile = pl.multiple_of(tile_at(sz, tables, 0, slot) * CHANNELS, CHANNELS)
        block[pl.ds(tile, CHANNELS), :] = (
            before[pl.ds(tile, CHANNELS), :] + flux[at : at + CHANNELS, :]
        )
        at = owner * sz.chunk + sz.own_rows + rank
        near_low[pl.ds(tile_at(sz, tables, 1, slot), 1), :] = flux[at : at + 1, :]
        at = at + cap
        near_high[pl.ds(tile_at(sz, tables, 2, slot), 1), :] = flux[at : at + 1, :]
    block[CHANNELS * sz.tiles :, :] = jnp.zeros((CHANNELS, WIDTH), jnp.float32)
    own = [row_tiles_of(sz, block, row) for row in range(rows)]
    sums = own_sums(sz, remap, own, 1.0)
    told = told_sums(sz, from_first, from_second)
    air = []
    for lat in range(NEAR_LAT):
        if lat < LAT_DEV:
            near, weights = near_low, [remap.of_low(lat, row) for row in range(rows)]
        else:
            near, weights = near_high, [remap.of_high(lat, row) for row in range(rows)]
        more = sum_of(weights, [near_row(sz, near, row) for row in range(rows)])
        one = jnp.tanh(sums[lat] + told[lat] + more)
        slope[lat * sz.pitch : lat * sz.pitch + sz.row_tiles, :] = 1.0 - one * one
        air.append(one)
    slope.start()
    for row in range(rows):
        weights = [remap.own(lat, row) for lat in range(NEAR_LAT)]
        put_row_tiles(sz, block, row, own[row] + FEEDBACK * sum_of(weights, air))
    if last:
        for row in range(rows):
            for tile in range(sz.row_tiles):
                at = row * sz.row_width + tile * CHANNELS
                scale = weight[at : at + CHANNELS, :]
                off = block[at : at + CHANNELS, :] - target[row, :, cols(tile)]
                block[at : at + CHANNELS, :] = scale * scale * off
        spread_back(
            sz, surface, slope, remap, tables, packed, near_low, near_high, tell_first, tell_second
        )
    else:
        store_rows(sz, surface, send_first, send_second)


def merge_kernel(
    sz, arrive, back, from_first, from_second, before, slope, tables, facts, diffusivity, surface, send_first, send_second
):
    rows = sz.rows
    remap = Remap(sz, facts)
    arrive_all(arrive)
    surface[...] = before[...]
    for slot in range(sz.slots):
        tile = pl.multiple_of(tile_at(sz, tables, 0, slot) * CHANNELS, CHANNELS)
        surface[pl.ds(tile, CHANNELS), :] = (
            before[pl.ds(tile, CHANNELS), :] + back[slot * CHANNELS : (slot + 1) * CHANNELS, :]
        )
    surface[CHANNELS * sz.tiles :, :] = jnp.zeros((CHANNELS, WIDTH), jnp.float32)
    told = told_sums(sz, from_first, from_second)
    lats = [lat_rows(sz, slope, lat) * told[lat] for lat in range(NEAR_LAT)]
    for row in range(rows):
        own = row_tiles_of(sz, surface, row)
        weights = [remap.own(lat, row) for lat in range(NEAR_LAT)]
        put_row_tiles(sz, surface, row, own + sum_of(weights, lats))
    store_rows(sz, surface, send_first, send_second, diffusivity)


def backward_load_kernel(sz, last, arrive, mix, diffusivity, field, drive, surface, *refs):
    refs = list(refs)
    if last:
        perturbation = refs.pop(0)
    mix_out, rows_out, local, bent_all, scaled = refs[:5]
    refs = refs[5:]
    if last:
        start_all = refs.pop(0)
    in_sems = refs[0]

    def arrivals(row):
        copies = [
            pltpu.make_async_copy(field.at[row], local.at[row], in_sems.at[0, row]),
            pltpu.make_async_copy(drive.at[row], bent_all.at[row], in_sems.at[1, row]),
        ]
        if last:
            copies.append(
                pltpu.make_async_copy(perturbation.at[row], start_all.at[row], in_sems.at[2, row])
            )
        return copies

    for row in range(sz.rows):
        for arrival in arrivals(row):
            arrival.start()
    arrive_all(arrive)
    mix_out[...] = mix[...]
    rows_out[...] = diffusivity[...]

    def one_row(row, carry):
        for arrival in arrivals(row):
            arrival.wait()
        load_surface_row(sz, local, row, surface, row * sz.row_width)
        for t in range(sz.row_tiles):
            coeff = jnp.broadcast_to(diffusivity[row, 0:1, cols(t)], (LEVELS, WIDTH))
            for c in range(CHANNELS):
                scaled[row, c, :, cols(t)] = coeff * local[row, c, :, cols(t)]
        return carry

    lax.fori_loop(0, sz.rows, one_row, 0)


def backward_kernel(sz, last, arrive, *refs):
    refs = list(refs)
    if not last:
        tables, weights, slope = refs[:3]
        refs = refs[3:]
    low, high, first_surface, second_surface, diffusivity, mix = refs[:6]
    local, bent_all, scaled_all = refs[6:9]
    refs = refs[9:]
    if last:
        start_all, out, sums, padded = refs
    else:
        out, new_surface, packed, tell_first, tell_second, edge_first, edge_second = refs[:7]
        padded, near_low, near_high = refs[7:]
        remap = Remap(sz, weights)
    count = sz.row_tiles
    place_edges(sz, padded, low, high, first_surface, second_surface)

    def ready(row):
        padded[row + 1] = scaled_all[row]

    ready(0)
    lane = lax.broadcasted_iota(jnp.int32, (LEVELS, WIDTH), 1)
    sub = lax.broadcasted_iota(jnp.int32, (LEVELS, WIDTH), 0)

    def one_row(row, carry):
        @pl.when(row < sz.rows - 1)
        def _():
            ready(row + 1)

        scaled = [[padded[row + 1, c, :, cols(t)] for t in range(count)] for c in range(CHANNELS)]
        for t in range(count):
            here, bent = [], []
            for c in range(CHANNELS):
                value = local[row, c, :, cols(t)]
                one = bent_all[row, c, :, cols(t)]
                here.append(value)
                bent.append((1.0 - one * one) * value)
            for c in range(CHANNELS):
                mixed = mix[c] * bent[0]
                for k in range(1, CHANNELS):
                    mixed = mixed + mix[k * CHANNELS + c] * bent[k]
                around = lanes_sum(
                    pltpu.roll(scaled[c][t], 1, 1),
                    pltpu.roll(scaled[c][(t - 1) % count], 1, 1),
                    pltpu.roll(scaled[c][t], WIDTH - 1, 1),
                    pltpu.roll(scaled[c][(t + 1) % count], WIDTH - 1, 1),
                    lane,
                )
                around = around + (padded[row, c, :, cols(t)] + padded[row + 2, c, :, cols(t)])
                stepped = (
                    ((1.0 - 2.0 * KAPPA_V) * here[c] - 4.0 * scaled[c][t])
                    + around
                    + KAPPA_V * levels_sum(here[c], sub)
                    + TIME_STEP * mixed
                )
                out[row, c, :, cols(t)] = stepped
                if last:
                    start = start_all[row, c, :, cols(t)]
                    carry = (
                        carry[0] + start * start,
                        carry[1] + start * stepped,
                        carry[2] + stepped * stepped,
                    )
                else:
                    new_surface[pl.ds((row * count + t) * CHANNELS + c, 1), :] = stepped[0:1, :]
        out.row(row).start()
        return carry

    blank = jnp.zeros((LEVELS, WIDTH), jnp.float32)
    totals = lax.fori_loop(0, sz.rows, one_row, (blank, blank, blank) if last else 0)
    if last:
        place = lax.broadcasted_iota(jnp.int32, sums.block.shape, 1)
        held = jnp.zeros(sums.block.shape, jnp.float32)
        for index in range(3):
            total = jnp.sum(jnp.sum(totals[index], axis=0, keepdims=True), axis=1, keepdims=True)
            held = jnp.where(place == index, total, held)
        sums[...] = held
    else:
        new_surface[CHANNELS * sz.tiles :, :] = jnp.zeros((CHANNELS, WIDTH), jnp.float32)
        arrive_all(arrive)
        spread_back(
            sz,
            new_surface,
            slope,
            remap,
            tables,
            packed,
            near_low,
            near_high,
            tell_first,
            tell_second,
        )
        packed.start()
        store_edges(sz, out, diffusivity, edge_first, edge_second)


def final_kernel(cell_total, arrive, everyones, perturbation, gradient, out):
    sums = jnp.sum(everyones[...], axis=0, keepdims=True) / cell_total
    place = lax.broadcasted_iota(jnp.int32, sums.shape, 1)
    means = [
        jnp.broadcast_to(
            jnp.sum(jnp.where(place == index, sums, 0.0), axis=1, keepdims=True), (1, WIDTH)
        )
        for index in range(3)
    ]
    scale = lax.rsqrt(means[2] + EPSILON)
    mean_sq = means[0] + 2.0 * ASCENT * scale * means[1] + ASCENT * ASCENT * scale * scale * means[2]
    shrink = lax.rsqrt(mean_sq + EPSILON)
    step = jnp.broadcast_to(ASCENT * scale * shrink, (CHANNELS, WIDTH))
    shrink = jnp.broadcast_to(shrink, (CHANNELS, WIDTH))
    levels, rows, _, cells = perturbation.shape

    def one_level(level, carry):
        for row in range(rows):
            for tile in range(cells // WIDTH):
                start = perturbation[level, row, :, cols(tile)]
                slope = gradient[level, row, :, cols(tile)]
                out[level, row, :, cols(tile)] = shrink * start + step * slope
        out.row(level).start()
        return carry

    lax.fori_loop(0, levels, one_level, 0)


class Operand:
    def __init__(self, array, space, fetch=None, at=()):
        self.array, self.space, self.fetch, self.at = array, space, fetch, at

    def block(self):
        whole = self.array.shape
        taken = [size for size, index in zip(whole, self.at) if isinstance(index, slice)]
        return self.fetch((*taken, *whole[len(self.at) :]), self.array.dtype)


def near_by(*arrays):
    return [Operand(array, pltpu.VMEM) for array in arrays]


def far_off(*arrays):
    return [
        Operand(pltpu.with_memory_space_constraint(array, pltpu.HBM), pltpu.HBM)
        for array in arrays
    ]


def fetched(*arrays, at=(), into=pltpu.VMEM):
    return [
        Operand(pltpu.with_memory_space_constraint(array, pltpu.HBM), pltpu.HBM, into, at)
        for array in arrays
    ]


def scalars(*arrays):
    return fetched(*arrays, into=pltpu.SMEM)


def call(kernel, name, inputs, kept=(), shipped=(), scratch=()):
    n_in, n_kept, n_out = len(inputs), len(kept), len(shipped)
    brought = [index for index, item in enumerate(inputs) if item.fetch is not None]

    def as_shape(item):
        return item if isinstance(item, jax.ShapeDtypeStruct) else jax.ShapeDtypeStruct(item, jnp.float32)

    kept = [as_shape(item) for item in kept]
    shipped = [as_shape(item) for item in shipped]

    def run(*refs):
        ins = list(refs[:n_in])
        kept_refs = refs[n_in : n_in + n_kept]
        homes = refs[n_in + n_kept : n_in + n_kept + n_out]
        rest = refs[n_in + n_kept + n_out :]
        outs = [
            Shipped(block, home, sems)
            for block, home, sems in zip(rest[:n_out], homes, rest[n_out : 2 * n_out])
        ]
        rest = rest[2 * n_out :]
        if brought:
            blocks, arrive_sems = rest[: len(brought)], rest[len(brought)]
            rest = rest[len(brought) + 1 :]
            copies = []
            for place, (index, block) in enumerate(zip(brought, blocks)):
                source = ins[index]
                if inputs[index].at:
                    source = source.at[inputs[index].at]
                copies.append(pltpu.make_async_copy(source, block, arrive_sems.at[place]))
                ins[index] = block
            for copy in copies:
                copy.start()
            arrive = [copy.wait for copy in copies]
        else:
            arrive = []
        kernel(arrive, *ins, *kept_refs, *outs, *rest)
        for out in outs:
            if not out.started:
                out.start()
        for out in outs:
            out.finish(out.block.shape[0])

    spaces = [pltpu.VMEM] * n_kept + [pltpu.HBM] * n_out
    blocks = [pltpu.VMEM(item.shape, item.dtype) for item in shipped]
    sems = [
        pltpu.SemaphoreType.DMA((item.shape[0] if len(item.shape) > 3 else 1,)) for item in shipped
    ]
    arriving = [inputs[index].block() for index in brought]
    if brought:
        arriving.append(pltpu.SemaphoreType.DMA((len(brought),)))
    more = [
        item if not isinstance(item, tuple) else pltpu.VMEM(item, jnp.float32) for item in scratch
    ]
    return pl.pallas_call(
        run,
        name=name,
        in_specs=[pl.BlockSpec(memory_space=item.space) for item in inputs],
        out_specs=[pl.BlockSpec(memory_space=space) for space in spaces],
        out_shape=kept + [pltpu.HBM(item.shape, item.dtype) for item in shipped],
        scratch_shapes=blocks + sems + arriving + more,
        compiler_params=pltpu.CompilerParams(vmem_limit_bytes=VMEM_BYTES),
    )(*[item.array for item in inputs])


def arrive_all(arrive):
    for wait in arrive:
        wait()


def swap(first, second):
    count = lax.axis_size("horiz")
    inner = [(i, i ^ 1) for i in range(count)]
    outer = [(i, i + 1) for i in range(1, count - 1, 2)]
    outer = outer + [(target, source) for source, target in outer]
    return lax.ppermute(first, "horiz", inner), lax.ppermute(second, "horiz", outer)


def exchange(array, devices):
    rows = array.shape[0] // devices
    step = CHANNELS if rows % CHANNELS == 0 else 2
    split = array.reshape(devices, rows // step, step, WIDTH)
    moved = lax.all_to_all(split, "horiz", split_axis=0, concat_axis=0, tiled=True)
    return moved.reshape(array.shape)


def body(
    perturbation,
    base_state,
    target_state,
    cost_weight,
    diffusivity,
    chan_mix,
    coupler_mix,
    owner_mix,
    air_temp,
    wind_speed,
    wet_list,
    wet_owner,
    remap_src,
    remap_tgt,
    remap_weight,
):
    devices = lax.axis_size("horiz")
    hours = air_temp.shape[0]
    sz = Sizes(devices, air_temp.shape[2] // devices, base_state.shape[1], base_state.shape[3])
    rows = sz.rows
    native_row = (LEVELS, CHANNELS, sz.cells)

    edge_inputs = []
    for array in (perturbation, base_state):
        for row in (0, rows - 1):
            edge_inputs += fetched(array, at=(slice(None), row))
    edges = swap(
        *call(functools.partial(edges_kernel, sz), "edges", edge_inputs, kept=[sz.edge, sz.edge])
    )
    me = lax.axis_index("horiz").astype(jnp.int32)

    def lined(first_row, second_row):
        size = -(-first_row.shape[0] // WIDTH) * WIDTH
        pair = jnp.stack([first_row.astype(jnp.float32), second_row.astype(jnp.float32)])
        return jnp.pad(pair, ((0, 0), (0, size - pair.shape[1])), constant_values=-1.0)

    places = jnp.arange(CHANNELS * CHANNELS, dtype=jnp.int32) + sz.bulk_at
    remap_at = (remap_tgt - (me * LAT_DEV - 1)) * rows + remap_src - me * rows
    remap_lines = lined(
        jnp.concatenate([remap_at, places]),
        jnp.concatenate([remap_weight, coupler_mix.reshape(-1)]),
    )
    mix_rows = chan_mix.transpose(1, 2, 0).reshape(CHANNELS * CHANNELS, LEVELS)
    row_lines = (rows, 1, sz.cells)
    tiles_lines = (CHANNELS * sz.tiles, WIDTH)
    first_mix, first_rows, table, facts, mix = call(
        functools.partial(setup_kernel, sz, wet_list.shape[1], remap_at.shape[0] + places.shape[0]),
        "setup",
        near_by(lined(wet_list[0], wet_owner[0]), remap_lines, mix_rows)
        + fetched(diffusivity),
        kept=[(CHANNELS * CHANNELS, LEVELS, WIDTH), row_lines],
        shipped=[
            jax.ShapeDtypeStruct((sz.slot_lines, WIDTH), jnp.int32),
            (sz.facts, WIDTH),
            (CHANNELS * CHANNELS, LEVELS, WIDTH),
        ],
    )
    wider = (rows + 2, CHANNELS, LEVELS, sz.cells)
    row_surface = (sz.row_width, WIDTH)
    by_row = (rows, *native_row)

    def row_sems(kinds):
        return pltpu.SemaphoreType.DMA((kinds, rows))

    (field,) = call(
        functools.partial(load_kernel, sz),
        "load",
        far_off(perturbation, base_state),
        kept=[sz.whole],
        scratch=[by_row, by_row, row_sems(2)],
    )

    def relayout(array):
        return call(
            functools.partial(relayout_kernel, sz),
            "relayout",
            far_off(array),
            shipped=[sz.whole],
            scratch=[by_row, row_sems(1)],
        )

    saved = []
    near = [sz.near, sz.near]
    mix_shape = (CHANNELS * CHANNELS, LEVELS, WIDTH)
    by_slot = (sz.slots, WIDTH)
    for hour in range(hours):
        first, last = hour == 0, hour == hours - 1
        inputs = scalars(table, facts)
        if first:
            inputs += near_by(*edges, first_rows, first_mix, field) + fetched(facts)
            assert not last
        else:
            loads = fetched(mix, diffusivity_rows, *([weight_rows] if last else []))
            loads += far_off(field) + near_by(surface) + (far_off(target) if last else [])
            mix_here, rows_here, field, *more = call(
                functools.partial(forward_load_kernel, sz, last),
                "step_load",
                loads,
                kept=[mix_shape, row_lines, sz.whole] + ([row_lines, sz.whole] if last else []),
                scratch=[row_sems(2)],
            )
            inputs += near_by(*edges, rows_here, mix_here, field, *surface_edges, *more)
        field, drive, surface, packed, *sends = call(
            functools.partial(forward_kernel, sz, first, last),
            "step",
            inputs,
            shipped=[sz.whole, sz.whole, sz.surface, sz.narrow]
            + [sz.told if first else sz.lats] * 2
            + [sz.edge] * 2,
            scratch=[wider],
        )
        arrived = exchange(packed, devices)
        got = swap(*sends[:2])
        arrived, *got = lax.optimization_barrier((arrived, *got))
        inputs = (
            near_by(arrived, owner_mix[0], air_temp[hour, 0], wind_speed[hour, 0])
            + scalars(facts)
        )
        decoded = []
        if first:
            inputs += near_by(*got) + fetched(table, facts)
            decoded = [jax.ShapeDtypeStruct(sz.tables, jnp.int32), sz.weights]
        *decoded, flux, mixed_slope, flux_slope = call(
            functools.partial(owner_kernel, sz, first),
            "owners",
            inputs,
            shipped=[*decoded, sz.wide, sz.by_slot, sz.by_slot],
            scratch=[sz.narrow, by_slot],
        )
        if first:
            tables, weights = decoded
        flux, *sends = lax.optimization_barrier((flux, *sends[2:]))
        if first:
            flux, diffusivity, target_state = lax.optimization_barrier(
                (flux, diffusivity, target_state)
            )
            beside = call(
                functools.partial(columns_kernel, sz),
                "columns",
                fetched(diffusivity, cost_weight),
                shipped=[row_lines, row_lines, tiles_lines, tiles_lines],
            ) + relayout(target_state)
        else:
            flux, perturbation = lax.optimization_barrier((flux, perturbation))
            beside = relayout(perturbation)
        flux = exchange(flux, devices)
        edges = swap(*sends)
        if last:
            flux, *edges = lax.optimization_barrier((flux, *edges))
        flux, *beside = lax.optimization_barrier((flux, *beside))
        if first:
            diffusivity_rows, weight_rows, diffusivity_tiles, weight_tiles, target = beside
        else:
            start_field = beside[0]
        inputs = near_by(flux, *got) + fetched(surface) + scalars(tables, weights)
        if last:
            surface, slope, packed, *sends = call(
                functools.partial(surface_kernel, sz, True),
                "surface",
                inputs + fetched(target_state, at=(0,)) + fetched(weight_tiles),
                shipped=[sz.surface, sz.slope, sz.wide, sz.lats, sz.lats],
                scratch=near,
            )
        else:
            surface, *sends, slope = call(
                functools.partial(surface_kernel, sz, False),
                "surface",
                inputs,
                kept=[sz.surface, row_surface, row_surface],
                shipped=[sz.slope],
                scratch=near,
            )
            surface_edges = swap(*sends)
        saved.append((drive, slope, mixed_slope, flux_slope))

    edge_sends = None
    for hour in reversed(range(hours)):
        drive, slope, mixed_slope, flux_slope = saved[hour]
        arrived = exchange(packed, devices)
        got = swap(*sends)
        arrived, *got = lax.optimization_barrier((arrived, *got))
        back = call(
            functools.partial(owner_back_kernel, sz),
            "owners_back",
            near_by(arrived, owner_mix[0]) + fetched(mixed_slope, flux_slope) + scalars(facts),
            shipped=[sz.narrow],
            scratch=[sz.narrow, by_slot],
        )[0]
        if edge_sends is not None:
            back, *edge_sends = lax.optimization_barrier((back, *edge_sends))
            edges = swap(*edge_sends)
        back = exchange(back, devices)
        surface, *row_sends = call(
            functools.partial(merge_kernel, sz),
            "merge",
            near_by(back, *got)
            + fetched(surface, slope)
            + scalars(table, facts)
            + fetched(diffusivity_tiles),
            kept=[sz.surface, row_surface, row_surface],
        )
        surface_edges = swap(*row_sends)
        last = hour == 0
        mix_here, rows_here, *loaded = call(
            functools.partial(backward_load_kernel, sz, last),
            "step_back_load",
            fetched(mix, diffusivity_rows)
            + far_off(field, drive)
            + near_by(surface)
            + (far_off(start_field) if last else []),
            kept=[mix_shape, row_lines] + [sz.whole] * (4 if last else 3),
            scratch=[row_sems(3)],
        )
        inputs = near_by(*edges, *surface_edges, rows_here, mix_here, *loaded)
        if last:
            gradient, sums = call(
                functools.partial(backward_kernel, sz, True),
                "step_back_sums",
                inputs,
                shipped=[sz.whole, (devices, WIDTH)],
                scratch=[wider],
            )
        else:
            field, surface, packed, *outs = call(
                functools.partial(backward_kernel, sz, False),
                "step_back",
                scalars(tables, weights) + fetched(saved[hour - 1][1]) + inputs,
                shipped=[sz.whole, sz.surface, sz.wide, sz.lats, sz.lats, sz.edge, sz.edge],
                scratch=[wider, *near],
            )
            sends, edge_sends = outs[:2], outs[2:]

    everyones = lax.all_to_all(sums, "horiz", split_axis=0, concat_axis=0, tiled=True)
    block = perturbation.shape
    return call(
        functools.partial(final_kernel, perturbation.size * devices),
        "finish",
        near_by(everyones, perturbation, gradient.transpose(2, 0, 1, 3)),
        shipped=[block],
    )[0]


def solution(mesh):
    placed = (
        P("member", "horiz", None, None),
        P(None, "horiz", None, None),
        P(None, "horiz", None, None),
        P("horiz", None),
        P("horiz", None),
        P(),
        P(),
        P("horiz", None, None),
        P(None, "horiz", None, None),
        P(None, "horiz", None, None),
        P("horiz", None),
        P("horiz", None),
        P("horiz"),
        P("horiz"),
        P("horiz"),
    )
    return jax.shard_map(
        body,
        mesh=mesh,
        in_specs=placed,
        out_specs=P("member", "horiz", None, None),
        check_vma=False,
    )
```

```python
import functools

import jax
import jax.numpy as jnp
from jax import lax
from jax.experimental import pallas as pl
from jax.experimental.pallas import tpu as pltpu
from jax.sharding import PartitionSpec as P

LAT_DEV = 2
NEAR_LAT = LAT_DEV + 2
CHANNELS = 4
LEVELS = 8
WIDTH = 128
SUBLANES = 8

KAPPA_V = 0.1
TIME_STEP = 0.3
FLUX_RATE = 0.05
FEEDBACK = 0.5
ASCENT = 0.5
EPSILON = 1e-06
HIGHEST = lax.Precision.HIGHEST
VMEM_BYTES = 32 * 1024 * 1024


class Sizes:
    def __init__(self, devices, capacity, rows, cells):
        self.devices = devices
        self.capacity = capacity
        self.slots = devices * capacity
        self.rows = rows
        self.cells = cells
        self.row_tiles = cells // WIDTH
        self.tiles = rows * self.row_tiles
        self.row_width = CHANNELS * self.row_tiles
        self.pitch = -(-self.row_tiles // SUBLANES) * SUBLANES
        self.own_rows = CHANNELS * capacity
        self.chunk = self.own_rows + 2 * capacity
        self.slot_lines = -(-self.slots // WIDTH)
        self.facts = -(-(self.slot_lines + 1) // SUBLANES) * SUBLANES
        self.lat_lines = LAT_DEV * self.pitch
        self.edge_lines = CHANNELS * self.row_tiles * LEVELS
        self.whole = (rows, CHANNELS, LEVELS, cells)
        self.edge = (self.edge_lines, WIDTH)
        self.told = (self.lat_lines + self.facts, WIDTH)
        self.surface = (CHANNELS * (self.tiles + 1), WIDTH)
        self.narrow = (CHANNELS * self.slots, WIDTH)
        self.wide = (devices * self.chunk, WIDTH)
        self.slope = (NEAR_LAT * self.pitch, WIDTH)
        self.lats = (self.lat_lines, WIDTH)
        self.bulk_at = NEAR_LAT * rows
        self.drive_at = self.bulk_at + CHANNELS * CHANNELS
        self.tables = (3 * self.slot_lines, WIDTH)
        self.weights = (3 * self.facts, WIDTH)
        self.near = (-(-(self.tiles + 1) // SUBLANES) * SUBLANES, WIDTH)
        self.by_slot = (CHANNELS, self.slots, WIDTH)


class Shipped:
    def __init__(self, block, home, sems):
        self.block, self.home, self.sems = block, home, sems
        self.by_row = False
        self.started = False

    def __getitem__(self, at):
        return self.block[at]

    def __setitem__(self, at, value):
        self.block[at] = value

    def row(self, index):
        self.by_row = True
        self.started = True
        return pltpu.make_async_copy(
            self.block.at[index], self.home.at[index], self.sems.at[index]
        )

    def all(self):
        return pltpu.make_async_copy(self.block, self.home, self.sems.at[0])

    def start(self):
        self.started = True
        self.all().start()

    def finish(self, rows):
        if self.by_row:
            for index in range(rows):
                self.row(index).wait()
        else:
            self.all().wait()


def cols(tile):
    return slice(tile * WIDTH, (tile + 1) * WIDTH)


def lanes_sum(left_here, left_before, right_here, right_after, lane):
    return jnp.where(lane == 0, left_before, left_here) + jnp.where(
        lane == WIDTH - 1, right_after, right_here
    )


def levels_sum(field, sub):
    return jnp.where(sub == 0, 0.0, pltpu.roll(field, 1, 0)) + jnp.where(
        sub == LEVELS - 1, 0.0, pltpu.roll(field, LEVELS - 1, 0)
    )


def row_tiles_of(sz, ref, row):
    return ref[pl.ds(row * sz.row_width, sz.row_tiles, stride=CHANNELS), :]


def put_row_tiles(sz, ref, row, value):
    ref[pl.ds(row * sz.row_width, sz.row_tiles, stride=CHANNELS), :] = value


def near_row(sz, ref, row):
    return ref[row * sz.row_tiles : (row + 1) * sz.row_tiles, :]


def high_first():
    return 1 - lax.rem(lax.axis_index("horiz").astype(jnp.int32), 2)


def pick(flag, one, other):
    return jnp.where(jnp.full(one.shape, flag, jnp.int32) == 1, one, other)


def sided(first, second):
    flag = high_first()
    return pick(flag, second, first), pick(flag, first, second)


def load_surface_row(sz, target, row, source, base):
    for tile in range(sz.row_tiles):
        for channel in range(CHANNELS):
            at = base + tile * CHANNELS + channel
            target[row, channel, 0:1, cols(tile)] = source[pl.ds(at, 1), :]


def as_column(row, size):
    shape = (size, row.shape[1])
    diagonal = lax.broadcasted_iota(jnp.int32, shape, 0) == lax.broadcasted_iota(jnp.int32, shape, 1)
    return jnp.sum(jnp.where(diagonal, row, 0.0), axis=1, keepdims=True)


def setup_kernel(sz, entries, remap_entries, arrive, wet, remap, mix_rows, diffusivity, weight, *outs):
    first_tiles, table, facts, mix, diffusivity_rows, weight_rows = outs
    arrive_all(arrive)
    for row in range(sz.rows):
        diffusivity_rows[row] = diffusivity[row : row + 1, :]
        weight_rows[row] = weight[row : row + 1, :]
        for tile in range(sz.row_tiles):
            at = row * sz.pitch + tile
            first_tiles[at : at + 1, :] = diffusivity[row : row + 1, cols(tile)]
    diffusivity_rows.start()
    weight_rows.start()
    for index in range(CHANNELS * CHANNELS):
        column = as_column(mix_rows[index : index + 1, :], LEVELS)
        mix[index] = jnp.broadcast_to(column, (LEVELS, WIDTH))
    mix.start()
    tiles, owners = wet[0:1, :], wet[1:2, :]
    size = -(-entries // SUBLANES) * SUBLANES
    shape = (size, wet.shape[1])
    tile_here, owner_here = as_column(tiles, size), as_column(owners, size)
    earlier = lax.broadcasted_iota(jnp.int32, shape, 1) < lax.broadcasted_iota(jnp.int32, shape, 0)
    same = (owner_here == owners) & earlier
    rank = jnp.sum(jnp.where(same, 1.0, 0.0), axis=1, keepdims=True)
    slot = jnp.where(owner_here >= 0.0, owner_here * sz.capacity + rank, -1.0)
    facts[...] = jnp.zeros((sz.facts, WIDTH), jnp.float32)
    for line in range(sz.slot_lines):
        place = lax.broadcasted_iota(jnp.int32, (size, WIDTH), 1) + line * WIDTH
        match = slot.astype(jnp.int32) == place
        told = jnp.sum(jnp.where(match, sz.tiles - tile_here, 0.0), axis=0, keepdims=True)
        facts[line : line + 1, :] = told
        table[line : line + 1, :] = sz.tiles - told.astype(jnp.int32)
    size = -(-remap_entries // SUBLANES) * SUBLANES
    at, amount = as_column(remap[0:1, :], size), as_column(remap[1:2, :], size)
    place = lax.broadcasted_iota(jnp.int32, (size, WIDTH), 1)
    facts[sz.slot_lines : sz.slot_lines + 1, :] = jnp.sum(
        jnp.where(at.astype(jnp.int32) == place, amount, 0.0), axis=0, keepdims=True
    )


def columns_kernel(sz, arrive, diffusivity, weight, diffusivity_tiles, weight_tiles):
    arrive_all(arrive)
    for source, by_tile in ((diffusivity, diffusivity_tiles), (weight, weight_tiles)):
        for row in range(sz.rows):
            for tile in range(sz.row_tiles):
                line = source[row : row + 1, cols(tile)]
                at = (row * sz.row_tiles + tile) * CHANNELS
                by_tile[at : at + CHANNELS, :] = jnp.broadcast_to(line, (CHANNELS, WIDTH))


def front_load_kernel(sz, arrive, perturbation, base, level_0, level_1, send_first, send_second):
    arrive_all(arrive)
    for level, out in ((0, level_0), (1, level_1)):
        for row in range(sz.rows):
            for tile in range(sz.row_tiles):
                at = (row * sz.row_tiles + tile) * CHANNELS
                out[at : at + CHANNELS, :] = (
                    perturbation[level, row, :, cols(tile)] + base[level, row, :, cols(tile)]
                )
        out[CHANNELS * sz.tiles :, :] = jnp.zeros((CHANNELS, WIDTH), jnp.float32)
    store_rows(sz, level_0, send_first, send_second)


def front_kernel(sz, arrive, tables, facts, facts_block, level_0, level_1, first, second, diffusivity, *refs):
    new_surface, packed, tell_first, tell_second, before, after = refs
    arrive_all(arrive)
    count, pitch = sz.row_tiles, sz.pitch
    lane = lax.broadcasted_iota(jnp.int32, (count, WIDTH), 1)

    def part(ref, row, channel, size=count):
        return ref[pl.ds(row * sz.row_width + channel, size, stride=CHANNELS), :]

    beside = [sided(part(first, 0, c), part(second, 0, c)) for c in range(CHANNELS)]
    for row in range(sz.rows):
        coeff = diffusivity[row * pitch : row * pitch + count, :]
        center = (1.0 - 2.0 * KAPPA_V) - 4.0 * coeff
        here = [part(level_0, row, c) for c in range(CHANNELS)]
        for c in range(CHANNELS):
            weights = [facts[sz.slot_lines, sz.drive_at + c * CHANNELS + k] for k in range(CHANNELS)]
            bent = jnp.tanh(sum_of(weights, here))
            up = part(level_0, row - 1, c) if row > 0 else beside[c][0]
            down = part(level_0, row + 1, c) if row < sz.rows - 1 else beside[c][1]
            index = row * CHANNELS + c
            full = part(level_0, row, c, pitch)
            left = pltpu.roll(full, 1, 1)[0:count, :]
            right = pltpu.roll(full, WIDTH - 1, 1)[0:count, :]
            before[index, 1 : count + 1, :] = left
            before[index, 0:1, :] = left[count - 1 : count, :]
            after[index, 0:count, :] = right
            after[index, count : count + 1, :] = right[0:1, :]
            around = lanes_sum(
                left, before[index, 0:count, :], right, after[index, 1 : count + 1, :], lane
            )
            around = around + (up + down)
            stepped = (
                center * here[c]
                + coeff * around
                + KAPPA_V * part(level_1, row, c)
                + TIME_STEP * bent
            )
            new_surface.block[pl.ds(row * sz.row_width + c, count, stride=CHANNELS), :] = stepped
    share_surface(sz, tables, facts, new_surface, packed, tell_first, tell_second, facts_block)


def gather_levels(block, channel, tile):
    sub = lax.broadcasted_iota(jnp.int32, (LEVELS, WIDTH), 0)
    total = None
    for level in range(LEVELS):
        line = block[level, channel : channel + 1, cols(tile)]
        line = jnp.broadcast_to(line, (LEVELS, WIDTH))
        total = line if total is None else jnp.where(sub == level, line, total)
    return total


def edges_kernel(sz, arrive, low_start, high_start, low_base, high_base, send_first, send_second):
    arrive_all(arrive)
    low_start[...] = low_start[...] + low_base[...]
    high_start[...] = high_start[...] + high_base[...]
    flag = high_first()
    for channel in range(CHANNELS):
        for tile in range(sz.row_tiles):
            low = gather_levels(low_start, channel, tile)
            high = gather_levels(high_start, channel, tile)
            at = (channel * sz.row_tiles + tile) * LEVELS
            send_first[at : at + LEVELS, :] = pick(flag, high, low)
            send_second[at : at + LEVELS, :] = pick(flag, low, high)


def load_kernel(sz, arrive, perturbation, base, field, start_block, base_block, in_sems):
    def arrivals(row):
        return [
            pltpu.make_async_copy(source.at[:, row], block.at[row], in_sems.at[index, row])
            for index, (source, block) in enumerate(
                ((perturbation, start_block), (base, base_block))
            )
        ]

    for row in range(sz.rows):
        for arrival in arrivals(row):
            arrival.start()

    def one_row(row, carry):
        for arrival in arrivals(row):
            arrival.wait()
        start_block[row] = start_block[row] + base_block[row]
        for channel in range(CHANNELS):
            for tile in range(sz.row_tiles):
                field[row, channel, :, cols(tile)] = gather_levels(
                    start_block.at[row], channel, tile
                )
        return carry

    lax.fori_loop(0, sz.rows, one_row, 0)


def relayout_kernel(sz, arrive, source, out, block, in_sems):
    def arrival(row):
        return pltpu.make_async_copy(source.at[:, row], block.at[row], in_sems.at[0, row])

    for row in range(sz.rows):
        arrival(row).start()

    def one_row(row, carry):
        arrival(row).wait()
        for channel in range(CHANNELS):
            for tile in range(sz.row_tiles):
                out[row, channel, :, cols(tile)] = gather_levels(block.at[row], channel, tile)
        out.row(row).start()
        return carry

    lax.fori_loop(0, sz.rows, one_row, 0)


class Remap:
    def __init__(self, sz, weights):
        self.sz, self.weights = sz, weights

    def weight(self, which, lat, row):
        line = which * self.sz.facts + self.sz.slot_lines
        return self.weights[line, lat * self.sz.rows + row]

    def own(self, lat, row):
        return self.weight(0, lat, row)

    def of_low(self, lat, row):
        return self.weight(1, lat + LAT_DEV, row)

    def of_high(self, lat, row):
        return self.weight(2, lat - LAT_DEV, row)


def tile_at(sz, tables, which, slot):
    return tables[which * sz.slot_lines + slot // WIDTH, slot % WIDTH]


def sum_of(weights, values):
    total = weights[0] * values[0]
    for weight, value in zip(weights[1:], values[1:]):
        total = total + weight * value
    return total


def own_sums(sz, remap, own, factor):
    return [
        factor * sum_of([remap.own(lat, row) for row in range(sz.rows)], own)
        for lat in range(NEAR_LAT)
    ]


def send_sums(sz, sums, tell_first, tell_second):
    flag = high_first()
    for index in range(LAT_DEV):
        low, high = sums[index], sums[LAT_DEV + index]
        at = index * sz.pitch
        tell_first[at : at + sz.row_tiles, :] = pick(flag, high, low)
        tell_second[at : at + sz.row_tiles, :] = pick(flag, low, high)


def lat_rows(sz, ref, lat):
    at = lat * sz.pitch
    return ref[at : at + sz.row_tiles, :]


def told_sums(sz, from_first, from_second):
    lows, highs = [], []
    for index in range(LAT_DEV):
        low, high = sided(lat_rows(sz, from_first, index), lat_rows(sz, from_second, index))
        lows.append(low)
        highs.append(high)
    return lows + highs


def place_edges(sz, padded, first, second, first_surface=None, second_surface=None):
    side = high_first() * (sz.rows + 1)
    for at, edge, surface in ((side, first, first_surface), (sz.rows + 1 - side, second, second_surface)):
        for channel in range(CHANNELS):
            for tile in range(sz.row_tiles):
                line = (channel * sz.row_tiles + tile) * LEVELS
                padded[at, channel, :, cols(tile)] = edge[line : line + LEVELS, :]
        if surface is not None:
            load_surface_row(sz, padded, at, surface, 0)


def store_rows(sz, surface, send_first, send_second, factor=None):
    row = high_first() * (sz.rows - 1)
    for at, send in ((row, send_first), (sz.rows - 1 - row, send_second)):
        for tile in range(sz.row_tiles):
            start = pl.multiple_of((at * sz.row_tiles + tile) * CHANNELS, CHANNELS)
            value = surface[pl.ds(start, CHANNELS), :]
            if factor is not None:
                value = factor[pl.ds(start, CHANNELS), :] * value
            send[tile * CHANNELS : (tile + 1) * CHANNELS, :] = value


def forward_load_kernel(sz, last, arrive, mix, diffusivity, *refs):
    refs = list(refs)
    if last:
        weight = refs.pop(0)
    field, surface = refs[:2]
    refs = refs[2:]
    if last:
        target = refs.pop(0)
    mix_out, rows_out, field_out = refs[:3]
    refs = refs[3:]
    if last:
        weight_out, target_out = refs[:2]
        refs = refs[2:]
    in_sems = refs[0]

    def arrivals(row):
        copies = [pltpu.make_async_copy(field.at[row], field_out.at[row], in_sems.at[0, row])]
        if last:
            copies.append(
                pltpu.make_async_copy(target.at[:, row], refs[1].at[row], in_sems.at[1, row])
            )
        return copies

    for row in range(sz.rows):
        for arrival in arrivals(row):
            arrival.start()
    arrive_all(arrive)
    mix_out[...] = mix[...]
    rows_out[...] = diffusivity[...]
    if last:
        weight_out[...] = weight[...]

    def one_row(row, carry):
        for arrival in arrivals(row):
            arrival.wait()
        load_surface_row(sz, field_out, row, surface, row * sz.row_width)
        if last:
            for c in range(CHANNELS):
                for t in range(sz.row_tiles):
                    target_out[row, c, :, cols(t)] = gather_levels(refs[1].at[row], c, t)
        return carry

    lax.fori_loop(0, sz.rows, one_row, 0)


def forward_kernel(sz, first, last, arrive, *refs):
    refs = list(refs)
    if not first:
        tables, facts = refs[:2]
        refs = refs[2:]
    low, high, diffusivity, mix, field = refs[:5]
    refs = refs[5:]
    surfaces = ()
    if not first:
        surfaces = refs[:2]
        refs = refs[2:]
    else:
        arrive_all(arrive)
    if last:
        weight, target = refs[:2]
        refs = refs[2:]
    out, drive, *refs = refs
    if not first:
        new_surface, packed, tell_first, tell_second = refs[:4]
        refs = refs[4:]
    edge_first, edge_second, padded = refs
    place_edges(sz, padded, low, high, *surfaces)

    def ready(row):
        padded[row + 1] = field[row]

    ready(0)
    lane = lax.broadcasted_iota(jnp.int32, (LEVELS, WIDTH), 1)
    sub = lax.broadcasted_iota(jnp.int32, (LEVELS, WIDTH), 0)
    count = sz.row_tiles

    def one_row(row, carry):
        @pl.when(row < sz.rows - 1)
        def _():
            ready(row + 1)

        here = [[padded[row + 1, c, :, cols(t)] for t in range(count)] for c in range(CHANNELS)]
        for t in range(count):
            coeff = jnp.broadcast_to(diffusivity[row, 0:1, cols(t)], (LEVELS, WIDTH))
            center = (1.0 - 2.0 * KAPPA_V) - 4.0 * coeff
            if last:
                scale = weight[row, 0:1, cols(t)]
                scale = jnp.broadcast_to(scale * scale, (LEVELS, WIDTH))
            for c in range(CHANNELS):
                mixed = mix[c * CHANNELS] * here[0][t]
                for k in range(1, CHANNELS):
                    mixed = mixed + mix[c * CHANNELS + k] * here[k][t]
                bent = jnp.tanh(mixed)
                drive[row, c, :, cols(t)] = bent
                field_here = here[c][t]
                around = lanes_sum(
                    pltpu.roll(field_here, 1, 1),
                    pltpu.roll(here[c][(t - 1) % count], 1, 1),
                    pltpu.roll(field_here, WIDTH - 1, 1),
                    pltpu.roll(here[c][(t + 1) % count], WIDTH - 1, 1),
                    lane,
                )
                around = around + (padded[row, c, :, cols(t)] + padded[row + 2, c, :, cols(t)])
                stepped = (
                    center * field_here
                    + coeff * around
                    + KAPPA_V * levels_sum(field_here, sub)
                    + TIME_STEP * bent
                )
                if not first:
                    at = (row * count + t) * CHANNELS + c
                    new_surface[pl.ds(at, 1), :] = stepped[0:1, :]
                if last:
                    stepped = scale * (stepped - target[row, c, :, cols(t)])
                out[row, c, :, cols(t)] = stepped
        drive.row(row).start()
        out.row(row).start()
        return carry

    lax.fori_loop(0, sz.rows, one_row, 0)
    if not first:
        arrive_all(arrive)
        share_surface(sz, tables, facts, new_surface, packed, tell_first, tell_second)
    store_edges(sz, out, diffusivity if last else None, edge_first, edge_second)


def share_surface(sz, tables, facts, surface, packed, tell_first, tell_second, facts_block=None):
    remap = Remap(sz, facts)
    surface[CHANNELS * sz.tiles :, :] = jnp.zeros((CHANNELS, WIDTH), jnp.float32)
    surface.start()
    pack_slots(sz, tables, surface, packed)
    packed.start()
    own = [row_tiles_of(sz, surface.block, row) for row in range(sz.rows)]
    send_sums(sz, own_sums(sz, remap, own, 1.0), tell_first, tell_second)
    for tell in (tell_first, tell_second):
        if facts_block is not None:
            tell[sz.lat_lines :, :] = facts_block[...]
        tell.start()


def pack_slots(sz, tables, surface, packed):
    for slot in range(sz.slots):
        at = pl.multiple_of(tile_at(sz, tables, 0, slot) * CHANNELS, CHANNELS)
        packed[slot * CHANNELS : (slot + 1) * CHANNELS, :] = surface[pl.ds(at, CHANNELS), :]


def store_edges(sz, field, diffusivity, send_first, send_second):
    outer = high_first() * (sz.rows - 1)
    for row, send in ((outer, send_first), (sz.rows - 1 - outer, send_second)):
        for channel in range(CHANNELS):
            for tile in range(sz.row_tiles):
                value = field[row, channel, :, cols(tile)]
                if diffusivity is not None:
                    value = value * jnp.broadcast_to(
                        diffusivity[row, 0:1, cols(tile)], (LEVELS, WIDTH)
                    )
                at = (channel * sz.row_tiles + tile) * LEVELS
                send[at : at + LEVELS, :] = value
        send.start()


def owner_kernel(sz, decode, arrive, arrived, mixing, air, wind, facts, *refs):
    slots = sz.slots
    if decode:
        told_first, told_second, own_table, own_facts, tables, weights = refs[:6]
        refs = refs[6:]
    flux, mixed_slope, flux_slope, flat, first = refs
    if decode:
        arrive_all(arrive)
        lines = sz.slot_lines
        tables[0:lines, :] = own_table[...]
        weights[0 : sz.facts, :] = own_facts[...]
        both = sided(told_first[sz.lat_lines :, :], told_second[sz.lat_lines :, :])
        for which, told in ((1, both[0]), (2, both[1])):
            got = told[0:lines, :].astype(jnp.int32)
            tables[which * lines : (which + 1) * lines, :] = sz.tiles - got
            at = which * sz.facts
            weights[at : at + sz.facts, :] = told
        tables.start()
        weights.start()

    def bulk(row, column):
        return facts[sz.slot_lines, sz.bulk_at + row * CHANNELS + column]

    values = [arrived[pl.ds(c, slots, stride=CHANNELS), :] for c in range(CHANNELS)]
    mixed = jnp.tanh(
        jnp.dot(
            mixing[...],
            jnp.concatenate(values, axis=1),
            precision=HIGHEST,
            preferred_element_type=jnp.float32,
        )
    )
    contrast = []
    for c in range(CHANNELS):
        mixed_here = mixed[:, cols(c)]
        mixed_slope[c] = 1.0 - mixed_here * mixed_here
        contrast.append((air[...] - values[0] if c == 0 else values[c]) + mixed_here)
    mixed_slope.start()
    if not decode:
        arrive_all(arrive)
    rate = FLUX_RATE * wind[...]
    for c in range(CHANNELS):
        forcing = bulk(c, 0) * contrast[0]
        for k in range(1, CHANNELS):
            forcing = forcing + bulk(c, k) * contrast[k]
        bent = jnp.tanh(forcing)
        flux_slope[c] = rate * (1.0 - bent * bent)
        one = rate * bent
        flat[pl.ds(c, slots, stride=CHANNELS), :] = one
        if c == 0:
            first[...] = one
    flux_slope.start()
    cap = sz.capacity
    gap = jnp.zeros((sz.chunk - sz.own_rows, WIDTH), jnp.float32)
    for d in range(sz.devices):
        at = d * sz.chunk
        flux[at : at + sz.own_rows, :] = flat[d * sz.own_rows : (d + 1) * sz.own_rows, :]
        at = at + sz.own_rows
        flux[at : (d + 1) * sz.chunk, :] = gap
        if d > 0:
            flux[at : at + cap, :] = first[(d - 1) * cap : d * cap, :]
        if d < sz.devices - 1:
            flux[at + cap : at + 2 * cap, :] = first[(d + 1) * cap : (d + 2) * cap, :]


def owner_back_kernel(sz, arrive, arrived, mixing, mixed_slope, flux_slope, facts, back, flat, extra):
    slots, cap = sz.slots, sz.capacity

    def bulk(row, column):
        return facts[sz.slot_lines, sz.bulk_at + row * CHANNELS + column]

    for d in range(sz.devices):
        at = d * sz.chunk
        flat[d * sz.own_rows : (d + 1) * sz.own_rows, :] = arrived[at : at + sz.own_rows, :]
        more = jnp.zeros((cap, WIDTH), jnp.float32)
        if d < sz.devices - 1:
            at = (d + 1) * sz.chunk + sz.own_rows
            more = more + arrived[at : at + cap, :]
        if d > 0:
            at = (d - 1) * sz.chunk + sz.own_rows + cap
            more = more + arrived[at : at + cap, :]
        extra[d * cap : (d + 1) * cap, :] = more
    arrive_all(arrive)
    forced = []
    for c in range(CHANNELS):
        got = flat[pl.ds(c, slots, stride=CHANNELS), :]
        if c == 0:
            got = got + extra[...]
        forced.append(flux_slope[c] * got)
    direct = []
    for k in range(CHANNELS):
        total = bulk(0, k) * forced[0]
        for c in range(1, CHANNELS):
            total = total + bulk(c, k) * forced[c]
        direct.append(total)
    through = lax.dot_general(
        mixing[...],
        jnp.concatenate([direct[k] * mixed_slope[k] for k in range(CHANNELS)], axis=1),
        (((0,), (0,)), ((), ())),
        precision=HIGHEST,
        preferred_element_type=jnp.float32,
    )
    for k in range(CHANNELS):
        sign = -1.0 if k == 0 else 1.0
        back.block[pl.ds(k, slots, stride=CHANNELS), :] = through[:, cols(k)] + sign * direct[k]


def spread_back(sz, surface, slope, remap, tables, packed, near_low, near_high, tell_first, tell_second):
    rows, count, cap = sz.rows, sz.row_tiles, sz.capacity
    block = surface.block
    own = [row_tiles_of(sz, block, row) for row in range(rows)]
    sums = own_sums(sz, remap, own, FEEDBACK)
    send_sums(sz, sums, tell_first, tell_second)
    tell_first.start()
    tell_second.start()
    lats = [lat_rows(sz, slope, lat) * sums[lat] for lat in range(NEAR_LAT)]
    every = range(NEAR_LAT)
    for row in range(rows):
        added = sum_of([remap.own(lat, row) for lat in every], lats)
        put_row_tiles(sz, block, row, own[row] + added)
        at = row * count
        near_low[at : at + count, :] = sum_of(
            [remap.of_low(lat, row) for lat in range(LAT_DEV)], lats[:LAT_DEV]
        )
        near_high[at : at + count, :] = sum_of(
            [remap.of_high(lat, row) for lat in range(LAT_DEV, NEAR_LAT)], lats[LAT_DEV:]
        )
    rest = sz.near[0] - sz.tiles
    near_low[sz.tiles :, :] = jnp.zeros((rest, WIDTH), jnp.float32)
    near_high[sz.tiles :, :] = jnp.zeros((rest, WIDTH), jnp.float32)
    surface.start()
    gap = jnp.zeros((sz.chunk - sz.own_rows, WIDTH), jnp.float32)
    for owner in range(sz.devices):
        packed[owner * sz.chunk + sz.own_rows : (owner + 1) * sz.chunk, :] = gap
    for slot in range(sz.slots):
        owner, rank = slot // cap, slot % cap
        at = owner * sz.chunk + rank * CHANNELS
        tile = pl.multiple_of(tile_at(sz, tables, 0, slot) * CHANNELS, CHANNELS)
        packed[at : at + CHANNELS, :] = surface[pl.ds(tile, CHANNELS), :]
        at = owner * sz.chunk + sz.own_rows + rank
        packed[at : at + 1, :] = near_low[pl.ds(tile_at(sz, tables, 1, slot), 1), :]
        at = at + cap
        packed[at : at + 1, :] = near_high[pl.ds(tile_at(sz, tables, 2, slot), 1), :]


def surface_kernel(sz, last, arrive, *refs):
    refs = list(refs)
    flux, from_first, from_second, before, tables, weights = refs[:6]
    refs = refs[6:]
    if last:
        target, weight = refs[:2]
        surface, slope, packed, tell_first, tell_second, near_low, near_high = refs[2:]
        block = surface.block
    else:
        surface, send_first, send_second, slope, near_low, near_high = refs
        block = surface
    remap = Remap(sz, weights)
    arrive_all(arrive)
    rows, cap = sz.rows, sz.capacity
    block[...] = before[...]
    near_low[...] = jnp.zeros(sz.near, jnp.float32)
    near_high[...] = jnp.zeros(sz.near, jnp.float32)
    for slot in range(sz.slots):
        owner, rank = slot // cap, slot % cap
        at = owner * sz.chunk + rank * CHANNELS
        tile = pl.multiple_of(tile_at(sz, tables, 0, slot) * CHANNELS, CHANNELS)
        block[pl.ds(tile, CHANNELS), :] = (
            before[pl.ds(tile, CHANNELS), :] + flux[at : at + CHANNELS, :]
        )
        at = owner * sz.chunk + sz.own_rows + rank
        near_low[pl.ds(tile_at(sz, tables, 1, slot), 1), :] = flux[at : at + 1, :]
        at = at + cap
        near_high[pl.ds(tile_at(sz, tables, 2, slot), 1), :] = flux[at : at + 1, :]
    block[CHANNELS * sz.tiles :, :] = jnp.zeros((CHANNELS, WIDTH), jnp.float32)
    own = [row_tiles_of(sz, block, row) for row in range(rows)]
    sums = own_sums(sz, remap, own, 1.0)
    told = told_sums(sz, from_first, from_second)
    air = []
    for lat in range(NEAR_LAT):
        if lat < LAT_DEV:
            near, weights = near_low, [remap.of_low(lat, row) for row in range(rows)]
        else:
            near, weights = near_high, [remap.of_high(lat, row) for row in range(rows)]
        more = sum_of(weights, [near_row(sz, near, row) for row in range(rows)])
        one = jnp.tanh(sums[lat] + told[lat] + more)
        slope[lat * sz.pitch : lat * sz.pitch + sz.row_tiles, :] = 1.0 - one * one
        air.append(one)
    slope.start()
    for row in range(rows):
        weights = [remap.own(lat, row) for lat in range(NEAR_LAT)]
        put_row_tiles(sz, block, row, own[row] + FEEDBACK * sum_of(weights, air))
    if last:
        for row in range(rows):
            for tile in range(sz.row_tiles):
                at = row * sz.row_width + tile * CHANNELS
                scale = weight[at : at + CHANNELS, :]
                off = block[at : at + CHANNELS, :] - target[row, :, cols(tile)]
                block[at : at + CHANNELS, :] = scale * scale * off
        spread_back(
            sz, surface, slope, remap, tables, packed, near_low, near_high, tell_first, tell_second
        )
    else:
        store_rows(sz, surface, send_first, send_second)


def merge_kernel(
    sz, arrive, back, from_first, from_second, before, slope, tables, facts, diffusivity, surface, send_first, send_second
):
    rows = sz.rows
    remap = Remap(sz, facts)
    arrive_all(arrive)
    surface[...] = before[...]
    for slot in range(sz.slots):
        tile = pl.multiple_of(tile_at(sz, tables, 0, slot) * CHANNELS, CHANNELS)
        surface[pl.ds(tile, CHANNELS), :] = (
            before[pl.ds(tile, CHANNELS), :] + back[slot * CHANNELS : (slot + 1) * CHANNELS, :]
        )
    surface[CHANNELS * sz.tiles :, :] = jnp.zeros((CHANNELS, WIDTH), jnp.float32)
    told = told_sums(sz, from_first, from_second)
    lats = [lat_rows(sz, slope, lat) * told[lat] for lat in range(NEAR_LAT)]
    for row in range(rows):
        own = row_tiles_of(sz, surface, row)
        weights = [remap.own(lat, row) for lat in range(NEAR_LAT)]
        put_row_tiles(sz, surface, row, own + sum_of(weights, lats))
    store_rows(sz, surface, send_first, send_second, diffusivity)


def backward_load_kernel(sz, last, arrive, mix, diffusivity, field, drive, surface, *refs):
    refs = list(refs)
    if last:
        perturbation = refs.pop(0)
    mix_out, rows_out, local, bent_all, scaled = refs[:5]
    refs = refs[5:]
    if last:
        start_all = refs.pop(0)
    in_sems = refs[0]

    def arrivals(row):
        copies = [
            pltpu.make_async_copy(field.at[row], local.at[row], in_sems.at[0, row]),
            pltpu.make_async_copy(drive.at[row], bent_all.at[row], in_sems.at[1, row]),
        ]
        if last:
            copies.append(
                pltpu.make_async_copy(perturbation.at[row], start_all.at[row], in_sems.at[2, row])
            )
        return copies

    for row in range(sz.rows):
        for arrival in arrivals(row):
            arrival.start()
    arrive_all(arrive)
    mix_out[...] = mix[...]
    rows_out[...] = diffusivity[...]

    def one_row(row, carry):
        for arrival in arrivals(row):
            arrival.wait()
        load_surface_row(sz, local, row, surface, row * sz.row_width)
        for t in range(sz.row_tiles):
            coeff = jnp.broadcast_to(diffusivity[row, 0:1, cols(t)], (LEVELS, WIDTH))
            for c in range(CHANNELS):
                scaled[row, c, :, cols(t)] = coeff * local[row, c, :, cols(t)]
        return carry

    lax.fori_loop(0, sz.rows, one_row, 0)


def backward_kernel(sz, last, arrive, *refs):
    refs = list(refs)
    if not last:
        tables, weights, slope = refs[:3]
        refs = refs[3:]
    low, high, first_surface, second_surface, diffusivity, mix = refs[:6]
    local, bent_all, scaled_all = refs[6:9]
    refs = refs[9:]
    if last:
        start_all, out, sums, padded = refs
    else:
        out, new_surface, packed, tell_first, tell_second, edge_first, edge_second = refs[:7]
        padded, near_low, near_high = refs[7:]
        remap = Remap(sz, weights)
    count = sz.row_tiles
    place_edges(sz, padded, low, high, first_surface, second_surface)

    def ready(row):
        padded[row + 1] = scaled_all[row]

    ready(0)
    lane = lax.broadcasted_iota(jnp.int32, (LEVELS, WIDTH), 1)
    sub = lax.broadcasted_iota(jnp.int32, (LEVELS, WIDTH), 0)

    def one_row(row, carry):
        @pl.when(row < sz.rows - 1)
        def _():
            ready(row + 1)

        scaled = [[padded[row + 1, c, :, cols(t)] for t in range(count)] for c in range(CHANNELS)]
        for t in range(count):
            here, bent = [], []
            for c in range(CHANNELS):
                value = local[row, c, :, cols(t)]
                one = bent_all[row, c, :, cols(t)]
                here.append(value)
                bent.append((1.0 - one * one) * value)
            for c in range(CHANNELS):
                mixed = mix[c] * bent[0]
                for k in range(1, CHANNELS):
                    mixed = mixed + mix[k * CHANNELS + c] * bent[k]
                around = lanes_sum(
                    pltpu.roll(scaled[c][t], 1, 1),
                    pltpu.roll(scaled[c][(t - 1) % count], 1, 1),
                    pltpu.roll(scaled[c][t], WIDTH - 1, 1),
                    pltpu.roll(scaled[c][(t + 1) % count], WIDTH - 1, 1),
                    lane,
                )
                around = around + (padded[row, c, :, cols(t)] + padded[row + 2, c, :, cols(t)])
                stepped = (
                    ((1.0 - 2.0 * KAPPA_V) * here[c] - 4.0 * scaled[c][t])
                    + around
                    + KAPPA_V * levels_sum(here[c], sub)
                    + TIME_STEP * mixed
                )
                out[row, c, :, cols(t)] = stepped
                if last:
                    start = start_all[row, c, :, cols(t)]
                    carry = (
                        carry[0] + start * start,
                        carry[1] + start * stepped,
                        carry[2] + stepped * stepped,
                    )
                else:
                    new_surface[pl.ds((row * count + t) * CHANNELS + c, 1), :] = stepped[0:1, :]
        out.row(row).start()
        return carry

    blank = jnp.zeros((LEVELS, WIDTH), jnp.float32)
    totals = lax.fori_loop(0, sz.rows, one_row, (blank, blank, blank) if last else 0)
    if last:
        place = lax.broadcasted_iota(jnp.int32, sums.block.shape, 1)
        held = jnp.zeros(sums.block.shape, jnp.float32)
        for index in range(3):
            total = jnp.sum(jnp.sum(totals[index], axis=0, keepdims=True), axis=1, keepdims=True)
            held = jnp.where(place == index, total, held)
        sums[...] = held
    else:
        new_surface[CHANNELS * sz.tiles :, :] = jnp.zeros((CHANNELS, WIDTH), jnp.float32)
        arrive_all(arrive)
        spread_back(
            sz,
            new_surface,
            slope,
            remap,
            tables,
            packed,
            near_low,
            near_high,
            tell_first,
            tell_second,
        )
        packed.start()
        store_edges(sz, out, diffusivity, edge_first, edge_second)


def final_kernel(cell_total, arrive, everyones, perturbation, gradient, out):
    sums = jnp.sum(everyones[...], axis=0, keepdims=True) / cell_total
    place = lax.broadcasted_iota(jnp.int32, sums.shape, 1)
    means = [
        jnp.broadcast_to(
            jnp.sum(jnp.where(place == index, sums, 0.0), axis=1, keepdims=True), (1, WIDTH)
        )
        for index in range(3)
    ]
    scale = lax.rsqrt(means[2] + EPSILON)
    mean_sq = means[0] + 2.0 * ASCENT * scale * means[1] + ASCENT * ASCENT * scale * scale * means[2]
    shrink = lax.rsqrt(mean_sq + EPSILON)
    step = jnp.broadcast_to(ASCENT * scale * shrink, (CHANNELS, WIDTH))
    shrink = jnp.broadcast_to(shrink, (CHANNELS, WIDTH))
    levels, rows, _, cells = perturbation.shape

    def one_level(level, carry):
        for row in range(rows):
            for tile in range(cells // WIDTH):
                start = perturbation[level, row, :, cols(tile)]
                slope = gradient[level, row, :, cols(tile)]
                out[level, row, :, cols(tile)] = shrink * start + step * slope
        out.row(level).start()
        return carry

    lax.fori_loop(0, levels, one_level, 0)


class Operand:
    def __init__(self, array, space, fetch=None, at=()):
        self.array, self.space, self.fetch, self.at = array, space, fetch, at

    def block(self):
        whole = self.array.shape
        taken = [
            len(range(*index.indices(size)))
            for size, index in zip(whole, self.at)
            if isinstance(index, slice)
        ]
        return self.fetch((*taken, *whole[len(self.at) :]), self.array.dtype)


def near_by(*arrays):
    return [Operand(array, pltpu.VMEM) for array in arrays]


def far_off(*arrays):
    return [
        Operand(pltpu.with_memory_space_constraint(array, pltpu.HBM), pltpu.HBM)
        for array in arrays
    ]


def fetched(*arrays, at=(), into=pltpu.VMEM):
    return [
        Operand(pltpu.with_memory_space_constraint(array, pltpu.HBM), pltpu.HBM, into, at)
        for array in arrays
    ]


def scalars(*arrays):
    return fetched(*arrays, into=pltpu.SMEM)


def call(kernel, name, inputs, kept=(), shipped=(), scratch=()):
    n_in, n_kept, n_out = len(inputs), len(kept), len(shipped)
    brought = [index for index, item in enumerate(inputs) if item.fetch is not None]

    def as_shape(item):
        return item if isinstance(item, jax.ShapeDtypeStruct) else jax.ShapeDtypeStruct(item, jnp.float32)

    kept = [as_shape(item) for item in kept]
    shipped = [as_shape(item) for item in shipped]

    def run(*refs):
        ins = list(refs[:n_in])
        kept_refs = refs[n_in : n_in + n_kept]
        homes = refs[n_in + n_kept : n_in + n_kept + n_out]
        rest = refs[n_in + n_kept + n_out :]
        outs = [
            Shipped(block, home, sems)
            for block, home, sems in zip(rest[:n_out], homes, rest[n_out : 2 * n_out])
        ]
        rest = rest[2 * n_out :]
        if brought:
            blocks, arrive_sems = rest[: len(brought)], rest[len(brought)]
            rest = rest[len(brought) + 1 :]
            copies = []
            for place, (index, block) in enumerate(zip(brought, blocks)):
                source = ins[index]
                if inputs[index].at:
                    source = source.at[inputs[index].at]
                copies.append(pltpu.make_async_copy(source, block, arrive_sems.at[place]))
                ins[index] = block
            for copy in copies:
                copy.start()
            arrive = [copy.wait for copy in copies]
        else:
            arrive = []
        kernel(arrive, *ins, *kept_refs, *outs, *rest)
        for out in outs:
            if not out.started:
                out.start()
        for out in outs:
            out.finish(out.block.shape[0])

    spaces = [pltpu.VMEM] * n_kept + [pltpu.HBM] * n_out
    blocks = [pltpu.VMEM(item.shape, item.dtype) for item in shipped]
    sems = [
        pltpu.SemaphoreType.DMA((item.shape[0] if len(item.shape) > 3 else 1,)) for item in shipped
    ]
    arriving = [inputs[index].block() for index in brought]
    if brought:
        arriving.append(pltpu.SemaphoreType.DMA((len(brought),)))
    more = [
        item if not isinstance(item, tuple) else pltpu.VMEM(item, jnp.float32) for item in scratch
    ]
    return pl.pallas_call(
        run,
        name=name,
        in_specs=[pl.BlockSpec(memory_space=item.space) for item in inputs],
        out_specs=[pl.BlockSpec(memory_space=space) for space in spaces],
        out_shape=kept + [pltpu.HBM(item.shape, item.dtype) for item in shipped],
        scratch_shapes=blocks + sems + arriving + more,
        compiler_params=pltpu.CompilerParams(vmem_limit_bytes=VMEM_BYTES),
    )(*[item.array for item in inputs])


def arrive_all(arrive):
    for wait in arrive:
        wait()


def swap(first, second):
    count = lax.axis_size("horiz")
    inner = [(i, i ^ 1) for i in range(count)]
    outer = [(i, i + 1) for i in range(1, count - 1, 2)]
    outer = outer + [(target, source) for source, target in outer]
    return lax.ppermute(first, "horiz", inner), lax.ppermute(second, "horiz", outer)


def exchange(array, devices):
    rows = array.shape[0] // devices
    step = CHANNELS if rows % CHANNELS == 0 else 2
    split = array.reshape(devices, rows // step, step, WIDTH)
    moved = lax.all_to_all(split, "horiz", split_axis=0, concat_axis=0, tiled=True)
    return moved.reshape(array.shape)


def body(
    perturbation,
    base_state,
    target_state,
    cost_weight,
    diffusivity,
    chan_mix,
    coupler_mix,
    owner_mix,
    air_temp,
    wind_speed,
    wet_list,
    wet_owner,
    remap_src,
    remap_tgt,
    remap_weight,
):
    devices = lax.axis_size("horiz")
    hours = air_temp.shape[0]
    sz = Sizes(devices, air_temp.shape[2] // devices, base_state.shape[1], base_state.shape[3])
    rows = sz.rows
    native_row = (LEVELS, CHANNELS, sz.cells)

    row_surface = (sz.row_width, WIDTH)
    level_0, level_1, *sends = call(
        functools.partial(front_load_kernel, sz),
        "front_load",
        fetched(perturbation, base_state, at=(slice(0, 2),)),
        kept=[sz.surface, sz.surface, row_surface, row_surface],
    )
    surface_edges = swap(*sends)
    me = lax.axis_index("horiz").astype(jnp.int32)

    def lined(first_row, second_row):
        size = -(-first_row.shape[0] // WIDTH) * WIDTH
        pair = jnp.stack([first_row.astype(jnp.float32), second_row.astype(jnp.float32)])
        return jnp.pad(pair, ((0, 0), (0, size - pair.shape[1])), constant_values=-1.0)

    places = jnp.arange(2 * CHANNELS * CHANNELS, dtype=jnp.int32) + sz.bulk_at
    remap_at = (remap_tgt - (me * LAT_DEV - 1)) * rows + remap_src - me * rows
    remap_lines = lined(
        jnp.concatenate([remap_at, places]),
        jnp.concatenate([remap_weight, coupler_mix.reshape(-1), chan_mix[0].reshape(-1)]),
    )
    mix_rows = chan_mix.transpose(1, 2, 0).reshape(CHANNELS * CHANNELS, LEVELS)
    row_lines = (rows, 1, sz.cells)
    tiles_lines = (CHANNELS * sz.tiles, WIDTH)
    first_tiles, table, facts, mix, diffusivity_rows, weight_rows = call(
        functools.partial(setup_kernel, sz, wet_list.shape[1], remap_at.shape[0] + places.shape[0]),
        "setup",
        near_by(lined(wet_list[0], wet_owner[0]), remap_lines, mix_rows)
        + fetched(diffusivity, cost_weight),
        kept=[(rows * sz.pitch, WIDTH)],
        shipped=[
            jax.ShapeDtypeStruct((sz.slot_lines, WIDTH), jnp.int32),
            (sz.facts, WIDTH),
            (CHANNELS * CHANNELS, LEVELS, WIDTH),
            row_lines,
            row_lines,
        ],
    )
    wider = (rows + 2, CHANNELS, LEVELS, sz.cells)
    by_row = (rows, *native_row)

    def row_sems(kinds):
        return pltpu.SemaphoreType.DMA((kinds, rows))

    shifted = (rows * CHANNELS, sz.pitch + SUBLANES, WIDTH)
    surface, packed, *sends = call(
        functools.partial(front_kernel, sz),
        "front",
        scalars(table, facts)
        + fetched(facts)
        + near_by(level_0, level_1, *surface_edges, first_tiles),
        shipped=[sz.surface, sz.narrow, sz.told, sz.told],
        scratch=[shifted, shifted],
    )
    packed, perturbation, base_state = lax.optimization_barrier((packed, perturbation, base_state))
    edge_inputs = []
    for array in (perturbation, base_state):
        for row in (0, rows - 1):
            edge_inputs += fetched(array, at=(slice(None), row))
    edges = swap(
        *call(functools.partial(edges_kernel, sz), "edges", edge_inputs, kept=[sz.edge, sz.edge])
    )

    def relayout(array):
        return call(
            functools.partial(relayout_kernel, sz),
            "relayout",
            far_off(array),
            shipped=[sz.whole],
            scratch=[by_row, row_sems(1)],
        )

    saved = []
    near = [sz.near, sz.near]
    mix_shape = (CHANNELS * CHANNELS, LEVELS, WIDTH)
    by_slot = (sz.slots, WIDTH)
    for hour in range(hours):
        first, last = hour == 0, hour == hours - 1
        assert not (first and last)
        if not first:
            loads = fetched(mix, diffusivity_rows, *([weight_rows] if last else []))
            loads += far_off(field) + near_by(surface) + (far_off(target_state) if last else [])
            mix_here, rows_here, field, *more = call(
                functools.partial(forward_load_kernel, sz, last),
                "step_load",
                loads,
                kept=[mix_shape, row_lines, sz.whole] + ([row_lines, sz.whole] if last else []),
                scratch=[row_sems(2)] + ([by_row] if last else []),
            )
            field, drive, surface, packed, *sends = call(
                functools.partial(forward_kernel, sz, False, last),
                "step",
                scalars(table, facts)
                + near_by(*edges, rows_here, mix_here, field, *surface_edges, *more),
                shipped=[sz.whole, sz.whole, sz.surface, sz.narrow]
                + [sz.lats] * 2
                + [sz.edge] * 2,
                scratch=[wider],
            )
        arrived = exchange(packed, devices)
        got = swap(*sends[:2])
        arrived, *got = lax.optimization_barrier((arrived, *got))
        inputs = (
            near_by(arrived, owner_mix[0], air_temp[hour, 0], wind_speed[hour, 0])
            + scalars(facts)
        )
        decoded = []
        if first:
            inputs += near_by(*got) + fetched(table, facts)
            decoded = [jax.ShapeDtypeStruct(sz.tables, jnp.int32), sz.weights]
        *decoded, flux, mixed_slope, flux_slope = call(
            functools.partial(owner_kernel, sz, first),
            "owners",
            inputs,
            shipped=[*decoded, sz.wide, sz.by_slot, sz.by_slot],
            scratch=[sz.narrow, by_slot],
        )
        if first:
            tables, weights = decoded
        if first:
            flux, perturbation, base_state, *edges = lax.optimization_barrier(
                (flux, perturbation, base_state, *edges)
            )
            (field,) = call(
                functools.partial(load_kernel, sz),
                "load",
                far_off(perturbation, base_state),
                kept=[sz.whole],
                scratch=[by_row, by_row, row_sems(2)],
            )
            field, drive, *sends = call(
                functools.partial(forward_kernel, sz, True, False),
                "step",
                fetched(*edges, diffusivity_rows, mix) + near_by(field),
                shipped=[sz.whole, sz.whole, sz.edge, sz.edge],
                scratch=[wider],
            )
            beside = [field, drive]
        else:
            flux, perturbation, diffusivity, *sends = lax.optimization_barrier(
                (flux, perturbation, diffusivity, *sends[2:])
            )
            beside = relayout(perturbation) + call(
                functools.partial(columns_kernel, sz),
                "columns",
                fetched(diffusivity, cost_weight),
                shipped=[tiles_lines, tiles_lines],
            )
        flux = exchange(flux, devices)
        flux, *beside = lax.optimization_barrier((flux, *beside))
        if first:
            field, drive = beside
        else:
            start_field, diffusivity_tiles, weight_tiles = beside
        edges = swap(*sends)
        inputs = near_by(flux, *got) + fetched(surface) + scalars(tables, weights)
        if last:
            surface, slope, packed, *sends = call(
                functools.partial(surface_kernel, sz, True),
                "surface",
                inputs + fetched(target_state, at=(0,)) + fetched(weight_tiles),
                shipped=[sz.surface, sz.slope, sz.wide, sz.lats, sz.lats],
                scratch=near,
            )
        else:
            surface, *sends, slope = call(
                functools.partial(surface_kernel, sz, False),
                "surface",
                inputs,
                kept=[sz.surface, row_surface, row_surface],
                shipped=[sz.slope],
                scratch=near,
            )
            surface_edges = swap(*sends)
        saved.append((drive, slope, mixed_slope, flux_slope))

    edge_sends = None
    for hour in reversed(range(hours)):
        drive, slope, mixed_slope, flux_slope = saved[hour]
        arrived = exchange(packed, devices)
        got = swap(*sends)
        arrived, *got = lax.optimization_barrier((arrived, *got))
        back = call(
            functools.partial(owner_back_kernel, sz),
            "owners_back",
            near_by(arrived, owner_mix[0]) + fetched(mixed_slope, flux_slope) + scalars(facts),
            shipped=[sz.narrow],
            scratch=[sz.narrow, by_slot],
        )[0]
        if edge_sends is not None:
            back, *edge_sends = lax.optimization_barrier((back, *edge_sends))
            edges = swap(*edge_sends)
        back = exchange(back, devices)
        surface, *row_sends = call(
            functools.partial(merge_kernel, sz),
            "merge",
            near_by(back, *got)
            + fetched(surface, slope)
            + scalars(table, facts)
            + fetched(diffusivity_tiles),
            kept=[sz.surface, row_surface, row_surface],
        )
        surface_edges = swap(*row_sends)
        last = hour == 0
        mix_here, rows_here, *loaded = call(
            functools.partial(backward_load_kernel, sz, last),
            "step_back_load",
            fetched(mix, diffusivity_rows)
            + far_off(field, drive)
            + near_by(surface)
            + (far_off(start_field) if last else []),
            kept=[mix_shape, row_lines] + [sz.whole] * (4 if last else 3),
            scratch=[row_sems(3)],
        )
        inputs = near_by(*edges, *surface_edges, rows_here, mix_here, *loaded)
        if last:
            gradient, sums = call(
                functools.partial(backward_kernel, sz, True),
                "step_back_sums",
                inputs,
                shipped=[sz.whole, (devices, WIDTH)],
                scratch=[wider],
            )
        else:
            field, surface, packed, *outs = call(
                functools.partial(backward_kernel, sz, False),
                "step_back",
                scalars(tables, weights) + fetched(saved[hour - 1][1]) + inputs,
                shipped=[sz.whole, sz.surface, sz.wide, sz.lats, sz.lats, sz.edge, sz.edge],
                scratch=[wider, *near],
            )
            sends, edge_sends = outs[:2], outs[2:]

    everyones = lax.all_to_all(sums, "horiz", split_axis=0, concat_axis=0, tiled=True)
    block = perturbation.shape
    return call(
        functools.partial(final_kernel, perturbation.size * devices),
        "finish",
        near_by(everyones, perturbation, gradient.transpose(2, 0, 1, 3)),
        shipped=[block],
    )[0]


def solution(mesh):
    placed = (
        P("member", "horiz", None, None),
        P(None, "horiz", None, None),
        P(None, "horiz", None, None),
        P("horiz", None),
        P("horiz", None),
        P(),
        P(),
        P("horiz", None, None),
        P(None, "horiz", None, None),
        P(None, "horiz", None, None),
        P("horiz", None),
        P("horiz", None),
        P("horiz"),
        P("horiz"),
        P("horiz"),
    )
    return jax.shard_map(
        body,
        mesh=mesh,
        in_specs=placed,
        out_specs=P("member", "horiz", None, None),
        check_vma=False,
    )
```

```python
import functools

import jax
import jax.numpy as jnp
from jax import lax
from jax.experimental import pallas as pl
from jax.experimental.pallas import tpu as pltpu
from jax.sharding import PartitionSpec as P

LAT_DEV = 2
NEAR_LAT = LAT_DEV + 2
CHANNELS = 4
LEVELS = 8
WIDTH = 128
SUBLANES = 8

KAPPA_V = 0.1
TIME_STEP = 0.3
FLUX_RATE = 0.05
FEEDBACK = 0.5
ASCENT = 0.5
EPSILON = 1e-06
HIGHEST = lax.Precision.HIGHEST
VMEM_BYTES = 32 * 1024 * 1024


class Sizes:
    def __init__(self, devices, capacity, rows, cells):
        self.devices = devices
        self.capacity = capacity
        self.slots = devices * capacity
        self.rows = rows
        self.cells = cells
        self.row_tiles = cells // WIDTH
        self.tiles = rows * self.row_tiles
        self.row_width = CHANNELS * self.row_tiles
        self.pitch = -(-self.row_tiles // SUBLANES) * SUBLANES
        self.own_rows = CHANNELS * capacity
        self.chunk = self.own_rows + 2 * capacity
        self.slot_lines = -(-self.slots // WIDTH)
        self.facts = -(-(self.slot_lines + 1) // SUBLANES) * SUBLANES
        self.lat_lines = LAT_DEV * self.pitch
        self.edge_lines = CHANNELS * self.row_tiles * LEVELS
        self.whole = (rows, CHANNELS, LEVELS, cells)
        self.edge = (self.edge_lines, WIDTH)
        self.told = (self.lat_lines + self.facts, WIDTH)
        self.surface = (CHANNELS * (self.tiles + 1), WIDTH)
        self.narrow = (CHANNELS * self.slots, WIDTH)
        self.wide = (devices * self.chunk, WIDTH)
        self.slope = (NEAR_LAT * self.pitch, WIDTH)
        self.lats = (self.lat_lines, WIDTH)
        self.bulk_at = NEAR_LAT * rows
        self.tables = (3 * self.slot_lines, WIDTH)
        self.weights = (3 * self.facts, WIDTH)
        self.near = (-(-(self.tiles + 1) // SUBLANES) * SUBLANES, WIDTH)
        self.by_slot = (CHANNELS, self.slots, WIDTH)


class Shipped:
    def __init__(self, block, home, sems):
        self.block, self.home, self.sems = block, home, sems
        self.by_row = False
        self.started = False

    def __getitem__(self, at):
        return self.block[at]

    def __setitem__(self, at, value):
        self.block[at] = value

    def row(self, index):
        self.by_row = True
        self.started = True
        return pltpu.make_async_copy(
            self.block.at[index], self.home.at[index], self.sems.at[index]
        )

    def all(self):
        return pltpu.make_async_copy(self.block, self.home, self.sems.at[0])

    def start(self):
        self.started = True
        self.all().start()

    def finish(self, rows):
        if self.by_row:
            for index in range(rows):
                self.row(index).wait()
        else:
            self.all().wait()


def cols(tile):
    return slice(tile * WIDTH, (tile + 1) * WIDTH)


def lanes_sum(left_here, left_before, right_here, right_after, lane):
    return jnp.where(lane == 0, left_before, left_here) + jnp.where(
        lane == WIDTH - 1, right_after, right_here
    )


def level_masks():
    sub = lax.broadcasted_iota(jnp.int32, (LEVELS, WIDTH), 0)
    return jnp.where(sub == 0, 0.0, KAPPA_V), jnp.where(sub == LEVELS - 1, 0.0, KAPPA_V)


def levels_sum(field, masks):
    return masks[0] * pltpu.roll(field, 1, 0) + masks[1] * pltpu.roll(field, LEVELS - 1, 0)


def rolled(tiles):
    return [pltpu.roll(tile, 1, 1) for tile in tiles], [
        pltpu.roll(tile, WIDTH - 1, 1) for tile in tiles
    ]


def row_tiles_of(sz, ref, row):
    return ref[pl.ds(row * sz.row_width, sz.row_tiles, stride=CHANNELS), :]


def put_row_tiles(sz, ref, row, value):
    ref[pl.ds(row * sz.row_width, sz.row_tiles, stride=CHANNELS), :] = value


def near_row(sz, ref, row):
    return ref[row * sz.row_tiles : (row + 1) * sz.row_tiles, :]


def high_first():
    return 1 - lax.rem(lax.axis_index("horiz").astype(jnp.int32), 2)


def pick(flag, one, other):
    return jnp.where(jnp.full(one.shape, flag, jnp.int32) == 1, one, other)


def sided(first, second):
    flag = high_first()
    return pick(flag, second, first), pick(flag, first, second)


def load_surface_row(sz, target, row, source, base):
    for tile in range(sz.row_tiles):
        for channel in range(CHANNELS):
            at = base + tile * CHANNELS + channel
            target[row, channel, 0:1, cols(tile)] = source[pl.ds(at, 1), :]


def as_column(row, size):
    shape = (size, row.shape[1])
    diagonal = lax.broadcasted_iota(jnp.int32, shape, 0) == lax.broadcasted_iota(jnp.int32, shape, 1)
    return jnp.sum(jnp.where(diagonal, row, 0.0), axis=1, keepdims=True)


def setup_kernel(sz, entries, remap_entries, arrive, wet, remap, mix_rows, diffusivity, *outs):
    first_mix, first_rows, table, facts, mix = outs
    arrive_all(arrive)
    for row in range(sz.rows):
        first_rows[row] = diffusivity[row : row + 1, :]
    for index in range(CHANNELS * CHANNELS):
        column = as_column(mix_rows[index : index + 1, :], LEVELS)
        mix[index] = jnp.broadcast_to(column, (LEVELS, WIDTH))
    mix.start()
    first_mix[...] = mix[...]
    tiles, owners = wet[0:1, :], wet[1:2, :]
    size = -(-entries // SUBLANES) * SUBLANES
    shape = (size, wet.shape[1])
    tile_here, owner_here = as_column(tiles, size), as_column(owners, size)
    earlier = lax.broadcasted_iota(jnp.int32, shape, 1) < lax.broadcasted_iota(jnp.int32, shape, 0)
    same = (owner_here == owners) & earlier
    rank = jnp.sum(jnp.where(same, 1.0, 0.0), axis=1, keepdims=True)
    slot = jnp.where(owner_here >= 0.0, owner_here * sz.capacity + rank, -1.0)
    facts[...] = jnp.zeros((sz.facts, WIDTH), jnp.float32)
    for line in range(sz.slot_lines):
        place = lax.broadcasted_iota(jnp.int32, (size, WIDTH), 1) + line * WIDTH
        match = slot.astype(jnp.int32) == place
        told = jnp.sum(jnp.where(match, sz.tiles - tile_here, 0.0), axis=0, keepdims=True)
        facts[line : line + 1, :] = told
        table[line : line + 1, :] = sz.tiles - told.astype(jnp.int32)
    size = -(-remap_entries // SUBLANES) * SUBLANES
    at, amount = as_column(remap[0:1, :], size), as_column(remap[1:2, :], size)
    place = lax.broadcasted_iota(jnp.int32, (size, WIDTH), 1)
    facts[sz.slot_lines : sz.slot_lines + 1, :] = jnp.sum(
        jnp.where(at.astype(jnp.int32) == place, amount, 0.0), axis=0, keepdims=True
    )


def columns_kernel(sz, arrive, diffusivity, weight, *outs):
    diffusivity_rows, weight_rows, diffusivity_tiles, weight_tiles = outs
    arrive_all(arrive)
    for source, by_row, by_tile in (
        (diffusivity, diffusivity_rows, diffusivity_tiles),
        (weight, weight_rows, weight_tiles),
    ):
        for row in range(sz.rows):
            by_row[row] = source[row : row + 1, :]
            for tile in range(sz.row_tiles):
                line = source[row : row + 1, cols(tile)]
                at = (row * sz.row_tiles + tile) * CHANNELS
                by_tile[at : at + CHANNELS, :] = jnp.broadcast_to(line, (CHANNELS, WIDTH))


def gather_levels(block, channel, tile):
    sub = lax.broadcasted_iota(jnp.int32, (LEVELS, WIDTH), 0)
    total = None
    for level in range(LEVELS):
        line = block[level, channel : channel + 1, cols(tile)]
        line = jnp.broadcast_to(line, (LEVELS, WIDTH))
        total = line if total is None else jnp.where(sub == level, line, total)
    return total


def edges_kernel(sz, arrive, low_start, high_start, low_base, high_base, send_first, send_second):
    arrive_all(arrive)
    low_start[...] = low_start[...] + low_base[...]
    high_start[...] = high_start[...] + high_base[...]
    flag = high_first()
    for channel in range(CHANNELS):
        for tile in range(sz.row_tiles):
            low = gather_levels(low_start, channel, tile)
            high = gather_levels(high_start, channel, tile)
            at = (channel * sz.row_tiles + tile) * LEVELS
            send_first[at : at + LEVELS, :] = pick(flag, high, low)
            send_second[at : at + LEVELS, :] = pick(flag, low, high)


def load_kernel(sz, arrive, perturbation, base, field, start_block, base_block, in_sems):
    def arrivals(row):
        return [
            pltpu.make_async_copy(source.at[:, row], block.at[row], in_sems.at[index, row])
            for index, (source, block) in enumerate(
                ((perturbation, start_block), (base, base_block))
            )
        ]

    for row in range(sz.rows):
        for arrival in arrivals(row):
            arrival.start()

    def one_row(row, carry):
        for arrival in arrivals(row):
            arrival.wait()
        start_block[row] = start_block[row] + base_block[row]
        for channel in range(CHANNELS):
            for tile in range(sz.row_tiles):
                field[row, channel, :, cols(tile)] = gather_levels(
                    start_block.at[row], channel, tile
                )
        return carry

    lax.fori_loop(0, sz.rows, one_row, 0)


def relayout_kernel(sz, arrive, source, out, block, in_sems):
    def arrival(row):
        return pltpu.make_async_copy(source.at[:, row], block.at[row], in_sems.at[0, row])

    for row in range(sz.rows):
        arrival(row).start()

    def one_row(row, carry):
        arrival(row).wait()
        for channel in range(CHANNELS):
            for tile in range(sz.row_tiles):
                out[row, channel, :, cols(tile)] = gather_levels(block.at[row], channel, tile)
        out.row(row).start()
        return carry

    lax.fori_loop(0, sz.rows, one_row, 0)


class Remap:
    def __init__(self, sz, weights):
        self.sz, self.weights = sz, weights

    def weight(self, which, lat, row):
        line = which * self.sz.facts + self.sz.slot_lines
        return self.weights[line, lat * self.sz.rows + row]

    def own(self, lat, row):
        return self.weight(0, lat, row)

    def of_low(self, lat, row):
        return self.weight(1, lat + LAT_DEV, row)

    def of_high(self, lat, row):
        return self.weight(2, lat - LAT_DEV, row)


def tile_at(sz, tables, which, slot):
    return tables[which * sz.slot_lines + slot // WIDTH, slot % WIDTH]


def sum_of(weights, values):
    total = weights[0] * values[0]
    for weight, value in zip(weights[1:], values[1:]):
        total = total + weight * value
    return total


def own_sums(sz, remap, own, factor):
    return [
        factor * sum_of([remap.own(lat, row) for row in range(sz.rows)], own)
        for lat in range(NEAR_LAT)
    ]


def send_sums(sz, sums, tell_first, tell_second):
    flag = high_first()
    for index in range(LAT_DEV):
        low, high = sums[index], sums[LAT_DEV + index]
        at = index * sz.pitch
        tell_first[at : at + sz.row_tiles, :] = pick(flag, high, low)
        tell_second[at : at + sz.row_tiles, :] = pick(flag, low, high)


def lat_rows(sz, ref, lat):
    at = lat * sz.pitch
    return ref[at : at + sz.row_tiles, :]


def told_sums(sz, from_first, from_second):
    lows, highs = [], []
    for index in range(LAT_DEV):
        low, high = sided(lat_rows(sz, from_first, index), lat_rows(sz, from_second, index))
        lows.append(low)
        highs.append(high)
    return lows + highs


def place_edges(sz, padded, first, second, first_surface=None, second_surface=None):
    side = high_first() * (sz.rows + 1)
    for at, edge, surface in ((side, first, first_surface), (sz.rows + 1 - side, second, second_surface)):
        for channel in range(CHANNELS):
            for tile in range(sz.row_tiles):
                line = (channel * sz.row_tiles + tile) * LEVELS
                padded[at, channel, :, cols(tile)] = edge[line : line + LEVELS, :]
        if surface is not None:
            load_surface_row(sz, padded, at, surface, 0)


def store_rows(sz, surface, send_first, send_second, factor=None):
    row = high_first() * (sz.rows - 1)
    for at, send in ((row, send_first), (sz.rows - 1 - row, send_second)):
        for tile in range(sz.row_tiles):
            start = pl.multiple_of((at * sz.row_tiles + tile) * CHANNELS, CHANNELS)
            value = surface[pl.ds(start, CHANNELS), :]
            if factor is not None:
                value = factor[pl.ds(start, CHANNELS), :] * value
            send[tile * CHANNELS : (tile + 1) * CHANNELS, :] = value


def forward_load_kernel(sz, last, arrive, mix, diffusivity, *refs):
    refs = list(refs)
    if last:
        weight = refs.pop(0)
    field, surface = refs[:2]
    refs = refs[2:]
    if last:
        target = refs.pop(0)
    mix_out, rows_out, field_out = refs[:3]
    refs = refs[3:]
    if last:
        weight_out, target_out = refs[:2]
        refs = refs[2:]
    in_sems = refs[0]

    def arrivals(row):
        copies = [pltpu.make_async_copy(field.at[row], field_out.at[row], in_sems.at[0, row])]
        if last:
            copies.append(
                pltpu.make_async_copy(target.at[row], target_out.at[row], in_sems.at[1, row])
            )
        return copies

    for row in range(sz.rows):
        for arrival in arrivals(row):
            arrival.start()
    arrive_all(arrive)
    mix_out[...] = mix[...]
    rows_out[...] = diffusivity[...]
    if last:
        weight_out[...] = weight[...]

    def one_row(row, carry):
        for arrival in arrivals(row):
            arrival.wait()
        load_surface_row(sz, field_out, row, surface, row * sz.row_width)
        return carry

    lax.fori_loop(0, sz.rows, one_row, 0)


def forward_kernel(sz, first, last, arrive, *refs):
    refs = list(refs)
    tables, facts, low, high, diffusivity, mix, field = refs[:7]
    refs = refs[7:]
    if first:
        facts_block = refs.pop(0)
    surfaces = ()
    if not first:
        surfaces = refs[:2]
        refs = refs[2:]
    if last:
        weight, target = refs[:2]
        refs = refs[2:]
    out, drive, new_surface, packed, tell_first, tell_second, edge_first, edge_second, padded = refs
    remap = Remap(sz, facts)
    place_edges(sz, padded, low, high, *surfaces)

    def ready(row):
        padded[row + 1] = field[row]

    ready(0)
    lane = lax.broadcasted_iota(jnp.int32, (LEVELS, WIDTH), 1)
    masks = level_masks()
    count = sz.row_tiles

    def one_row(row, carry):
        @pl.when(row < sz.rows - 1)
        def _():
            ready(row + 1)

        here = [[padded[row + 1, c, :, cols(t)] for t in range(count)] for c in range(CHANNELS)]
        moved = [rolled(tiles) for tiles in here]
        for t in range(count):
            coeff = jnp.broadcast_to(diffusivity[row, 0:1, cols(t)], (LEVELS, WIDTH))
            center = (1.0 - 2.0 * KAPPA_V) - 4.0 * coeff
            if last:
                scale = weight[row, 0:1, cols(t)]
                scale = jnp.broadcast_to(scale * scale, (LEVELS, WIDTH))
            for c in range(CHANNELS):
                mixed = mix[c * CHANNELS] * here[0][t]
                for k in range(1, CHANNELS):
                    mixed = mixed + mix[c * CHANNELS + k] * here[k][t]
                bent = jnp.tanh(mixed)
                drive[row, c, :, cols(t)] = bent
                field_here = here[c][t]
                to_right, to_left = moved[c]
                around = lanes_sum(
                    to_right[t], to_right[t - 1], to_left[t], to_left[(t + 1) % count], lane
                )
                around = around + (padded[row, c, :, cols(t)] + padded[row + 2, c, :, cols(t)])
                stepped = (
                    center * field_here
                    + coeff * around
                    + levels_sum(field_here, masks)
                    + TIME_STEP * bent
                )
                new_surface[pl.ds((row * count + t) * CHANNELS + c, 1), :] = stepped[0:1, :]
                if last:
                    stepped = scale * (stepped - target[row, c, :, cols(t)])
                out[row, c, :, cols(t)] = stepped
        drive.row(row).start()
        out.row(row).start()
        return carry

    lax.fori_loop(0, sz.rows, one_row, 0)
    new_surface[CHANNELS * sz.tiles :, :] = jnp.zeros((CHANNELS, WIDTH), jnp.float32)
    new_surface.start()
    arrive_all(arrive)
    pack_slots(sz, tables, new_surface, packed)
    packed.start()
    own = [row_tiles_of(sz, new_surface.block, row) for row in range(sz.rows)]
    send_sums(sz, own_sums(sz, remap, own, 1.0), tell_first, tell_second)
    for tell in (tell_first, tell_second):
        if first:
            tell[sz.lat_lines :, :] = facts_block[...]
        tell.start()
    store_edges(sz, out, diffusivity if last else None, edge_first, edge_second)


def pack_slots(sz, tables, surface, packed):
    for slot in range(sz.slots):
        at = pl.multiple_of(tile_at(sz, tables, 0, slot) * CHANNELS, CHANNELS)
        packed[slot * CHANNELS : (slot + 1) * CHANNELS, :] = surface[pl.ds(at, CHANNELS), :]


def store_edges(sz, field, diffusivity, send_first, send_second):
    outer = high_first() * (sz.rows - 1)
    for row, send in ((outer, send_first), (sz.rows - 1 - outer, send_second)):
        for channel in range(CHANNELS):
            for tile in range(sz.row_tiles):
                value = field[row, channel, :, cols(tile)]
                if diffusivity is not None:
                    value = value * jnp.broadcast_to(
                        diffusivity[row, 0:1, cols(tile)], (LEVELS, WIDTH)
                    )
                at = (channel * sz.row_tiles + tile) * LEVELS
                send[at : at + LEVELS, :] = value
        send.start()


def owner_kernel(sz, decode, arrive, arrived, mixing, air, wind, facts, *refs):
    slots = sz.slots
    if decode:
        told_first, told_second, own_table, own_facts, tables, weights = refs[:6]
        refs = refs[6:]
    flux, mixed_slope, flux_slope, flat, first = refs
    if decode:
        arrive_all(arrive)
        lines = sz.slot_lines
        tables[0:lines, :] = own_table[...]
        weights[0 : sz.facts, :] = own_facts[...]
        both = sided(told_first[sz.lat_lines :, :], told_second[sz.lat_lines :, :])
        for which, told in ((1, both[0]), (2, both[1])):
            got = told[0:lines, :].astype(jnp.int32)
            tables[which * lines : (which + 1) * lines, :] = sz.tiles - got
            at = which * sz.facts
            weights[at : at + sz.facts, :] = told
        tables.start()
        weights.start()

    def bulk(row, column):
        return facts[sz.slot_lines, sz.bulk_at + row * CHANNELS + column]

    values = [arrived[pl.ds(c, slots, stride=CHANNELS), :] for c in range(CHANNELS)]
    mixed = jnp.tanh(
        jnp.dot(
            mixing[...],
            jnp.concatenate(values, axis=1),
            precision=HIGHEST,
            preferred_element_type=jnp.float32,
        )
    )
    contrast = []
    for c in range(CHANNELS):
        mixed_here = mixed[:, cols(c)]
        mixed_slope[c] = 1.0 - mixed_here * mixed_here
        contrast.append((air[...] - values[0] if c == 0 else values[c]) + mixed_here)
    mixed_slope.start()
    if not decode:
        arrive_all(arrive)
    rate = FLUX_RATE * wind[...]
    for c in range(CHANNELS):
        forcing = bulk(c, 0) * contrast[0]
        for k in range(1, CHANNELS):
            forcing = forcing + bulk(c, k) * contrast[k]
        bent = jnp.tanh(forcing)
        flux_slope[c] = rate * (1.0 - bent * bent)
        one = rate * bent
        flat[pl.ds(c, slots, stride=CHANNELS), :] = one
        if c == 0:
            first[...] = one
    flux_slope.start()
    cap = sz.capacity
    gap = jnp.zeros((sz.chunk - sz.own_rows, WIDTH), jnp.float32)
    for d in range(sz.devices):
        at = d * sz.chunk
        flux[at : at + sz.own_rows, :] = flat[d * sz.own_rows : (d + 1) * sz.own_rows, :]
        at = at + sz.own_rows
        flux[at : (d + 1) * sz.chunk, :] = gap
        if d > 0:
            flux[at : at + cap, :] = first[(d - 1) * cap : d * cap, :]
        if d < sz.devices - 1:
            flux[at + cap : at + 2 * cap, :] = first[(d + 1) * cap : (d + 2) * cap, :]


def owner_back_kernel(sz, arrive, arrived, mixing, mixed_slope, flux_slope, facts, back, flat, extra):
    slots, cap = sz.slots, sz.capacity

    def bulk(row, column):
        return facts[sz.slot_lines, sz.bulk_at + row * CHANNELS + column]

    for d in range(sz.devices):
        at = d * sz.chunk
        flat[d * sz.own_rows : (d + 1) * sz.own_rows, :] = arrived[at : at + sz.own_rows, :]
        more = jnp.zeros((cap, WIDTH), jnp.float32)
        if d < sz.devices - 1:
            at = (d + 1) * sz.chunk + sz.own_rows
            more = more + arrived[at : at + cap, :]
        if d > 0:
            at = (d - 1) * sz.chunk + sz.own_rows + cap
            more = more + arrived[at : at + cap, :]
        extra[d * cap : (d + 1) * cap, :] = more
    arrive_all(arrive)
    forced = []
    for c in range(CHANNELS):
        got = flat[pl.ds(c, slots, stride=CHANNELS), :]
        if c == 0:
            got = got + extra[...]
        forced.append(flux_slope[c] * got)
    direct = []
    for k in range(CHANNELS):
        total = bulk(0, k) * forced[0]
        for c in range(1, CHANNELS):
            total = total + bulk(c, k) * forced[c]
        direct.append(total)
    through = lax.dot_general(
        mixing[...],
        jnp.concatenate([direct[k] * mixed_slope[k] for k in range(CHANNELS)], axis=1),
        (((0,), (0,)), ((), ())),
        precision=HIGHEST,
        preferred_element_type=jnp.float32,
    )
    for k in range(CHANNELS):
        sign = -1.0 if k == 0 else 1.0
        back.block[pl.ds(k, slots, stride=CHANNELS), :] = through[:, cols(k)] + sign * direct[k]


def spread_back(sz, surface, slope, remap, tables, packed, near_low, near_high, tell_first, tell_second):
    rows, count, cap = sz.rows, sz.row_tiles, sz.capacity
    block = surface.block
    own = [row_tiles_of(sz, block, row) for row in range(rows)]
    sums = own_sums(sz, remap, own, FEEDBACK)
    send_sums(sz, sums, tell_first, tell_second)
    tell_first.start()
    tell_second.start()
    lats = [lat_rows(sz, slope, lat) * sums[lat] for lat in range(NEAR_LAT)]
    every = range(NEAR_LAT)
    for row in range(rows):
        added = sum_of([remap.own(lat, row) for lat in every], lats)
        put_row_tiles(sz, block, row, own[row] + added)
        at = row * count
        near_low[at : at + count, :] = sum_of(
            [remap.of_low(lat, row) for lat in range(LAT_DEV)], lats[:LAT_DEV]
        )
        near_high[at : at + count, :] = sum_of(
            [remap.of_high(lat, row) for lat in range(LAT_DEV, NEAR_LAT)], lats[LAT_DEV:]
        )
    rest = sz.near[0] - sz.tiles
    near_low[sz.tiles :, :] = jnp.zeros((rest, WIDTH), jnp.float32)
    near_high[sz.tiles :, :] = jnp.zeros((rest, WIDTH), jnp.float32)
    surface.start()
    gap = jnp.zeros((sz.chunk - sz.own_rows, WIDTH), jnp.float32)
    for owner in range(sz.devices):
        packed[owner * sz.chunk + sz.own_rows : (owner + 1) * sz.chunk, :] = gap
    for slot in range(sz.slots):
        owner, rank = slot // cap, slot % cap
        at = owner * sz.chunk + rank * CHANNELS
        tile = pl.multiple_of(tile_at(sz, tables, 0, slot) * CHANNELS, CHANNELS)
        packed[at : at + CHANNELS, :] = surface[pl.ds(tile, CHANNELS), :]
        at = owner * sz.chunk + sz.own_rows + rank
        packed[at : at + 1, :] = near_low[pl.ds(tile_at(sz, tables, 1, slot), 1), :]
        at = at + cap
        packed[at : at + 1, :] = near_high[pl.ds(tile_at(sz, tables, 2, slot), 1), :]


def surface_kernel(sz, last, arrive, *refs):
    refs = list(refs)
    flux, from_first, from_second, before, tables, weights = refs[:6]
    refs = refs[6:]
    if last:
        target, weight = refs[:2]
        surface, slope, packed, tell_first, tell_second, near_low, near_high = refs[2:]
        block = surface.block
    else:
        surface, send_first, send_second, slope, near_low, near_high = refs
        block = surface
    remap = Remap(sz, weights)
    arrive_all(arrive)
    rows, cap = sz.rows, sz.capacity
    block[...] = before[...]
    near_low[...] = jnp.zeros(sz.near, jnp.float32)
    near_high[...] = jnp.zeros(sz.near, jnp.float32)
    for slot in range(sz.slots):
        owner, rank = slot // cap, slot % cap
        at = owner * sz.chunk + rank * CHANNELS
        tile = pl.multiple_of(tile_at(sz, tables, 0, slot) * CHANNELS, CHANNELS)
        block[pl.ds(tile, CHANNELS), :] = (
            before[pl.ds(tile, CHANNELS), :] + flux[at : at + CHANNELS, :]
        )
        at = owner * sz.chunk + sz.own_rows + rank
        near_low[pl.ds(tile_at(sz, tables, 1, slot), 1), :] = flux[at : at + 1, :]
        at = at + cap
        near_high[pl.ds(tile_at(sz, tables, 2, slot), 1), :] = flux[at : at + 1, :]
    block[CHANNELS * sz.tiles :, :] = jnp.zeros((CHANNELS, WIDTH), jnp.float32)
    own = [row_tiles_of(sz, block, row) for row in range(rows)]
    sums = own_sums(sz, remap, own, 1.0)
    told = told_sums(sz, from_first, from_second)
    air = []
    for lat in range(NEAR_LAT):
        if lat < LAT_DEV:
            near, weights = near_low, [remap.of_low(lat, row) for row in range(rows)]
        else:
            near, weights = near_high, [remap.of_high(lat, row) for row in range(rows)]
        more = sum_of(weights, [near_row(sz, near, row) for row in range(rows)])
        one = jnp.tanh(sums[lat] + told[lat] + more)
        slope[lat * sz.pitch : lat * sz.pitch + sz.row_tiles, :] = 1.0 - one * one
        air.append(one)
    slope.start()
    for row in range(rows):
        weights = [remap.own(lat, row) for lat in range(NEAR_LAT)]
        put_row_tiles(sz, block, row, own[row] + FEEDBACK * sum_of(weights, air))
    if last:
        for row in range(rows):
            for tile in range(sz.row_tiles):
                at = row * sz.row_width + tile * CHANNELS
                scale = weight[at : at + CHANNELS, :]
                off = block[at : at + CHANNELS, :] - target[row, :, cols(tile)]
                block[at : at + CHANNELS, :] = scale * scale * off
        spread_back(
            sz, surface, slope, remap, tables, packed, near_low, near_high, tell_first, tell_second
        )
    else:
        store_rows(sz, surface, send_first, send_second)


def merge_kernel(
    sz, arrive, back, from_first, from_second, before, slope, tables, facts, diffusivity, surface, send_first, send_second
):
    rows = sz.rows
    remap = Remap(sz, facts)
    arrive_all(arrive)
    surface[...] = before[...]
    for slot in range(sz.slots):
        tile = pl.multiple_of(tile_at(sz, tables, 0, slot) * CHANNELS, CHANNELS)
        surface[pl.ds(tile, CHANNELS), :] = (
            before[pl.ds(tile, CHANNELS), :] + back[slot * CHANNELS : (slot + 1) * CHANNELS, :]
        )
    surface[CHANNELS * sz.tiles :, :] = jnp.zeros((CHANNELS, WIDTH), jnp.float32)
    told = told_sums(sz, from_first, from_second)
    lats = [lat_rows(sz, slope, lat) * told[lat] for lat in range(NEAR_LAT)]
    for row in range(rows):
        own = row_tiles_of(sz, surface, row)
        weights = [remap.own(lat, row) for lat in range(NEAR_LAT)]
        put_row_tiles(sz, surface, row, own + sum_of(weights, lats))
    store_rows(sz, surface, send_first, send_second, diffusivity)


def backward_load_kernel(sz, last, arrive, mix, diffusivity, field, drive, surface, *refs):
    refs = list(refs)
    if last:
        perturbation = refs.pop(0)
    mix_out, rows_out, local, bent_all, scaled = refs[:5]
    refs = refs[5:]
    if last:
        start_all = refs.pop(0)
    in_sems = refs[0]

    def arrivals(row):
        copies = [
            pltpu.make_async_copy(field.at[row], local.at[row], in_sems.at[0, row]),
            pltpu.make_async_copy(drive.at[row], bent_all.at[row], in_sems.at[1, row]),
        ]
        if last:
            copies.append(
                pltpu.make_async_copy(perturbation.at[row], start_all.at[row], in_sems.at[2, row])
            )
        return copies

    for row in range(sz.rows):
        for arrival in arrivals(row):
            arrival.start()
    arrive_all(arrive)
    mix_out[...] = mix[...]
    rows_out[...] = diffusivity[...]

    def one_row(row, carry):
        for arrival in arrivals(row):
            arrival.wait()
        load_surface_row(sz, local, row, surface, row * sz.row_width)
        for t in range(sz.row_tiles):
            coeff = jnp.broadcast_to(diffusivity[row, 0:1, cols(t)], (LEVELS, WIDTH))
            for c in range(CHANNELS):
                scaled[row, c, :, cols(t)] = coeff * local[row, c, :, cols(t)]
        return carry

    lax.fori_loop(0, sz.rows, one_row, 0)


def backward_kernel(sz, last, arrive, *refs):
    refs = list(refs)
    if not last:
        tables, weights, slope = refs[:3]
        refs = refs[3:]
    low, high, first_surface, second_surface, diffusivity, mix = refs[:6]
    local, bent_all, scaled_all = refs[6:9]
    refs = refs[9:]
    if last:
        start_all, out, sums, padded = refs
    else:
        out, new_surface, packed, tell_first, tell_second, edge_first, edge_second = refs[:7]
        padded, near_low, near_high = refs[7:]
        remap = Remap(sz, weights)
    count = sz.row_tiles
    place_edges(sz, padded, low, high, first_surface, second_surface)

    def ready(row):
        padded[row + 1] = scaled_all[row]

    ready(0)
    lane = lax.broadcasted_iota(jnp.int32, (LEVELS, WIDTH), 1)
    masks = level_masks()

    def one_row(row, carry):
        @pl.when(row < sz.rows - 1)
        def _():
            ready(row + 1)

        scaled = [[padded[row + 1, c, :, cols(t)] for t in range(count)] for c in range(CHANNELS)]
        moved = [rolled(tiles) for tiles in scaled]
        for t in range(count):
            here, bent = [], []
            for c in range(CHANNELS):
                value = local[row, c, :, cols(t)]
                one = bent_all[row, c, :, cols(t)]
                here.append(value)
                bent.append((1.0 - one * one) * value)
            for c in range(CHANNELS):
                mixed = mix[c] * bent[0]
                for k in range(1, CHANNELS):
                    mixed = mixed + mix[k * CHANNELS + c] * bent[k]
                to_right, to_left = moved[c]
                around = lanes_sum(
                    to_right[t], to_right[t - 1], to_left[t], to_left[(t + 1) % count], lane
                )
                around = around + (padded[row, c, :, cols(t)] + padded[row + 2, c, :, cols(t)])
                stepped = (
                    ((1.0 - 2.0 * KAPPA_V) * here[c] - 4.0 * scaled[c][t])
                    + around
                    + levels_sum(here[c], masks)
                    + TIME_STEP * mixed
                )
                out[row, c, :, cols(t)] = stepped
                if last:
                    start = start_all[row, c, :, cols(t)]
                    carry = (
                        carry[0] + start * start,
                        carry[1] + start * stepped,
                        carry[2] + stepped * stepped,
                    )
                else:
                    new_surface[pl.ds((row * count + t) * CHANNELS + c, 1), :] = stepped[0:1, :]
        out.row(row).start()
        return carry

    blank = jnp.zeros((LEVELS, WIDTH), jnp.float32)
    totals = lax.fori_loop(0, sz.rows, one_row, (blank, blank, blank) if last else 0)
    if last:
        place = lax.broadcasted_iota(jnp.int32, sums.block.shape, 1)
        held = jnp.zeros(sums.block.shape, jnp.float32)
        for index in range(3):
            total = jnp.sum(jnp.sum(totals[index], axis=0, keepdims=True), axis=1, keepdims=True)
            held = jnp.where(place == index, total, held)
        sums[...] = held
    else:
        new_surface[CHANNELS * sz.tiles :, :] = jnp.zeros((CHANNELS, WIDTH), jnp.float32)
        arrive_all(arrive)
        spread_back(
            sz,
            new_surface,
            slope,
            remap,
            tables,
            packed,
            near_low,
            near_high,
            tell_first,
            tell_second,
        )
        packed.start()
        store_edges(sz, out, diffusivity, edge_first, edge_second)


def final_kernel(cell_total, arrive, everyones, perturbation, gradient, out):
    sums = jnp.sum(everyones[...], axis=0, keepdims=True) / cell_total
    place = lax.broadcasted_iota(jnp.int32, sums.shape, 1)
    means = [
        jnp.broadcast_to(
            jnp.sum(jnp.where(place == index, sums, 0.0), axis=1, keepdims=True), (1, WIDTH)
        )
        for index in range(3)
    ]
    scale = lax.rsqrt(means[2] + EPSILON)
    mean_sq = means[0] + 2.0 * ASCENT * scale * means[1] + ASCENT * ASCENT * scale * scale * means[2]
    shrink = lax.rsqrt(mean_sq + EPSILON)
    step = jnp.broadcast_to(ASCENT * scale * shrink, (CHANNELS, WIDTH))
    shrink = jnp.broadcast_to(shrink, (CHANNELS, WIDTH))
    levels, rows, _, cells = perturbation.shape

    def one_level(level, carry):
        for row in range(rows):
            for tile in range(cells // WIDTH):
                start = perturbation[level, row, :, cols(tile)]
                slope = gradient[level, row, :, cols(tile)]
                out[level, row, :, cols(tile)] = shrink * start + step * slope
        out.row(level).start()
        return carry

    lax.fori_loop(0, levels, one_level, 0)


class Operand:
    def __init__(self, array, space, fetch=None, at=()):
        self.array, self.space, self.fetch, self.at = array, space, fetch, at

    def block(self):
        whole = self.array.shape
        taken = [size for size, index in zip(whole, self.at) if isinstance(index, slice)]
        return self.fetch((*taken, *whole[len(self.at) :]), self.array.dtype)


def near_by(*arrays):
    return [Operand(array, pltpu.VMEM) for array in arrays]


def far_off(*arrays):
    return [
        Operand(pltpu.with_memory_space_constraint(array, pltpu.HBM), pltpu.HBM)
        for array in arrays
    ]


def fetched(*arrays, at=(), into=pltpu.VMEM):
    return [
        Operand(pltpu.with_memory_space_constraint(array, pltpu.HBM), pltpu.HBM, into, at)
        for array in arrays
    ]


def scalars(*arrays):
    return fetched(*arrays, into=pltpu.SMEM)


def call(kernel, name, inputs, kept=(), shipped=(), scratch=()):
    n_in, n_kept, n_out = len(inputs), len(kept), len(shipped)
    brought = [index for index, item in enumerate(inputs) if item.fetch is not None]

    def as_shape(item):
        return item if isinstance(item, jax.ShapeDtypeStruct) else jax.ShapeDtypeStruct(item, jnp.float32)

    kept = [as_shape(item) for item in kept]
    shipped = [as_shape(item) for item in shipped]

    def run(*refs):
        ins = list(refs[:n_in])
        kept_refs = refs[n_in : n_in + n_kept]
        homes = refs[n_in + n_kept : n_in + n_kept + n_out]
        rest = refs[n_in + n_kept + n_out :]
        outs = [
            Shipped(block, home, sems)
            for block, home, sems in zip(rest[:n_out], homes, rest[n_out : 2 * n_out])
        ]
        rest = rest[2 * n_out :]
        if brought:
            blocks, arrive_sems = rest[: len(brought)], rest[len(brought)]
            rest = rest[len(brought) + 1 :]
            copies = []
            for place, (index, block) in enumerate(zip(brought, blocks)):
                source = ins[index]
                if inputs[index].at:
                    source = source.at[inputs[index].at]
                copies.append(pltpu.make_async_copy(source, block, arrive_sems.at[place]))
                ins[index] = block
            for copy in copies:
                copy.start()
            arrive = [copy.wait for copy in copies]
        else:
            arrive = []
        kernel(arrive, *ins, *kept_refs, *outs, *rest)
        for out in outs:
            if not out.started:
                out.start()
        for out in outs:
            out.finish(out.block.shape[0])

    spaces = [pltpu.VMEM] * n_kept + [pltpu.HBM] * n_out
    blocks = [pltpu.VMEM(item.shape, item.dtype) for item in shipped]
    sems = [
        pltpu.SemaphoreType.DMA((item.shape[0] if len(item.shape) > 3 else 1,)) for item in shipped
    ]
    arriving = [inputs[index].block() for index in brought]
    if brought:
        arriving.append(pltpu.SemaphoreType.DMA((len(brought),)))
    more = [
        item if not isinstance(item, tuple) else pltpu.VMEM(item, jnp.float32) for item in scratch
    ]
    return pl.pallas_call(
        run,
        name=name,
        in_specs=[pl.BlockSpec(memory_space=item.space) for item in inputs],
        out_specs=[pl.BlockSpec(memory_space=space) for space in spaces],
        out_shape=kept + [pltpu.HBM(item.shape, item.dtype) for item in shipped],
        scratch_shapes=blocks + sems + arriving + more,
        compiler_params=pltpu.CompilerParams(vmem_limit_bytes=VMEM_BYTES),
    )(*[item.array for item in inputs])


def arrive_all(arrive):
    for wait in arrive:
        wait()


def swap(first, second):
    count = lax.axis_size("horiz")
    inner = [(i, i ^ 1) for i in range(count)]
    outer = [(i, i + 1) for i in range(1, count - 1, 2)]
    outer = outer + [(target, source) for source, target in outer]
    return lax.ppermute(first, "horiz", inner), lax.ppermute(second, "horiz", outer)


def exchange(array, devices):
    rows = array.shape[0] // devices
    step = CHANNELS if rows % CHANNELS == 0 else 2
    split = array.reshape(devices, rows // step, step, WIDTH)
    moved = lax.all_to_all(split, "horiz", split_axis=0, concat_axis=0, tiled=True)
    return moved.reshape(array.shape)


def body(
    perturbation,
    base_state,
    target_state,
    cost_weight,
    diffusivity,
    chan_mix,
    coupler_mix,
    owner_mix,
    air_temp,
    wind_speed,
    wet_list,
    wet_owner,
    remap_src,
    remap_tgt,
    remap_weight,
):
    devices = lax.axis_size("horiz")
    hours = air_temp.shape[0]
    sz = Sizes(devices, air_temp.shape[2] // devices, base_state.shape[1], base_state.shape[3])
    rows = sz.rows
    native_row = (LEVELS, CHANNELS, sz.cells)

    edge_inputs = []
    for array in (perturbation, base_state):
        for row in (0, rows - 1):
            edge_inputs += fetched(array, at=(slice(None), row))
    edges = swap(
        *call(functools.partial(edges_kernel, sz), "edges", edge_inputs, kept=[sz.edge, sz.edge])
    )
    me = lax.axis_index("horiz").astype(jnp.int32)

    def lined(first_row, second_row):
        size = -(-first_row.shape[0] // WIDTH) * WIDTH
        pair = jnp.stack([first_row.astype(jnp.float32), second_row.astype(jnp.float32)])
        return jnp.pad(pair, ((0, 0), (0, size - pair.shape[1])), constant_values=-1.0)

    places = jnp.arange(CHANNELS * CHANNELS, dtype=jnp.int32) + sz.bulk_at
    remap_at = (remap_tgt - (me * LAT_DEV - 1)) * rows + remap_src - me * rows
    remap_lines = lined(
        jnp.concatenate([remap_at, places]),
        jnp.concatenate([remap_weight, coupler_mix.reshape(-1)]),
    )
    mix_rows = chan_mix.transpose(1, 2, 0).reshape(CHANNELS * CHANNELS, LEVELS)
    row_lines = (rows, 1, sz.cells)
    tiles_lines = (CHANNELS * sz.tiles, WIDTH)
    first_mix, first_rows, table, facts, mix = call(
        functools.partial(setup_kernel, sz, wet_list.shape[1], remap_at.shape[0] + places.shape[0]),
        "setup",
        near_by(lined(wet_list[0], wet_owner[0]), remap_lines, mix_rows)
        + fetched(diffusivity),
        kept=[(CHANNELS * CHANNELS, LEVELS, WIDTH), row_lines],
        shipped=[
            jax.ShapeDtypeStruct((sz.slot_lines, WIDTH), jnp.int32),
            (sz.facts, WIDTH),
            (CHANNELS * CHANNELS, LEVELS, WIDTH),
        ],
    )
    wider = (rows + 2, CHANNELS, LEVELS, sz.cells)
    row_surface = (sz.row_width, WIDTH)
    by_row = (rows, *native_row)

    def row_sems(kinds):
        return pltpu.SemaphoreType.DMA((kinds, rows))

    (field,) = call(
        functools.partial(load_kernel, sz),
        "load",
        far_off(perturbation, base_state),
        kept=[sz.whole],
        scratch=[by_row, by_row, row_sems(2)],
    )

    def relayout(array):
        return call(
            functools.partial(relayout_kernel, sz),
            "relayout",
            far_off(array),
            shipped=[sz.whole],
            scratch=[by_row, row_sems(1)],
        )

    saved = []
    near = [sz.near, sz.near]
    mix_shape = (CHANNELS * CHANNELS, LEVELS, WIDTH)
    by_slot = (sz.slots, WIDTH)
    for hour in range(hours):
        first, last = hour == 0, hour == hours - 1
        inputs = scalars(table, facts)
        if first:
            inputs += near_by(*edges, first_rows, first_mix, field) + fetched(facts)
            assert not last
        else:
            loads = fetched(mix, diffusivity_rows, *([weight_rows] if last else []))
            loads += far_off(field) + near_by(surface) + (far_off(target) if last else [])
            mix_here, rows_here, field, *more = call(
                functools.partial(forward_load_kernel, sz, last),
                "step_load",
                loads,
                kept=[mix_shape, row_lines, sz.whole] + ([row_lines, sz.whole] if last else []),
                scratch=[row_sems(2)],
            )
            inputs += near_by(*edges, rows_here, mix_here, field, *surface_edges, *more)
        field, drive, surface, packed, *sends = call(
            functools.partial(forward_kernel, sz, first, last),
            "step",
            inputs,
            shipped=[sz.whole, sz.whole, sz.surface, sz.narrow]
            + [sz.told if first else sz.lats] * 2
            + [sz.edge] * 2,
            scratch=[wider],
        )
        arrived = exchange(packed, devices)
        got = swap(*sends[:2])
        arrived, *got = lax.optimization_barrier((arrived, *got))
        inputs = (
            near_by(arrived, owner_mix[0], air_temp[hour, 0], wind_speed[hour, 0])
            + scalars(facts)
        )
        decoded = []
        if first:
            inputs += near_by(*got) + fetched(table, facts)
            decoded = [jax.ShapeDtypeStruct(sz.tables, jnp.int32), sz.weights]
        *decoded, flux, mixed_slope, flux_slope = call(
            functools.partial(owner_kernel, sz, first),
            "owners",
            inputs,
            shipped=[*decoded, sz.wide, sz.by_slot, sz.by_slot],
            scratch=[sz.narrow, by_slot],
        )
        if first:
            tables, weights = decoded
        flux, *sends = lax.optimization_barrier((flux, *sends[2:]))
        if first:
            flux, diffusivity, target_state = lax.optimization_barrier(
                (flux, diffusivity, target_state)
            )
            beside = call(
                functools.partial(columns_kernel, sz),
                "columns",
                fetched(diffusivity, cost_weight),
                shipped=[row_lines, row_lines, tiles_lines, tiles_lines],
            ) + relayout(target_state)
        else:
            flux, perturbation = lax.optimization_barrier((flux, perturbation))
            beside = relayout(perturbation)
        flux = exchange(flux, devices)
        flux, *beside = lax.optimization_barrier((flux, *beside))
        if first:
            diffusivity_rows, weight_rows, diffusivity_tiles, weight_tiles, target = beside
        else:
            start_field = beside[0]
        edges = swap(*sends)
        inputs = near_by(flux, *got) + fetched(surface) + scalars(tables, weights)
        if last:
            surface, slope, packed, *sends = call(
                functools.partial(surface_kernel, sz, True),
                "surface",
                inputs + fetched(target_state, at=(0,)) + fetched(weight_tiles),
                shipped=[sz.surface, sz.slope, sz.wide, sz.lats, sz.lats],
                scratch=near,
            )
        else:
            surface, *sends, slope = call(
                functools.partial(surface_kernel, sz, False),
                "surface",
                inputs,
                kept=[sz.surface, row_surface, row_surface],
                shipped=[sz.slope],
                scratch=near,
            )
            surface_edges = swap(*sends)
        saved.append((drive, slope, mixed_slope, flux_slope))

    edge_sends = None
    for hour in reversed(range(hours)):
        drive, slope, mixed_slope, flux_slope = saved[hour]
        arrived = exchange(packed, devices)
        got = swap(*sends)
        arrived, *got = lax.optimization_barrier((arrived, *got))
        back = call(
            functools.partial(owner_back_kernel, sz),
            "owners_back",
            near_by(arrived, owner_mix[0]) + fetched(mixed_slope, flux_slope) + scalars(facts),
            shipped=[sz.narrow],
            scratch=[sz.narrow, by_slot],
        )[0]
        if edge_sends is not None:
            back, *edge_sends = lax.optimization_barrier((back, *edge_sends))
            edges = swap(*edge_sends)
        back = exchange(back, devices)
        surface, *row_sends = call(
            functools.partial(merge_kernel, sz),
            "merge",
            near_by(back, *got)
            + fetched(surface, slope)
            + scalars(table, facts)
            + fetched(diffusivity_tiles),
            kept=[sz.surface, row_surface, row_surface],
        )
        surface_edges = swap(*row_sends)
        last = hour == 0
        mix_here, rows_here, *loaded = call(
            functools.partial(backward_load_kernel, sz, last),
            "step_back_load",
            fetched(mix, diffusivity_rows)
            + far_off(field, drive)
            + near_by(surface)
            + (far_off(start_field) if last else []),
            kept=[mix_shape, row_lines] + [sz.whole] * (4 if last else 3),
            scratch=[row_sems(3)],
        )
        inputs = near_by(*edges, *surface_edges, rows_here, mix_here, *loaded)
        if last:
            gradient, sums = call(
                functools.partial(backward_kernel, sz, True),
                "step_back_sums",
                inputs,
                shipped=[sz.whole, (devices, WIDTH)],
                scratch=[wider],
            )
        else:
            field, surface, packed, *outs = call(
                functools.partial(backward_kernel, sz, False),
                "step_back",
                scalars(tables, weights) + fetched(saved[hour - 1][1]) + inputs,
                shipped=[sz.whole, sz.surface, sz.wide, sz.lats, sz.lats, sz.edge, sz.edge],
                scratch=[wider, *near],
            )
            sends, edge_sends = outs[:2], outs[2:]

    everyones = lax.all_to_all(sums, "horiz", split_axis=0, concat_axis=0, tiled=True)
    block = perturbation.shape
    return call(
        functools.partial(final_kernel, perturbation.size * devices),
        "finish",
        near_by(everyones, perturbation, gradient.transpose(2, 0, 1, 3)),
        shipped=[block],
    )[0]


def solution(mesh):
    placed = (
        P("member", "horiz", None, None),
        P(None, "horiz", None, None),
        P(None, "horiz", None, None),
        P("horiz", None),
        P("horiz", None),
        P(),
        P(),
        P("horiz", None, None),
        P(None, "horiz", None, None),
        P(None, "horiz", None, None),
        P("horiz", None),
        P("horiz", None),
        P("horiz"),
        P("horiz"),
        P("horiz"),
    )
    return jax.shard_map(
        body,
        mesh=mesh,
        in_specs=placed,
        out_specs=P("member", "horiz", None, None),
        check_vma=False,
    )
```

```python
import functools

import jax
import jax.numpy as jnp
from jax import lax
from jax.experimental import pallas as pl
from jax.experimental.pallas import tpu as pltpu
from jax.sharding import PartitionSpec as P

LAT_DEV = 2
NEAR_LAT = LAT_DEV + 2
CHANNELS = 4
LEVELS = 8
WIDTH = 128
SUBLANES = 8

KAPPA_V = 0.1
TIME_STEP = 0.3
FLUX_RATE = 0.05
FEEDBACK = 0.5
ASCENT = 0.5
EPSILON = 1e-06
HIGHEST = lax.Precision.HIGHEST
VMEM_BYTES = 32 * 1024 * 1024


class Sizes:
    def __init__(self, devices, capacity, rows, cells):
        self.devices = devices
        self.capacity = capacity
        self.slots = devices * capacity
        self.rows = rows
        self.cells = cells
        self.row_tiles = cells // WIDTH
        self.tiles = rows * self.row_tiles
        self.row_width = CHANNELS * self.row_tiles
        self.pitch = -(-self.row_tiles // SUBLANES) * SUBLANES
        self.own_rows = CHANNELS * capacity
        self.chunk = self.own_rows + 2 * capacity
        self.slot_lines = -(-self.slots // WIDTH)
        self.facts = -(-(self.slot_lines + 1) // SUBLANES) * SUBLANES
        self.lat_lines = LAT_DEV * self.pitch
        self.edge_lines = CHANNELS * self.row_tiles * LEVELS
        self.whole = (rows, CHANNELS, LEVELS, cells)
        self.edge = (self.edge_lines, WIDTH)
        self.told = (self.lat_lines + self.facts, WIDTH)
        self.surface = (CHANNELS * (self.tiles + 1), WIDTH)
        self.narrow = (CHANNELS * self.slots, WIDTH)
        self.wide = (devices * self.chunk, WIDTH)
        self.slope = (NEAR_LAT * self.pitch, WIDTH)
        self.lats = (self.lat_lines, WIDTH)
        self.bulk_at = NEAR_LAT * rows
        self.tables = (3 * self.slot_lines, WIDTH)
        self.weights = (3 * self.facts, WIDTH)
        self.near = (-(-(self.tiles + 1) // SUBLANES) * SUBLANES, WIDTH)
        self.by_slot = (CHANNELS, self.slots, WIDTH)


class Shipped:
    def __init__(self, block, home, sems):
        self.block, self.home, self.sems = block, home, sems
        self.by_row = False
        self.started = False

    def __getitem__(self, at):
        return self.block[at]

    def __setitem__(self, at, value):
        self.block[at] = value

    def row(self, index):
        self.by_row = True
        self.started = True
        return pltpu.make_async_copy(
            self.block.at[index], self.home.at[index], self.sems.at[index]
        )

    def all(self):
        return pltpu.make_async_copy(self.block, self.home, self.sems.at[0])

    def start(self):
        self.started = True
        self.all().start()

    def finish(self, rows):
        if self.by_row:
            for index in range(rows):
                self.row(index).wait()
        else:
            self.all().wait()


def cols(tile):
    return slice(tile * WIDTH, (tile + 1) * WIDTH)


def lanes_sum(left_here, left_before, right_here, right_after, lane):
    return jnp.where(lane == 0, left_before, left_here) + jnp.where(
        lane == WIDTH - 1, right_after, right_here
    )


def level_masks():
    sub = lax.broadcasted_iota(jnp.int32, (LEVELS, WIDTH), 0)
    return jnp.where(sub == 0, 0.0, KAPPA_V), jnp.where(sub == LEVELS - 1, 0.0, KAPPA_V)


def levels_sum(field, masks):
    return masks[0] * pltpu.roll(field, 1, 0) + masks[1] * pltpu.roll(field, LEVELS - 1, 0)


class RowTiles:
    def __init__(self, count, load):
        self.count, self.load, self.held = count, load, {}

    def make(self, channel, tile):
        value = self.load(channel, tile)
        return value, pltpu.roll(value, 1, 1), pltpu.roll(value, WIDTH - 1, 1)

    def get(self, channel, tile):
        if (channel, tile) not in self.held:
            self.held[channel, tile] = self.make(channel, tile)
        return self.held[channel, tile]

    def here(self, channel, tile):
        return self.get(channel, tile)[0]

    def around(self, channel, tile, lane):
        last = self.count - 1
        before = self.get(channel, tile - 1) if tile > 0 else self.make(channel, last)
        after = self.get(channel, tile + 1) if tile < last else self.make(channel, 0)
        _, to_right, to_left = self.get(channel, tile)
        return lanes_sum(to_right, before[1], to_left, after[2], lane)


def row_tiles_of(sz, ref, row):
    return ref[pl.ds(row * sz.row_width, sz.row_tiles, stride=CHANNELS), :]


def put_row_tiles(sz, ref, row, value):
    ref[pl.ds(row * sz.row_width, sz.row_tiles, stride=CHANNELS), :] = value


def near_row(sz, ref, row):
    return ref[row * sz.row_tiles : (row + 1) * sz.row_tiles, :]


def high_first():
    return 1 - lax.rem(lax.axis_index("horiz").astype(jnp.int32), 2)


def pick(flag, one, other):
    return jnp.where(jnp.full(one.shape, flag, jnp.int32) == 1, one, other)


def sided(first, second):
    flag = high_first()
    return pick(flag, second, first), pick(flag, first, second)


def load_surface_row(sz, target, row, source, base):
    for tile in range(sz.row_tiles):
        for channel in range(CHANNELS):
            at = base + tile * CHANNELS + channel
            target[row, channel, 0:1, cols(tile)] = source[pl.ds(at, 1), :]


def as_column(row, size):
    shape = (size, row.shape[1])
    diagonal = lax.broadcasted_iota(jnp.int32, shape, 0) == lax.broadcasted_iota(jnp.int32, shape, 1)
    return jnp.sum(jnp.where(diagonal, row, 0.0), axis=1, keepdims=True)


def setup_kernel(sz, entries, remap_entries, arrive, wet, remap, mix_rows, diffusivity, *outs):
    first_mix, first_rows, table, facts, mix = outs
    arrive_all(arrive)
    for row in range(sz.rows):
        first_rows[row] = diffusivity[row : row + 1, :]
    for index in range(CHANNELS * CHANNELS):
        column = as_column(mix_rows[index : index + 1, :], LEVELS)
        mix[index] = jnp.broadcast_to(column, (LEVELS, WIDTH))
    mix.start()
    first_mix[...] = mix[...]
    tiles, owners = wet[0:1, :], wet[1:2, :]
    size = -(-entries // SUBLANES) * SUBLANES
    shape = (size, wet.shape[1])
    tile_here, owner_here = as_column(tiles, size), as_column(owners, size)
    earlier = lax.broadcasted_iota(jnp.int32, shape, 1) < lax.broadcasted_iota(jnp.int32, shape, 0)
    same = (owner_here == owners) & earlier
    rank = jnp.sum(jnp.where(same, 1.0, 0.0), axis=1, keepdims=True)
    slot = jnp.where(owner_here >= 0.0, owner_here * sz.capacity + rank, -1.0)
    facts[...] = jnp.zeros((sz.facts, WIDTH), jnp.float32)
    for line in range(sz.slot_lines):
        place = lax.broadcasted_iota(jnp.int32, (size, WIDTH), 1) + line * WIDTH
        match = slot.astype(jnp.int32) == place
        told = jnp.sum(jnp.where(match, sz.tiles - tile_here, 0.0), axis=0, keepdims=True)
        facts[line : line + 1, :] = told
        table[line : line + 1, :] = sz.tiles - told.astype(jnp.int32)
    size = -(-remap_entries // SUBLANES) * SUBLANES
    at, amount = as_column(remap[0:1, :], size), as_column(remap[1:2, :], size)
    place = lax.broadcasted_iota(jnp.int32, (size, WIDTH), 1)
    facts[sz.slot_lines : sz.slot_lines + 1, :] = jnp.sum(
        jnp.where(at.astype(jnp.int32) == place, amount, 0.0), axis=0, keepdims=True
    )


def columns_kernel(sz, arrive, diffusivity, weight, *outs):
    diffusivity_rows, weight_rows, diffusivity_tiles, weight_tiles = outs
    arrive_all(arrive)
    for source, by_row, by_tile in (
        (diffusivity, diffusivity_rows, diffusivity_tiles),
        (weight, weight_rows, weight_tiles),
    ):
        for row in range(sz.rows):
            by_row[row] = source[row : row + 1, :]
            for tile in range(sz.row_tiles):
                line = source[row : row + 1, cols(tile)]
                at = (row * sz.row_tiles + tile) * CHANNELS
                by_tile[at : at + CHANNELS, :] = jnp.broadcast_to(line, (CHANNELS, WIDTH))


def gather_levels(block, channel, tile):
    sub = lax.broadcasted_iota(jnp.int32, (LEVELS, WIDTH), 0)
    total = None
    for level in range(LEVELS):
        line = block[level, channel : channel + 1, cols(tile)]
        line = jnp.broadcast_to(line, (LEVELS, WIDTH))
        total = line if total is None else jnp.where(sub == level, line, total)
    return total


def edges_kernel(sz, arrive, low_start, high_start, low_base, high_base, send_first, send_second):
    arrive_all(arrive)
    low_start[...] = low_start[...] + low_base[...]
    high_start[...] = high_start[...] + high_base[...]
    flag = high_first()
    for channel in range(CHANNELS):
        for tile in range(sz.row_tiles):
            low = gather_levels(low_start, channel, tile)
            high = gather_levels(high_start, channel, tile)
            at = (channel * sz.row_tiles + tile) * LEVELS
            send_first[at : at + LEVELS, :] = pick(flag, high, low)
            send_second[at : at + LEVELS, :] = pick(flag, low, high)


def load_kernel(sz, arrive, perturbation, base, field, start_block, base_block, in_sems):
    def arrivals(row):
        return [
            pltpu.make_async_copy(source.at[:, row], block.at[row], in_sems.at[index, row])
            for index, (source, block) in enumerate(
                ((perturbation, start_block), (base, base_block))
            )
        ]

    for row in range(sz.rows):
        for arrival in arrivals(row):
            arrival.start()

    def one_row(row, carry):
        for arrival in arrivals(row):
            arrival.wait()
        start_block[row] = start_block[row] + base_block[row]
        for channel in range(CHANNELS):
            for tile in range(sz.row_tiles):
                field[row, channel, :, cols(tile)] = gather_levels(
                    start_block.at[row], channel, tile
                )
        return carry

    lax.fori_loop(0, sz.rows, one_row, 0)


def relayout_kernel(sz, arrive, source, out, block, in_sems):
    def arrival(row):
        return pltpu.make_async_copy(source.at[:, row], block.at[row], in_sems.at[0, row])

    for row in range(sz.rows):
        arrival(row).start()

    def one_row(row, carry):
        arrival(row).wait()
        for channel in range(CHANNELS):
            for tile in range(sz.row_tiles):
                out[row, channel, :, cols(tile)] = gather_levels(block.at[row], channel, tile)
        out.row(row).start()
        return carry

    lax.fori_loop(0, sz.rows, one_row, 0)


class Remap:
    def __init__(self, sz, weights):
        self.sz, self.weights = sz, weights

    def weight(self, which, lat, row):
        line = which * self.sz.facts + self.sz.slot_lines
        return self.weights[line, lat * self.sz.rows + row]

    def own(self, lat, row):
        return self.weight(0, lat, row)

    def of_low(self, lat, row):
        return self.weight(1, lat + LAT_DEV, row)

    def of_high(self, lat, row):
        return self.weight(2, lat - LAT_DEV, row)


def tile_at(sz, tables, which, slot):
    return tables[which * sz.slot_lines + slot // WIDTH, slot % WIDTH]


def sum_of(weights, values):
    total = weights[0] * values[0]
    for weight, value in zip(weights[1:], values[1:]):
        total = total + weight * value
    return total


def own_sums(sz, remap, own, factor):
    return [
        factor * sum_of([remap.own(lat, row) for row in range(sz.rows)], own)
        for lat in range(NEAR_LAT)
    ]


def send_sums(sz, sums, tell_first, tell_second):
    flag = high_first()
    for index in range(LAT_DEV):
        low, high = sums[index], sums[LAT_DEV + index]
        at = index * sz.pitch
        tell_first[at : at + sz.row_tiles, :] = pick(flag, high, low)
        tell_second[at : at + sz.row_tiles, :] = pick(flag, low, high)


def lat_rows(sz, ref, lat):
    at = lat * sz.pitch
    return ref[at : at + sz.row_tiles, :]


def told_sums(sz, from_first, from_second):
    lows, highs = [], []
    for index in range(LAT_DEV):
        low, high = sided(lat_rows(sz, from_first, index), lat_rows(sz, from_second, index))
        lows.append(low)
        highs.append(high)
    return lows + highs


def place_edges(sz, padded, first, second, first_surface=None, second_surface=None):
    side = high_first() * (sz.rows + 1)
    for at, edge, surface in ((side, first, first_surface), (sz.rows + 1 - side, second, second_surface)):
        for channel in range(CHANNELS):
            for tile in range(sz.row_tiles):
                line = (channel * sz.row_tiles + tile) * LEVELS
                padded[at, channel, :, cols(tile)] = edge[line : line + LEVELS, :]
        if surface is not None:
            load_surface_row(sz, padded, at, surface, 0)


def store_rows(sz, surface, send_first, send_second, factor=None):
    row = high_first() * (sz.rows - 1)
    for at, send in ((row, send_first), (sz.rows - 1 - row, send_second)):
        for tile in range(sz.row_tiles):
            start = pl.multiple_of((at * sz.row_tiles + tile) * CHANNELS, CHANNELS)
            value = surface[pl.ds(start, CHANNELS), :]
            if factor is not None:
                value = factor[pl.ds(start, CHANNELS), :] * value
            send[tile * CHANNELS : (tile + 1) * CHANNELS, :] = value


def forward_load_kernel(sz, last, arrive, mix, diffusivity, *refs):
    refs = list(refs)
    if last:
        weight = refs.pop(0)
    field, surface = refs[:2]
    refs = refs[2:]
    if last:
        target = refs.pop(0)
    mix_out, rows_out, field_out = refs[:3]
    refs = refs[3:]
    if last:
        weight_out, target_out = refs[:2]
        refs = refs[2:]
    in_sems = refs[0]

    def arrivals(row):
        copies = [pltpu.make_async_copy(field.at[row], field_out.at[row], in_sems.at[0, row])]
        if last:
            copies.append(
                pltpu.make_async_copy(target.at[row], target_out.at[row], in_sems.at[1, row])
            )
        return copies

    for row in range(sz.rows):
        for arrival in arrivals(row):
            arrival.start()
    arrive_all(arrive)
    mix_out[...] = mix[...]
    rows_out[...] = diffusivity[...]
    if last:
        weight_out[...] = weight[...]

    def one_row(row, carry):
        for arrival in arrivals(row):
            arrival.wait()
        load_surface_row(sz, field_out, row, surface, row * sz.row_width)
        return carry

    lax.fori_loop(0, sz.rows, one_row, 0)


def forward_kernel(sz, first, last, arrive, *refs):
    refs = list(refs)
    tables, facts, low, high, diffusivity, mix, field = refs[:7]
    refs = refs[7:]
    if first:
        facts_block = refs.pop(0)
    surfaces = ()
    if not first:
        surfaces = refs[:2]
        refs = refs[2:]
    if last:
        weight, target = refs[:2]
        refs = refs[2:]
    out, drive, new_surface, packed, tell_first, tell_second, edge_first, edge_second, padded = refs
    remap = Remap(sz, facts)
    place_edges(sz, padded, low, high, *surfaces)

    def ready(row):
        padded[row + 1] = field[row]

    ready(0)
    lane = lax.broadcasted_iota(jnp.int32, (LEVELS, WIDTH), 1)
    masks = level_masks()
    count = sz.row_tiles

    def one_row(row, carry):
        @pl.when(row < sz.rows - 1)
        def _():
            ready(row + 1)

        tiles = RowTiles(count, lambda c, t: padded[row + 1, c, :, cols(t)])
        for t in range(count):
            coeff = jnp.broadcast_to(diffusivity[row, 0:1, cols(t)], (LEVELS, WIDTH))
            center = (1.0 - 2.0 * KAPPA_V) - 4.0 * coeff
            if last:
                scale = weight[row, 0:1, cols(t)]
                scale = jnp.broadcast_to(scale * scale, (LEVELS, WIDTH))
            for c in range(CHANNELS):
                mixed = mix[c * CHANNELS] * tiles.here(0, t)
                for k in range(1, CHANNELS):
                    mixed = mixed + mix[c * CHANNELS + k] * tiles.here(k, t)
                bent = jnp.tanh(mixed)
                drive[row, c, :, cols(t)] = bent
                field_here = tiles.here(c, t)
                around = tiles.around(c, t, lane)
                around = around + (padded[row, c, :, cols(t)] + padded[row + 2, c, :, cols(t)])
                stepped = (
                    center * field_here
                    + coeff * around
                    + levels_sum(field_here, masks)
                    + TIME_STEP * bent
                )
                new_surface[pl.ds((row * count + t) * CHANNELS + c, 1), :] = stepped[0:1, :]
                if last:
                    stepped = scale * (stepped - target[row, c, :, cols(t)])
                out[row, c, :, cols(t)] = stepped
        drive.row(row).start()
        out.row(row).start()
        return carry

    lax.fori_loop(0, sz.rows, one_row, 0)
    new_surface[CHANNELS * sz.tiles :, :] = jnp.zeros((CHANNELS, WIDTH), jnp.float32)
    new_surface.start()
    arrive_all(arrive)
    pack_slots(sz, tables, new_surface, packed)
    packed.start()
    own = [row_tiles_of(sz, new_surface.block, row) for row in range(sz.rows)]
    send_sums(sz, own_sums(sz, remap, own, 1.0), tell_first, tell_second)
    for tell in (tell_first, tell_second):
        if first:
            tell[sz.lat_lines :, :] = facts_block[...]
        tell.start()
    store_edges(sz, out, diffusivity if last else None, edge_first, edge_second)


def pack_slots(sz, tables, surface, packed):
    for slot in range(sz.slots):
        at = pl.multiple_of(tile_at(sz, tables, 0, slot) * CHANNELS, CHANNELS)
        packed[slot * CHANNELS : (slot + 1) * CHANNELS, :] = surface[pl.ds(at, CHANNELS), :]


def store_edges(sz, field, diffusivity, send_first, send_second):
    outer = high_first() * (sz.rows - 1)
    for row, send in ((outer, send_first), (sz.rows - 1 - outer, send_second)):
        for channel in range(CHANNELS):
            for tile in range(sz.row_tiles):
                value = field[row, channel, :, cols(tile)]
                if diffusivity is not None:
                    value = value * jnp.broadcast_to(
                        diffusivity[row, 0:1, cols(tile)], (LEVELS, WIDTH)
                    )
                at = (channel * sz.row_tiles + tile) * LEVELS
                send[at : at + LEVELS, :] = value
        send.start()


def owner_kernel(sz, decode, arrive, arrived, mixing, air, wind, facts, *refs):
    slots = sz.slots
    if decode:
        told_first, told_second, own_table, own_facts, tables, weights = refs[:6]
        refs = refs[6:]
    flux, mixed_slope, flux_slope, flat, first = refs
    def bulk(row, column):
        return facts[sz.slot_lines, sz.bulk_at + row * CHANNELS + column]

    values = [arrived[pl.ds(c, slots, stride=CHANNELS), :] for c in range(CHANNELS)]
    mixed = jnp.tanh(
        jnp.dot(
            mixing[...],
            jnp.concatenate(values, axis=1),
            precision=HIGHEST,
            preferred_element_type=jnp.float32,
        )
    )
    contrast = []
    for c in range(CHANNELS):
        mixed_here = mixed[:, cols(c)]
        mixed_slope[c] = 1.0 - mixed_here * mixed_here
        contrast.append((air[...] - values[0] if c == 0 else values[c]) + mixed_here)
    mixed_slope.start()
    arrive_all(arrive)
    if decode:
        lines = sz.slot_lines
        tables[0:lines, :] = own_table[...]
        weights[0 : sz.facts, :] = own_facts[...]
        both = sided(told_first[sz.lat_lines :, :], told_second[sz.lat_lines :, :])
        for which, told in ((1, both[0]), (2, both[1])):
            got = told[0:lines, :].astype(jnp.int32)
            tables[which * lines : (which + 1) * lines, :] = sz.tiles - got
            at = which * sz.facts
            weights[at : at + sz.facts, :] = told
        tables.start()
        weights.start()

    rate = FLUX_RATE * wind[...]
    for c in range(CHANNELS):
        forcing = bulk(c, 0) * contrast[0]
        for k in range(1, CHANNELS):
            forcing = forcing + bulk(c, k) * contrast[k]
        bent = jnp.tanh(forcing)
        flux_slope[c] = rate * (1.0 - bent * bent)
        one = rate * bent
        flat[pl.ds(c, slots, stride=CHANNELS), :] = one
        if c == 0:
            first[...] = one
    flux_slope.start()
    cap = sz.capacity
    gap = jnp.zeros((sz.chunk - sz.own_rows, WIDTH), jnp.float32)
    for d in range(sz.devices):
        at = d * sz.chunk
        flux[at : at + sz.own_rows, :] = flat[d * sz.own_rows : (d + 1) * sz.own_rows, :]
        at = at + sz.own_rows
        flux[at : (d + 1) * sz.chunk, :] = gap
        if d > 0:
            flux[at : at + cap, :] = first[(d - 1) * cap : d * cap, :]
        if d < sz.devices - 1:
            flux[at + cap : at + 2 * cap, :] = first[(d + 1) * cap : (d + 2) * cap, :]


def owner_back_kernel(sz, arrive, arrived, mixing, mixed_slope, flux_slope, facts, back, flat, extra):
    slots, cap = sz.slots, sz.capacity

    def bulk(row, column):
        return facts[sz.slot_lines, sz.bulk_at + row * CHANNELS + column]

    for d in range(sz.devices):
        at = d * sz.chunk
        flat[d * sz.own_rows : (d + 1) * sz.own_rows, :] = arrived[at : at + sz.own_rows, :]
        more = jnp.zeros((cap, WIDTH), jnp.float32)
        if d < sz.devices - 1:
            at = (d + 1) * sz.chunk + sz.own_rows
            more = more + arrived[at : at + cap, :]
        if d > 0:
            at = (d - 1) * sz.chunk + sz.own_rows + cap
            more = more + arrived[at : at + cap, :]
        extra[d * cap : (d + 1) * cap, :] = more
    arrive_all(arrive)
    forced = []
    for c in range(CHANNELS):
        got = flat[pl.ds(c, slots, stride=CHANNELS), :]
        if c == 0:
            got = got + extra[...]
        forced.append(flux_slope[c] * got)
    direct = []
    for k in range(CHANNELS):
        total = bulk(0, k) * forced[0]
        for c in range(1, CHANNELS):
            total = total + bulk(c, k) * forced[c]
        direct.append(total)
    through = lax.dot_general(
        mixing[...],
        jnp.concatenate([direct[k] * mixed_slope[k] for k in range(CHANNELS)], axis=1),
        (((0,), (0,)), ((), ())),
        precision=HIGHEST,
        preferred_element_type=jnp.float32,
    )
    for k in range(CHANNELS):
        sign = -1.0 if k == 0 else 1.0
        back.block[pl.ds(k, slots, stride=CHANNELS), :] = through[:, cols(k)] + sign * direct[k]


def spread_back(sz, surface, slope, remap, tables, packed, near_low, near_high, tell_first, tell_second):
    rows, count, cap = sz.rows, sz.row_tiles, sz.capacity
    block = surface.block
    own = [row_tiles_of(sz, block, row) for row in range(rows)]
    sums = own_sums(sz, remap, own, FEEDBACK)
    send_sums(sz, sums, tell_first, tell_second)
    tell_first.start()
    tell_second.start()
    lats = [lat_rows(sz, slope, lat) * sums[lat] for lat in range(NEAR_LAT)]
    every = range(NEAR_LAT)
    for row in range(rows):
        added = sum_of([remap.own(lat, row) for lat in every], lats)
        put_row_tiles(sz, block, row, own[row] + added)
        at = row * count
        near_low[at : at + count, :] = sum_of(
            [remap.of_low(lat, row) for lat in range(LAT_DEV)], lats[:LAT_DEV]
        )
        near_high[at : at + count, :] = sum_of(
            [remap.of_high(lat, row) for lat in range(LAT_DEV, NEAR_LAT)], lats[LAT_DEV:]
        )
    rest = sz.near[0] - sz.tiles
    near_low[sz.tiles :, :] = jnp.zeros((rest, WIDTH), jnp.float32)
    near_high[sz.tiles :, :] = jnp.zeros((rest, WIDTH), jnp.float32)
    surface.start()
    gap = jnp.zeros((sz.chunk - sz.own_rows, WIDTH), jnp.float32)
    for owner in range(sz.devices):
        packed[owner * sz.chunk + sz.own_rows : (owner + 1) * sz.chunk, :] = gap
    for slot in range(sz.slots):
        owner, rank = slot // cap, slot % cap
        at = owner * sz.chunk + rank * CHANNELS
        tile = pl.multiple_of(tile_at(sz, tables, 0, slot) * CHANNELS, CHANNELS)
        packed[at : at + CHANNELS, :] = surface[pl.ds(tile, CHANNELS), :]
        at = owner * sz.chunk + sz.own_rows + rank
        packed[at : at + 1, :] = near_low[pl.ds(tile_at(sz, tables, 1, slot), 1), :]
        at = at + cap
        packed[at : at + 1, :] = near_high[pl.ds(tile_at(sz, tables, 2, slot), 1), :]


def surface_kernel(sz, last, arrive, *refs):
    refs = list(refs)
    flux, from_first, from_second, before, tables, weights = refs[:6]
    refs = refs[6:]
    if last:
        target, weight = refs[:2]
        surface, slope, packed, tell_first, tell_second, near_low, near_high = refs[2:]
        block = surface.block
    else:
        surface, send_first, send_second, slope, near_low, near_high = refs
        block = surface
    remap = Remap(sz, weights)
    arrive_all(arrive)
    rows, cap = sz.rows, sz.capacity
    block[...] = before[...]
    near_low[...] = jnp.zeros(sz.near, jnp.float32)
    near_high[...] = jnp.zeros(sz.near, jnp.float32)
    for slot in range(sz.slots):
        owner, rank = slot // cap, slot % cap
        at = owner * sz.chunk + rank * CHANNELS
        tile = pl.multiple_of(tile_at(sz, tables, 0, slot) * CHANNELS, CHANNELS)
        block[pl.ds(tile, CHANNELS), :] = (
            before[pl.ds(tile, CHANNELS), :] + flux[at : at + CHANNELS, :]
        )
        at = owner * sz.chunk + sz.own_rows + rank
        near_low[pl.ds(tile_at(sz, tables, 1, slot), 1), :] = flux[at : at + 1, :]
        at = at + cap
        near_high[pl.ds(tile_at(sz, tables, 2, slot), 1), :] = flux[at : at + 1, :]
    block[CHANNELS * sz.tiles :, :] = jnp.zeros((CHANNELS, WIDTH), jnp.float32)
    own = [row_tiles_of(sz, block, row) for row in range(rows)]
    sums = own_sums(sz, remap, own, 1.0)
    told = told_sums(sz, from_first, from_second)
    air = []
    for lat in range(NEAR_LAT):
        if lat < LAT_DEV:
            near, weights = near_low, [remap.of_low(lat, row) for row in range(rows)]
        else:
            near, weights = near_high, [remap.of_high(lat, row) for row in range(rows)]
        more = sum_of(weights, [near_row(sz, near, row) for row in range(rows)])
        one = jnp.tanh(sums[lat] + told[lat] + more)
        slope[lat * sz.pitch : lat * sz.pitch + sz.row_tiles, :] = 1.0 - one * one
        air.append(one)
    slope.start()
    for row in range(rows):
        weights = [remap.own(lat, row) for lat in range(NEAR_LAT)]
        put_row_tiles(sz, block, row, own[row] + FEEDBACK * sum_of(weights, air))
    if last:
        for row in range(rows):
            for tile in range(sz.row_tiles):
                at = row * sz.row_width + tile * CHANNELS
                scale = weight[at : at + CHANNELS, :]
                off = block[at : at + CHANNELS, :] - target[row, :, cols(tile)]
                block[at : at + CHANNELS, :] = scale * scale * off
        spread_back(
            sz, surface, slope, remap, tables, packed, near_low, near_high, tell_first, tell_second
        )
    else:
        store_rows(sz, surface, send_first, send_second)


def merge_kernel(
    sz, arrive, back, from_first, from_second, before, slope, tables, facts, diffusivity, surface, send_first, send_second
):
    rows = sz.rows
    remap = Remap(sz, facts)
    arrive_all(arrive)
    surface[...] = before[...]
    for slot in range(sz.slots):
        tile = pl.multiple_of(tile_at(sz, tables, 0, slot) * CHANNELS, CHANNELS)
        surface[pl.ds(tile, CHANNELS), :] = (
            before[pl.ds(tile, CHANNELS), :] + back[slot * CHANNELS : (slot + 1) * CHANNELS, :]
        )
    surface[CHANNELS * sz.tiles :, :] = jnp.zeros((CHANNELS, WIDTH), jnp.float32)
    told = told_sums(sz, from_first, from_second)
    lats = [lat_rows(sz, slope, lat) * told[lat] for lat in range(NEAR_LAT)]
    for row in range(rows):
        own = row_tiles_of(sz, surface, row)
        weights = [remap.own(lat, row) for lat in range(NEAR_LAT)]
        put_row_tiles(sz, surface, row, own + sum_of(weights, lats))
    store_rows(sz, surface, send_first, send_second, diffusivity)


def backward_load_kernel(sz, last, arrive, mix, diffusivity, field, drive, surface, *refs):
    refs = list(refs)
    if last:
        perturbation = refs.pop(0)
    mix_out, rows_out, local, bent_all, scaled = refs[:5]
    refs = refs[5:]
    if last:
        start_all = refs.pop(0)
    in_sems = refs[0]

    def arrivals(row):
        copies = [
            pltpu.make_async_copy(field.at[row], local.at[row], in_sems.at[0, row]),
            pltpu.make_async_copy(drive.at[row], bent_all.at[row], in_sems.at[1, row]),
        ]
        if last:
            copies.append(
                pltpu.make_async_copy(perturbation.at[row], start_all.at[row], in_sems.at[2, row])
            )
        return copies

    for row in range(sz.rows):
        for arrival in arrivals(row):
            arrival.start()
    arrive_all(arrive)
    mix_out[...] = mix[...]
    rows_out[...] = diffusivity[...]

    def one_row(row, carry):
        for arrival in arrivals(row):
            arrival.wait()
        load_surface_row(sz, local, row, surface, row * sz.row_width)
        for t in range(sz.row_tiles):
            coeff = jnp.broadcast_to(diffusivity[row, 0:1, cols(t)], (LEVELS, WIDTH))
            for c in range(CHANNELS):
                scaled[row, c, :, cols(t)] = coeff * local[row, c, :, cols(t)]
        return carry

    lax.fori_loop(0, sz.rows, one_row, 0)


def backward_kernel(sz, last, arrive, *refs):
    refs = list(refs)
    if not last:
        tables, weights, slope = refs[:3]
        refs = refs[3:]
    low, high, first_surface, second_surface, diffusivity, mix = refs[:6]
    local, bent_all, scaled_all = refs[6:9]
    refs = refs[9:]
    if last:
        start_all, out, sums, padded = refs
    else:
        out, new_surface, packed, tell_first, tell_second, edge_first, edge_second = refs[:7]
        padded, near_low, near_high = refs[7:]
        remap = Remap(sz, weights)
    count = sz.row_tiles
    place_edges(sz, padded, low, high, first_surface, second_surface)

    def ready(row):
        padded[row + 1] = scaled_all[row]

    ready(0)
    lane = lax.broadcasted_iota(jnp.int32, (LEVELS, WIDTH), 1)
    masks = level_masks()

    def one_row(row, carry):
        @pl.when(row < sz.rows - 1)
        def _():
            ready(row + 1)

        tiles = RowTiles(count, lambda c, t: padded[row + 1, c, :, cols(t)])
        for t in range(count):
            here, bent = [], []
            for c in range(CHANNELS):
                value = local[row, c, :, cols(t)]
                one = bent_all[row, c, :, cols(t)]
                here.append(value)
                bent.append((1.0 - one * one) * value)
            for c in range(CHANNELS):
                mixed = mix[c] * bent[0]
                for k in range(1, CHANNELS):
                    mixed = mixed + mix[k * CHANNELS + c] * bent[k]
                around = tiles.around(c, t, lane)
                around = around + (padded[row, c, :, cols(t)] + padded[row + 2, c, :, cols(t)])
                stepped = (
                    ((1.0 - 2.0 * KAPPA_V) * here[c] - 4.0 * tiles.here(c, t))
                    + around
                    + levels_sum(here[c], masks)
                    + TIME_STEP * mixed
                )
                out[row, c, :, cols(t)] = stepped
                if last:
                    start = start_all[row, c, :, cols(t)]
                    carry = (
                        carry[0] + start * start,
                        carry[1] + start * stepped,
                        carry[2] + stepped * stepped,
                    )
                else:
                    new_surface[pl.ds((row * count + t) * CHANNELS + c, 1), :] = stepped[0:1, :]
        out.row(row).start()
        return carry

    blank = jnp.zeros((LEVELS, WIDTH), jnp.float32)
    totals = lax.fori_loop(0, sz.rows, one_row, (blank, blank, blank) if last else 0)
    if last:
        place = lax.broadcasted_iota(jnp.int32, sums.block.shape, 1)
        held = jnp.zeros(sums.block.shape, jnp.float32)
        for index in range(3):
            total = jnp.sum(jnp.sum(totals[index], axis=0, keepdims=True), axis=1, keepdims=True)
            held = jnp.where(place == index, total, held)
        sums[...] = held
    else:
        new_surface[CHANNELS * sz.tiles :, :] = jnp.zeros((CHANNELS, WIDTH), jnp.float32)
        arrive_all(arrive)
        spread_back(
            sz,
            new_surface,
            slope,
            remap,
            tables,
            packed,
            near_low,
            near_high,
            tell_first,
            tell_second,
        )
        packed.start()
        store_edges(sz, out, diffusivity, edge_first, edge_second)


def final_kernel(cell_total, arrive, everyones, perturbation, gradient, out):
    sums = jnp.sum(everyones[...], axis=0, keepdims=True) / cell_total
    place = lax.broadcasted_iota(jnp.int32, sums.shape, 1)
    means = [
        jnp.broadcast_to(
            jnp.sum(jnp.where(place == index, sums, 0.0), axis=1, keepdims=True), (1, WIDTH)
        )
        for index in range(3)
    ]
    scale = lax.rsqrt(means[2] + EPSILON)
    mean_sq = means[0] + 2.0 * ASCENT * scale * means[1] + ASCENT * ASCENT * scale * scale * means[2]
    shrink = lax.rsqrt(mean_sq + EPSILON)
    step = jnp.broadcast_to(ASCENT * scale * shrink, (CHANNELS, WIDTH))
    shrink = jnp.broadcast_to(shrink, (CHANNELS, WIDTH))
    levels, rows, _, cells = perturbation.shape

    def one_level(level, carry):
        for row in range(rows):
            for tile in range(cells // WIDTH):
                start = perturbation[level, row, :, cols(tile)]
                slope = gradient[level, row, :, cols(tile)]
                out[level, row, :, cols(tile)] = shrink * start + step * slope
        out.row(level).start()
        return carry

    lax.fori_loop(0, levels, one_level, 0)


class Operand:
    def __init__(self, array, space, fetch=None, at=()):
        self.array, self.space, self.fetch, self.at = array, space, fetch, at

    def block(self):
        whole = self.array.shape
        taken = [size for size, index in zip(whole, self.at) if isinstance(index, slice)]
        return self.fetch((*taken, *whole[len(self.at) :]), self.array.dtype)


def near_by(*arrays):
    return [Operand(array, pltpu.VMEM) for array in arrays]


def far_off(*arrays):
    return [
        Operand(pltpu.with_memory_space_constraint(array, pltpu.HBM), pltpu.HBM)
        for array in arrays
    ]


def fetched(*arrays, at=(), into=pltpu.VMEM):
    return [
        Operand(pltpu.with_memory_space_constraint(array, pltpu.HBM), pltpu.HBM, into, at)
        for array in arrays
    ]


def scalars(*arrays):
    return fetched(*arrays, into=pltpu.SMEM)


def call(kernel, name, inputs, kept=(), shipped=(), scratch=()):
    n_in, n_kept, n_out = len(inputs), len(kept), len(shipped)
    brought = [index for index, item in enumerate(inputs) if item.fetch is not None]

    def as_shape(item):
        return item if isinstance(item, jax.ShapeDtypeStruct) else jax.ShapeDtypeStruct(item, jnp.float32)

    kept = [as_shape(item) for item in kept]
    shipped = [as_shape(item) for item in shipped]

    def run(*refs):
        ins = list(refs[:n_in])
        kept_refs = refs[n_in : n_in + n_kept]
        homes = refs[n_in + n_kept : n_in + n_kept + n_out]
        rest = refs[n_in + n_kept + n_out :]
        outs = [
            Shipped(block, home, sems)
            for block, home, sems in zip(rest[:n_out], homes, rest[n_out : 2 * n_out])
        ]
        rest = rest[2 * n_out :]
        if brought:
            blocks, arrive_sems = rest[: len(brought)], rest[len(brought)]
            rest = rest[len(brought) + 1 :]
            copies = []
            for place, (index, block) in enumerate(zip(brought, blocks)):
                source = ins[index]
                if inputs[index].at:
                    source = source.at[inputs[index].at]
                copies.append(pltpu.make_async_copy(source, block, arrive_sems.at[place]))
                ins[index] = block
            for copy in copies:
                copy.start()
            arrive = [copy.wait for copy in copies]
        else:
            arrive = []
        kernel(arrive, *ins, *kept_refs, *outs, *rest)
        for out in outs:
            if not out.started:
                out.start()
        for out in outs:
            out.finish(out.block.shape[0])

    spaces = [pltpu.VMEM] * n_kept + [pltpu.HBM] * n_out
    blocks = [pltpu.VMEM(item.shape, item.dtype) for item in shipped]
    sems = [
        pltpu.SemaphoreType.DMA((item.shape[0] if len(item.shape) > 3 else 1,)) for item in shipped
    ]
    arriving = [inputs[index].block() for index in brought]
    if brought:
        arriving.append(pltpu.SemaphoreType.DMA((len(brought),)))
    more = [
        item if not isinstance(item, tuple) else pltpu.VMEM(item, jnp.float32) for item in scratch
    ]
    return pl.pallas_call(
        run,
        name=name,
        in_specs=[pl.BlockSpec(memory_space=item.space) for item in inputs],
        out_specs=[pl.BlockSpec(memory_space=space) for space in spaces],
        out_shape=kept + [pltpu.HBM(item.shape, item.dtype) for item in shipped],
        scratch_shapes=blocks + sems + arriving + more,
        compiler_params=pltpu.CompilerParams(vmem_limit_bytes=VMEM_BYTES),
    )(*[item.array for item in inputs])


def arrive_all(arrive):
    for wait in arrive:
        wait()


def swap(first, second):
    count = lax.axis_size("horiz")
    inner = [(i, i ^ 1) for i in range(count)]
    outer = [(i, i + 1) for i in range(1, count - 1, 2)]
    outer = outer + [(target, source) for source, target in outer]
    return lax.ppermute(first, "horiz", inner), lax.ppermute(second, "horiz", outer)


def exchange(array, devices):
    rows = array.shape[0] // devices
    step = CHANNELS if rows % CHANNELS == 0 else 2
    split = array.reshape(devices, rows // step, step, WIDTH)
    moved = lax.all_to_all(split, "horiz", split_axis=0, concat_axis=0, tiled=True)
    return moved.reshape(array.shape)


def body(
    perturbation,
    base_state,
    target_state,
    cost_weight,
    diffusivity,
    chan_mix,
    coupler_mix,
    owner_mix,
    air_temp,
    wind_speed,
    wet_list,
    wet_owner,
    remap_src,
    remap_tgt,
    remap_weight,
):
    devices = lax.axis_size("horiz")
    hours = air_temp.shape[0]
    sz = Sizes(devices, air_temp.shape[2] // devices, base_state.shape[1], base_state.shape[3])
    rows = sz.rows
    native_row = (LEVELS, CHANNELS, sz.cells)

    edge_inputs = []
    for array in (perturbation, base_state):
        for row in (0, rows - 1):
            edge_inputs += fetched(array, at=(slice(None), row))
    edges = swap(
        *call(functools.partial(edges_kernel, sz), "edges", edge_inputs, kept=[sz.edge, sz.edge])
    )
    me = lax.axis_index("horiz").astype(jnp.int32)

    def lined(first_row, second_row):
        size = -(-first_row.shape[0] // WIDTH) * WIDTH
        pair = jnp.stack([first_row.astype(jnp.float32), second_row.astype(jnp.float32)])
        return jnp.pad(pair, ((0, 0), (0, size - pair.shape[1])), constant_values=-1.0)

    places = jnp.arange(CHANNELS * CHANNELS, dtype=jnp.int32) + sz.bulk_at
    remap_at = (remap_tgt - (me * LAT_DEV - 1)) * rows + remap_src - me * rows
    remap_lines = lined(
        jnp.concatenate([remap_at, places]),
        jnp.concatenate([remap_weight, coupler_mix.reshape(-1)]),
    )
    mix_rows = chan_mix.transpose(1, 2, 0).reshape(CHANNELS * CHANNELS, LEVELS)
    row_lines = (rows, 1, sz.cells)
    tiles_lines = (CHANNELS * sz.tiles, WIDTH)
    first_mix, first_rows, table, facts, mix = call(
        functools.partial(setup_kernel, sz, wet_list.shape[1], remap_at.shape[0] + places.shape[0]),
        "setup",
        near_by(lined(wet_list[0], wet_owner[0]), remap_lines, mix_rows)
        + fetched(diffusivity),
        kept=[(CHANNELS * CHANNELS, LEVELS, WIDTH), row_lines],
        shipped=[
            jax.ShapeDtypeStruct((sz.slot_lines, WIDTH), jnp.int32),
            (sz.facts, WIDTH),
            (CHANNELS * CHANNELS, LEVELS, WIDTH),
        ],
    )
    wider = (rows + 2, CHANNELS, LEVELS, sz.cells)
    row_surface = (sz.row_width, WIDTH)
    by_row = (rows, *native_row)

    def row_sems(kinds):
        return pltpu.SemaphoreType.DMA((kinds, rows))

    (field,) = call(
        functools.partial(load_kernel, sz),
        "load",
        far_off(perturbation, base_state),
        kept=[sz.whole],
        scratch=[by_row, by_row, row_sems(2)],
    )

    def relayout(array):
        return call(
            functools.partial(relayout_kernel, sz),
            "relayout",
            far_off(array),
            shipped=[sz.whole],
            scratch=[by_row, row_sems(1)],
        )

    saved = []
    near = [sz.near, sz.near]
    mix_shape = (CHANNELS * CHANNELS, LEVELS, WIDTH)
    by_slot = (sz.slots, WIDTH)
    for hour in range(hours):
        first, last = hour == 0, hour == hours - 1
        inputs = scalars(table, facts)
        if first:
            inputs += near_by(*edges, first_rows, first_mix, field) + fetched(facts)
            assert not last
        else:
            loads = fetched(mix, diffusivity_rows, *([weight_rows] if last else []))
            loads += far_off(field) + near_by(surface) + (far_off(target) if last else [])
            mix_here, rows_here, field, *more = call(
                functools.partial(forward_load_kernel, sz, last),
                "step_load",
                loads,
                kept=[mix_shape, row_lines, sz.whole] + ([row_lines, sz.whole] if last else []),
                scratch=[row_sems(2)],
            )
            inputs += near_by(*edges, rows_here, mix_here, field, *surface_edges, *more)
        field, drive, surface, packed, *sends = call(
            functools.partial(forward_kernel, sz, first, last),
            "step",
            inputs,
            shipped=[sz.whole, sz.whole, sz.surface, sz.narrow]
            + [sz.told if first else sz.lats] * 2
            + [sz.edge] * 2,
            scratch=[wider],
        )
        arrived = exchange(packed, devices)
        got = swap(*sends[:2])
        arrived, *got = lax.optimization_barrier((arrived, *got))
        inputs = (
            near_by(arrived, owner_mix[0], air_temp[hour, 0], wind_speed[hour, 0])
            + scalars(facts)
        )
        decoded = []
        if first:
            inputs += near_by(*got) + fetched(table, facts)
            decoded = [jax.ShapeDtypeStruct(sz.tables, jnp.int32), sz.weights]
        *decoded, flux, mixed_slope, flux_slope = call(
            functools.partial(owner_kernel, sz, first),
            "owners",
            inputs,
            shipped=[*decoded, sz.wide, sz.by_slot, sz.by_slot],
            scratch=[sz.narrow, by_slot],
        )
        if first:
            tables, weights = decoded
        flux, *sends = lax.optimization_barrier((flux, *sends[2:]))
        if first:
            flux, diffusivity, target_state = lax.optimization_barrier(
                (flux, diffusivity, target_state)
            )
            beside = call(
                functools.partial(columns_kernel, sz),
                "columns",
                fetched(diffusivity, cost_weight),
                shipped=[row_lines, row_lines, tiles_lines, tiles_lines],
            ) + relayout(target_state)
        else:
            flux, perturbation = lax.optimization_barrier((flux, perturbation))
            beside = relayout(perturbation)
        flux = exchange(flux, devices)
        flux, *beside = lax.optimization_barrier((flux, *beside))
        if first:
            diffusivity_rows, weight_rows, diffusivity_tiles, weight_tiles, target = beside
        else:
            start_field = beside[0]
        edges = swap(*sends)
        inputs = near_by(flux, *got) + fetched(surface) + scalars(tables, weights)
        if last:
            surface, slope, packed, *sends = call(
                functools.partial(surface_kernel, sz, True),
                "surface",
                inputs + fetched(target_state, at=(0,)) + fetched(weight_tiles),
                shipped=[sz.surface, sz.slope, sz.wide, sz.lats, sz.lats],
                scratch=near,
            )
        else:
            surface, *sends, slope = call(
                functools.partial(surface_kernel, sz, False),
                "surface",
                inputs,
                kept=[sz.surface, row_surface, row_surface],
                shipped=[sz.slope],
                scratch=near,
            )
            surface_edges = swap(*sends)
        saved.append((drive, slope, mixed_slope, flux_slope))

    edge_sends = None
    for hour in reversed(range(hours)):
        drive, slope, mixed_slope, flux_slope = saved[hour]
        arrived = exchange(packed, devices)
        got = swap(*sends)
        arrived, *got = lax.optimization_barrier((arrived, *got))
        back = call(
            functools.partial(owner_back_kernel, sz),
            "owners_back",
            near_by(arrived, owner_mix[0]) + fetched(mixed_slope, flux_slope) + scalars(facts),
            shipped=[sz.narrow],
            scratch=[sz.narrow, by_slot],
        )[0]
        if edge_sends is not None:
            back, *edge_sends = lax.optimization_barrier((back, *edge_sends))
            edges = swap(*edge_sends)
        back = exchange(back, devices)
        surface, *row_sends = call(
            functools.partial(merge_kernel, sz),
            "merge",
            near_by(back, *got)
            + fetched(surface, slope)
            + scalars(table, facts)
            + fetched(diffusivity_tiles),
            kept=[sz.surface, row_surface, row_surface],
        )
        surface_edges = swap(*row_sends)
        last = hour == 0
        mix_here, rows_here, *loaded = call(
            functools.partial(backward_load_kernel, sz, last),
            "step_back_load",
            fetched(mix, diffusivity_rows)
            + far_off(field, drive)
            + near_by(surface)
            + (far_off(start_field) if last else []),
            kept=[mix_shape, row_lines] + [sz.whole] * (4 if last else 3),
            scratch=[row_sems(3)],
        )
        inputs = near_by(*edges, *surface_edges, rows_here, mix_here, *loaded)
        if last:
            gradient, sums = call(
                functools.partial(backward_kernel, sz, True),
                "step_back_sums",
                inputs,
                shipped=[sz.whole, (devices, WIDTH)],
                scratch=[wider],
            )
        else:
            field, surface, packed, *outs = call(
                functools.partial(backward_kernel, sz, False),
                "step_back",
                scalars(tables, weights) + fetched(saved[hour - 1][1]) + inputs,
                shipped=[sz.whole, sz.surface, sz.wide, sz.lats, sz.lats, sz.edge, sz.edge],
                scratch=[wider, *near],
            )
            sends, edge_sends = outs[:2], outs[2:]

    everyones = lax.all_to_all(sums, "horiz", split_axis=0, concat_axis=0, tiled=True)
    block = perturbation.shape
    return call(
        functools.partial(final_kernel, perturbation.size * devices),
        "finish",
        near_by(everyones, perturbation, gradient.transpose(2, 0, 1, 3)),
        shipped=[block],
    )[0]


def solution(mesh):
    placed = (
        P("member", "horiz", None, None),
        P(None, "horiz", None, None),
        P(None, "horiz", None, None),
        P("horiz", None),
        P("horiz", None),
        P(),
        P(),
        P("horiz", None, None),
        P(None, "horiz", None, None),
        P(None, "horiz", None, None),
        P("horiz", None),
        P("horiz", None),
        P("horiz"),
        P("horiz"),
        P("horiz"),
    )
    return jax.shard_map(
        body,
        mesh=mesh,
        in_specs=placed,
        out_specs=P("member", "horiz", None, None),
        check_vma=False,
    )
```

```python
import functools

import jax
import jax.numpy as jnp
from jax import lax
from jax.experimental import pallas as pl
from jax.experimental.pallas import tpu as pltpu
from jax.sharding import PartitionSpec as P

LAT_DEV = 2
NEAR_LAT = LAT_DEV + 2
CHANNELS = 4
LEVELS = 8
WIDTH = 128
SUBLANES = 8

KAPPA_V = 0.1
TIME_STEP = 0.3
FLUX_RATE = 0.05
FEEDBACK = 0.5
ASCENT = 0.5
EPSILON = 1e-06
HIGHEST = lax.Precision.HIGHEST
VMEM_BYTES = 32 * 1024 * 1024


class Sizes:
    def __init__(self, devices, capacity, rows, cells):
        self.devices = devices
        self.capacity = capacity
        self.slots = devices * capacity
        self.rows = rows
        self.cells = cells
        self.row_tiles = cells // WIDTH
        self.tiles = rows * self.row_tiles
        self.row_width = CHANNELS * self.row_tiles
        self.pitch = -(-self.row_tiles // SUBLANES) * SUBLANES
        self.own_rows = CHANNELS * capacity
        self.chunk = self.own_rows + 2 * capacity
        self.slot_lines = -(-self.slots // WIDTH)
        self.facts = -(-(self.slot_lines + 1) // SUBLANES) * SUBLANES
        self.lat_lines = LAT_DEV * self.pitch
        self.edge_lines = CHANNELS * self.row_tiles * LEVELS
        self.whole = (rows, CHANNELS, LEVELS, cells)
        self.edge = (self.edge_lines, WIDTH)
        self.told = (self.lat_lines + self.facts, WIDTH)
        self.surface = (CHANNELS * (self.tiles + 1), WIDTH)
        self.narrow = (CHANNELS * self.slots, WIDTH)
        self.wide = (devices * self.chunk, WIDTH)
        self.slope = (NEAR_LAT * self.pitch, WIDTH)
        self.lats = (self.lat_lines, WIDTH)
        self.bulk_at = NEAR_LAT * rows
        self.tables = (3 * self.slot_lines, WIDTH)
        self.weights = (3, WIDTH)
        self.near = (-(-(self.tiles + 1) // SUBLANES) * SUBLANES, WIDTH)
        self.by_slot = (CHANNELS, self.slots, WIDTH)


class Shipped:
    def __init__(self, block, home, sems):
        self.block, self.home, self.sems = block, home, sems
        self.by_row = False
        self.started = False

    def __getitem__(self, at):
        return self.block[at]

    def __setitem__(self, at, value):
        self.block[at] = value

    def row(self, index):
        self.by_row = True
        self.started = True
        return pltpu.make_async_copy(
            self.block.at[index], self.home.at[index], self.sems.at[index]
        )

    def all(self):
        return pltpu.make_async_copy(self.block, self.home, self.sems.at[0])

    def start(self):
        self.started = True
        self.all().start()

    def finish(self, rows):
        if self.by_row:
            for index in range(rows):
                self.row(index).wait()
        else:
            self.all().wait()


def cols(tile):
    return slice(tile * WIDTH, (tile + 1) * WIDTH)


def lanes_sum(left_here, left_before, right_here, right_after, lane):
    return jnp.where(lane == 0, left_before, left_here) + jnp.where(
        lane == WIDTH - 1, right_after, right_here
    )


def level_masks():
    sub = lax.broadcasted_iota(jnp.int32, (LEVELS, WIDTH), 0)
    return jnp.where(sub == 0, 0.0, KAPPA_V), jnp.where(sub == LEVELS - 1, 0.0, KAPPA_V)


def levels_sum(field, masks):
    return masks[0] * pltpu.roll(field, 1, 0) + masks[1] * pltpu.roll(field, LEVELS - 1, 0)


class RowTiles:
    def __init__(self, count, load):
        self.count, self.load, self.held = count, load, {}

    def make(self, channel, tile):
        value = self.load(channel, tile)
        return value, pltpu.roll(value, 1, 1), pltpu.roll(value, WIDTH - 1, 1)

    def get(self, channel, tile):
        if (channel, tile) not in self.held:
            self.held[channel, tile] = self.make(channel, tile)
        return self.held[channel, tile]

    def here(self, channel, tile):
        return self.get(channel, tile)[0]

    def around(self, channel, tile, lane):
        last = self.count - 1
        before = self.get(channel, tile - 1) if tile > 0 else self.make(channel, last)
        after = self.get(channel, tile + 1) if tile < last else self.make(channel, 0)
        _, to_right, to_left = self.get(channel, tile)
        return lanes_sum(to_right, before[1], to_left, after[2], lane)


def row_tiles_of(sz, ref, row):
    return ref[pl.ds(row * sz.row_width, sz.row_tiles, stride=CHANNELS), :]


def put_row_tiles(sz, ref, row, value):
    ref[pl.ds(row * sz.row_width, sz.row_tiles, stride=CHANNELS), :] = value


def near_row(sz, ref, row):
    return ref[row * sz.row_tiles : (row + 1) * sz.row_tiles, :]


def high_first():
    return 1 - lax.rem(lax.axis_index("horiz").astype(jnp.int32), 2)


def pick(flag, one, other):
    return jnp.where(jnp.full(one.shape, flag, jnp.int32) == 1, one, other)


def sided(first, second):
    flag = high_first()
    return pick(flag, second, first), pick(flag, first, second)


def load_surface_row(sz, target, row, source, base):
    for tile in range(sz.row_tiles):
        for channel in range(CHANNELS):
            at = base + tile * CHANNELS + channel
            target[row, channel, 0:1, cols(tile)] = source[pl.ds(at, 1), :]


def as_column(row, size):
    shape = (size, row.shape[1])
    diagonal = lax.broadcasted_iota(jnp.int32, shape, 0) == lax.broadcasted_iota(jnp.int32, shape, 1)
    return jnp.sum(jnp.where(diagonal, row, 0.0), axis=1, keepdims=True)


def setup_kernel(sz, entries, remap_entries, arrive, wet, remap, mix_rows, diffusivity, *outs):
    first_mix, first_rows, table, facts, line, mix = outs
    arrive_all(arrive)
    for row in range(sz.rows):
        first_rows[row] = diffusivity[row : row + 1, :]
    for index in range(CHANNELS * CHANNELS):
        column = as_column(mix_rows[index : index + 1, :], LEVELS)
        mix[index] = jnp.broadcast_to(column, (LEVELS, WIDTH))
    mix.start()
    first_mix[...] = mix[...]
    tiles, owners = wet[0:1, :], wet[1:2, :]
    size = -(-entries // SUBLANES) * SUBLANES
    shape = (size, wet.shape[1])
    tile_here, owner_here = as_column(tiles, size), as_column(owners, size)
    earlier = lax.broadcasted_iota(jnp.int32, shape, 1) < lax.broadcasted_iota(jnp.int32, shape, 0)
    same = (owner_here == owners) & earlier
    rank = jnp.sum(jnp.where(same, 1.0, 0.0), axis=1, keepdims=True)
    slot = jnp.where(owner_here >= 0.0, owner_here * sz.capacity + rank, -1.0)
    facts[...] = jnp.zeros((sz.facts, WIDTH), jnp.float32)
    for index in range(sz.slot_lines):
        place = lax.broadcasted_iota(jnp.int32, (size, WIDTH), 1) + index * WIDTH
        match = slot.astype(jnp.int32) == place
        told = jnp.sum(jnp.where(match, sz.tiles - tile_here, 0.0), axis=0, keepdims=True)
        facts[index : index + 1, :] = told
        table[index : index + 1, :] = sz.tiles - told.astype(jnp.int32)
    size = -(-remap_entries // SUBLANES) * SUBLANES
    at, amount = as_column(remap[0:1, :], size), as_column(remap[1:2, :], size)
    place = lax.broadcasted_iota(jnp.int32, (size, WIDTH), 1)
    line[...] = jnp.sum(
        jnp.where(at.astype(jnp.int32) == place, amount, 0.0), axis=0, keepdims=True
    )
    facts[sz.slot_lines : sz.slot_lines + 1, :] = line[...]


def columns_kernel(sz, arrive, diffusivity, weight, *outs):
    diffusivity_rows, weight_rows, diffusivity_tiles, weight_tiles = outs
    arrive_all(arrive)
    for source, by_row, by_tile in (
        (diffusivity, diffusivity_rows, diffusivity_tiles),
        (weight, weight_rows, weight_tiles),
    ):
        for row in range(sz.rows):
            by_row[row] = source[row : row + 1, :]
            for tile in range(sz.row_tiles):
                line = source[row : row + 1, cols(tile)]
                at = (row * sz.row_tiles + tile) * CHANNELS
                by_tile[at : at + CHANNELS, :] = jnp.broadcast_to(line, (CHANNELS, WIDTH))


def gather_levels(block, channel, tile):
    sub = lax.broadcasted_iota(jnp.int32, (LEVELS, WIDTH), 0)
    total = None
    for level in range(LEVELS):
        line = block[level, channel : channel + 1, cols(tile)]
        line = jnp.broadcast_to(line, (LEVELS, WIDTH))
        total = line if total is None else jnp.where(sub == level, line, total)
    return total


def edges_kernel(sz, arrive, low_start, high_start, low_base, high_base, send_first, send_second):
    arrive_all(arrive)
    low_start[...] = low_start[...] + low_base[...]
    high_start[...] = high_start[...] + high_base[...]
    flag = high_first()
    for channel in range(CHANNELS):
        for tile in range(sz.row_tiles):
            low = gather_levels(low_start, channel, tile)
            high = gather_levels(high_start, channel, tile)
            at = (channel * sz.row_tiles + tile) * LEVELS
            send_first[at : at + LEVELS, :] = pick(flag, high, low)
            send_second[at : at + LEVELS, :] = pick(flag, low, high)


def load_kernel(sz, arrive, perturbation, base, field, start_block, base_block, in_sems):
    def arrivals(row):
        return [
            pltpu.make_async_copy(source.at[:, row], block.at[row], in_sems.at[index, row])
            for index, (source, block) in enumerate(
                ((perturbation, start_block), (base, base_block))
            )
        ]

    for row in range(sz.rows):
        for arrival in arrivals(row):
            arrival.start()

    def one_row(row, carry):
        for arrival in arrivals(row):
            arrival.wait()
        start_block[row] = start_block[row] + base_block[row]
        for channel in range(CHANNELS):
            for tile in range(sz.row_tiles):
                field[row, channel, :, cols(tile)] = gather_levels(
                    start_block.at[row], channel, tile
                )
        return carry

    lax.fori_loop(0, sz.rows, one_row, 0)


def relayout_kernel(sz, arrive, source, out, block, in_sems):
    def arrival(row):
        return pltpu.make_async_copy(source.at[:, row], block.at[row], in_sems.at[0, row])

    for row in range(sz.rows):
        arrival(row).start()

    def one_row(row, carry):
        arrival(row).wait()
        for channel in range(CHANNELS):
            for tile in range(sz.row_tiles):
                out[row, channel, :, cols(tile)] = gather_levels(block.at[row], channel, tile)
        out.row(row).start()
        return carry

    lax.fori_loop(0, sz.rows, one_row, 0)


class Remap:
    def __init__(self, sz, weights):
        self.sz, self.weights = sz, weights

    def weight(self, which, lat, row):
        return self.weights[which, lat * self.sz.rows + row]

    def own(self, lat, row):
        return self.weight(0, lat, row)

    def of_low(self, lat, row):
        return self.weight(1, lat + LAT_DEV, row)

    def of_high(self, lat, row):
        return self.weight(2, lat - LAT_DEV, row)


def tile_at(sz, tables, which, slot):
    return tables[which * sz.slot_lines + slot // WIDTH, slot % WIDTH]


def sum_of(weights, values):
    total = weights[0] * values[0]
    for weight, value in zip(weights[1:], values[1:]):
        total = total + weight * value
    return total


def own_sums(sz, remap, own, factor):
    return [
        factor * sum_of([remap.own(lat, row) for row in range(sz.rows)], own)
        for lat in range(NEAR_LAT)
    ]


def send_sums(sz, sums, tell_first, tell_second):
    flag = high_first()
    for index in range(LAT_DEV):
        low, high = sums[index], sums[LAT_DEV + index]
        at = index * sz.pitch
        tell_first[at : at + sz.row_tiles, :] = pick(flag, high, low)
        tell_second[at : at + sz.row_tiles, :] = pick(flag, low, high)


def lat_rows(sz, ref, lat):
    at = lat * sz.pitch
    return ref[at : at + sz.row_tiles, :]


def told_sums(sz, from_first, from_second):
    lows, highs = [], []
    for index in range(LAT_DEV):
        low, high = sided(lat_rows(sz, from_first, index), lat_rows(sz, from_second, index))
        lows.append(low)
        highs.append(high)
    return lows + highs


def place_edges(sz, padded, first, second, first_surface=None, second_surface=None):
    side = high_first() * (sz.rows + 1)
    for at, edge, surface in ((side, first, first_surface), (sz.rows + 1 - side, second, second_surface)):
        for channel in range(CHANNELS):
            for tile in range(sz.row_tiles):
                line = (channel * sz.row_tiles + tile) * LEVELS
                padded[at, channel, :, cols(tile)] = edge[line : line + LEVELS, :]
        if surface is not None:
            load_surface_row(sz, padded, at, surface, 0)


def store_rows(sz, surface, send_first, send_second, factor=None):
    row = high_first() * (sz.rows - 1)
    for at, send in ((row, send_first), (sz.rows - 1 - row, send_second)):
        for tile in range(sz.row_tiles):
            start = pl.multiple_of((at * sz.row_tiles + tile) * CHANNELS, CHANNELS)
            value = surface[pl.ds(start, CHANNELS), :]
            if factor is not None:
                value = factor[pl.ds(start, CHANNELS), :] * value
            send[tile * CHANNELS : (tile + 1) * CHANNELS, :] = value


def forward_load_kernel(sz, last, arrive, mix, diffusivity, *refs):
    refs = list(refs)
    if last:
        weight = refs.pop(0)
    field, surface = refs[:2]
    refs = refs[2:]
    if last:
        target = refs.pop(0)
    mix_out, rows_out, field_out = refs[:3]
    refs = refs[3:]
    if last:
        weight_out, target_out = refs[:2]
        refs = refs[2:]
    in_sems = refs[0]

    def arrivals(row):
        copies = [pltpu.make_async_copy(field.at[row], field_out.at[row], in_sems.at[0, row])]
        if last:
            copies.append(
                pltpu.make_async_copy(target.at[row], target_out.at[row], in_sems.at[1, row])
            )
        return copies

    for row in range(sz.rows):
        for arrival in arrivals(row):
            arrival.start()
    arrive_all(arrive)
    mix_out[...] = mix[...]
    rows_out[...] = diffusivity[...]
    if last:
        weight_out[...] = weight[...]

    def one_row(row, carry):
        for arrival in arrivals(row):
            arrival.wait()
        load_surface_row(sz, field_out, row, surface, row * sz.row_width)
        return carry

    lax.fori_loop(0, sz.rows, one_row, 0)


def forward_kernel(sz, first, last, arrive, *refs):
    refs = list(refs)
    tables, facts, low, high, diffusivity, mix, field = refs[:7]
    refs = refs[7:]
    if first:
        facts_block = refs.pop(0)
    surfaces = ()
    if not first:
        surfaces = refs[:2]
        refs = refs[2:]
    if last:
        weight, target = refs[:2]
        refs = refs[2:]
    out, drive, new_surface, packed, tell_first, tell_second, edge_first, edge_second, padded = refs
    remap = Remap(sz, facts)
    place_edges(sz, padded, low, high, *surfaces)

    def ready(row):
        padded[row + 1] = field[row]

    ready(0)
    lane = lax.broadcasted_iota(jnp.int32, (LEVELS, WIDTH), 1)
    masks = level_masks()
    count = sz.row_tiles

    def one_row(row, carry):
        @pl.when(row < sz.rows - 1)
        def _():
            ready(row + 1)

        tiles = RowTiles(count, lambda c, t: padded[row + 1, c, :, cols(t)])
        for t in range(count):
            coeff = jnp.broadcast_to(diffusivity[row, 0:1, cols(t)], (LEVELS, WIDTH))
            center = (1.0 - 2.0 * KAPPA_V) - 4.0 * coeff
            if last:
                scale = weight[row, 0:1, cols(t)]
                scale = jnp.broadcast_to(scale * scale, (LEVELS, WIDTH))
            for c in range(CHANNELS):
                mixed = mix[c * CHANNELS] * tiles.here(0, t)
                for k in range(1, CHANNELS):
                    mixed = mixed + mix[c * CHANNELS + k] * tiles.here(k, t)
                bent = jnp.tanh(mixed)
                drive[row, c, :, cols(t)] = bent
                field_here = tiles.here(c, t)
                around = tiles.around(c, t, lane)
                around = around + (padded[row, c, :, cols(t)] + padded[row + 2, c, :, cols(t)])
                stepped = (
                    center * field_here
                    + coeff * around
                    + levels_sum(field_here, masks)
                    + TIME_STEP * bent
                )
                new_surface[pl.ds((row * count + t) * CHANNELS + c, 1), :] = stepped[0:1, :]
                if last:
                    stepped = scale * (stepped - target[row, c, :, cols(t)])
                out[row, c, :, cols(t)] = stepped
        drive.row(row).start()
        out.row(row).start()
        return carry

    lax.fori_loop(0, sz.rows, one_row, 0)
    new_surface[CHANNELS * sz.tiles :, :] = jnp.zeros((CHANNELS, WIDTH), jnp.float32)
    new_surface.start()
    arrive_all(arrive)
    pack_slots(sz, tables, new_surface, packed)
    packed.start()
    own = [row_tiles_of(sz, new_surface.block, row) for row in range(sz.rows)]
    send_sums(sz, own_sums(sz, remap, own, 1.0), tell_first, tell_second)
    for tell in (tell_first, tell_second):
        if first:
            tell[sz.lat_lines :, :] = facts_block[...]
        tell.start()
    store_edges(sz, out, diffusivity if last else None, edge_first, edge_second)


def pack_slots(sz, tables, surface, packed):
    for slot in range(sz.slots):
        at = pl.multiple_of(tile_at(sz, tables, 0, slot) * CHANNELS, CHANNELS)
        packed[slot * CHANNELS : (slot + 1) * CHANNELS, :] = surface[pl.ds(at, CHANNELS), :]


def store_edges(sz, field, diffusivity, send_first, send_second):
    outer = high_first() * (sz.rows - 1)
    for row, send in ((outer, send_first), (sz.rows - 1 - outer, send_second)):
        for channel in range(CHANNELS):
            for tile in range(sz.row_tiles):
                value = field[row, channel, :, cols(tile)]
                if diffusivity is not None:
                    value = value * jnp.broadcast_to(
                        diffusivity[row, 0:1, cols(tile)], (LEVELS, WIDTH)
                    )
                at = (channel * sz.row_tiles + tile) * LEVELS
                send[at : at + LEVELS, :] = value
        send.start()


def owner_kernel(sz, decode, arrive, arrived, mixing, air, wind, facts, *refs):
    slots = sz.slots
    if decode:
        told_first, told_second, own_table, own_facts, tables, weights = refs[:6]
        refs = refs[6:]
    flux, mixed_slope, flux_slope, flat, first = refs

    def bulk(row, column):
        return facts[0, sz.bulk_at + row * CHANNELS + column]

    values = [arrived[pl.ds(c, slots, stride=CHANNELS), :] for c in range(CHANNELS)]
    mixed = jnp.tanh(
        jnp.dot(
            mixing[...],
            jnp.concatenate(values, axis=1),
            precision=HIGHEST,
            preferred_element_type=jnp.float32,
        )
    )
    contrast = []
    for c in range(CHANNELS):
        mixed_here = mixed[:, cols(c)]
        mixed_slope[c] = 1.0 - mixed_here * mixed_here
        contrast.append((air[...] - values[0] if c == 0 else values[c]) + mixed_here)
    mixed_slope.start()
    arrive_all(arrive)
    if decode:
        lines = sz.slot_lines
        tables[0:lines, :] = own_table[...]
        weights[0:1, :] = own_facts[...]
        both = sided(told_first[sz.lat_lines :, :], told_second[sz.lat_lines :, :])
        for which, told in ((1, both[0]), (2, both[1])):
            got = told[0:lines, :].astype(jnp.int32)
            tables[which * lines : (which + 1) * lines, :] = sz.tiles - got
            weights[which : which + 1, :] = told[lines : lines + 1, :]
        tables.start()
        weights.start()

    rate = FLUX_RATE * wind[...]
    for c in range(CHANNELS):
        forcing = bulk(c, 0) * contrast[0]
        for k in range(1, CHANNELS):
            forcing = forcing + bulk(c, k) * contrast[k]
        bent = jnp.tanh(forcing)
        flux_slope[c] = rate * (1.0 - bent * bent)
        one = rate * bent
        flat[pl.ds(c, slots, stride=CHANNELS), :] = one
        if c == 0:
            first[...] = one
    flux_slope.start()
    cap = sz.capacity
    gap = jnp.zeros((sz.chunk - sz.own_rows, WIDTH), jnp.float32)
    for d in range(sz.devices):
        at = d * sz.chunk
        flux[at : at + sz.own_rows, :] = flat[d * sz.own_rows : (d + 1) * sz.own_rows, :]
        at = at + sz.own_rows
        flux[at : (d + 1) * sz.chunk, :] = gap
        if d > 0:
            flux[at : at + cap, :] = first[(d - 1) * cap : d * cap, :]
        if d < sz.devices - 1:
            flux[at + cap : at + 2 * cap, :] = first[(d + 1) * cap : (d + 2) * cap, :]


def owner_back_kernel(sz, arrive, arrived, mixing, mixed_slope, flux_slope, facts, back, flat, extra):
    slots, cap = sz.slots, sz.capacity

    def bulk(row, column):
        return facts[0, sz.bulk_at + row * CHANNELS + column]

    for d in range(sz.devices):
        at = d * sz.chunk
        flat[d * sz.own_rows : (d + 1) * sz.own_rows, :] = arrived[at : at + sz.own_rows, :]
        more = jnp.zeros((cap, WIDTH), jnp.float32)
        if d < sz.devices - 1:
            at = (d + 1) * sz.chunk + sz.own_rows
            more = more + arrived[at : at + cap, :]
        if d > 0:
            at = (d - 1) * sz.chunk + sz.own_rows + cap
            more = more + arrived[at : at + cap, :]
        extra[d * cap : (d + 1) * cap, :] = more
    arrive_all(arrive)
    forced = []
    for c in range(CHANNELS):
        got = flat[pl.ds(c, slots, stride=CHANNELS), :]
        if c == 0:
            got = got + extra[...]
        forced.append(flux_slope[c] * got)
    direct = []
    for k in range(CHANNELS):
        total = bulk(0, k) * forced[0]
        for c in range(1, CHANNELS):
            total = total + bulk(c, k) * forced[c]
        direct.append(total)
    through = lax.dot_general(
        mixing[...],
        jnp.concatenate([direct[k] * mixed_slope[k] for k in range(CHANNELS)], axis=1),
        (((0,), (0,)), ((), ())),
        precision=HIGHEST,
        preferred_element_type=jnp.float32,
    )
    for k in range(CHANNELS):
        sign = -1.0 if k == 0 else 1.0
        back.block[pl.ds(k, slots, stride=CHANNELS), :] = through[:, cols(k)] + sign * direct[k]


def spread_back(sz, surface, slope, remap, tables, packed, near_low, near_high, tell_first, tell_second):
    rows, count, cap = sz.rows, sz.row_tiles, sz.capacity
    block = surface.block
    own = [row_tiles_of(sz, block, row) for row in range(rows)]
    sums = own_sums(sz, remap, own, FEEDBACK)
    send_sums(sz, sums, tell_first, tell_second)
    tell_first.start()
    tell_second.start()
    lats = [lat_rows(sz, slope, lat) * sums[lat] for lat in range(NEAR_LAT)]
    every = range(NEAR_LAT)
    for row in range(rows):
        added = sum_of([remap.own(lat, row) for lat in every], lats)
        put_row_tiles(sz, block, row, own[row] + added)
        at = row * count
        near_low[at : at + count, :] = sum_of(
            [remap.of_low(lat, row) for lat in range(LAT_DEV)], lats[:LAT_DEV]
        )
        near_high[at : at + count, :] = sum_of(
            [remap.of_high(lat, row) for lat in range(LAT_DEV, NEAR_LAT)], lats[LAT_DEV:]
        )
    rest = sz.near[0] - sz.tiles
    near_low[sz.tiles :, :] = jnp.zeros((rest, WIDTH), jnp.float32)
    near_high[sz.tiles :, :] = jnp.zeros((rest, WIDTH), jnp.float32)
    surface.start()
    gap = jnp.zeros((sz.chunk - sz.own_rows, WIDTH), jnp.float32)
    for owner in range(sz.devices):
        packed[owner * sz.chunk + sz.own_rows : (owner + 1) * sz.chunk, :] = gap
    for slot in range(sz.slots):
        owner, rank = slot // cap, slot % cap
        at = owner * sz.chunk + rank * CHANNELS
        tile = pl.multiple_of(tile_at(sz, tables, 0, slot) * CHANNELS, CHANNELS)
        packed[at : at + CHANNELS, :] = surface[pl.ds(tile, CHANNELS), :]
        at = owner * sz.chunk + sz.own_rows + rank
        packed[at : at + 1, :] = near_low[pl.ds(tile_at(sz, tables, 1, slot), 1), :]
        at = at + cap
        packed[at : at + 1, :] = near_high[pl.ds(tile_at(sz, tables, 2, slot), 1), :]


def surface_kernel(sz, last, arrive, *refs):
    refs = list(refs)
    flux, from_first, from_second, before, tables, weights = refs[:6]
    refs = refs[6:]
    if last:
        target, weight = refs[:2]
        surface, slope, packed, tell_first, tell_second, near_low, near_high = refs[2:]
        block = surface.block
    else:
        surface, send_first, send_second, slope, near_low, near_high = refs
        block = surface
    remap = Remap(sz, weights)
    arrive_all(arrive)
    rows, cap = sz.rows, sz.capacity
    block[...] = before[...]
    near_low[...] = jnp.zeros(sz.near, jnp.float32)
    near_high[...] = jnp.zeros(sz.near, jnp.float32)
    for slot in range(sz.slots):
        owner, rank = slot // cap, slot % cap
        at = owner * sz.chunk + rank * CHANNELS
        tile = pl.multiple_of(tile_at(sz, tables, 0, slot) * CHANNELS, CHANNELS)
        block[pl.ds(tile, CHANNELS), :] = (
            before[pl.ds(tile, CHANNELS), :] + flux[at : at + CHANNELS, :]
        )
        at = owner * sz.chunk + sz.own_rows + rank
        near_low[pl.ds(tile_at(sz, tables, 1, slot), 1), :] = flux[at : at + 1, :]
        at = at + cap
        near_high[pl.ds(tile_at(sz, tables, 2, slot), 1), :] = flux[at : at + 1, :]
    block[CHANNELS * sz.tiles :, :] = jnp.zeros((CHANNELS, WIDTH), jnp.float32)
    own = [row_tiles_of(sz, block, row) for row in range(rows)]
    sums = own_sums(sz, remap, own, 1.0)
    told = told_sums(sz, from_first, from_second)
    air = []
    for lat in range(NEAR_LAT):
        if lat < LAT_DEV:
            near, weights = near_low, [remap.of_low(lat, row) for row in range(rows)]
        else:
            near, weights = near_high, [remap.of_high(lat, row) for row in range(rows)]
        more = sum_of(weights, [near_row(sz, near, row) for row in range(rows)])
        one = jnp.tanh(sums[lat] + told[lat] + more)
        slope[lat * sz.pitch : lat * sz.pitch + sz.row_tiles, :] = 1.0 - one * one
        air.append(one)
    slope.start()
    for row in range(rows):
        weights = [remap.own(lat, row) for lat in range(NEAR_LAT)]
        put_row_tiles(sz, block, row, own[row] + FEEDBACK * sum_of(weights, air))
    if last:
        for row in range(rows):
            for tile in range(sz.row_tiles):
                at = row * sz.row_width + tile * CHANNELS
                scale = weight[at : at + CHANNELS, :]
                off = block[at : at + CHANNELS, :] - target[row, :, cols(tile)]
                block[at : at + CHANNELS, :] = scale * scale * off
        spread_back(
            sz, surface, slope, remap, tables, packed, near_low, near_high, tell_first, tell_second
        )
    else:
        store_rows(sz, surface, send_first, send_second)


def merge_kernel(
    sz, arrive, back, from_first, from_second, before, slope, tables, facts, diffusivity, surface, send_first, send_second
):
    rows = sz.rows
    remap = Remap(sz, facts)
    arrive_all(arrive)
    surface[...] = before[...]
    for slot in range(sz.slots):
        tile = pl.multiple_of(tile_at(sz, tables, 0, slot) * CHANNELS, CHANNELS)
        surface[pl.ds(tile, CHANNELS), :] = (
            before[pl.ds(tile, CHANNELS), :] + back[slot * CHANNELS : (slot + 1) * CHANNELS, :]
        )
    surface[CHANNELS * sz.tiles :, :] = jnp.zeros((CHANNELS, WIDTH), jnp.float32)
    told = told_sums(sz, from_first, from_second)
    lats = [lat_rows(sz, slope, lat) * told[lat] for lat in range(NEAR_LAT)]
    for row in range(rows):
        own = row_tiles_of(sz, surface, row)
        weights = [remap.own(lat, row) for lat in range(NEAR_LAT)]
        put_row_tiles(sz, surface, row, own + sum_of(weights, lats))
    store_rows(sz, surface, send_first, send_second, diffusivity)


def backward_load_kernel(sz, last, arrive, mix, diffusivity, field, drive, surface, *refs):
    refs = list(refs)
    if last:
        perturbation = refs.pop(0)
    mix_out, rows_out, local, bent_all, scaled = refs[:5]
    refs = refs[5:]
    if last:
        start_all = refs.pop(0)
    in_sems = refs[0]

    def arrivals(row):
        copies = [
            pltpu.make_async_copy(field.at[row], local.at[row], in_sems.at[0, row]),
            pltpu.make_async_copy(drive.at[row], bent_all.at[row], in_sems.at[1, row]),
        ]
        if last:
            copies.append(
                pltpu.make_async_copy(perturbation.at[row], start_all.at[row], in_sems.at[2, row])
            )
        return copies

    for row in range(sz.rows):
        for arrival in arrivals(row):
            arrival.start()
    arrive_all(arrive)
    mix_out[...] = mix[...]
    rows_out[...] = diffusivity[...]

    def one_row(row, carry):
        for arrival in arrivals(row):
            arrival.wait()
        load_surface_row(sz, local, row, surface, row * sz.row_width)
        for t in range(sz.row_tiles):
            coeff = jnp.broadcast_to(diffusivity[row, 0:1, cols(t)], (LEVELS, WIDTH))
            for c in range(CHANNELS):
                scaled[row, c, :, cols(t)] = coeff * local[row, c, :, cols(t)]
        return carry

    lax.fori_loop(0, sz.rows, one_row, 0)


def backward_kernel(sz, last, arrive, *refs):
    refs = list(refs)
    if not last:
        tables, weights, slope = refs[:3]
        refs = refs[3:]
    low, high, first_surface, second_surface, diffusivity, mix = refs[:6]
    local, bent_all, scaled_all = refs[6:9]
    refs = refs[9:]
    if last:
        start_all, out, sums, padded = refs
    else:
        out, new_surface, packed, tell_first, tell_second, edge_first, edge_second = refs[:7]
        padded, near_low, near_high = refs[7:]
        remap = Remap(sz, weights)
    count = sz.row_tiles
    place_edges(sz, padded, low, high, first_surface, second_surface)

    def ready(row):
        padded[row + 1] = scaled_all[row]

    ready(0)
    lane = lax.broadcasted_iota(jnp.int32, (LEVELS, WIDTH), 1)
    masks = level_masks()

    def one_row(row, carry):
        @pl.when(row < sz.rows - 1)
        def _():
            ready(row + 1)

        tiles = RowTiles(count, lambda c, t: padded[row + 1, c, :, cols(t)])
        for t in range(count):
            here, bent = [], []
            for c in range(CHANNELS):
                value = local[row, c, :, cols(t)]
                one = bent_all[row, c, :, cols(t)]
                here.append(value)
                bent.append((1.0 - one * one) * value)
            for c in range(CHANNELS):
                mixed = mix[c] * bent[0]
                for k in range(1, CHANNELS):
                    mixed = mixed + mix[k * CHANNELS + c] * bent[k]
                around = tiles.around(c, t, lane)
                around = around + (padded[row, c, :, cols(t)] + padded[row + 2, c, :, cols(t)])
                stepped = (
                    ((1.0 - 2.0 * KAPPA_V) * here[c] - 4.0 * tiles.here(c, t))
                    + around
                    + levels_sum(here[c], masks)
                    + TIME_STEP * mixed
                )
                out[row, c, :, cols(t)] = stepped
                if last:
                    start = start_all[row, c, :, cols(t)]
                    carry = (
                        carry[0] + start * start,
                        carry[1] + start * stepped,
                        carry[2] + stepped * stepped,
                    )
                else:
                    new_surface[pl.ds((row * count + t) * CHANNELS + c, 1), :] = stepped[0:1, :]
        out.row(row).start()
        return carry

    blank = jnp.zeros((LEVELS, WIDTH), jnp.float32)
    totals = lax.fori_loop(0, sz.rows, one_row, (blank, blank, blank) if last else 0)
    if last:
        place = lax.broadcasted_iota(jnp.int32, sums.block.shape, 1)
        held = jnp.zeros(sums.block.shape, jnp.float32)
        for index in range(3):
            total = jnp.sum(jnp.sum(totals[index], axis=0, keepdims=True), axis=1, keepdims=True)
            held = jnp.where(place == index, total, held)
        sums[...] = held
    else:
        new_surface[CHANNELS * sz.tiles :, :] = jnp.zeros((CHANNELS, WIDTH), jnp.float32)
        arrive_all(arrive)
        spread_back(
            sz,
            new_surface,
            slope,
            remap,
            tables,
            packed,
            near_low,
            near_high,
            tell_first,
            tell_second,
        )
        packed.start()
        store_edges(sz, out, diffusivity, edge_first, edge_second)


def final_kernel(cell_total, arrive, everyones, perturbation, gradient, out):
    sums = jnp.sum(everyones[...], axis=0, keepdims=True) / cell_total
    place = lax.broadcasted_iota(jnp.int32, sums.shape, 1)
    means = [
        jnp.broadcast_to(
            jnp.sum(jnp.where(place == index, sums, 0.0), axis=1, keepdims=True), (1, WIDTH)
        )
        for index in range(3)
    ]
    scale = lax.rsqrt(means[2] + EPSILON)
    mean_sq = means[0] + 2.0 * ASCENT * scale * means[1] + ASCENT * ASCENT * scale * scale * means[2]
    shrink = lax.rsqrt(mean_sq + EPSILON)
    step = jnp.broadcast_to(ASCENT * scale * shrink, (CHANNELS, WIDTH))
    shrink = jnp.broadcast_to(shrink, (CHANNELS, WIDTH))
    levels, rows, _, cells = perturbation.shape

    def one_level(level, carry):
        for row in range(rows):
            for tile in range(cells // WIDTH):
                start = perturbation[level, row, :, cols(tile)]
                slope = gradient[level, row, :, cols(tile)]
                out[level, row, :, cols(tile)] = shrink * start + step * slope
        out.row(level).start()
        return carry

    lax.fori_loop(0, levels, one_level, 0)


class Operand:
    def __init__(self, array, space, fetch=None, at=()):
        self.array, self.space, self.fetch, self.at = array, space, fetch, at

    def block(self):
        whole = self.array.shape
        taken = [size for size, index in zip(whole, self.at) if isinstance(index, slice)]
        return self.fetch((*taken, *whole[len(self.at) :]), self.array.dtype)


def near_by(*arrays):
    return [Operand(array, pltpu.VMEM) for array in arrays]


def far_off(*arrays):
    return [
        Operand(pltpu.with_memory_space_constraint(array, pltpu.HBM), pltpu.HBM)
        for array in arrays
    ]


def fetched(*arrays, at=(), into=pltpu.VMEM):
    return [
        Operand(pltpu.with_memory_space_constraint(array, pltpu.HBM), pltpu.HBM, into, at)
        for array in arrays
    ]


def scalars(*arrays):
    return fetched(*arrays, into=pltpu.SMEM)


def call(kernel, name, inputs, kept=(), shipped=(), scratch=()):
    n_in, n_kept, n_out = len(inputs), len(kept), len(shipped)
    brought = [index for index, item in enumerate(inputs) if item.fetch is not None]

    def as_shape(item):
        return item if isinstance(item, jax.ShapeDtypeStruct) else jax.ShapeDtypeStruct(item, jnp.float32)

    kept = [as_shape(item) for item in kept]
    shipped = [as_shape(item) for item in shipped]

    def run(*refs):
        ins = list(refs[:n_in])
        kept_refs = refs[n_in : n_in + n_kept]
        homes = refs[n_in + n_kept : n_in + n_kept + n_out]
        rest = refs[n_in + n_kept + n_out :]
        outs = [
            Shipped(block, home, sems)
            for block, home, sems in zip(rest[:n_out], homes, rest[n_out : 2 * n_out])
        ]
        rest = rest[2 * n_out :]
        if brought:
            blocks, arrive_sems = rest[: len(brought)], rest[len(brought)]
            rest = rest[len(brought) + 1 :]
            copies = []
            for place, (index, block) in enumerate(zip(brought, blocks)):
                source = ins[index]
                if inputs[index].at:
                    source = source.at[inputs[index].at]
                copies.append(pltpu.make_async_copy(source, block, arrive_sems.at[place]))
                ins[index] = block
            for copy in copies:
                copy.start()
            arrive = [copy.wait for copy in copies]
        else:
            arrive = []
        kernel(arrive, *ins, *kept_refs, *outs, *rest)
        for out in outs:
            if not out.started:
                out.start()
        for out in outs:
            out.finish(out.block.shape[0])

    spaces = [pltpu.VMEM] * n_kept + [pltpu.HBM] * n_out
    blocks = [pltpu.VMEM(item.shape, item.dtype) for item in shipped]
    sems = [
        pltpu.SemaphoreType.DMA((item.shape[0] if len(item.shape) > 3 else 1,)) for item in shipped
    ]
    arriving = [inputs[index].block() for index in brought]
    if brought:
        arriving.append(pltpu.SemaphoreType.DMA((len(brought),)))
    more = [
        item if not isinstance(item, tuple) else pltpu.VMEM(item, jnp.float32) for item in scratch
    ]
    return pl.pallas_call(
        run,
        name=name,
        in_specs=[pl.BlockSpec(memory_space=item.space) for item in inputs],
        out_specs=[pl.BlockSpec(memory_space=space) for space in spaces],
        out_shape=kept + [pltpu.HBM(item.shape, item.dtype) for item in shipped],
        scratch_shapes=blocks + sems + arriving + more,
        compiler_params=pltpu.CompilerParams(vmem_limit_bytes=VMEM_BYTES),
    )(*[item.array for item in inputs])


def arrive_all(arrive):
    for wait in arrive:
        wait()


def swap(first, second):
    count = lax.axis_size("horiz")
    inner = [(i, i ^ 1) for i in range(count)]
    outer = [(i, i + 1) for i in range(1, count - 1, 2)]
    outer = outer + [(target, source) for source, target in outer]
    return lax.ppermute(first, "horiz", inner), lax.ppermute(second, "horiz", outer)


def exchange(array, devices):
    rows = array.shape[0] // devices
    step = CHANNELS if rows % CHANNELS == 0 else 2
    split = array.reshape(devices, rows // step, step, WIDTH)
    moved = lax.all_to_all(split, "horiz", split_axis=0, concat_axis=0, tiled=True)
    return moved.reshape(array.shape)


def body(
    perturbation,
    base_state,
    target_state,
    cost_weight,
    diffusivity,
    chan_mix,
    coupler_mix,
    owner_mix,
    air_temp,
    wind_speed,
    wet_list,
    wet_owner,
    remap_src,
    remap_tgt,
    remap_weight,
):
    devices = lax.axis_size("horiz")
    hours = air_temp.shape[0]
    sz = Sizes(devices, air_temp.shape[2] // devices, base_state.shape[1], base_state.shape[3])
    rows = sz.rows
    native_row = (LEVELS, CHANNELS, sz.cells)

    edge_inputs = []
    for array in (perturbation, base_state):
        for row in (0, rows - 1):
            edge_inputs += fetched(array, at=(slice(None), row))
    edges = swap(
        *call(functools.partial(edges_kernel, sz), "edges", edge_inputs, kept=[sz.edge, sz.edge])
    )
    me = lax.axis_index("horiz").astype(jnp.int32)

    def lined(first_row, second_row):
        size = -(-first_row.shape[0] // WIDTH) * WIDTH
        pair = jnp.stack([first_row.astype(jnp.float32), second_row.astype(jnp.float32)])
        return jnp.pad(pair, ((0, 0), (0, size - pair.shape[1])), constant_values=-1.0)

    places = jnp.arange(CHANNELS * CHANNELS, dtype=jnp.int32) + sz.bulk_at
    remap_at = (remap_tgt - (me * LAT_DEV - 1)) * rows + remap_src - me * rows
    remap_lines = lined(
        jnp.concatenate([remap_at, places]),
        jnp.concatenate([remap_weight, coupler_mix.reshape(-1)]),
    )
    mix_rows = chan_mix.transpose(1, 2, 0).reshape(CHANNELS * CHANNELS, LEVELS)
    row_lines = (rows, 1, sz.cells)
    tiles_lines = (CHANNELS * sz.tiles, WIDTH)
    first_mix, first_rows, table, facts, line, mix = call(
        functools.partial(setup_kernel, sz, wet_list.shape[1], remap_at.shape[0] + places.shape[0]),
        "setup",
        near_by(lined(wet_list[0], wet_owner[0]), remap_lines, mix_rows)
        + fetched(diffusivity),
        kept=[(CHANNELS * CHANNELS, LEVELS, WIDTH), row_lines],
        shipped=[
            jax.ShapeDtypeStruct((sz.slot_lines, WIDTH), jnp.int32),
            (sz.facts, WIDTH),
            (1, WIDTH),
            (CHANNELS * CHANNELS, LEVELS, WIDTH),
        ],
    )
    wider = (rows + 2, CHANNELS, LEVELS, sz.cells)
    row_surface = (sz.row_width, WIDTH)
    by_row = (rows, *native_row)

    def row_sems(kinds):
        return pltpu.SemaphoreType.DMA((kinds, rows))

    (field,) = call(
        functools.partial(load_kernel, sz),
        "load",
        far_off(perturbation, base_state),
        kept=[sz.whole],
        scratch=[by_row, by_row, row_sems(2)],
    )

    def relayout(array):
        return call(
            functools.partial(relayout_kernel, sz),
            "relayout",
            far_off(array),
            shipped=[sz.whole],
            scratch=[by_row, row_sems(1)],
        )

    saved = []
    near = [sz.near, sz.near]
    mix_shape = (CHANNELS * CHANNELS, LEVELS, WIDTH)
    by_slot = (sz.slots, WIDTH)
    for hour in range(hours):
        first, last = hour == 0, hour == hours - 1
        inputs = scalars(table, line)
        if first:
            inputs += near_by(*edges, first_rows, first_mix, field) + fetched(facts)
            assert not last
        else:
            loads = fetched(mix, diffusivity_rows, *([weight_rows] if last else []))
            loads += far_off(field) + near_by(surface) + (far_off(target) if last else [])
            mix_here, rows_here, field, *more = call(
                functools.partial(forward_load_kernel, sz, last),
                "step_load",
                loads,
                kept=[mix_shape, row_lines, sz.whole] + ([row_lines, sz.whole] if last else []),
                scratch=[row_sems(2)],
            )
            inputs += near_by(*edges, rows_here, mix_here, field, *surface_edges, *more)
        field, drive, surface, packed, *sends = call(
            functools.partial(forward_kernel, sz, first, last),
            "step",
            inputs,
            shipped=[sz.whole, sz.whole, sz.surface, sz.narrow]
            + [sz.told if first else sz.lats] * 2
            + [sz.edge] * 2,
            scratch=[wider],
        )
        arrived = exchange(packed, devices)
        got = swap(*sends[:2])
        arrived, *got = lax.optimization_barrier((arrived, *got))
        inputs = (
            near_by(arrived, owner_mix[0], air_temp[hour, 0], wind_speed[hour, 0])
            + scalars(line)
        )
        decoded = []
        if first:
            inputs += near_by(*got) + fetched(table, line)
            decoded = [jax.ShapeDtypeStruct(sz.tables, jnp.int32), sz.weights]
        *decoded, flux, mixed_slope, flux_slope = call(
            functools.partial(owner_kernel, sz, first),
            "owners",
            inputs,
            shipped=[*decoded, sz.wide, sz.by_slot, sz.by_slot],
            scratch=[sz.narrow, by_slot],
        )
        if first:
            tables, weights = decoded
        flux, *sends = lax.optimization_barrier((flux, *sends[2:]))
        if first:
            flux, diffusivity, target_state = lax.optimization_barrier(
                (flux, diffusivity, target_state)
            )
            beside = call(
                functools.partial(columns_kernel, sz),
                "columns",
                fetched(diffusivity, cost_weight),
                shipped=[row_lines, row_lines, tiles_lines, tiles_lines],
            ) + relayout(target_state)
        else:
            flux, perturbation = lax.optimization_barrier((flux, perturbation))
            beside = relayout(perturbation)
        flux = exchange(flux, devices)
        flux, *beside = lax.optimization_barrier((flux, *beside))
        if first:
            diffusivity_rows, weight_rows, diffusivity_tiles, weight_tiles, target = beside
        else:
            start_field = beside[0]
        edges = swap(*sends)
        inputs = near_by(flux, *got) + fetched(surface) + scalars(tables, weights)
        if last:
            surface, slope, packed, *sends = call(
                functools.partial(surface_kernel, sz, True),
                "surface",
                inputs + fetched(target_state, at=(0,)) + fetched(weight_tiles),
                shipped=[sz.surface, sz.slope, sz.wide, sz.lats, sz.lats],
                scratch=near,
            )
        else:
            surface, *sends, slope = call(
                functools.partial(surface_kernel, sz, False),
                "surface",
                inputs,
                kept=[sz.surface, row_surface, row_surface],
                shipped=[sz.slope],
                scratch=near,
            )
            surface_edges = swap(*sends)
        saved.append((drive, slope, mixed_slope, flux_slope))

    edge_sends = None
    for hour in reversed(range(hours)):
        drive, slope, mixed_slope, flux_slope = saved[hour]
        arrived = exchange(packed, devices)
        got = swap(*sends)
        arrived, *got = lax.optimization_barrier((arrived, *got))
        back = call(
            functools.partial(owner_back_kernel, sz),
            "owners_back",
            near_by(arrived, owner_mix[0]) + fetched(mixed_slope, flux_slope) + scalars(line),
            shipped=[sz.narrow],
            scratch=[sz.narrow, by_slot],
        )[0]
        if edge_sends is not None:
            back, *edge_sends = lax.optimization_barrier((back, *edge_sends))
            edges = swap(*edge_sends)
        back = exchange(back, devices)
        surface, *row_sends = call(
            functools.partial(merge_kernel, sz),
            "merge",
            near_by(back, *got)
            + fetched(surface, slope)
            + scalars(table, line)
            + fetched(diffusivity_tiles),
            kept=[sz.surface, row_surface, row_surface],
        )
        surface_edges = swap(*row_sends)
        last = hour == 0
        mix_here, rows_here, *loaded = call(
            functools.partial(backward_load_kernel, sz, last),
            "step_back_load",
            fetched(mix, diffusivity_rows)
            + far_off(field, drive)
            + near_by(surface)
            + (far_off(start_field) if last else []),
            kept=[mix_shape, row_lines] + [sz.whole] * (4 if last else 3),
            scratch=[row_sems(3)],
        )
        inputs = near_by(*edges, *surface_edges, rows_here, mix_here, *loaded)
        if last:
            gradient, sums = call(
                functools.partial(backward_kernel, sz, True),
                "step_back_sums",
                inputs,
                shipped=[sz.whole, (devices, WIDTH)],
                scratch=[wider],
            )
        else:
            field, surface, packed, *outs = call(
                functools.partial(backward_kernel, sz, False),
                "step_back",
                scalars(tables, weights) + fetched(saved[hour - 1][1]) + inputs,
                shipped=[sz.whole, sz.surface, sz.wide, sz.lats, sz.lats, sz.edge, sz.edge],
                scratch=[wider, *near],
            )
            sends, edge_sends = outs[:2], outs[2:]

    everyones = lax.all_to_all(sums, "horiz", split_axis=0, concat_axis=0, tiled=True)
    block = perturbation.shape
    return call(
        functools.partial(final_kernel, perturbation.size * devices),
        "finish",
        near_by(everyones, perturbation, gradient.transpose(2, 0, 1, 3)),
        shipped=[block],
    )[0]


def solution(mesh):
    placed = (
        P("member", "horiz", None, None),
        P(None, "horiz", None, None),
        P(None, "horiz", None, None),
        P("horiz", None),
        P("horiz", None),
        P(),
        P(),
        P("horiz", None, None),
        P(None, "horiz", None, None),
        P(None, "horiz", None, None),
        P("horiz", None),
        P("horiz", None),
        P("horiz"),
        P("horiz"),
        P("horiz"),
    )
    return jax.shard_map(
        body,
        mesh=mesh,
        in_specs=placed,
        out_specs=P("member", "horiz", None, None),
        check_vma=False,
    )
```

```python
import functools

import jax
import jax.numpy as jnp
from jax import lax
from jax.experimental import pallas as pl
from jax.experimental.pallas import tpu as pltpu
from jax.sharding import PartitionSpec as P

LAT_DEV = 2
NEAR_LAT = LAT_DEV + 2
CHANNELS = 4
LEVELS = 8
WIDTH = 128
SUBLANES = 8

KAPPA_V = 0.1
TIME_STEP = 0.3
FLUX_RATE = 0.05
FEEDBACK = 0.5
ASCENT = 0.5
EPSILON = 1e-06
HIGHEST = lax.Precision.HIGHEST
VMEM_BYTES = 32 * 1024 * 1024


class Sizes:
    def __init__(self, devices, capacity, rows, cells):
        self.devices = devices
        self.capacity = capacity
        self.slots = devices * capacity
        self.rows = rows
        self.cells = cells
        self.row_tiles = cells // WIDTH
        self.tiles = rows * self.row_tiles
        self.row_width = CHANNELS * self.row_tiles
        self.pitch = -(-self.row_tiles // SUBLANES) * SUBLANES
        self.own_rows = CHANNELS * capacity
        self.chunk = self.own_rows + 2 * capacity
        self.slot_lines = -(-self.slots // WIDTH)
        self.facts = -(-(self.slot_lines + 1) // SUBLANES) * SUBLANES
        self.lat_lines = LAT_DEV * self.pitch
        self.edge_lines = CHANNELS * self.row_tiles * LEVELS
        self.whole = (rows, CHANNELS, LEVELS, cells)
        self.edge = (self.edge_lines, WIDTH)
        self.told = (self.lat_lines + self.facts, WIDTH)
        self.surface = (CHANNELS * (self.tiles + 1), WIDTH)
        self.narrow = (CHANNELS * self.slots, WIDTH)
        self.wide = (devices * self.chunk, WIDTH)
        self.slope = (NEAR_LAT * self.pitch, WIDTH)
        self.lats = (self.lat_lines, WIDTH)
        self.bulk_at = NEAR_LAT * rows
        self.tables = (3 * self.slot_lines, WIDTH)
        self.weights = (3, WIDTH)
        self.near = (-(-(self.tiles + 1) // SUBLANES) * SUBLANES, WIDTH)
        self.by_slot = (CHANNELS, self.slots, WIDTH)


class Shipped:
    def __init__(self, block, home, sems):
        self.block, self.home, self.sems = block, home, sems
        self.by_row = False
        self.started = False

    def __getitem__(self, at):
        return self.block[at]

    def __setitem__(self, at, value):
        self.block[at] = value

    def row(self, index):
        self.by_row = True
        self.started = True
        return pltpu.make_async_copy(
            self.block.at[index], self.home.at[index], self.sems.at[index]
        )

    def row_from(self, block, index):
        self.by_row = True
        self.started = True
        return pltpu.make_async_copy(block.at[index], self.home.at[index], self.sems.at[index])

    def all(self):
        return pltpu.make_async_copy(self.block, self.home, self.sems.at[0])

    def start(self):
        self.started = True
        self.all().start()

    def finish(self, rows):
        if self.by_row:
            for index in range(rows):
                self.row(index).wait()
        else:
            self.all().wait()


def cols(tile):
    return slice(tile * WIDTH, (tile + 1) * WIDTH)


def lanes_sum(left_here, left_before, right_here, right_after, lane):
    return jnp.where(lane == 0, left_before, left_here) + jnp.where(
        lane == WIDTH - 1, right_after, right_here
    )


def level_masks():
    sub = lax.broadcasted_iota(jnp.int32, (LEVELS, WIDTH), 0)
    return jnp.where(sub == 0, 0.0, KAPPA_V), jnp.where(sub == LEVELS - 1, 0.0, KAPPA_V)


def levels_sum(field, masks):
    return masks[0] * pltpu.roll(field, 1, 0) + masks[1] * pltpu.roll(field, LEVELS - 1, 0)


class RowTiles:
    def __init__(self, count, load):
        self.count, self.load, self.held = count, load, {}

    def make(self, channel, tile):
        value = self.load(channel, tile)
        return value, pltpu.roll(value, 1, 1), pltpu.roll(value, WIDTH - 1, 1)

    def get(self, channel, tile):
        if (channel, tile) not in self.held:
            self.held[channel, tile] = self.make(channel, tile)
        return self.held[channel, tile]

    def here(self, channel, tile):
        return self.get(channel, tile)[0]

    def around(self, channel, tile, lane):
        last = self.count - 1
        before = self.get(channel, tile - 1) if tile > 0 else self.make(channel, last)
        after = self.get(channel, tile + 1) if tile < last else self.make(channel, 0)
        _, to_right, to_left = self.get(channel, tile)
        return lanes_sum(to_right, before[1], to_left, after[2], lane)


def row_tiles_of(sz, ref, row):
    return ref[pl.ds(row * sz.row_width, sz.row_tiles, stride=CHANNELS), :]


def put_row_tiles(sz, ref, row, value):
    ref[pl.ds(row * sz.row_width, sz.row_tiles, stride=CHANNELS), :] = value


def near_row(sz, ref, row):
    return ref[row * sz.row_tiles : (row + 1) * sz.row_tiles, :]


def high_first():
    return 1 - lax.rem(lax.axis_index("horiz").astype(jnp.int32), 2)


def pick(flag, one, other):
    return jnp.where(jnp.full(one.shape, flag, jnp.int32) == 1, one, other)


def sided(first, second):
    flag = high_first()
    return pick(flag, second, first), pick(flag, first, second)


def load_surface_row(sz, target, row, source, base):
    for tile in range(sz.row_tiles):
        for channel in range(CHANNELS):
            at = base + tile * CHANNELS + channel
            target[row, channel, 0:1, cols(tile)] = source[pl.ds(at, 1), :]


def as_column(row, size):
    shape = (size, row.shape[1])
    diagonal = lax.broadcasted_iota(jnp.int32, shape, 0) == lax.broadcasted_iota(jnp.int32, shape, 1)
    return jnp.sum(jnp.where(diagonal, row, 0.0), axis=1, keepdims=True)


def setup_kernel(sz, entries, remap_entries, arrive, wet, remap, mix_rows, diffusivity, *outs):
    first_mix, first_rows, table, facts, line, mix = outs
    arrive_all(arrive)
    for row in range(sz.rows):
        first_rows[row] = diffusivity[row : row + 1, :]
    for index in range(CHANNELS * CHANNELS):
        column = as_column(mix_rows[index : index + 1, :], LEVELS)
        mix[index] = jnp.broadcast_to(column, (LEVELS, WIDTH))
    mix.start()
    first_mix[...] = mix[...]
    tiles, owners = wet[0:1, :], wet[1:2, :]
    size = -(-entries // SUBLANES) * SUBLANES
    shape = (size, wet.shape[1])
    tile_here, owner_here = as_column(tiles, size), as_column(owners, size)
    earlier = lax.broadcasted_iota(jnp.int32, shape, 1) < lax.broadcasted_iota(jnp.int32, shape, 0)
    same = (owner_here == owners) & earlier
    rank = jnp.sum(jnp.where(same, 1.0, 0.0), axis=1, keepdims=True)
    slot = jnp.where(owner_here >= 0.0, owner_here * sz.capacity + rank, -1.0)
    facts[...] = jnp.zeros((sz.facts, WIDTH), jnp.float32)
    for index in range(sz.slot_lines):
        place = lax.broadcasted_iota(jnp.int32, (size, WIDTH), 1) + index * WIDTH
        match = slot.astype(jnp.int32) == place
        told = jnp.sum(jnp.where(match, sz.tiles - tile_here, 0.0), axis=0, keepdims=True)
        facts[index : index + 1, :] = told
        table[index : index + 1, :] = sz.tiles - told.astype(jnp.int32)
    size = -(-remap_entries // SUBLANES) * SUBLANES
    at, amount = as_column(remap[0:1, :], size), as_column(remap[1:2, :], size)
    place = lax.broadcasted_iota(jnp.int32, (size, WIDTH), 1)
    line[...] = jnp.sum(
        jnp.where(at.astype(jnp.int32) == place, amount, 0.0), axis=0, keepdims=True
    )
    facts[sz.slot_lines : sz.slot_lines + 1, :] = line[...]


def columns_kernel(sz, arrive, diffusivity, weight, *outs):
    diffusivity_rows, weight_rows, diffusivity_tiles, weight_tiles = outs
    arrive_all(arrive)
    for source, by_row, by_tile in (
        (diffusivity, diffusivity_rows, diffusivity_tiles),
        (weight, weight_rows, weight_tiles),
    ):
        for row in range(sz.rows):
            by_row[row] = source[row : row + 1, :]
            for tile in range(sz.row_tiles):
                line = source[row : row + 1, cols(tile)]
                at = (row * sz.row_tiles + tile) * CHANNELS
                by_tile[at : at + CHANNELS, :] = jnp.broadcast_to(line, (CHANNELS, WIDTH))


def gather_levels(block, channel, tile):
    sub = lax.broadcasted_iota(jnp.int32, (LEVELS, WIDTH), 0)
    total = None
    for level in range(LEVELS):
        line = block[level, channel : channel + 1, cols(tile)]
        line = jnp.broadcast_to(line, (LEVELS, WIDTH))
        total = line if total is None else jnp.where(sub == level, line, total)
    return total


def edges_kernel(sz, arrive, low_start, high_start, low_base, high_base, send_first, send_second):
    arrive_all(arrive)
    low_start[...] = low_start[...] + low_base[...]
    high_start[...] = high_start[...] + high_base[...]
    flag = high_first()
    for channel in range(CHANNELS):
        for tile in range(sz.row_tiles):
            low = gather_levels(low_start, channel, tile)
            high = gather_levels(high_start, channel, tile)
            at = (channel * sz.row_tiles + tile) * LEVELS
            send_first[at : at + LEVELS, :] = pick(flag, high, low)
            send_second[at : at + LEVELS, :] = pick(flag, low, high)


def load_kernel(sz, arrive, perturbation, base, field, start_block, base_block, in_sems):
    def arrivals(row):
        return [
            pltpu.make_async_copy(source.at[:, row], block.at[row], in_sems.at[index, row])
            for index, (source, block) in enumerate(
                ((perturbation, start_block), (base, base_block))
            )
        ]

    for row in range(sz.rows):
        for arrival in arrivals(row):
            arrival.start()

    def one_row(row, carry):
        for arrival in arrivals(row):
            arrival.wait()
        start_block[row] = start_block[row] + base_block[row]
        for channel in range(CHANNELS):
            for tile in range(sz.row_tiles):
                field[row, channel, :, cols(tile)] = gather_levels(
                    start_block.at[row], channel, tile
                )
        return carry

    lax.fori_loop(0, sz.rows, one_row, 0)


def relayout_kernel(sz, arrive, source, out, block, in_sems):
    def arrival(row):
        return pltpu.make_async_copy(source.at[:, row], block.at[row], in_sems.at[0, row])

    for row in range(sz.rows):
        arrival(row).start()

    def one_row(row, carry):
        arrival(row).wait()
        for channel in range(CHANNELS):
            for tile in range(sz.row_tiles):
                out[row, channel, :, cols(tile)] = gather_levels(block.at[row], channel, tile)
        out.row(row).start()
        return carry

    lax.fori_loop(0, sz.rows, one_row, 0)


class Remap:
    def __init__(self, sz, weights):
        self.sz, self.weights = sz, weights

    def weight(self, which, lat, row):
        return self.weights[which, lat * self.sz.rows + row]

    def own(self, lat, row):
        return self.weight(0, lat, row)

    def of_low(self, lat, row):
        return self.weight(1, lat + LAT_DEV, row)

    def of_high(self, lat, row):
        return self.weight(2, lat - LAT_DEV, row)


def tile_at(sz, tables, which, slot):
    return tables[which * sz.slot_lines + slot // WIDTH, slot % WIDTH]


def sum_of(weights, values):
    total = weights[0] * values[0]
    for weight, value in zip(weights[1:], values[1:]):
        total = total + weight * value
    return total


def own_sums(sz, remap, own, factor):
    return [
        factor * sum_of([remap.own(lat, row) for row in range(sz.rows)], own)
        for lat in range(NEAR_LAT)
    ]


def send_sums(sz, sums, tell_first, tell_second):
    flag = high_first()
    for index in range(LAT_DEV):
        low, high = sums[index], sums[LAT_DEV + index]
        at = index * sz.pitch
        tell_first[at : at + sz.row_tiles, :] = pick(flag, high, low)
        tell_second[at : at + sz.row_tiles, :] = pick(flag, low, high)


def lat_rows(sz, ref, lat):
    at = lat * sz.pitch
    return ref[at : at + sz.row_tiles, :]


def told_sums(sz, from_first, from_second):
    lows, highs = [], []
    for index in range(LAT_DEV):
        low, high = sided(lat_rows(sz, from_first, index), lat_rows(sz, from_second, index))
        lows.append(low)
        highs.append(high)
    return lows + highs


def place_edge(sz, padded, at, edge, surface=None):
    for channel in range(CHANNELS):
        for tile in range(sz.row_tiles):
            line = (channel * sz.row_tiles + tile) * LEVELS
            padded[at, channel, :, cols(tile)] = edge[line : line + LEVELS, :]
    if surface is not None:
        load_surface_row(sz, padded, at, surface, 0)


def place_edges(sz, padded, first, second, first_surface=None, second_surface=None):
    side = high_first() * (sz.rows + 1)
    place_edge(sz, padded, side, first, first_surface)
    place_edge(sz, padded, sz.rows + 1 - side, second, second_surface)


def store_rows(sz, surface, send_first, send_second, factor=None):
    row = high_first() * (sz.rows - 1)
    for at, send in ((row, send_first), (sz.rows - 1 - row, send_second)):
        for tile in range(sz.row_tiles):
            start = pl.multiple_of((at * sz.row_tiles + tile) * CHANNELS, CHANNELS)
            value = surface[pl.ds(start, CHANNELS), :]
            if factor is not None:
                value = factor[pl.ds(start, CHANNELS), :] * value
            send[tile * CHANNELS : (tile + 1) * CHANNELS, :] = value


def forward_load_kernel(sz, last, arrive, mix, diffusivity, *refs):
    refs = list(refs)
    if last:
        weight = refs.pop(0)
    field, surface = refs[:2]
    refs = refs[2:]
    if last:
        target = refs.pop(0)
    mix_out, rows_out, field_out = refs[:3]
    refs = refs[3:]
    if last:
        weight_out, target_out = refs[:2]
        refs = refs[2:]
    in_sems = refs[0]

    def arrivals(row):
        copies = [pltpu.make_async_copy(field.at[row], field_out.at[row], in_sems.at[0, row])]
        if last:
            copies.append(
                pltpu.make_async_copy(target.at[row], target_out.at[row], in_sems.at[1, row])
            )
        return copies

    for row in range(sz.rows):
        for arrival in arrivals(row):
            arrival.start()
    arrive_all(arrive)
    mix_out[...] = mix[...]
    rows_out[...] = diffusivity[...]
    if last:
        weight_out[...] = weight[...]

    def one_row(row, carry):
        for arrival in arrivals(row):
            arrival.wait()
        load_surface_row(sz, field_out, row, surface, row * sz.row_width)
        return carry

    lax.fori_loop(0, sz.rows, one_row, 0)


def forward_kernel(sz, first, last, part, arrive, *refs):
    refs = list(refs)
    if part != 1:
        tables, facts = refs[:2]
        refs = refs[2:]
    edges = refs[: 1 if part else 2]
    refs = refs[len(edges) :]
    diffusivity, mix, field = refs[:3]
    refs = refs[3:]
    if part == 2:
        facts_block, out_before, drive_before, surface_before = refs[:4]
        refs = refs[4:]
    surfaces = ()
    if not first:
        surfaces = refs[:2]
        refs = refs[2:]
    if last:
        weight, target = refs[:2]
        refs = refs[2:]
    out, drive, new_surface, *refs = refs
    if part != 1:
        packed, tell_first, tell_second, edge_first, edge_second = refs[:5]
        refs = refs[5:]
        remap = Remap(sz, facts)
    padded = refs[0]
    flag = high_first()
    near_side = flag * (sz.rows + 1)
    if part == 0:
        place_edges(sz, padded, *edges, *surfaces)
    else:
        place_edge(sz, padded, near_side if part == 1 else sz.rows + 1 - near_side, edges[0])
    if part == 2:
        new_surface[...] = surface_before[...]
        for index in range(sz.rows - 1):
            row = index + flag
            out.row_from(out_before, row).start()
            drive.row_from(drive_before, row).start()

    def ready(row):
        padded[row + 1] = field[row]

    if part == 0:
        ready(0)
    else:
        for row in range(sz.rows):
            ready(row)
    lane = lax.broadcasted_iota(jnp.int32, (LEVELS, WIDTH), 1)
    masks = level_masks()
    count = sz.row_tiles

    def one_row(row, carry):
        if part == 0:

            @pl.when(row < sz.rows - 1)
            def _():
                ready(row + 1)

        tiles = RowTiles(count, lambda c, t: padded[row + 1, c, :, cols(t)])
        for t in range(count):
            coeff = jnp.broadcast_to(diffusivity[row, 0:1, cols(t)], (LEVELS, WIDTH))
            center = (1.0 - 2.0 * KAPPA_V) - 4.0 * coeff
            if last:
                scale = weight[row, 0:1, cols(t)]
                scale = jnp.broadcast_to(scale * scale, (LEVELS, WIDTH))
            for c in range(CHANNELS):
                mixed = mix[c * CHANNELS] * tiles.here(0, t)
                for k in range(1, CHANNELS):
                    mixed = mixed + mix[c * CHANNELS + k] * tiles.here(k, t)
                bent = jnp.tanh(mixed)
                drive[row, c, :, cols(t)] = bent
                field_here = tiles.here(c, t)
                around = tiles.around(c, t, lane)
                around = around + (padded[row, c, :, cols(t)] + padded[row + 2, c, :, cols(t)])
                stepped = (
                    center * field_here
                    + coeff * around
                    + levels_sum(field_here, masks)
                    + TIME_STEP * bent
                )
                new_surface[pl.ds((row * count + t) * CHANNELS + c, 1), :] = stepped[0:1, :]
                if last:
                    stepped = scale * (stepped - target[row, c, :, cols(t)])
                out[row, c, :, cols(t)] = stepped
        if part != 1:
            drive.row(row).start()
            out.row(row).start()
        return carry

    if part == 0:
        lax.fori_loop(0, sz.rows, one_row, 0)
    elif part == 1:
        lax.fori_loop(0, sz.rows - 1, lambda index, carry: one_row(index + flag, carry), 0)
        return
    else:
        one_row((1 - flag) * (sz.rows - 1), 0)
        out[flag * (sz.rows - 1)] = out_before[flag * (sz.rows - 1)]
    new_surface[CHANNELS * sz.tiles :, :] = jnp.zeros((CHANNELS, WIDTH), jnp.float32)
    new_surface.start()
    arrive_all(arrive)
    pack_slots(sz, tables, new_surface, packed)
    packed.start()
    own = [row_tiles_of(sz, new_surface.block, row) for row in range(sz.rows)]
    send_sums(sz, own_sums(sz, remap, own, 1.0), tell_first, tell_second)
    for tell in (tell_first, tell_second):
        if part == 2:
            tell[sz.lat_lines :, :] = facts_block[...]
        tell.start()
    store_edges(sz, out, diffusivity if last else None, edge_first, edge_second)


def pack_slots(sz, tables, surface, packed):
    for slot in range(sz.slots):
        at = pl.multiple_of(tile_at(sz, tables, 0, slot) * CHANNELS, CHANNELS)
        packed[slot * CHANNELS : (slot + 1) * CHANNELS, :] = surface[pl.ds(at, CHANNELS), :]


def store_edges(sz, field, diffusivity, send_first, send_second):
    outer = high_first() * (sz.rows - 1)
    for row, send in ((outer, send_first), (sz.rows - 1 - outer, send_second)):
        for channel in range(CHANNELS):
            for tile in range(sz.row_tiles):
                value = field[row, channel, :, cols(tile)]
                if diffusivity is not None:
                    value = value * jnp.broadcast_to(
                        diffusivity[row, 0:1, cols(tile)], (LEVELS, WIDTH)
                    )
                at = (channel * sz.row_tiles + tile) * LEVELS
                send[at : at + LEVELS, :] = value
        send.start()


def owner_kernel(sz, decode, arrive, arrived, mixing, air, wind, facts, *refs):
    slots = sz.slots
    if decode:
        told_first, told_second, own_table, own_facts, tables, weights = refs[:6]
        refs = refs[6:]
    flux, mixed_slope, flux_slope, flat, first = refs

    def bulk(row, column):
        return facts[0, sz.bulk_at + row * CHANNELS + column]

    values = [arrived[pl.ds(c, slots, stride=CHANNELS), :] for c in range(CHANNELS)]
    mixed = jnp.tanh(
        jnp.dot(
            mixing[...],
            jnp.concatenate(values, axis=1),
            precision=HIGHEST,
            preferred_element_type=jnp.float32,
        )
    )
    contrast = []
    for c in range(CHANNELS):
        mixed_here = mixed[:, cols(c)]
        mixed_slope[c] = 1.0 - mixed_here * mixed_here
        contrast.append((air[...] - values[0] if c == 0 else values[c]) + mixed_here)
    mixed_slope.start()
    arrive_all(arrive)
    if decode:
        lines = sz.slot_lines
        tables[0:lines, :] = own_table[...]
        weights[0:1, :] = own_facts[...]
        both = sided(told_first[sz.lat_lines :, :], told_second[sz.lat_lines :, :])
        for which, told in ((1, both[0]), (2, both[1])):
            got = told[0:lines, :].astype(jnp.int32)
            tables[which * lines : (which + 1) * lines, :] = sz.tiles - got
            weights[which : which + 1, :] = told[lines : lines + 1, :]
        tables.start()
        weights.start()

    rate = FLUX_RATE * wind[...]
    for c in range(CHANNELS):
        forcing = bulk(c, 0) * contrast[0]
        for k in range(1, CHANNELS):
            forcing = forcing + bulk(c, k) * contrast[k]
        bent = jnp.tanh(forcing)
        flux_slope[c] = rate * (1.0 - bent * bent)
        one = rate * bent
        flat[pl.ds(c, slots, stride=CHANNELS), :] = one
        if c == 0:
            first[...] = one
    flux_slope.start()
    cap = sz.capacity
    gap = jnp.zeros((sz.chunk - sz.own_rows, WIDTH), jnp.float32)
    for d in range(sz.devices):
        at = d * sz.chunk
        flux[at : at + sz.own_rows, :] = flat[d * sz.own_rows : (d + 1) * sz.own_rows, :]
        at = at + sz.own_rows
        flux[at : (d + 1) * sz.chunk, :] = gap
        if d > 0:
            flux[at : at + cap, :] = first[(d - 1) * cap : d * cap, :]
        if d < sz.devices - 1:
            flux[at + cap : at + 2 * cap, :] = first[(d + 1) * cap : (d + 2) * cap, :]


def owner_back_kernel(sz, arrive, arrived, mixing, mixed_slope, flux_slope, facts, back, flat, extra):
    slots, cap = sz.slots, sz.capacity

    def bulk(row, column):
        return facts[0, sz.bulk_at + row * CHANNELS + column]

    for d in range(sz.devices):
        at = d * sz.chunk
        flat[d * sz.own_rows : (d + 1) * sz.own_rows, :] = arrived[at : at + sz.own_rows, :]
        more = jnp.zeros((cap, WIDTH), jnp.float32)
        if d < sz.devices - 1:
            at = (d + 1) * sz.chunk + sz.own_rows
            more = more + arrived[at : at + cap, :]
        if d > 0:
            at = (d - 1) * sz.chunk + sz.own_rows + cap
            more = more + arrived[at : at + cap, :]
        extra[d * cap : (d + 1) * cap, :] = more
    arrive_all(arrive)
    forced = []
    for c in range(CHANNELS):
        got = flat[pl.ds(c, slots, stride=CHANNELS), :]
        if c == 0:
            got = got + extra[...]
        forced.append(flux_slope[c] * got)
    direct = []
    for k in range(CHANNELS):
        total = bulk(0, k) * forced[0]
        for c in range(1, CHANNELS):
            total = total + bulk(c, k) * forced[c]
        direct.append(total)
    through = lax.dot_general(
        mixing[...],
        jnp.concatenate([direct[k] * mixed_slope[k] for k in range(CHANNELS)], axis=1),
        (((0,), (0,)), ((), ())),
        precision=HIGHEST,
        preferred_element_type=jnp.float32,
    )
    for k in range(CHANNELS):
        sign = -1.0 if k == 0 else 1.0
        back.block[pl.ds(k, slots, stride=CHANNELS), :] = through[:, cols(k)] + sign * direct[k]


def spread_back(sz, surface, slope, remap, tables, packed, near_low, near_high, tell_first, tell_second):
    rows, count, cap = sz.rows, sz.row_tiles, sz.capacity
    block = surface.block
    own = [row_tiles_of(sz, block, row) for row in range(rows)]
    sums = own_sums(sz, remap, own, FEEDBACK)
    send_sums(sz, sums, tell_first, tell_second)
    tell_first.start()
    tell_second.start()
    lats = [lat_rows(sz, slope, lat) * sums[lat] for lat in range(NEAR_LAT)]
    every = range(NEAR_LAT)
    for row in range(rows):
        added = sum_of([remap.own(lat, row) for lat in every], lats)
        put_row_tiles(sz, block, row, own[row] + added)
        at = row * count
        near_low[at : at + count, :] = sum_of(
            [remap.of_low(lat, row) for lat in range(LAT_DEV)], lats[:LAT_DEV]
        )
        near_high[at : at + count, :] = sum_of(
            [remap.of_high(lat, row) for lat in range(LAT_DEV, NEAR_LAT)], lats[LAT_DEV:]
        )
    rest = sz.near[0] - sz.tiles
    near_low[sz.tiles :, :] = jnp.zeros((rest, WIDTH), jnp.float32)
    near_high[sz.tiles :, :] = jnp.zeros((rest, WIDTH), jnp.float32)
    surface.start()
    gap = jnp.zeros((sz.chunk - sz.own_rows, WIDTH), jnp.float32)
    for owner in range(sz.devices):
        packed[owner * sz.chunk + sz.own_rows : (owner + 1) * sz.chunk, :] = gap
    for slot in range(sz.slots):
        owner, rank = slot // cap, slot % cap
        at = owner * sz.chunk + rank * CHANNELS
        tile = pl.multiple_of(tile_at(sz, tables, 0, slot) * CHANNELS, CHANNELS)
        packed[at : at + CHANNELS, :] = surface[pl.ds(tile, CHANNELS), :]
        at = owner * sz.chunk + sz.own_rows + rank
        packed[at : at + 1, :] = near_low[pl.ds(tile_at(sz, tables, 1, slot), 1), :]
        at = at + cap
        packed[at : at + 1, :] = near_high[pl.ds(tile_at(sz, tables, 2, slot), 1), :]


def surface_kernel(sz, last, arrive, *refs):
    refs = list(refs)
    flux, from_first, from_second, before, tables, weights = refs[:6]
    refs = refs[6:]
    if last:
        target, weight = refs[:2]
        surface, slope, packed, tell_first, tell_second, near_low, near_high = refs[2:]
        block = surface.block
    else:
        surface, send_first, send_second, slope, near_low, near_high = refs
        block = surface
    remap = Remap(sz, weights)
    arrive_all(arrive)
    rows, cap = sz.rows, sz.capacity
    block[...] = before[...]
    near_low[...] = jnp.zeros(sz.near, jnp.float32)
    near_high[...] = jnp.zeros(sz.near, jnp.float32)
    for slot in range(sz.slots):
        owner, rank = slot // cap, slot % cap
        at = owner * sz.chunk + rank * CHANNELS
        tile = pl.multiple_of(tile_at(sz, tables, 0, slot) * CHANNELS, CHANNELS)
        block[pl.ds(tile, CHANNELS), :] = (
            before[pl.ds(tile, CHANNELS), :] + flux[at : at + CHANNELS, :]
        )
        at = owner * sz.chunk + sz.own_rows + rank
        near_low[pl.ds(tile_at(sz, tables, 1, slot), 1), :] = flux[at : at + 1, :]
        at = at + cap
        near_high[pl.ds(tile_at(sz, tables, 2, slot), 1), :] = flux[at : at + 1, :]
    block[CHANNELS * sz.tiles :, :] = jnp.zeros((CHANNELS, WIDTH), jnp.float32)
    own = [row_tiles_of(sz, block, row) for row in range(rows)]
    sums = own_sums(sz, remap, own, 1.0)
    told = told_sums(sz, from_first, from_second)
    air = []
    for lat in range(NEAR_LAT):
        if lat < LAT_DEV:
            near, weights = near_low, [remap.of_low(lat, row) for row in range(rows)]
        else:
            near, weights = near_high, [remap.of_high(lat, row) for row in range(rows)]
        more = sum_of(weights, [near_row(sz, near, row) for row in range(rows)])
        one = jnp.tanh(sums[lat] + told[lat] + more)
        slope[lat * sz.pitch : lat * sz.pitch + sz.row_tiles, :] = 1.0 - one * one
        air.append(one)
    slope.start()
    for row in range(rows):
        weights = [remap.own(lat, row) for lat in range(NEAR_LAT)]
        put_row_tiles(sz, block, row, own[row] + FEEDBACK * sum_of(weights, air))
    if last:
        for row in range(rows):
            for tile in range(sz.row_tiles):
                at = row * sz.row_width + tile * CHANNELS
                scale = weight[at : at + CHANNELS, :]
                off = block[at : at + CHANNELS, :] - target[row, :, cols(tile)]
                block[at : at + CHANNELS, :] = scale * scale * off
        spread_back(
            sz, surface, slope, remap, tables, packed, near_low, near_high, tell_first, tell_second
        )
    else:
        store_rows(sz, surface, send_first, send_second)


def merge_kernel(
    sz, arrive, back, from_first, from_second, before, slope, tables, facts, diffusivity, surface, send_first, send_second
):
    rows = sz.rows
    remap = Remap(sz, facts)
    arrive_all(arrive)
    surface[...] = before[...]
    for slot in range(sz.slots):
        tile = pl.multiple_of(tile_at(sz, tables, 0, slot) * CHANNELS, CHANNELS)
        surface[pl.ds(tile, CHANNELS), :] = (
            before[pl.ds(tile, CHANNELS), :] + back[slot * CHANNELS : (slot + 1) * CHANNELS, :]
        )
    surface[CHANNELS * sz.tiles :, :] = jnp.zeros((CHANNELS, WIDTH), jnp.float32)
    told = told_sums(sz, from_first, from_second)
    lats = [lat_rows(sz, slope, lat) * told[lat] for lat in range(NEAR_LAT)]
    for row in range(rows):
        own = row_tiles_of(sz, surface, row)
        weights = [remap.own(lat, row) for lat in range(NEAR_LAT)]
        put_row_tiles(sz, surface, row, own + sum_of(weights, lats))
    store_rows(sz, surface, send_first, send_second, diffusivity)


def backward_load_kernel(sz, last, arrive, mix, diffusivity, field, drive, surface, *refs):
    refs = list(refs)
    if last:
        perturbation = refs.pop(0)
    mix_out, rows_out, local, bent_all, scaled = refs[:5]
    refs = refs[5:]
    if last:
        start_all = refs.pop(0)
    in_sems = refs[0]

    def arrivals(row):
        copies = [
            pltpu.make_async_copy(field.at[row], local.at[row], in_sems.at[0, row]),
            pltpu.make_async_copy(drive.at[row], bent_all.at[row], in_sems.at[1, row]),
        ]
        if last:
            copies.append(
                pltpu.make_async_copy(perturbation.at[row], start_all.at[row], in_sems.at[2, row])
            )
        return copies

    for row in range(sz.rows):
        for arrival in arrivals(row):
            arrival.start()
    arrive_all(arrive)
    mix_out[...] = mix[...]
    rows_out[...] = diffusivity[...]

    def one_row(row, carry):
        for arrival in arrivals(row):
            arrival.wait()
        load_surface_row(sz, local, row, surface, row * sz.row_width)
        for t in range(sz.row_tiles):
            coeff = jnp.broadcast_to(diffusivity[row, 0:1, cols(t)], (LEVELS, WIDTH))
            for c in range(CHANNELS):
                scaled[row, c, :, cols(t)] = coeff * local[row, c, :, cols(t)]
        return carry

    lax.fori_loop(0, sz.rows, one_row, 0)


def backward_kernel(sz, last, arrive, *refs):
    refs = list(refs)
    if not last:
        tables, weights, slope = refs[:3]
        refs = refs[3:]
    low, high, first_surface, second_surface, diffusivity, mix = refs[:6]
    local, bent_all, scaled_all = refs[6:9]
    refs = refs[9:]
    if last:
        start_all, out, sums, padded = refs
    else:
        out, new_surface, packed, tell_first, tell_second, edge_first, edge_second = refs[:7]
        padded, near_low, near_high = refs[7:]
        remap = Remap(sz, weights)
    count = sz.row_tiles
    place_edges(sz, padded, low, high, first_surface, second_surface)

    def ready(row):
        padded[row + 1] = scaled_all[row]

    ready(0)
    lane = lax.broadcasted_iota(jnp.int32, (LEVELS, WIDTH), 1)
    masks = level_masks()

    def one_row(row, carry):
        @pl.when(row < sz.rows - 1)
        def _():
            ready(row + 1)

        tiles = RowTiles(count, lambda c, t: padded[row + 1, c, :, cols(t)])
        for t in range(count):
            here, bent = [], []
            for c in range(CHANNELS):
                value = local[row, c, :, cols(t)]
                one = bent_all[row, c, :, cols(t)]
                here.append(value)
                bent.append((1.0 - one * one) * value)
            for c in range(CHANNELS):
                mixed = mix[c] * bent[0]
                for k in range(1, CHANNELS):
                    mixed = mixed + mix[k * CHANNELS + c] * bent[k]
                around = tiles.around(c, t, lane)
                around = around + (padded[row, c, :, cols(t)] + padded[row + 2, c, :, cols(t)])
                stepped = (
                    ((1.0 - 2.0 * KAPPA_V) * here[c] - 4.0 * tiles.here(c, t))
                    + around
                    + levels_sum(here[c], masks)
                    + TIME_STEP * mixed
                )
                out[row, c, :, cols(t)] = stepped
                if last:
                    start = start_all[row, c, :, cols(t)]
                    carry = (
                        carry[0] + start * start,
                        carry[1] + start * stepped,
                        carry[2] + stepped * stepped,
                    )
                else:
                    new_surface[pl.ds((row * count + t) * CHANNELS + c, 1), :] = stepped[0:1, :]
        out.row(row).start()
        return carry

    blank = jnp.zeros((LEVELS, WIDTH), jnp.float32)
    totals = lax.fori_loop(0, sz.rows, one_row, (blank, blank, blank) if last else 0)
    if last:
        place = lax.broadcasted_iota(jnp.int32, sums.block.shape, 1)
        held = jnp.zeros(sums.block.shape, jnp.float32)
        for index in range(3):
            total = jnp.sum(jnp.sum(totals[index], axis=0, keepdims=True), axis=1, keepdims=True)
            held = jnp.where(place == index, total, held)
        sums[...] = held
    else:
        new_surface[CHANNELS * sz.tiles :, :] = jnp.zeros((CHANNELS, WIDTH), jnp.float32)
        arrive_all(arrive)
        spread_back(
            sz,
            new_surface,
            slope,
            remap,
            tables,
            packed,
            near_low,
            near_high,
            tell_first,
            tell_second,
        )
        packed.start()
        store_edges(sz, out, diffusivity, edge_first, edge_second)


def final_kernel(cell_total, arrive, everyones, perturbation, gradient, out):
    sums = jnp.sum(everyones[...], axis=0, keepdims=True) / cell_total
    place = lax.broadcasted_iota(jnp.int32, sums.shape, 1)
    means = [
        jnp.broadcast_to(
            jnp.sum(jnp.where(place == index, sums, 0.0), axis=1, keepdims=True), (1, WIDTH)
        )
        for index in range(3)
    ]
    scale = lax.rsqrt(means[2] + EPSILON)
    mean_sq = means[0] + 2.0 * ASCENT * scale * means[1] + ASCENT * ASCENT * scale * scale * means[2]
    shrink = lax.rsqrt(mean_sq + EPSILON)
    step = jnp.broadcast_to(ASCENT * scale * shrink, (CHANNELS, WIDTH))
    shrink = jnp.broadcast_to(shrink, (CHANNELS, WIDTH))
    levels, rows, _, cells = perturbation.shape

    def one_level(level, carry):
        for row in range(rows):
            for tile in range(cells // WIDTH):
                start = perturbation[level, row, :, cols(tile)]
                slope = gradient[level, row, :, cols(tile)]
                out[level, row, :, cols(tile)] = shrink * start + step * slope
        out.row(level).start()
        return carry

    lax.fori_loop(0, levels, one_level, 0)


class Operand:
    def __init__(self, array, space, fetch=None, at=()):
        self.array, self.space, self.fetch, self.at = array, space, fetch, at

    def block(self):
        whole = self.array.shape
        taken = [size for size, index in zip(whole, self.at) if isinstance(index, slice)]
        return self.fetch((*taken, *whole[len(self.at) :]), self.array.dtype)


def near_by(*arrays):
    return [Operand(array, pltpu.VMEM) for array in arrays]


def far_off(*arrays):
    return [
        Operand(pltpu.with_memory_space_constraint(array, pltpu.HBM), pltpu.HBM)
        for array in arrays
    ]


def fetched(*arrays, at=(), into=pltpu.VMEM):
    return [
        Operand(pltpu.with_memory_space_constraint(array, pltpu.HBM), pltpu.HBM, into, at)
        for array in arrays
    ]


def scalars(*arrays):
    return fetched(*arrays, into=pltpu.SMEM)


def call(kernel, name, inputs, kept=(), shipped=(), scratch=()):
    n_in, n_kept, n_out = len(inputs), len(kept), len(shipped)
    brought = [index for index, item in enumerate(inputs) if item.fetch is not None]

    def as_shape(item):
        return item if isinstance(item, jax.ShapeDtypeStruct) else jax.ShapeDtypeStruct(item, jnp.float32)

    kept = [as_shape(item) for item in kept]
    shipped = [as_shape(item) for item in shipped]

    def run(*refs):
        ins = list(refs[:n_in])
        kept_refs = refs[n_in : n_in + n_kept]
        homes = refs[n_in + n_kept : n_in + n_kept + n_out]
        rest = refs[n_in + n_kept + n_out :]
        outs = [
            Shipped(block, home, sems)
            for block, home, sems in zip(rest[:n_out], homes, rest[n_out : 2 * n_out])
        ]
        rest = rest[2 * n_out :]
        if brought:
            blocks, arrive_sems = rest[: len(brought)], rest[len(brought)]
            rest = rest[len(brought) + 1 :]
            copies = []
            for place, (index, block) in enumerate(zip(brought, blocks)):
                source = ins[index]
                if inputs[index].at:
                    source = source.at[inputs[index].at]
                copies.append(pltpu.make_async_copy(source, block, arrive_sems.at[place]))
                ins[index] = block
            for copy in copies:
                copy.start()
            arrive = [copy.wait for copy in copies]
        else:
            arrive = []
        kernel(arrive, *ins, *kept_refs, *outs, *rest)
        for out in outs:
            if not out.started:
                out.start()
        for out in outs:
            out.finish(out.block.shape[0])

    spaces = [pltpu.VMEM] * n_kept + [pltpu.HBM] * n_out
    blocks = [pltpu.VMEM(item.shape, item.dtype) for item in shipped]
    sems = [
        pltpu.SemaphoreType.DMA((item.shape[0] if len(item.shape) > 3 else 1,)) for item in shipped
    ]
    arriving = [inputs[index].block() for index in brought]
    if brought:
        arriving.append(pltpu.SemaphoreType.DMA((len(brought),)))
    more = [
        item if not isinstance(item, tuple) else pltpu.VMEM(item, jnp.float32) for item in scratch
    ]
    return pl.pallas_call(
        run,
        name=name,
        in_specs=[pl.BlockSpec(memory_space=item.space) for item in inputs],
        out_specs=[pl.BlockSpec(memory_space=space) for space in spaces],
        out_shape=kept + [pltpu.HBM(item.shape, item.dtype) for item in shipped],
        scratch_shapes=blocks + sems + arriving + more,
        compiler_params=pltpu.CompilerParams(vmem_limit_bytes=VMEM_BYTES),
    )(*[item.array for item in inputs])


def arrive_all(arrive):
    for wait in arrive:
        wait()


def swap(first, second):
    count = lax.axis_size("horiz")
    inner = [(i, i ^ 1) for i in range(count)]
    outer = [(i, i + 1) for i in range(1, count - 1, 2)]
    outer = outer + [(target, source) for source, target in outer]
    return lax.ppermute(first, "horiz", inner), lax.ppermute(second, "horiz", outer)


def exchange(array, devices):
    rows = array.shape[0] // devices
    step = CHANNELS if rows % CHANNELS == 0 else 2
    split = array.reshape(devices, rows // step, step, WIDTH)
    moved = lax.all_to_all(split, "horiz", split_axis=0, concat_axis=0, tiled=True)
    return moved.reshape(array.shape)


def body(
    perturbation,
    base_state,
    target_state,
    cost_weight,
    diffusivity,
    chan_mix,
    coupler_mix,
    owner_mix,
    air_temp,
    wind_speed,
    wet_list,
    wet_owner,
    remap_src,
    remap_tgt,
    remap_weight,
):
    devices = lax.axis_size("horiz")
    hours = air_temp.shape[0]
    sz = Sizes(devices, air_temp.shape[2] // devices, base_state.shape[1], base_state.shape[3])
    rows = sz.rows
    native_row = (LEVELS, CHANNELS, sz.cells)

    edge_inputs = []
    for array in (perturbation, base_state):
        for row in (0, rows - 1):
            edge_inputs += fetched(array, at=(slice(None), row))
    edges = swap(
        *call(functools.partial(edges_kernel, sz), "edges", edge_inputs, kept=[sz.edge, sz.edge])
    )
    me = lax.axis_index("horiz").astype(jnp.int32)

    def lined(first_row, second_row):
        size = -(-first_row.shape[0] // WIDTH) * WIDTH
        pair = jnp.stack([first_row.astype(jnp.float32), second_row.astype(jnp.float32)])
        return jnp.pad(pair, ((0, 0), (0, size - pair.shape[1])), constant_values=-1.0)

    places = jnp.arange(CHANNELS * CHANNELS, dtype=jnp.int32) + sz.bulk_at
    remap_at = (remap_tgt - (me * LAT_DEV - 1)) * rows + remap_src - me * rows
    remap_lines = lined(
        jnp.concatenate([remap_at, places]),
        jnp.concatenate([remap_weight, coupler_mix.reshape(-1)]),
    )
    mix_rows = chan_mix.transpose(1, 2, 0).reshape(CHANNELS * CHANNELS, LEVELS)
    row_lines = (rows, 1, sz.cells)
    tiles_lines = (CHANNELS * sz.tiles, WIDTH)
    first_mix, first_rows, table, facts, line, mix = call(
        functools.partial(setup_kernel, sz, wet_list.shape[1], remap_at.shape[0] + places.shape[0]),
        "setup",
        near_by(lined(wet_list[0], wet_owner[0]), remap_lines, mix_rows)
        + fetched(diffusivity),
        kept=[(CHANNELS * CHANNELS, LEVELS, WIDTH), row_lines],
        shipped=[
            jax.ShapeDtypeStruct((sz.slot_lines, WIDTH), jnp.int32),
            (sz.facts, WIDTH),
            (1, WIDTH),
            (CHANNELS * CHANNELS, LEVELS, WIDTH),
        ],
    )
    wider = (rows + 2, CHANNELS, LEVELS, sz.cells)
    row_surface = (sz.row_width, WIDTH)
    by_row = (rows, *native_row)

    def row_sems(kinds):
        return pltpu.SemaphoreType.DMA((kinds, rows))

    (field,) = call(
        functools.partial(load_kernel, sz),
        "load",
        far_off(perturbation, base_state),
        kept=[sz.whole],
        scratch=[by_row, by_row, row_sems(2)],
    )

    def relayout(array):
        return call(
            functools.partial(relayout_kernel, sz),
            "relayout",
            far_off(array),
            shipped=[sz.whole],
            scratch=[by_row, row_sems(1)],
        )

    saved = []
    near = [sz.near, sz.near]
    mix_shape = (CHANNELS * CHANNELS, LEVELS, WIDTH)
    by_slot = (sz.slots, WIDTH)
    for hour in range(hours):
        first, last = hour == 0, hour == hours - 1
        assert not (first and last)
        inputs = scalars(table, line)
        if first:
            same = near_by(first_rows, first_mix, field)
            before = call(
                functools.partial(forward_kernel, sz, True, False, 1),
                "step_near",
                near_by(edges[0]) + same,
                kept=[sz.whole, sz.whole, sz.surface],
                scratch=[wider],
            )
            inputs += near_by(edges[1]) + same + fetched(facts) + near_by(*before)
        else:
            loads = fetched(mix, diffusivity_rows, *([weight_rows] if last else []))
            loads += far_off(field) + near_by(surface) + (far_off(target) if last else [])
            mix_here, rows_here, field, *more = call(
                functools.partial(forward_load_kernel, sz, last),
                "step_load",
                loads,
                kept=[mix_shape, row_lines, sz.whole] + ([row_lines, sz.whole] if last else []),
                scratch=[row_sems(2)],
            )
            inputs += near_by(*edges, rows_here, mix_here, field, *surface_edges, *more)
        field, drive, surface, packed, *sends = call(
            functools.partial(forward_kernel, sz, first, last, 2 if first else 0),
            "step",
            inputs,
            shipped=[sz.whole, sz.whole, sz.surface, sz.narrow]
            + [sz.told if first else sz.lats] * 2
            + [sz.edge] * 2,
            scratch=[wider],
        )
        arrived = exchange(packed, devices)
        got = swap(*sends[:2])
        arrived, *got = lax.optimization_barrier((arrived, *got))
        inputs = (
            near_by(arrived, owner_mix[0], air_temp[hour, 0], wind_speed[hour, 0])
            + scalars(line)
        )
        decoded = []
        if first:
            inputs += near_by(*got) + fetched(table, line)
            decoded = [jax.ShapeDtypeStruct(sz.tables, jnp.int32), sz.weights]
        *decoded, flux, mixed_slope, flux_slope = call(
            functools.partial(owner_kernel, sz, first),
            "owners",
            inputs,
            shipped=[*decoded, sz.wide, sz.by_slot, sz.by_slot],
            scratch=[sz.narrow, by_slot],
        )
        if first:
            tables, weights = decoded
        flux, *sends = lax.optimization_barrier((flux, *sends[2:]))
        if first:
            flux, diffusivity, target_state = lax.optimization_barrier(
                (flux, diffusivity, target_state)
            )
            beside = call(
                functools.partial(columns_kernel, sz),
                "columns",
                fetched(diffusivity, cost_weight),
                shipped=[row_lines, row_lines, tiles_lines, tiles_lines],
            ) + relayout(target_state)
        else:
            flux, perturbation = lax.optimization_barrier((flux, perturbation))
            beside = relayout(perturbation)
        flux = exchange(flux, devices)
        flux, *beside = lax.optimization_barrier((flux, *beside))
        if first:
            diffusivity_rows, weight_rows, diffusivity_tiles, weight_tiles, target = beside
        else:
            start_field = beside[0]
        edges = swap(*sends)
        inputs = near_by(flux, *got) + fetched(surface) + scalars(tables, weights)
        if last:
            surface, slope, packed, *sends = call(
                functools.partial(surface_kernel, sz, True),
                "surface",
                inputs + fetched(target_state, at=(0,)) + fetched(weight_tiles),
                shipped=[sz.surface, sz.slope, sz.wide, sz.lats, sz.lats],
                scratch=near,
            )
        else:
            surface, *sends, slope = call(
                functools.partial(surface_kernel, sz, False),
                "surface",
                inputs,
                kept=[sz.surface, row_surface, row_surface],
                shipped=[sz.slope],
                scratch=near,
            )
            surface_edges = swap(*sends)
        saved.append((drive, slope, mixed_slope, flux_slope))

    edge_sends = None
    for hour in reversed(range(hours)):
        drive, slope, mixed_slope, flux_slope = saved[hour]
        arrived = exchange(packed, devices)
        got = swap(*sends)
        arrived, *got = lax.optimization_barrier((arrived, *got))
        back = call(
            functools.partial(owner_back_kernel, sz),
            "owners_back",
            near_by(arrived, owner_mix[0]) + fetched(mixed_slope, flux_slope) + scalars(line),
            shipped=[sz.narrow],
            scratch=[sz.narrow, by_slot],
        )[0]
        if edge_sends is not None:
            back, *edge_sends = lax.optimization_barrier((back, *edge_sends))
            edges = swap(*edge_sends)
        back = exchange(back, devices)
        surface, *row_sends = call(
            functools.partial(merge_kernel, sz),
            "merge",
            near_by(back, *got)
            + fetched(surface, slope)
            + scalars(table, line)
            + fetched(diffusivity_tiles),
            kept=[sz.surface, row_surface, row_surface],
        )
        surface_edges = swap(*row_sends)
        last = hour == 0
        mix_here, rows_here, *loaded = call(
            functools.partial(backward_load_kernel, sz, last),
            "step_back_load",
            fetched(mix, diffusivity_rows)
            + far_off(field, drive)
            + near_by(surface)
            + (far_off(start_field) if last else []),
            kept=[mix_shape, row_lines] + [sz.whole] * (4 if last else 3),
            scratch=[row_sems(3)],
        )
        inputs = near_by(*edges, *surface_edges, rows_here, mix_here, *loaded)
        if last:
            gradient, sums = call(
                functools.partial(backward_kernel, sz, True),
                "step_back_sums",
                inputs,
                shipped=[sz.whole, (devices, WIDTH)],
                scratch=[wider],
            )
        else:
            field, surface, packed, *outs = call(
                functools.partial(backward_kernel, sz, False),
                "step_back",
                scalars(tables, weights) + fetched(saved[hour - 1][1]) + inputs,
                shipped=[sz.whole, sz.surface, sz.wide, sz.lats, sz.lats, sz.edge, sz.edge],
                scratch=[wider, *near],
            )
            sends, edge_sends = outs[:2], outs[2:]

    everyones = lax.all_to_all(sums, "horiz", split_axis=0, concat_axis=0, tiled=True)
    block = perturbation.shape
    return call(
        functools.partial(final_kernel, perturbation.size * devices),
        "finish",
        near_by(everyones, perturbation, gradient.transpose(2, 0, 1, 3)),
        shipped=[block],
    )[0]


def solution(mesh):
    placed = (
        P("member", "horiz", None, None),
        P(None, "horiz", None, None),
        P(None, "horiz", None, None),
        P("horiz", None),
        P("horiz", None),
        P(),
        P(),
        P("horiz", None, None),
        P(None, "horiz", None, None),
        P(None, "horiz", None, None),
        P("horiz", None),
        P("horiz", None),
        P("horiz"),
        P("horiz"),
        P("horiz"),
    )
    return jax.shard_map(
        body,
        mesh=mesh,
        in_specs=placed,
        out_specs=P("member", "horiz", None, None),
        check_vma=False,
    )
```

```python
import functools

import jax
import jax.numpy as jnp
from jax import lax
from jax.experimental import pallas as pl
from jax.experimental.pallas import tpu as pltpu
from jax.sharding import PartitionSpec as P

LAT_DEV = 2
NEAR_LAT = LAT_DEV + 2
CHANNELS = 4
LEVELS = 8
WIDTH = 128
SUBLANES = 8

KAPPA_V = 0.1
TIME_STEP = 0.3
FLUX_RATE = 0.05
FEEDBACK = 0.5
ASCENT = 0.5
EPSILON = 1e-06
HIGHEST = lax.Precision.HIGHEST
VMEM_BYTES = 32 * 1024 * 1024


class Sizes:
    def __init__(self, devices, capacity, rows, cells):
        self.devices = devices
        self.capacity = capacity
        self.slots = devices * capacity
        self.rows = rows
        self.cells = cells
        self.row_tiles = cells // WIDTH
        self.tiles = rows * self.row_tiles
        self.row_width = CHANNELS * self.row_tiles
        self.pitch = -(-self.row_tiles // SUBLANES) * SUBLANES
        self.own_rows = CHANNELS * capacity
        self.chunk = self.own_rows + 2 * capacity
        self.slot_lines = -(-self.slots // WIDTH)
        self.facts = -(-(self.slot_lines + 1) // SUBLANES) * SUBLANES
        self.lat_lines = LAT_DEV * self.pitch
        self.edge_lines = CHANNELS * self.row_tiles * LEVELS
        self.whole = (rows, CHANNELS, LEVELS, cells)
        self.edge = (self.edge_lines, WIDTH)
        self.told = (self.lat_lines + self.facts, WIDTH)
        self.surface = (CHANNELS * (self.tiles + 1), WIDTH)
        self.narrow = (CHANNELS * self.slots, WIDTH)
        self.wide = (devices * self.chunk, WIDTH)
        self.slope = (NEAR_LAT * self.pitch, WIDTH)
        self.lats = (self.lat_lines, WIDTH)
        self.bulk_at = NEAR_LAT * rows
        self.tables = (3 * self.slot_lines, WIDTH)
        self.weights = (3, WIDTH)
        self.near = (-(-(self.tiles + 1) // SUBLANES) * SUBLANES, WIDTH)
        self.by_slot = (CHANNELS, self.slots, WIDTH)


class Shipped:
    def __init__(self, block, home, sems):
        self.block, self.home, self.sems = block, home, sems
        self.by_row = False
        self.started = False

    def __getitem__(self, at):
        return self.block[at]

    def __setitem__(self, at, value):
        self.block[at] = value

    def row(self, index):
        self.by_row = True
        self.started = True
        return pltpu.make_async_copy(
            self.block.at[index], self.home.at[index], self.sems.at[index]
        )

    def row_from(self, block, index):
        self.by_row = True
        self.started = True
        return pltpu.make_async_copy(block.at[index], self.home.at[index], self.sems.at[index])

    def all(self):
        return pltpu.make_async_copy(self.block, self.home, self.sems.at[0])

    def start(self):
        self.started = True
        self.all().start()

    def finish(self, rows):
        if self.by_row:
            for index in range(rows):
                self.row(index).wait()
        else:
            self.all().wait()


def cols(tile):
    return slice(tile * WIDTH, (tile + 1) * WIDTH)


def lanes_sum(left_here, left_before, right_here, right_after, lane):
    return jnp.where(lane == 0, left_before, left_here) + jnp.where(
        lane == WIDTH - 1, right_after, right_here
    )


def level_masks():
    sub = lax.broadcasted_iota(jnp.int32, (LEVELS, WIDTH), 0)
    return jnp.where(sub == 0, 0.0, KAPPA_V), jnp.where(sub == LEVELS - 1, 0.0, KAPPA_V)


def levels_sum(field, masks):
    return masks[0] * pltpu.roll(field, 1, 0) + masks[1] * pltpu.roll(field, LEVELS - 1, 0)


class RowTiles:
    def __init__(self, count, load):
        self.count, self.load, self.held = count, load, {}

    def make(self, channel, tile):
        value = self.load(channel, tile)
        return value, pltpu.roll(value, 1, 1), pltpu.roll(value, WIDTH - 1, 1)

    def get(self, channel, tile):
        if (channel, tile) not in self.held:
            self.held[channel, tile] = self.make(channel, tile)
        return self.held[channel, tile]

    def here(self, channel, tile):
        return self.get(channel, tile)[0]

    def around(self, channel, tile, lane):
        last = self.count - 1
        before = self.get(channel, tile - 1) if tile > 0 else self.make(channel, last)
        after = self.get(channel, tile + 1) if tile < last else self.make(channel, 0)
        _, to_right, to_left = self.get(channel, tile)
        return lanes_sum(to_right, before[1], to_left, after[2], lane)


def row_tiles_of(sz, ref, row):
    return ref[pl.ds(row * sz.row_width, sz.row_tiles, stride=CHANNELS), :]


def put_row_tiles(sz, ref, row, value):
    ref[pl.ds(row * sz.row_width, sz.row_tiles, stride=CHANNELS), :] = value


def near_row(sz, ref, row):
    return ref[row * sz.row_tiles : (row + 1) * sz.row_tiles, :]


def high_first():
    return 1 - lax.rem(lax.axis_index("horiz").astype(jnp.int32), 2)


def pick(flag, one, other):
    return jnp.where(jnp.full(one.shape, flag, jnp.int32) == 1, one, other)


def sided(first, second):
    flag = high_first()
    return pick(flag, second, first), pick(flag, first, second)


def load_surface_row(sz, target, row, source, base):
    for tile in range(sz.row_tiles):
        for channel in range(CHANNELS):
            at = base + tile * CHANNELS + channel
            target[row, channel, 0:1, cols(tile)] = source[pl.ds(at, 1), :]


def as_column(row, size):
    shape = (size, row.shape[1])
    diagonal = lax.broadcasted_iota(jnp.int32, shape, 0) == lax.broadcasted_iota(jnp.int32, shape, 1)
    return jnp.sum(jnp.where(diagonal, row, 0.0), axis=1, keepdims=True)


def setup_kernel(sz, entries, remap_entries, arrive, wet, remap, mix_rows, diffusivity, *outs):
    first_mix, first_rows, table, facts, line, mix = outs
    arrive_all(arrive)
    for row in range(sz.rows):
        first_rows[row] = diffusivity[row : row + 1, :]
    for index in range(CHANNELS * CHANNELS):
        column = as_column(mix_rows[index : index + 1, :], LEVELS)
        mix[index] = jnp.broadcast_to(column, (LEVELS, WIDTH))
    mix.start()
    first_mix[...] = mix[...]
    tiles, owners = wet[0:1, :], wet[1:2, :]
    size = -(-entries // SUBLANES) * SUBLANES
    shape = (size, wet.shape[1])
    tile_here, owner_here = as_column(tiles, size), as_column(owners, size)
    earlier = lax.broadcasted_iota(jnp.int32, shape, 1) < lax.broadcasted_iota(jnp.int32, shape, 0)
    same = (owner_here == owners) & earlier
    rank = jnp.sum(jnp.where(same, 1.0, 0.0), axis=1, keepdims=True)
    slot = jnp.where(owner_here >= 0.0, owner_here * sz.capacity + rank, -1.0)
    facts[...] = jnp.zeros((sz.facts, WIDTH), jnp.float32)
    for index in range(sz.slot_lines):
        place = lax.broadcasted_iota(jnp.int32, (size, WIDTH), 1) + index * WIDTH
        match = slot.astype(jnp.int32) == place
        told = jnp.sum(jnp.where(match, sz.tiles - tile_here, 0.0), axis=0, keepdims=True)
        facts[index : index + 1, :] = told
        table[index : index + 1, :] = sz.tiles - told.astype(jnp.int32)
    size = -(-remap_entries // SUBLANES) * SUBLANES
    at, amount = as_column(remap[0:1, :], size), as_column(remap[1:2, :], size)
    place = lax.broadcasted_iota(jnp.int32, (size, WIDTH), 1)
    line[...] = jnp.sum(
        jnp.where(at.astype(jnp.int32) == place, amount, 0.0), axis=0, keepdims=True
    )
    facts[sz.slot_lines : sz.slot_lines + 1, :] = line[...]


def columns_kernel(sz, arrive, diffusivity, weight, *outs):
    diffusivity_rows, weight_rows, diffusivity_tiles, weight_tiles = outs
    arrive_all(arrive)
    for source, by_row, by_tile in (
        (diffusivity, diffusivity_rows, diffusivity_tiles),
        (weight, weight_rows, weight_tiles),
    ):
        for row in range(sz.rows):
            by_row[row] = source[row : row + 1, :]
            for tile in range(sz.row_tiles):
                line = source[row : row + 1, cols(tile)]
                at = (row * sz.row_tiles + tile) * CHANNELS
                by_tile[at : at + CHANNELS, :] = jnp.broadcast_to(line, (CHANNELS, WIDTH))


def gather_levels(block, channel, tile):
    sub = lax.broadcasted_iota(jnp.int32, (LEVELS, WIDTH), 0)
    total = None
    for level in range(LEVELS):
        line = block[level, channel : channel + 1, cols(tile)]
        line = jnp.broadcast_to(line, (LEVELS, WIDTH))
        total = line if total is None else jnp.where(sub == level, line, total)
    return total


def edges_kernel(sz, arrive, low_start, high_start, low_base, high_base, send_first, send_second):
    arrive_all(arrive)
    low_start[...] = low_start[...] + low_base[...]
    high_start[...] = high_start[...] + high_base[...]
    flag = high_first()
    for channel in range(CHANNELS):
        for tile in range(sz.row_tiles):
            low = gather_levels(low_start, channel, tile)
            high = gather_levels(high_start, channel, tile)
            at = (channel * sz.row_tiles + tile) * LEVELS
            send_first[at : at + LEVELS, :] = pick(flag, high, low)
            send_second[at : at + LEVELS, :] = pick(flag, low, high)


def load_kernel(sz, arrive, perturbation, base, field, start_block, base_block, in_sems):
    def arrivals(row):
        return [
            pltpu.make_async_copy(source.at[:, row], block.at[row], in_sems.at[index, row])
            for index, (source, block) in enumerate(
                ((perturbation, start_block), (base, base_block))
            )
        ]

    for row in range(sz.rows):
        for arrival in arrivals(row):
            arrival.start()

    def one_row(row, carry):
        for arrival in arrivals(row):
            arrival.wait()
        start_block[row] = start_block[row] + base_block[row]
        for channel in range(CHANNELS):
            for tile in range(sz.row_tiles):
                field[row, channel, :, cols(tile)] = gather_levels(
                    start_block.at[row], channel, tile
                )
        return carry

    lax.fori_loop(0, sz.rows, one_row, 0)


def relayout_kernel(sz, arrive, source, out, block, in_sems):
    def arrival(row):
        return pltpu.make_async_copy(source.at[:, row], block.at[row], in_sems.at[0, row])

    for row in range(sz.rows):
        arrival(row).start()

    def one_row(row, carry):
        arrival(row).wait()
        for channel in range(CHANNELS):
            for tile in range(sz.row_tiles):
                out[row, channel, :, cols(tile)] = gather_levels(block.at[row], channel, tile)
        out.row(row).start()
        return carry

    lax.fori_loop(0, sz.rows, one_row, 0)


class Remap:
    def __init__(self, sz, weights):
        self.sz, self.weights = sz, weights

    def weight(self, which, lat, row):
        return self.weights[which, lat * self.sz.rows + row]

    def own(self, lat, row):
        return self.weight(0, lat, row)

    def of_low(self, lat, row):
        return self.weight(1, lat + LAT_DEV, row)

    def of_high(self, lat, row):
        return self.weight(2, lat - LAT_DEV, row)


def tile_at(sz, tables, which, slot):
    return tables[which * sz.slot_lines + slot // WIDTH, slot % WIDTH]


def sum_of(weights, values):
    total = weights[0] * values[0]
    for weight, value in zip(weights[1:], values[1:]):
        total = total + weight * value
    return total


def own_sums(sz, remap, own, factor):
    return [
        factor * sum_of([remap.own(lat, row) for row in range(sz.rows)], own)
        for lat in range(NEAR_LAT)
    ]


def send_sums(sz, sums, tell_first, tell_second):
    flag = high_first()
    for index in range(LAT_DEV):
        low, high = sums[index], sums[LAT_DEV + index]
        at = index * sz.pitch
        tell_first[at : at + sz.row_tiles, :] = pick(flag, high, low)
        tell_second[at : at + sz.row_tiles, :] = pick(flag, low, high)


def lat_rows(sz, ref, lat):
    at = lat * sz.pitch
    return ref[at : at + sz.row_tiles, :]


def told_sums(sz, from_first, from_second):
    lows, highs = [], []
    for index in range(LAT_DEV):
        low, high = sided(lat_rows(sz, from_first, index), lat_rows(sz, from_second, index))
        lows.append(low)
        highs.append(high)
    return lows + highs


def place_edge(sz, padded, at, edge, surface=None):
    for channel in range(CHANNELS):
        for tile in range(sz.row_tiles):
            line = (channel * sz.row_tiles + tile) * LEVELS
            padded[at, channel, :, cols(tile)] = edge[line : line + LEVELS, :]
    if surface is not None:
        load_surface_row(sz, padded, at, surface, 0)


def place_edges(sz, padded, first, second, first_surface=None, second_surface=None):
    side = high_first() * (sz.rows + 1)
    place_edge(sz, padded, side, first, first_surface)
    place_edge(sz, padded, sz.rows + 1 - side, second, second_surface)


def store_rows(sz, surface, send_first, send_second, factor=None):
    row = high_first() * (sz.rows - 1)
    for at, send in ((row, send_first), (sz.rows - 1 - row, send_second)):
        for tile in range(sz.row_tiles):
            start = pl.multiple_of((at * sz.row_tiles + tile) * CHANNELS, CHANNELS)
            value = surface[pl.ds(start, CHANNELS), :]
            if factor is not None:
                value = factor[pl.ds(start, CHANNELS), :] * value
            send[tile * CHANNELS : (tile + 1) * CHANNELS, :] = value


def forward_load_kernel(sz, last, arrive, mix, diffusivity, *refs):
    refs = list(refs)
    if last:
        weight = refs.pop(0)
    field, surface = refs[:2]
    refs = refs[2:]
    if last:
        target = refs.pop(0)
    mix_out, rows_out, field_out = refs[:3]
    refs = refs[3:]
    if last:
        weight_out, target_out = refs[:2]
        refs = refs[2:]
    in_sems = refs[0]

    def arrivals(row):
        copies = [pltpu.make_async_copy(field.at[row], field_out.at[row], in_sems.at[0, row])]
        if last:
            copies.append(
                pltpu.make_async_copy(target.at[row], target_out.at[row], in_sems.at[1, row])
            )
        return copies

    for row in range(sz.rows):
        for arrival in arrivals(row):
            arrival.start()
    arrive_all(arrive)
    mix_out[...] = mix[...]
    rows_out[...] = diffusivity[...]
    if last:
        weight_out[...] = weight[...]

    def one_row(row, carry):
        for arrival in arrivals(row):
            arrival.wait()
        load_surface_row(sz, field_out, row, surface, row * sz.row_width)
        return carry

    lax.fori_loop(0, sz.rows, one_row, 0)


def forward_kernel(sz, first, last, part, arrive, *refs):
    refs = list(refs)
    if part != 1:
        tables, facts = refs[:2]
        refs = refs[2:]
    edges = refs[: 1 if part else 2]
    refs = refs[len(edges) :]
    diffusivity, mix, field = refs[:3]
    refs = refs[3:]
    if part == 2:
        facts_block, out_before, drive_before, surface_before = refs[:4]
        refs = refs[4:]
    surfaces = ()
    if not first:
        surfaces = refs[:2]
        refs = refs[2:]
    if last:
        weight, target = refs[:2]
        refs = refs[2:]
    out, drive, new_surface, *refs = refs
    if part != 1:
        packed, tell_first, tell_second, edge_first, edge_second = refs[:5]
        refs = refs[5:]
        remap = Remap(sz, facts)
    padded = refs[0]
    flag = high_first()
    near_side = flag * (sz.rows + 1)
    if part == 0:
        place_edges(sz, padded, *edges, *surfaces)
    else:
        place_edge(sz, padded, near_side if part == 1 else sz.rows + 1 - near_side, edges[0])
    if part == 2:
        new_surface[...] = surface_before[...]
        for index in range(sz.rows - 1):
            row = index + flag
            out.row_from(out_before, row).start()
            drive.row_from(drive_before, row).start()

    def ready(row):
        padded[row + 1] = field[row]

    if part == 0:
        ready(0)
    elif part == 1:
        for row in range(sz.rows):
            ready(row)
    else:
        ready((1 - flag) * (sz.rows - 1))
        ready((1 - flag) * (sz.rows - 1) + 2 * flag - 1)
    lane = lax.broadcasted_iota(jnp.int32, (LEVELS, WIDTH), 1)
    masks = level_masks()
    count = sz.row_tiles

    def one_row(row, carry):
        if part == 0:

            @pl.when(row < sz.rows - 1)
            def _():
                ready(row + 1)

        tiles = RowTiles(count, lambda c, t: padded[row + 1, c, :, cols(t)])
        for t in range(count):
            coeff = jnp.broadcast_to(diffusivity[row, 0:1, cols(t)], (LEVELS, WIDTH))
            center = (1.0 - 2.0 * KAPPA_V) - 4.0 * coeff
            if last:
                scale = weight[row, 0:1, cols(t)]
                scale = jnp.broadcast_to(scale * scale, (LEVELS, WIDTH))
            for c in range(CHANNELS):
                mixed = mix[c * CHANNELS] * tiles.here(0, t)
                for k in range(1, CHANNELS):
                    mixed = mixed + mix[c * CHANNELS + k] * tiles.here(k, t)
                bent = jnp.tanh(mixed)
                drive[row, c, :, cols(t)] = bent
                field_here = tiles.here(c, t)
                around = tiles.around(c, t, lane)
                around = around + (padded[row, c, :, cols(t)] + padded[row + 2, c, :, cols(t)])
                stepped = (
                    center * field_here
                    + coeff * around
                    + levels_sum(field_here, masks)
                    + TIME_STEP * bent
                )
                new_surface[pl.ds((row * count + t) * CHANNELS + c, 1), :] = stepped[0:1, :]
                if last:
                    stepped = scale * (stepped - target[row, c, :, cols(t)])
                out[row, c, :, cols(t)] = stepped
        if part != 1:
            drive.row(row).start()
            out.row(row).start()
        return carry

    if part == 0:
        lax.fori_loop(0, sz.rows, one_row, 0)
    elif part == 1:
        lax.fori_loop(0, sz.rows - 1, lambda index, carry: one_row(index + flag, carry), 0)
        return
    else:
        one_row((1 - flag) * (sz.rows - 1), 0)
        out[flag * (sz.rows - 1)] = out_before[flag * (sz.rows - 1)]
    new_surface[CHANNELS * sz.tiles :, :] = jnp.zeros((CHANNELS, WIDTH), jnp.float32)
    new_surface.start()
    arrive_all(arrive)
    pack_slots(sz, tables, new_surface, packed)
    packed.start()
    own = [row_tiles_of(sz, new_surface.block, row) for row in range(sz.rows)]
    send_sums(sz, own_sums(sz, remap, own, 1.0), tell_first, tell_second)
    for tell in (tell_first, tell_second):
        if part == 2:
            tell[sz.lat_lines :, :] = facts_block[...]
        tell.start()
    store_edges(sz, out, diffusivity if last else None, edge_first, edge_second)


def pack_slots(sz, tables, surface, packed):
    for slot in range(sz.slots):
        at = pl.multiple_of(tile_at(sz, tables, 0, slot) * CHANNELS, CHANNELS)
        packed[slot * CHANNELS : (slot + 1) * CHANNELS, :] = surface[pl.ds(at, CHANNELS), :]


def store_edges(sz, field, diffusivity, send_first, send_second):
    outer = high_first() * (sz.rows - 1)
    for row, send in ((outer, send_first), (sz.rows - 1 - outer, send_second)):
        for channel in range(CHANNELS):
            for tile in range(sz.row_tiles):
                value = field[row, channel, :, cols(tile)]
                if diffusivity is not None:
                    value = value * jnp.broadcast_to(
                        diffusivity[row, 0:1, cols(tile)], (LEVELS, WIDTH)
                    )
                at = (channel * sz.row_tiles + tile) * LEVELS
                send[at : at + LEVELS, :] = value
        send.start()


def owner_kernel(sz, decode, arrive, arrived, mixing, air, wind, facts, *refs):
    slots = sz.slots
    if decode:
        told_first, told_second, own_table, own_facts, tables, weights = refs[:6]
        refs = refs[6:]
    flux, mixed_slope, flux_slope, flat, first = refs

    def bulk(row, column):
        return facts[0, sz.bulk_at + row * CHANNELS + column]

    values = [arrived[pl.ds(c, slots, stride=CHANNELS), :] for c in range(CHANNELS)]
    mixed = jnp.tanh(
        jnp.dot(
            mixing[...],
            jnp.concatenate(values, axis=1),
            precision=HIGHEST,
            preferred_element_type=jnp.float32,
        )
    )
    contrast = []
    for c in range(CHANNELS):
        mixed_here = mixed[:, cols(c)]
        mixed_slope[c] = 1.0 - mixed_here * mixed_here
        contrast.append((air[...] - values[0] if c == 0 else values[c]) + mixed_here)
    mixed_slope.start()
    arrive_all(arrive)
    if decode:
        lines = sz.slot_lines
        tables[0:lines, :] = own_table[...]
        weights[0:1, :] = own_facts[...]
        both = sided(told_first[sz.lat_lines :, :], told_second[sz.lat_lines :, :])
        for which, told in ((1, both[0]), (2, both[1])):
            got = told[0:lines, :].astype(jnp.int32)
            tables[which * lines : (which + 1) * lines, :] = sz.tiles - got
            weights[which : which + 1, :] = told[lines : lines + 1, :]
        tables.start()
        weights.start()

    rate = FLUX_RATE * wind[...]
    for c in range(CHANNELS):
        forcing = bulk(c, 0) * contrast[0]
        for k in range(1, CHANNELS):
            forcing = forcing + bulk(c, k) * contrast[k]
        bent = jnp.tanh(forcing)
        flux_slope[c] = rate * (1.0 - bent * bent)
        one = rate * bent
        flat[pl.ds(c, slots, stride=CHANNELS), :] = one
        if c == 0:
            first[...] = one
    flux_slope.start()
    cap = sz.capacity
    gap = jnp.zeros((sz.chunk - sz.own_rows, WIDTH), jnp.float32)
    for d in range(sz.devices):
        at = d * sz.chunk
        flux[at : at + sz.own_rows, :] = flat[d * sz.own_rows : (d + 1) * sz.own_rows, :]
        at = at + sz.own_rows
        flux[at : (d + 1) * sz.chunk, :] = gap
        if d > 0:
            flux[at : at + cap, :] = first[(d - 1) * cap : d * cap, :]
        if d < sz.devices - 1:
            flux[at + cap : at + 2 * cap, :] = first[(d + 1) * cap : (d + 2) * cap, :]


def owner_back_kernel(sz, arrive, arrived, mixing, mixed_slope, flux_slope, facts, back, flat, extra):
    slots, cap = sz.slots, sz.capacity

    def bulk(row, column):
        return facts[0, sz.bulk_at + row * CHANNELS + column]

    for d in range(sz.devices):
        at = d * sz.chunk
        flat[d * sz.own_rows : (d + 1) * sz.own_rows, :] = arrived[at : at + sz.own_rows, :]
        more = jnp.zeros((cap, WIDTH), jnp.float32)
        if d < sz.devices - 1:
            at = (d + 1) * sz.chunk + sz.own_rows
            more = more + arrived[at : at + cap, :]
        if d > 0:
            at = (d - 1) * sz.chunk + sz.own_rows + cap
            more = more + arrived[at : at + cap, :]
        extra[d * cap : (d + 1) * cap, :] = more
    arrive_all(arrive)
    forced = []
    for c in range(CHANNELS):
        got = flat[pl.ds(c, slots, stride=CHANNELS), :]
        if c == 0:
            got = got + extra[...]
        forced.append(flux_slope[c] * got)
    direct = []
    for k in range(CHANNELS):
        total = bulk(0, k) * forced[0]
        for c in range(1, CHANNELS):
            total = total + bulk(c, k) * forced[c]
        direct.append(total)
    through = lax.dot_general(
        mixing[...],
        jnp.concatenate([direct[k] * mixed_slope[k] for k in range(CHANNELS)], axis=1),
        (((0,), (0,)), ((), ())),
        precision=HIGHEST,
        preferred_element_type=jnp.float32,
    )
    for k in range(CHANNELS):
        sign = -1.0 if k == 0 else 1.0
        back.block[pl.ds(k, slots, stride=CHANNELS), :] = through[:, cols(k)] + sign * direct[k]


def spread_back(sz, surface, slope, remap, tables, packed, near_low, near_high, tell_first, tell_second):
    rows, count, cap = sz.rows, sz.row_tiles, sz.capacity
    block = surface.block
    own = [row_tiles_of(sz, block, row) for row in range(rows)]
    sums = own_sums(sz, remap, own, FEEDBACK)
    send_sums(sz, sums, tell_first, tell_second)
    tell_first.start()
    tell_second.start()
    lats = [lat_rows(sz, slope, lat) * sums[lat] for lat in range(NEAR_LAT)]
    every = range(NEAR_LAT)
    for row in range(rows):
        added = sum_of([remap.own(lat, row) for lat in every], lats)
        put_row_tiles(sz, block, row, own[row] + added)
        at = row * count
        near_low[at : at + count, :] = sum_of(
            [remap.of_low(lat, row) for lat in range(LAT_DEV)], lats[:LAT_DEV]
        )
        near_high[at : at + count, :] = sum_of(
            [remap.of_high(lat, row) for lat in range(LAT_DEV, NEAR_LAT)], lats[LAT_DEV:]
        )
    rest = sz.near[0] - sz.tiles
    near_low[sz.tiles :, :] = jnp.zeros((rest, WIDTH), jnp.float32)
    near_high[sz.tiles :, :] = jnp.zeros((rest, WIDTH), jnp.float32)
    surface.start()
    gap = jnp.zeros((sz.chunk - sz.own_rows, WIDTH), jnp.float32)
    for owner in range(sz.devices):
        packed[owner * sz.chunk + sz.own_rows : (owner + 1) * sz.chunk, :] = gap
    for slot in range(sz.slots):
        owner, rank = slot // cap, slot % cap
        at = owner * sz.chunk + rank * CHANNELS
        tile = pl.multiple_of(tile_at(sz, tables, 0, slot) * CHANNELS, CHANNELS)
        packed[at : at + CHANNELS, :] = surface[pl.ds(tile, CHANNELS), :]
        at = owner * sz.chunk + sz.own_rows + rank
        packed[at : at + 1, :] = near_low[pl.ds(tile_at(sz, tables, 1, slot), 1), :]
        at = at + cap
        packed[at : at + 1, :] = near_high[pl.ds(tile_at(sz, tables, 2, slot), 1), :]


def surface_kernel(sz, last, arrive, *refs):
    refs = list(refs)
    flux, from_first, from_second, before, tables, weights = refs[:6]
    refs = refs[6:]
    if last:
        target, weight = refs[:2]
        surface, slope, packed, tell_first, tell_second, near_low, near_high = refs[2:]
        block = surface.block
    else:
        surface, send_first, send_second, slope, near_low, near_high = refs
        block = surface
    remap = Remap(sz, weights)
    arrive_all(arrive)
    rows, cap = sz.rows, sz.capacity
    block[...] = before[...]
    near_low[...] = jnp.zeros(sz.near, jnp.float32)
    near_high[...] = jnp.zeros(sz.near, jnp.float32)
    for slot in range(sz.slots):
        owner, rank = slot // cap, slot % cap
        at = owner * sz.chunk + rank * CHANNELS
        tile = pl.multiple_of(tile_at(sz, tables, 0, slot) * CHANNELS, CHANNELS)
        block[pl.ds(tile, CHANNELS), :] = (
            before[pl.ds(tile, CHANNELS), :] + flux[at : at + CHANNELS, :]
        )
        at = owner * sz.chunk + sz.own_rows + rank
        near_low[pl.ds(tile_at(sz, tables, 1, slot), 1), :] = flux[at : at + 1, :]
        at = at + cap
        near_high[pl.ds(tile_at(sz, tables, 2, slot), 1), :] = flux[at : at + 1, :]
    block[CHANNELS * sz.tiles :, :] = jnp.zeros((CHANNELS, WIDTH), jnp.float32)
    own = [row_tiles_of(sz, block, row) for row in range(rows)]
    sums = own_sums(sz, remap, own, 1.0)
    told = told_sums(sz, from_first, from_second)
    air = []
    for lat in range(NEAR_LAT):
        if lat < LAT_DEV:
            near, weights = near_low, [remap.of_low(lat, row) for row in range(rows)]
        else:
            near, weights = near_high, [remap.of_high(lat, row) for row in range(rows)]
        more = sum_of(weights, [near_row(sz, near, row) for row in range(rows)])
        one = jnp.tanh(sums[lat] + told[lat] + more)
        slope[lat * sz.pitch : lat * sz.pitch + sz.row_tiles, :] = 1.0 - one * one
        air.append(one)
    slope.start()
    for row in range(rows):
        weights = [remap.own(lat, row) for lat in range(NEAR_LAT)]
        put_row_tiles(sz, block, row, own[row] + FEEDBACK * sum_of(weights, air))
    if last:
        for row in range(rows):
            for tile in range(sz.row_tiles):
                at = row * sz.row_width + tile * CHANNELS
                scale = weight[at : at + CHANNELS, :]
                off = block[at : at + CHANNELS, :] - target[row, :, cols(tile)]
                block[at : at + CHANNELS, :] = scale * scale * off
        spread_back(
            sz, surface, slope, remap, tables, packed, near_low, near_high, tell_first, tell_second
        )
    else:
        store_rows(sz, surface, send_first, send_second)


def merge_kernel(
    sz, arrive, back, from_first, from_second, before, slope, tables, facts, diffusivity, surface, send_first, send_second
):
    rows = sz.rows
    remap = Remap(sz, facts)
    arrive_all(arrive)
    surface[...] = before[...]
    for slot in range(sz.slots):
        tile = pl.multiple_of(tile_at(sz, tables, 0, slot) * CHANNELS, CHANNELS)
        surface[pl.ds(tile, CHANNELS), :] = (
            before[pl.ds(tile, CHANNELS), :] + back[slot * CHANNELS : (slot + 1) * CHANNELS, :]
        )
    surface[CHANNELS * sz.tiles :, :] = jnp.zeros((CHANNELS, WIDTH), jnp.float32)
    told = told_sums(sz, from_first, from_second)
    lats = [lat_rows(sz, slope, lat) * told[lat] for lat in range(NEAR_LAT)]
    for row in range(rows):
        own = row_tiles_of(sz, surface, row)
        weights = [remap.own(lat, row) for lat in range(NEAR_LAT)]
        put_row_tiles(sz, surface, row, own + sum_of(weights, lats))
    store_rows(sz, surface, send_first, send_second, diffusivity)


def backward_load_kernel(sz, last, arrive, mix, diffusivity, field, drive, surface, *refs):
    refs = list(refs)
    if last:
        perturbation = refs.pop(0)
    mix_out, rows_out, local, bent_all, scaled = refs[:5]
    refs = refs[5:]
    if last:
        start_all = refs.pop(0)
    in_sems = refs[0]

    def arrivals(row):
        copies = [
            pltpu.make_async_copy(field.at[row], local.at[row], in_sems.at[0, row]),
            pltpu.make_async_copy(drive.at[row], bent_all.at[row], in_sems.at[1, row]),
        ]
        if last:
            copies.append(
                pltpu.make_async_copy(perturbation.at[row], start_all.at[row], in_sems.at[2, row])
            )
        return copies

    for row in range(sz.rows):
        for arrival in arrivals(row):
            arrival.start()
    arrive_all(arrive)
    mix_out[...] = mix[...]
    rows_out[...] = diffusivity[...]

    def one_row(row, carry):
        for arrival in arrivals(row):
            arrival.wait()
        load_surface_row(sz, local, row, surface, row * sz.row_width)
        for t in range(sz.row_tiles):
            coeff = jnp.broadcast_to(diffusivity[row, 0:1, cols(t)], (LEVELS, WIDTH))
            for c in range(CHANNELS):
                scaled[row, c, :, cols(t)] = coeff * local[row, c, :, cols(t)]
        return carry

    lax.fori_loop(0, sz.rows, one_row, 0)


def backward_kernel(sz, last, arrive, *refs):
    refs = list(refs)
    if not last:
        tables, weights, slope = refs[:3]
        refs = refs[3:]
    low, high, first_surface, second_surface, diffusivity, mix = refs[:6]
    local, bent_all, scaled_all = refs[6:9]
    refs = refs[9:]
    if last:
        start_all, out, sums, padded = refs
    else:
        out, new_surface, packed, tell_first, tell_second, edge_first, edge_second = refs[:7]
        padded, near_low, near_high = refs[7:]
        remap = Remap(sz, weights)
    count = sz.row_tiles
    place_edges(sz, padded, low, high, first_surface, second_surface)

    def ready(row):
        padded[row + 1] = scaled_all[row]

    ready(0)
    lane = lax.broadcasted_iota(jnp.int32, (LEVELS, WIDTH), 1)
    masks = level_masks()

    def one_row(row, carry):
        @pl.when(row < sz.rows - 1)
        def _():
            ready(row + 1)

        tiles = RowTiles(count, lambda c, t: padded[row + 1, c, :, cols(t)])
        for t in range(count):
            here, bent = [], []
            for c in range(CHANNELS):
                value = local[row, c, :, cols(t)]
                one = bent_all[row, c, :, cols(t)]
                here.append(value)
                bent.append((1.0 - one * one) * value)
            for c in range(CHANNELS):
                mixed = mix[c] * bent[0]
                for k in range(1, CHANNELS):
                    mixed = mixed + mix[k * CHANNELS + c] * bent[k]
                around = tiles.around(c, t, lane)
                around = around + (padded[row, c, :, cols(t)] + padded[row + 2, c, :, cols(t)])
                stepped = (
                    ((1.0 - 2.0 * KAPPA_V) * here[c] - 4.0 * tiles.here(c, t))
                    + around
                    + levels_sum(here[c], masks)
                    + TIME_STEP * mixed
                )
                out[row, c, :, cols(t)] = stepped
                if last:
                    start = start_all[row, c, :, cols(t)]
                    carry = (
                        carry[0] + start * start,
                        carry[1] + start * stepped,
                        carry[2] + stepped * stepped,
                    )
                else:
                    new_surface[pl.ds((row * count + t) * CHANNELS + c, 1), :] = stepped[0:1, :]
        out.row(row).start()
        return carry

    blank = jnp.zeros((LEVELS, WIDTH), jnp.float32)
    totals = lax.fori_loop(0, sz.rows, one_row, (blank, blank, blank) if last else 0)
    if last:
        place = lax.broadcasted_iota(jnp.int32, sums.block.shape, 1)
        held = jnp.zeros(sums.block.shape, jnp.float32)
        for index in range(3):
            total = jnp.sum(jnp.sum(totals[index], axis=0, keepdims=True), axis=1, keepdims=True)
            held = jnp.where(place == index, total, held)
        sums[...] = held
    else:
        new_surface[CHANNELS * sz.tiles :, :] = jnp.zeros((CHANNELS, WIDTH), jnp.float32)
        arrive_all(arrive)
        spread_back(
            sz,
            new_surface,
            slope,
            remap,
            tables,
            packed,
            near_low,
            near_high,
            tell_first,
            tell_second,
        )
        packed.start()
        store_edges(sz, out, diffusivity, edge_first, edge_second)


def final_kernel(cell_total, arrive, everyones, perturbation, gradient, out):
    sums = jnp.sum(everyones[...], axis=0, keepdims=True) / cell_total
    place = lax.broadcasted_iota(jnp.int32, sums.shape, 1)
    means = [
        jnp.broadcast_to(
            jnp.sum(jnp.where(place == index, sums, 0.0), axis=1, keepdims=True), (1, WIDTH)
        )
        for index in range(3)
    ]
    scale = lax.rsqrt(means[2] + EPSILON)
    mean_sq = means[0] + 2.0 * ASCENT * scale * means[1] + ASCENT * ASCENT * scale * scale * means[2]
    shrink = lax.rsqrt(mean_sq + EPSILON)
    step = jnp.broadcast_to(ASCENT * scale * shrink, (CHANNELS, WIDTH))
    shrink = jnp.broadcast_to(shrink, (CHANNELS, WIDTH))
    levels, rows, _, cells = perturbation.shape

    def one_level(level, carry):
        for row in range(rows):
            for tile in range(cells // WIDTH):
                start = perturbation[level, row, :, cols(tile)]
                slope = gradient[level, row, :, cols(tile)]
                out[level, row, :, cols(tile)] = shrink * start + step * slope
        out.row(level).start()
        return carry

    lax.fori_loop(0, levels, one_level, 0)


class Operand:
    def __init__(self, array, space, fetch=None, at=()):
        self.array, self.space, self.fetch, self.at = array, space, fetch, at

    def block(self):
        whole = self.array.shape
        taken = [size for size, index in zip(whole, self.at) if isinstance(index, slice)]
        return self.fetch((*taken, *whole[len(self.at) :]), self.array.dtype)


def near_by(*arrays):
    return [Operand(array, pltpu.VMEM) for array in arrays]


def far_off(*arrays):
    return [
        Operand(pltpu.with_memory_space_constraint(array, pltpu.HBM), pltpu.HBM)
        for array in arrays
    ]


def fetched(*arrays, at=(), into=pltpu.VMEM):
    return [
        Operand(pltpu.with_memory_space_constraint(array, pltpu.HBM), pltpu.HBM, into, at)
        for array in arrays
    ]


def scalars(*arrays):
    return fetched(*arrays, into=pltpu.SMEM)


def call(kernel, name, inputs, kept=(), shipped=(), scratch=()):
    n_in, n_kept, n_out = len(inputs), len(kept), len(shipped)
    brought = [index for index, item in enumerate(inputs) if item.fetch is not None]

    def as_shape(item):
        return item if isinstance(item, jax.ShapeDtypeStruct) else jax.ShapeDtypeStruct(item, jnp.float32)

    kept = [as_shape(item) for item in kept]
    shipped = [as_shape(item) for item in shipped]

    def run(*refs):
        ins = list(refs[:n_in])
        kept_refs = refs[n_in : n_in + n_kept]
        homes = refs[n_in + n_kept : n_in + n_kept + n_out]
        rest = refs[n_in + n_kept + n_out :]
        outs = [
            Shipped(block, home, sems)
            for block, home, sems in zip(rest[:n_out], homes, rest[n_out : 2 * n_out])
        ]
        rest = rest[2 * n_out :]
        if brought:
            blocks, arrive_sems = rest[: len(brought)], rest[len(brought)]
            rest = rest[len(brought) + 1 :]
            copies = []
            for place, (index, block) in enumerate(zip(brought, blocks)):
                source = ins[index]
                if inputs[index].at:
                    source = source.at[inputs[index].at]
                copies.append(pltpu.make_async_copy(source, block, arrive_sems.at[place]))
                ins[index] = block
            for copy in copies:
                copy.start()
            arrive = [copy.wait for copy in copies]
        else:
            arrive = []
        kernel(arrive, *ins, *kept_refs, *outs, *rest)
        for out in outs:
            if not out.started:
                out.start()
        for out in outs:
            out.finish(out.block.shape[0])

    spaces = [pltpu.VMEM] * n_kept + [pltpu.HBM] * n_out
    blocks = [pltpu.VMEM(item.shape, item.dtype) for item in shipped]
    sems = [
        pltpu.SemaphoreType.DMA((item.shape[0] if len(item.shape) > 3 else 1,)) for item in shipped
    ]
    arriving = [inputs[index].block() for index in brought]
    if brought:
        arriving.append(pltpu.SemaphoreType.DMA((len(brought),)))
    more = [
        item if not isinstance(item, tuple) else pltpu.VMEM(item, jnp.float32) for item in scratch
    ]
    return pl.pallas_call(
        run,
        name=name,
        in_specs=[pl.BlockSpec(memory_space=item.space) for item in inputs],
        out_specs=[pl.BlockSpec(memory_space=space) for space in spaces],
        out_shape=kept + [pltpu.HBM(item.shape, item.dtype) for item in shipped],
        scratch_shapes=blocks + sems + arriving + more,
        compiler_params=pltpu.CompilerParams(vmem_limit_bytes=VMEM_BYTES),
    )(*[item.array for item in inputs])


def arrive_all(arrive):
    for wait in arrive:
        wait()


def swap(first, second):
    count = lax.axis_size("horiz")
    inner = [(i, i ^ 1) for i in range(count)]
    outer = [(i, i + 1) for i in range(1, count - 1, 2)]
    outer = outer + [(target, source) for source, target in outer]
    return lax.ppermute(first, "horiz", inner), lax.ppermute(second, "horiz", outer)


def exchange(array, devices):
    rows = array.shape[0] // devices
    step = CHANNELS if rows % CHANNELS == 0 else 2
    split = array.reshape(devices, rows // step, step, WIDTH)
    moved = lax.all_to_all(split, "horiz", split_axis=0, concat_axis=0, tiled=True)
    return moved.reshape(array.shape)


def body(
    perturbation,
    base_state,
    target_state,
    cost_weight,
    diffusivity,
    chan_mix,
    coupler_mix,
    owner_mix,
    air_temp,
    wind_speed,
    wet_list,
    wet_owner,
    remap_src,
    remap_tgt,
    remap_weight,
):
    devices = lax.axis_size("horiz")
    hours = air_temp.shape[0]
    sz = Sizes(devices, air_temp.shape[2] // devices, base_state.shape[1], base_state.shape[3])
    rows = sz.rows
    native_row = (LEVELS, CHANNELS, sz.cells)

    edge_inputs = []
    for array in (perturbation, base_state):
        for row in (0, rows - 1):
            edge_inputs += fetched(array, at=(slice(None), row))
    edges = swap(
        *call(functools.partial(edges_kernel, sz), "edges", edge_inputs, kept=[sz.edge, sz.edge])
    )
    me = lax.axis_index("horiz").astype(jnp.int32)

    def lined(first_row, second_row):
        size = -(-first_row.shape[0] // WIDTH) * WIDTH
        pair = jnp.stack([first_row.astype(jnp.float32), second_row.astype(jnp.float32)])
        return jnp.pad(pair, ((0, 0), (0, size - pair.shape[1])), constant_values=-1.0)

    places = jnp.arange(CHANNELS * CHANNELS, dtype=jnp.int32) + sz.bulk_at
    remap_at = (remap_tgt - (me * LAT_DEV - 1)) * rows + remap_src - me * rows
    remap_lines = lined(
        jnp.concatenate([remap_at, places]),
        jnp.concatenate([remap_weight, coupler_mix.reshape(-1)]),
    )
    mix_rows = chan_mix.transpose(1, 2, 0).reshape(CHANNELS * CHANNELS, LEVELS)
    row_lines = (rows, 1, sz.cells)
    tiles_lines = (CHANNELS * sz.tiles, WIDTH)
    first_mix, first_rows, table, facts, line, mix = call(
        functools.partial(setup_kernel, sz, wet_list.shape[1], remap_at.shape[0] + places.shape[0]),
        "setup",
        near_by(lined(wet_list[0], wet_owner[0]), remap_lines, mix_rows)
        + fetched(diffusivity),
        kept=[(CHANNELS * CHANNELS, LEVELS, WIDTH), row_lines],
        shipped=[
            jax.ShapeDtypeStruct((sz.slot_lines, WIDTH), jnp.int32),
            (sz.facts, WIDTH),
            (1, WIDTH),
            (CHANNELS * CHANNELS, LEVELS, WIDTH),
        ],
    )
    wider = (rows + 2, CHANNELS, LEVELS, sz.cells)
    row_surface = (sz.row_width, WIDTH)
    by_row = (rows, *native_row)

    def row_sems(kinds):
        return pltpu.SemaphoreType.DMA((kinds, rows))

    (field,) = call(
        functools.partial(load_kernel, sz),
        "load",
        far_off(perturbation, base_state),
        kept=[sz.whole],
        scratch=[by_row, by_row, row_sems(2)],
    )

    def relayout(array):
        return call(
            functools.partial(relayout_kernel, sz),
            "relayout",
            far_off(array),
            shipped=[sz.whole],
            scratch=[by_row, row_sems(1)],
        )

    saved = []
    near = [sz.near, sz.near]
    mix_shape = (CHANNELS * CHANNELS, LEVELS, WIDTH)
    by_slot = (sz.slots, WIDTH)
    for hour in range(hours):
        first, last = hour == 0, hour == hours - 1
        assert not (first and last)
        inputs = scalars(table, line)
        if first:
            same = near_by(first_rows, first_mix, field)
            before = call(
                functools.partial(forward_kernel, sz, True, False, 1),
                "step_near",
                near_by(edges[0]) + same,
                kept=[sz.whole, sz.whole, sz.surface],
                scratch=[wider],
            )
            inputs += near_by(edges[1]) + same + fetched(facts) + near_by(*before)
        else:
            loads = fetched(mix, diffusivity_rows, *([weight_rows] if last else []))
            loads += far_off(field) + near_by(surface) + (far_off(target) if last else [])
            mix_here, rows_here, field, *more = call(
                functools.partial(forward_load_kernel, sz, last),
                "step_load",
                loads,
                kept=[mix_shape, row_lines, sz.whole] + ([row_lines, sz.whole] if last else []),
                scratch=[row_sems(2)],
            )
            inputs += near_by(*edges, rows_here, mix_here, field, *surface_edges, *more)
        field, drive, surface, packed, *sends = call(
            functools.partial(forward_kernel, sz, first, last, 2 if first else 0),
            "step",
            inputs,
            shipped=[sz.whole, sz.whole, sz.surface, sz.narrow]
            + [sz.told if first else sz.lats] * 2
            + [sz.edge] * 2,
            scratch=[wider],
        )
        arrived = exchange(packed, devices)
        got = swap(*sends[:2])
        arrived, *got = lax.optimization_barrier((arrived, *got))
        inputs = (
            near_by(arrived, owner_mix[0], air_temp[hour, 0], wind_speed[hour, 0])
            + scalars(line)
        )
        decoded = []
        if first:
            inputs += near_by(*got) + fetched(table, line)
            decoded = [jax.ShapeDtypeStruct(sz.tables, jnp.int32), sz.weights]
        *decoded, flux, mixed_slope, flux_slope = call(
            functools.partial(owner_kernel, sz, first),
            "owners",
            inputs,
            shipped=[*decoded, sz.wide, sz.by_slot, sz.by_slot],
            scratch=[sz.narrow, by_slot],
        )
        if first:
            tables, weights = decoded
        flux, *sends = lax.optimization_barrier((flux, *sends[2:]))
        if first:
            flux, diffusivity, target_state = lax.optimization_barrier(
                (flux, diffusivity, target_state)
            )
            beside = call(
                functools.partial(columns_kernel, sz),
                "columns",
                fetched(diffusivity, cost_weight),
                shipped=[row_lines, row_lines, tiles_lines, tiles_lines],
            ) + relayout(target_state)
        else:
            flux, perturbation = lax.optimization_barrier((flux, perturbation))
            beside = relayout(perturbation)
        flux = exchange(flux, devices)
        flux, *beside = lax.optimization_barrier((flux, *beside))
        if first:
            diffusivity_rows, weight_rows, diffusivity_tiles, weight_tiles, target = beside
        else:
            start_field = beside[0]
        edges = swap(*sends)
        inputs = near_by(flux, *got) + fetched(surface) + scalars(tables, weights)
        if last:
            surface, slope, packed, *sends = call(
                functools.partial(surface_kernel, sz, True),
                "surface",
                inputs + fetched(target_state, at=(0,)) + fetched(weight_tiles),
                shipped=[sz.surface, sz.slope, sz.wide, sz.lats, sz.lats],
                scratch=near,
            )
        else:
            surface, *sends, slope = call(
                functools.partial(surface_kernel, sz, False),
                "surface",
                inputs,
                kept=[sz.surface, row_surface, row_surface],
                shipped=[sz.slope],
                scratch=near,
            )
            surface_edges = swap(*sends)
        saved.append((drive, slope, mixed_slope, flux_slope))

    edge_sends = None
    for hour in reversed(range(hours)):
        drive, slope, mixed_slope, flux_slope = saved[hour]
        arrived = exchange(packed, devices)
        got = swap(*sends)
        arrived, *got = lax.optimization_barrier((arrived, *got))
        back = call(
            functools.partial(owner_back_kernel, sz),
            "owners_back",
            near_by(arrived, owner_mix[0]) + fetched(mixed_slope, flux_slope) + scalars(line),
            shipped=[sz.narrow],
            scratch=[sz.narrow, by_slot],
        )[0]
        if edge_sends is not None:
            back, *edge_sends = lax.optimization_barrier((back, *edge_sends))
            edges = swap(*edge_sends)
        back = exchange(back, devices)
        surface, *row_sends = call(
            functools.partial(merge_kernel, sz),
            "merge",
            near_by(back, *got)
            + fetched(surface, slope)
            + scalars(table, line)
            + fetched(diffusivity_tiles),
            kept=[sz.surface, row_surface, row_surface],
        )
        surface_edges = swap(*row_sends)
        last = hour == 0
        mix_here, rows_here, *loaded = call(
            functools.partial(backward_load_kernel, sz, last),
            "step_back_load",
            fetched(mix, diffusivity_rows)
            + far_off(field, drive)
            + near_by(surface)
            + (far_off(start_field) if last else []),
            kept=[mix_shape, row_lines] + [sz.whole] * (4 if last else 3),
            scratch=[row_sems(3)],
        )
        inputs = near_by(*edges, *surface_edges, rows_here, mix_here, *loaded)
        if last:
            gradient, sums = call(
                functools.partial(backward_kernel, sz, True),
                "step_back_sums",
                inputs,
                shipped=[sz.whole, (devices, WIDTH)],
                scratch=[wider],
            )
        else:
            field, surface, packed, *outs = call(
                functools.partial(backward_kernel, sz, False),
                "step_back",
                scalars(tables, weights) + fetched(saved[hour - 1][1]) + inputs,
                shipped=[sz.whole, sz.surface, sz.wide, sz.lats, sz.lats, sz.edge, sz.edge],
                scratch=[wider, *near],
            )
            sends, edge_sends = outs[:2], outs[2:]

    everyones = lax.all_to_all(sums, "horiz", split_axis=0, concat_axis=0, tiled=True)
    block = perturbation.shape
    return call(
        functools.partial(final_kernel, perturbation.size * devices),
        "finish",
        near_by(everyones, perturbation, gradient.transpose(2, 0, 1, 3)),
        shipped=[block],
    )[0]


def solution(mesh):
    placed = (
        P("member", "horiz", None, None),
        P(None, "horiz", None, None),
        P(None, "horiz", None, None),
        P("horiz", None),
        P("horiz", None),
        P(),
        P(),
        P("horiz", None, None),
        P(None, "horiz", None, None),
        P(None, "horiz", None, None),
        P("horiz", None),
        P("horiz", None),
        P("horiz"),
        P("horiz"),
        P("horiz"),
    )
    return jax.shard_map(
        body,
        mesh=mesh,
        in_specs=placed,
        out_specs=P("member", "horiz", None, None),
        check_vma=False,
    )
```
